32 devices in a mesh: fsdp: 32 (over z, y, x, core).
Axes of the slice: x: 2, y: 2, z: 4, core: 2. Of those that a mesh axis runs over, the one named last changes fastest.
Arguments:
- src_in: bfloat16 [32768, 512], P('fsdp'), may hold values from -6 to 6
- tgt_in: bfloat16 [32768, 512], P('fsdp'), may hold values from -6 to 6
- src_len: int32 [32, 16], P('fsdp'), may hold values from 0 to 250, as said below
- tgt_len: int32 [32, 16], P('fsdp'), may hold values from 0 to 250, as said below
- tgt_mask: int32 [32768], P('fsdp'), may hold values 0 or 1
- enc_cot: bfloat16 [32768, 512], P('fsdp'), may hold values from -6 to 6
- dec_cot: bfloat16 [32768, 512], P('fsdp'), may hold values from -6 to 6
- enc_master: float32 [6144, 512], P('fsdp')
- enc_first: float32 [6144, 512], P('fsdp')
- enc_second: float32 [6144, 512], P('fsdp'), as said below
- dec_master: float32 [8192, 512], P('fsdp')
- dec_first: float32 [8192, 512], P('fsdp')
- dec_second: float32 [8192, 512], P('fsdp'), as said below
- small_master: float32 [11, 512], P(None, 'fsdp')
- small_first: float32 [11, 512], P(None, 'fsdp')
- small_second: float32 [11, 512], P(None, 'fsdp'), as said below
Outputs:
- enc_out: bfloat16 [32768, 512], P('fsdp')
- dec_out: bfloat16 [32768, 512], P('fsdp')
- src_grad: float32 [32768, 512], P('fsdp')
- tgt_grad: float32 [32768, 512], P('fsdp')
- enc_new: float32 [6144, 512], P('fsdp')
- enc_first_new: float32 [6144, 512], P('fsdp')
- encoder_second_moment_updated: float32 [6144, 512], P('fsdp')
- enc_copy_new: bfloat16 [6144, 512], P('fsdp')
- dec_new: float32 [8192, 512], P('fsdp')
- dec_first_new: float32 [8192, 512], P('fsdp')
- dec_second_new: float32 [8192, 512], P('fsdp')
- dec_copy_new: bfloat16 [8192, 512], P('fsdp')
- small_grad: float32 [11, 512], P(None, 'fsdp')
- small_first_new: float32 [11, 512], P(None, 'fsdp')
- small_second_new: float32 [11, 512], P(None, 'fsdp')
The draws below stay inside these ranges and needn't reach their ends.
Inputs may be any that keep to these rules, and one draw needn't show every extreme that they name: `src_len`: nonzero lengths are at least 5; zeros stand only after all nonzero entries of a row; a row sums to at most 1024; every row holds the length 250. `tgt_len`: zero exactly where src_len is zero; nonzero lengths are at least 5; a row sums to at most 1024; every row holds the length 250. `enc_second`: Positive. `dec_second`: Positive. `small_second`: Positive.
All inputs are finite; a program needn't handle non-finite values. No bound on the sum of `tgt_mask` on one device may be relied on, other than what follows from the above.
Results may differ from the reference program's by a relative error of at most 0.02.
The reference program's roundings to bfloat16 on the way count: a program that leaves them out, or rounds other values in their place, can miss the bound.
Values may be sent and summed in bfloat16 or wider, within the bound.
No kernel may reach another device: no remote copies, remote signals or barrier semaphores. Data moves between devices by JAX's collectives and lax.ppermute only.
A program may use at most 256 MiB of HBM per device.

```python
import jax
import jax.numpy as jnp
from jax import lax

D = 512
HEADS = 8
HEAD_DIM = 64
FF = 2048
SRC_DEV = 1024
LONGEST = 250
SHORTEST = 5
STEPS = 7
TGT_DEV = 1024
PAIRS = 16
BUCKETS = 32
SRC_TOKENS = 32768
TGT_TOKENS = 32768
ENC_ROWS = 6144
DEC_ROWS = 8192
SMALL_ROWS = 11


def spread_draw(key, shape, low_end, high_end):
    return jnp.exp(jax.random.uniform(key, shape, jnp.float32, jnp.log(low_end), jnp.log(high_end)))


def enc_profile():
    rows = jnp.arange(ENC_ROWS)
    column_part = rows % 3
    std_rows = jnp.where(rows < 3 * D, jnp.where(column_part < 2, 1.3, 1.0), jnp.where(rows < 4 * D, 5.0, jnp.where(rows < 4 * D + FF, 1.0, 1.4 * (D / FF) ** 0.5))) / D ** 0.5
    grad_rows = jnp.where(rows < 3 * D, jnp.where(column_part < 2, 0.15, 0.3), jnp.where(rows < 4 * D, 0.3, jnp.where(rows < 4 * D + FF, 0.35, 0.6))) * SRC_TOKENS ** 0.5 / BUCKETS
    return (std_rows, grad_rows)


def dec_profile():
    rows = jnp.arange(DEC_ROWS)
    column_part = rows % 3
    pair_part = rows % 2
    std_rows = jnp.where(rows < 3 * D, jnp.where(column_part < 2, 1.3, 1.0), jnp.where(rows < 4 * D, 5.0, jnp.where(rows < 5 * D, 1.3, jnp.where(rows < 7 * D, jnp.where(pair_part < 1, 1.3, 1.0), jnp.where(rows < 8 * D, 5.0, jnp.where(rows < 8 * D + FF, 1.0, 1.4 * (D / FF) ** 0.5)))))) / D ** 0.5
    grad_rows = jnp.where(rows < 3 * D, jnp.where(column_part < 2, 0.15, 0.3), jnp.where(rows < 4 * D, 0.3, jnp.where(rows < 5 * D, 0.15, jnp.where(rows < 7 * D, jnp.where(pair_part < 1, 0.15, 0.3), jnp.where(rows < 8 * D, 0.3, jnp.where(rows < 8 * D + FF, 0.35, 0.6)))))) * TGT_TOKENS ** 0.5 / BUCKETS
    return (std_rows, grad_rows)


def small_profile():
    rows = jnp.arange(SMALL_ROWS)
    return jnp.where(rows < 4, SRC_TOKENS ** 0.5, jnp.where(rows < 10, TGT_TOKENS ** 0.5, 0.5 * TGT_TOKENS ** 0.5)) / BUCKETS


def first_moment(key, shape, grad_rows):
    keys = jax.random.split(key, 2)
    signs = jnp.where(jax.random.bernoulli(keys[0], 0.5, shape), 1.0, -1.0)
    return (signs * spread_draw(keys[1], shape, 0.5, 2.0) * (grad_rows[:, None] / 9.0)).astype(jnp.float32)


def second_moment(key, shape, grad_rows):
    return (spread_draw(key, shape, 0.5, 8.0) * (grad_rows[:, None] ** 2 / 49.0)).astype(jnp.float32)


def draw_enc_master(key, part):
    std_rows, grad_rows = enc_profile()
    values = jnp.clip(jax.random.normal(jax.random.fold_in(key, 101), (ENC_ROWS, D), jnp.float32), -4.0, 4.0)
    return values * std_rows[:, None]


def draw_enc_first(key, part):
    std_rows, grad_rows = enc_profile()
    return first_moment(jax.random.fold_in(key, 102), (ENC_ROWS, D), grad_rows)


def draw_enc_second(key, part):
    std_rows, grad_rows = enc_profile()
    return second_moment(jax.random.fold_in(key, 103), (ENC_ROWS, D), grad_rows)


def draw_dec_master(key, part):
    std_rows, grad_rows = dec_profile()
    values = jnp.clip(jax.random.normal(jax.random.fold_in(key, 201), (DEC_ROWS, D), jnp.float32), -4.0, 4.0)
    return values * std_rows[:, None]


def draw_dec_first(key, part):
    std_rows, grad_rows = dec_profile()
    return first_moment(jax.random.fold_in(key, 202), (DEC_ROWS, D), grad_rows)


def draw_dec_second(key, part):
    std_rows, grad_rows = dec_profile()
    return second_moment(jax.random.fold_in(key, 203), (DEC_ROWS, D), grad_rows)


def draw_small_master(key, part):
    keys = jax.random.split(jax.random.fold_in(key, 301), 2)
    rows = jnp.arange(SMALL_ROWS)[:, None]
    gains = jax.random.uniform(keys[0], (SMALL_ROWS, D), jnp.float32, 0.7, 1.3)
    normals = jnp.clip(jax.random.normal(keys[1], (SMALL_ROWS, D), jnp.float32), -4.0, 4.0)
    is_gain = (rows % 2 == 0) & (rows < 10)
    return jnp.where(is_gain, gains, jnp.where(rows < 10, 0.3 * normals, normals))


def draw_small_first(key, part):
    return first_moment(jax.random.fold_in(key, 302), (SMALL_ROWS, D), small_profile())


def draw_small_second(key, part):
    return second_moment(jax.random.fold_in(key, 303), (SMALL_ROWS, D), small_profile())


def pair_lengths(key):
    keys = jax.random.split(jax.random.fold_in(key, 401), 4)
    source = jax.random.randint(keys[0], (BUCKETS, PAIRS), SHORTEST, LONGEST + 1)
    target = jax.random.randint(keys[1], (BUCKETS, PAIRS), SHORTEST, LONGEST + 1)
    spot_source = jax.random.randint(keys[2], (BUCKETS, 1), 0, 2)
    spot_target = jax.random.randint(keys[3], (BUCKETS, 1), 0, 2)
    column = jnp.arange(PAIRS)[None, :]
    source = jnp.where(column == spot_source, LONGEST, source)
    target = jnp.where(column == spot_target, LONGEST, target)
    keeping = (jnp.cumsum(source, axis=1) <= SRC_DEV) & (jnp.cumsum(target, axis=1) <= TGT_DEV)
    return (jnp.where(keeping, source, 0).astype(jnp.int32), jnp.where(keeping, target, 0).astype(jnp.int32))


def draw_src_len(key, part):
    return pair_lengths(key)[0]


def draw_tgt_len(key, part):
    return pair_lengths(key)[1]


def plant(entries, rng, least, top_value):
    dims = entries.shape
    spot = [jax.random.randint(jax.random.fold_in(rng, axis), (), 0, dims[axis]) for axis in range(len(dims))]
    entries = entries.at[tuple(spot)].set(least)
    longest = dims.index(max(dims))
    spot[longest] = (spot[longest] + 1) % dims[longest]
    return entries.at[tuple(spot)].set(top_value)


def level_of(own_key, dims, cuts, smallest, largest):
    def one(position, blocks):
        draws = jax.random.uniform(jax.random.fold_in(jax.random.fold_in(own_key, 6), position), (blocks,), jnp.float32, smallest / len(cuts), largest / len(cuts))
        return jnp.repeat(jnp.exp(draws), dims[position] // blocks).reshape((-1,) + (1,) * (len(dims) - position - 1))

    level = one(*cuts[0])
    for cut in cuts[1:]:
        level = level * one(*cut)
    return level


def scatter_about(own_key, shape, deviation, most, cuts=(), kind=jnp.bfloat16):
    drawn = jax.random.normal(own_key, shape, jnp.float32) * deviation
    if len(cuts) > 0:
        drawn = level_of(own_key, shape, cuts, -0.22, 0.18) * drawn
    return jnp.clip(drawn, min=-most, max=most).astype(kind)


def setup_inputs(seed: int = 0) -> dict:
    key_list = jax.random.split(jax.random.key(seed), 17)
    return {
        "src_in": scatter_about(key_list[0], (SRC_TOKENS, D), 1.0, 6.0, ((0, 32),)),
        "tgt_in": scatter_about(key_list[1], (TGT_TOKENS, D), 1.0, 6.0, ((0, 32),)),
        "src_len": draw_src_len(jax.random.fold_in(key_list[16], 71), 0),
        "tgt_len": draw_tgt_len(jax.random.fold_in(key_list[16], 71), 0),
        "tgt_mask": plant((jax.random.randint(key_list[4], (TGT_TOKENS,), 0, 2) < 1).astype(jnp.int32), jax.random.fold_in(key_list[4], 1), 0, 1),
        "enc_cot": scatter_about(key_list[5], (SRC_TOKENS, D), 1.0, 6.0, ((0, 32),)),
        "dec_cot": scatter_about(key_list[6], (TGT_TOKENS, D), 1.0, 6.0, ((0, 32),)),
        "enc_master": draw_enc_master(jax.random.fold_in(key_list[16], 71), 0),
        "enc_first": draw_enc_first(jax.random.fold_in(key_list[16], 71), 0),
        "enc_second": draw_enc_second(jax.random.fold_in(key_list[16], 71), 0),
        "dec_master": draw_dec_master(jax.random.fold_in(key_list[16], 71), 0),
        "dec_first": draw_dec_first(jax.random.fold_in(key_list[16], 71), 0),
        "dec_second": draw_dec_second(jax.random.fold_in(key_list[16], 71), 0),
        "small_master": draw_small_master(jax.random.fold_in(key_list[16], 71), 0),
        "small_first": draw_small_first(jax.random.fold_in(key_list[16], 71), 0),
        "small_second": draw_small_second(jax.random.fold_in(key_list[16], 71), 0),
    }


highest = lax.Precision.HIGHEST
rate = 0.02
beta_one = 0.9
beta_two = 0.98
epsilon = 1e-06
decay = 0.01

@jax.custom_vjp
def low(v):
    return lax.optimization_barrier(v.astype(jnp.bfloat16)).astype(jnp.float32)

@jax.custom_vjp
def low_back(v):
    return v

def low_keep(v):
    return (low(v), None)

def low_pass(kept, grad):
    return (grad,)

def back_keep(v):
    return (v, None)

def back_low(kept, grad):
    return (low(grad),)
low.defvjp(low_keep, low_pass)
low_back.defvjp(back_keep, back_low)

def product(former, latter):
    return jnp.dot(former, latter, precision=highest)

def smooth_gate(values):
    return jax.nn.gelu(values, approximate=False)

def norm_forward(values, gain_row, shift_row):
    average = lax.optimization_barrier(jnp.mean(values, axis=-1, keepdims=True))
    centered = values - average
    spread = lax.optimization_barrier(jnp.mean(centered * centered, axis=-1, keepdims=True))
    return centered * lax.rsqrt(spread + 1e-05) * gain_row + shift_row

def segments(lengths, number):
    bounds = jnp.cumsum(lengths).astype(jnp.int32)
    places = jnp.arange(number, dtype=jnp.int32)
    owners = lax.optimization_barrier(jnp.sum((places[:, None] >= bounds[None, :]).astype(jnp.int32), axis=1))
    return (owners, places < bounds[-1])

def attention(queries, key_rows, value_rows, allowed):
    query_heads = queries.reshape(queries.shape[0], HEADS, HEAD_DIM)
    key_heads = key_rows.reshape(key_rows.shape[0], HEADS, HEAD_DIM)
    value_heads = value_rows.reshape(value_rows.shape[0], HEADS, HEAD_DIM)
    scores = jnp.einsum('qhd,khd->hqk', query_heads, key_heads, precision=highest) * HEAD_DIM ** (-0.5)
    scores = low_back(jnp.where(allowed[None], scores, -1000000000.0))
    weights = low(jax.nn.softmax(scores, axis=-1))
    context = jnp.einsum('hqk,khd->qhd', weights, value_heads, precision=highest)
    return context.reshape(queries.shape[0], HEADS * HEAD_DIM)

def enc_split(rows):
    inner = (rows.shape[0] - 4 * D) // 2
    return (rows[:3 * D].reshape(D, 3 * D), rows[3 * D:4 * D], rows[4 * D:4 * D + inner].reshape(D, inner), rows[4 * D + inner:].reshape(inner, D))

def dec_split(rows):
    inner = (rows.shape[0] - 8 * D) // 2
    return (rows[:3 * D].reshape(D, 3 * D), rows[3 * D:4 * D], rows[4 * D:5 * D], rows[5 * D:7 * D].reshape(D, 2 * D), rows[7 * D:8 * D], rows[8 * D:8 * D + inner].reshape(D, inner), rows[8 * D + inner:].reshape(inner, D))

def bucket_layers(enc_parts, dec_parts, smalls, source, target, src_lengths, tgt_lengths, masked_row):
    qkv_w, out_w, up_w, down_w = enc_parts
    sqkv_w, sout_w, cq_w, ckv_w, cout_w, dup_w, ddown_w = dec_parts
    src_owners, src_filled = segments(src_lengths, SRC_DEV)
    tgt_owners, tgt_filled = segments(tgt_lengths, TGT_DEV)
    enc_allowed = (src_owners[:, None] == src_owners[None, :]) & src_filled[None, :]
    self_allowed = (tgt_owners[:, None] == tgt_owners[None, :]) & tgt_filled[None, :]
    cross_allowed = (tgt_owners[:, None] == src_owners[None, :]) & src_filled[None, :]
    src_live = src_filled.astype(jnp.float32)[:, None]
    tgt_live = tgt_filled.astype(jnp.float32)[:, None]
    enc_qkv = low(low_back(product(source, qkv_w)))
    enc_context = low(low_back(attention(enc_qkv[:, :D], enc_qkv[:, D:2 * D], enc_qkv[:, 2 * D:], enc_allowed)))
    enc_attn = low_back(product(enc_context, out_w)) * src_live
    enc_mid = norm_forward(source + enc_attn, smalls[0], smalls[1])
    enc_inner = low_back(product(low(enc_mid), up_w))
    enc_hidden = low(smooth_gate(enc_inner))
    encoded = norm_forward(enc_mid + low_back(product(enc_hidden, down_w)), smalls[2], smalls[3])
    start = jnp.where(masked_row[:, None] == 1, smalls[10][None, :], target)
    self_qkv = low(low_back(product(start, sqkv_w)))
    self_context = low(low_back(attention(self_qkv[:, :D], self_qkv[:, D:2 * D], self_qkv[:, 2 * D:], self_allowed)))
    self_attn = low_back(product(self_context, sout_w)) * tgt_live
    dec_one = norm_forward(start + self_attn, smalls[4], smalls[5])
    cross_query = low(low_back(product(low(dec_one), cq_w)))
    cross_pair = low(low_back(product(low(encoded), ckv_w)))
    cross_context = low(low_back(attention(cross_query, cross_pair[:, :D], cross_pair[:, D:], cross_allowed)))
    cross_attn = low_back(product(cross_context, cout_w)) * tgt_live
    dec_two = norm_forward(dec_one + cross_attn, smalls[6], smalls[7])
    dec_inner = low_back(product(low(dec_two), dup_w))
    dec_hidden = low(smooth_gate(dec_inner))
    decoded = norm_forward(dec_two + low_back(product(dec_hidden, ddown_w)), smalls[8], smalls[9])
    return (encoded, decoded)

def moments(gradient, first, second):
    first_new = beta_one * first + (1.0 - beta_one) * gradient
    second_new = beta_two * second + (1.0 - beta_two) * gradient * gradient
    return (first_new, second_new)

def adamw(weight, gradient, first, second):
    first_new, second_new = moments(gradient, first, second)
    moved = weight - rate * (first_new / (1.0 - beta_one ** STEPS) / (jnp.sqrt(second_new / (1.0 - beta_two ** STEPS)) + epsilon) + decay * weight)
    return (moved, first_new, second_new)

def reference(src_in, tgt_in, src_len, tgt_len, tgt_mask, enc_cot, dec_cot, enc_master, enc_first, enc_second, dec_master, dec_first, dec_second, small_master, small_first, small_second):
    source_all = src_in.astype(jnp.float32)
    target_all = tgt_in.astype(jnp.float32)

    def forward(enc_weights, dec_weights, small_weights, sources, targets):
        enc_parts = enc_split(low(enc_weights))
        dec_parts = dec_split(low(dec_weights))
        smalls = low(small_weights)

        def one_bucket(bucket_items):
            source, target, src_lengths, tgt_lengths, masked_row = bucket_items
            return bucket_layers(enc_parts, dec_parts, smalls, source, target, src_lengths, tgt_lengths, masked_row)
        encoded, decoded = lax.map(jax.checkpoint(one_bucket), (sources.reshape(BUCKETS, SRC_DEV, D), targets.reshape(BUCKETS, TGT_DEV, D), src_len, tgt_len, tgt_mask.reshape(BUCKETS, TGT_DEV)))
        return (encoded.reshape(-1, D), decoded.reshape(-1, D))
    (encoded, decoded), pullback = jax.vjp(forward, enc_master, dec_master, small_master, source_all, target_all)
    enc_grad, dec_grad, small_grad, src_grad, tgt_grad = pullback((enc_cot.astype(jnp.float32), dec_cot.astype(jnp.float32)))
    enc_grad = enc_grad / BUCKETS
    dec_grad = dec_grad / BUCKETS
    small_grad = small_grad / BUCKETS
    enc_new, enc_first_new, encoder_second_moment_updated = adamw(enc_master, enc_grad, enc_first, enc_second)
    dec_new, dec_first_new, dec_second_new = adamw(dec_master, dec_grad, dec_first, dec_second)
    small_first_new, small_second_new = moments(small_grad, small_first, small_second)
    return (encoded.astype(jnp.bfloat16), decoded.astype(jnp.bfloat16), src_grad, tgt_grad, enc_new, enc_first_new, encoder_second_moment_updated, enc_new.astype(jnp.bfloat16), dec_new, dec_first_new, dec_second_new, dec_new.astype(jnp.bfloat16), small_grad, small_first_new, small_second_new)
```

```python
import functools

import jax
import jax.numpy as jnp
from jax import lax
from jax.experimental import pallas as pl
from jax.experimental.pallas import tpu as pltpu
from jax.sharding import PartitionSpec as P

HEADS = 8
HEAD = 64
STEPS = 7
TILE = 256
LANES = 128

rate = 0.02
beta_one = 0.9
beta_two = 0.98
epsilon = 1e-06
decay = 0.01
floor_value = -1000000000.0
root_half = 0.7071067811865476
inverse_root_tau = 0.3989422804014327

F32 = jnp.float32
LOW = jnp.bfloat16
VMEM_BYTES = 56 * 2**20


def nn(former, latter):
    return lax.dot_general(
        former, latter, (((1,), (0,)), ((), ())), preferred_element_type=F32
    )


def nt(former, latter):
    return lax.dot_general(
        former, latter, (((1,), (1,)), ((), ())), preferred_element_type=F32
    )


def turned(values):
    return values.astype(F32).T.astype(LOW)


def column_of(row):
    return jnp.broadcast_to(row, (8, row.shape[1])).T[:, 0:1]


def ln_forward(values, gain, shift):
    centered = values - jnp.mean(values, axis=-1, keepdims=True)
    spread = jnp.mean(centered * centered, axis=-1, keepdims=True)
    inverse = lax.rsqrt(spread + 1e-05)
    normed = centered * inverse
    return normed * gain + shift, normed, inverse


def ln_backward(upstream, normed, inverse, gain):
    scaled = upstream * gain
    first = jnp.mean(scaled, axis=-1, keepdims=True)
    second = jnp.mean(scaled * normed, axis=-1, keepdims=True)
    return inverse * (scaled - first - normed * second)


def phi_and_slope(values):
    size = jnp.abs(values)
    bell = jnp.exp(-0.5 * (values * values))
    part = 1.0 / (1.0 + (0.3275911 * root_half) * size)
    series = part * (
        0.254829592
        + part
        * (-0.284496736 + part * (1.421413741 + part * (-1.453152027 + part * 1.061405429)))
    )
    half_tail = (0.5 * series) * bell
    phi = jnp.where(values >= 0, 1.0 - half_tail, half_tail)
    return phi, phi + values * (bell * inverse_root_tau)


def one_head(pair, head):
    lane = lax.broadcasted_iota(jnp.int32, pair.shape, 1)
    keep = lane < HEAD if head % 2 == 0 else lane >= HEAD
    return jnp.where(keep, pair, jnp.zeros_like(pair))


def pair_columns(head):
    return slice(LANES * (head // 2), LANES * (head // 2) + LANES)


def head_rows(head):
    return slice(HEAD * head, HEAD * head + HEAD)


def block_of(ref, j):
    if len(ref.shape) == 4:
        return ref[:, j].reshape(ref.shape[0] * ref.shape[2], ref.shape[3])
    return ref[j]


def put_block(ref, j, values):
    if len(ref.shape) == 4:
        ref[:, j] = values.reshape(ref.shape[0], ref.shape[2], ref.shape[3])
    else:
        ref[j] = values


def call(kernel, grid, in_specs, out_specs, out_shape, scratch, flops, moved, name):
    return pl.pallas_call(
        kernel,
        grid_spec=pltpu.PrefetchScalarGridSpec(
            num_scalar_prefetch=1,
            grid=grid,
            in_specs=in_specs,
            out_specs=out_specs,
            scratch_shapes=scratch,
        ),
        out_shape=out_shape,
        compiler_params=pltpu.CompilerParams(vmem_limit_bytes=VMEM_BYTES),
        cost_estimate=pl.CostEstimate(
            flops=flops, bytes_accessed=moved, transcendentals=0
        ),
        name=name,
    )


def whole(shape):
    zeros = (0,) * len(shape)
    return pl.BlockSpec(shape, lambda i, *_: zeros)


def rows_of(width):
    return pl.BlockSpec((TILE, width), lambda i, *_: (i, 0))


def at_block(shape, *index):
    return pl.BlockSpec(shape, lambda i, *_: index)


def shaped(shape, kind):
    return jax.ShapeDtypeStruct(shape, kind)


def attend_tile(plan, i, keys, key_cols, query, owner_row, key_owner, vt, sc):
    scores, acc, top, total, masked_q = sc
    query = query * jnp.asarray(HEAD**-0.5, LOW)
    for h in range(HEADS):
        masked_q[h] = one_head(query[:, pair_columns(h)], h)
    top[...] = jnp.full_like(top, -1e30)
    total[...] = jnp.zeros_like(total)
    acc[...] = jnp.zeros_like(acc)
    lo = plan[0, i]
    hi = plan[1, i]

    def score_tile(j, carry):
        rows = pl.ds(pl.multiple_of(j * TILE, TILE), TILE)
        bias = jnp.where(key_owner[rows, 0:1] == owner_row, 0.0, floor_value)
        tops = []
        for h in range(HEADS):
            cols = pl.ds(key_cols + LANES * (h // 2), LANES)
            s = nt(keys[rows, cols], masked_q[h]) + bias
            scores[j, h] = s
            tops.append(jnp.max(s, axis=0, keepdims=True))
        top[...] = jnp.maximum(top[...], jnp.concatenate(tops, axis=0))
        return carry

    lax.fori_loop(lo, hi, score_tile, 0)

    def weigh_tile(j, carry):
        rows = pl.ds(pl.multiple_of(j * TILE, TILE), TILE)
        sums = []
        for h in range(HEADS):
            p = jnp.exp(scores[j, h] - top[h : h + 1, :])
            sums.append(jnp.sum(p, axis=0, keepdims=True))
            acc[head_rows(h), :] += nn(vt[head_rows(h), rows], p.astype(LOW))
        total[...] += jnp.concatenate(sums, axis=0)
        return carry

    lax.fori_loop(lo, hi, weigh_tile, 0)


def fwd_block_kernel(plan, *refs, cross, gain_row):
    if cross:
        (normed_in, memory, wq, wk_a, wk_b, wo, small, owner_q, owner_k,
         q_out, kv_out, ctx_out, lse_out, normed_out, inverse_out,
         kv, vt, mean_v, key_owner, scores, acc, top, total, masked_q) = refs
    else:
        (x_all, wqkv, wo, small, owner_q, owner_k,
         q_out, kv_out, ctx_out, lse_out, normed_out, inverse_out,
         kv, vt, mean_v, key_owner, scores, acc, top, total, masked_q, q_all) = refs
    i = pl.program_id(0)
    width = kv.shape[1] // 2

    @pl.when(i == 0)
    def _():
        key_owner[...] = jnp.broadcast_to(owner_k[...], (8, owner_k.shape[1])).T
        if cross:
            wk = jnp.concatenate([block_of(wk_a, 0), block_of(wk_b, 0)], axis=0)
            wv = jnp.concatenate([block_of(wk_a, 1), block_of(wk_b, 1)], axis=0)
        else:
            wq_all = block_of(wqkv, 0)
            wk = block_of(wqkv, 1)
            wv = block_of(wqkv, 2)
        sums = jnp.zeros((1, width), F32)
        for t in range(kv.shape[0] // TILE):
            rows = slice(t * TILE, t * TILE + TILE)
            x = memory[rows, :] if cross else x_all[rows, :]
            if not cross:
                q_all[rows, :] = nn(x, wq_all).astype(LOW)
            kv[rows, :width] = nn(x, wk).astype(LOW)
            v = nn(x, wv).astype(LOW)
            kv[rows, width:] = v
            v = v.astype(F32)
            vt[:, rows] = v.T.astype(LOW)
            sums = sums + jnp.sum(v, axis=0, keepdims=True)
        mean_v[...] = sums * (1.0 / kv.shape[0])

    mine = pl.ds(pl.multiple_of(i * TILE, TILE), TILE)
    if cross:
        resid = normed_in[...] * small[4:5, :] + small[5:6, :]
        query = nn(resid.astype(LOW), wq[...]).astype(LOW)
        q_out[...] = query
    else:
        resid = x_all[mine, :].astype(F32)
        query = q_all[mine, :]
        q_out[...] = query
    kv_out[...] = kv[mine, :]
    owner_row = owner_q[...]
    attend_tile(plan, i, kv, 0, query, owner_row, key_owner, vt, (scores, acc, top, total, masked_q))
    dead = owner_row < 0
    sums = jnp.where(dead, 1.0, total[...])
    share = 1.0 / sums
    lse_out[...] = jnp.where(dead, 0.0, top[...] + jnp.log(sums))
    for h in range(HEADS):
        acc[head_rows(h), :] = acc[head_rows(h), :] * share[h : h + 1, :]
    live = column_of(owner_row) >= 0
    context = jnp.where(live, acc[...].T, mean_v[...]).astype(LOW)
    ctx_out[...] = context
    added = nn(context, wo[...]) * live.astype(F32)
    _, normed, inverse = ln_forward(
        resid + added, small[gain_row : gain_row + 1, :], small[gain_row + 1 : gain_row + 2, :]
    )
    normed_out[...] = normed
    inverse_out[...] = jnp.broadcast_to(inverse, inverse_out.shape)


def attention_scratch(keys, width):
    return [
        pltpu.VMEM((keys, 2 * width), LOW),
        pltpu.VMEM((width, keys), LOW),
        pltpu.VMEM((1, width), F32),
        pltpu.VMEM((keys, 8), F32),
        pltpu.VMEM((keys // TILE, HEADS, TILE, TILE), F32),
        pltpu.VMEM((width, TILE), F32),
        pltpu.VMEM((HEADS, TILE), F32),
        pltpu.VMEM((HEADS, TILE), F32),
        pltpu.VMEM((HEADS, TILE, LANES), LOW),
    ]


def block_outs(queries, width):
    specs = [
        rows_of(width),
        rows_of(2 * width),
        rows_of(width),
        pl.BlockSpec((HEADS, TILE), lambda i, *_: (0, i)),
        rows_of(width),
        rows_of(LANES),
    ]
    shapes = [
        shaped((queries, width), LOW),
        shaped((queries, 2 * width), LOW),
        shaped((queries, width), LOW),
        shaped((HEADS, queries), F32),
        shaped((queries, width), F32),
        shaped((queries, LANES), F32),
    ]
    return specs, shapes


def owner_specs(keys):
    return [pl.BlockSpec((1, TILE), lambda i, *_: (0, i)), whole((1, keys))]


def self_block(plan, x, wqkv, wqkv_spec, wo, wo_spec, small, gain_row, owner, key_owner, name):
    number, width = x.shape
    specs, shapes = block_outs(number, width)
    return call(
        functools.partial(fwd_block_kernel, cross=False, gain_row=gain_row),
        (number // TILE,),
        [whole(x.shape), wqkv_spec, wo_spec, whole(small.shape)] + owner_specs(number),
        specs,
        shapes,
        attention_scratch(number, width) + [pltpu.VMEM((number, width), LOW)],
        8 * number * width * width + number * number * width * 2,
        16 * number * width,
        name,
    )(plan, x, wqkv, wo, small, owner, key_owner)


def cross_block(plan, normed, memory, dec_rows, wk_two, small, owner, key_owner):
    number, width = normed.shape
    specs, shapes = block_outs(number, width)
    half = (width // 32, 2, 16, width)
    return call(
        functools.partial(fwd_block_kernel, cross=True, gain_row=6),
        (number // TILE,),
        [
            rows_of(width),
            whole(memory.shape),
            at_block((width, width), 4, 0),
            at_block(half, 5, 0, 0, 0),
            at_block(half, 6, 0, 0, 0),
            at_block((width, width), 7, 0),
            whole(small.shape),
        ]
        + owner_specs(number),
        specs,
        shapes,
        attention_scratch(number, width),
        8 * number * width * width + number * number * width * 2,
        16 * number * width,
        "cross_block",
    )(plan, normed, memory, dec_rows, wk_two, wk_two, dec_rows, small, owner, key_owner)


def ffn_kernel(plan, normed, wup, wdown, small, hidden, slope, out, normed_out, inverse_out, *, mid_row, top_row):
    mid = normed[...] * small[mid_row : mid_row + 1, :] + small[mid_row + 1 : mid_row + 2, :]
    low = mid.astype(LOW)
    width = mid.shape[1]
    total = mid
    for j in range(hidden.shape[1] // width):
        cols = slice(j * width, j * width + width)
        inner = nn(low, block_of(wup, j))
        phi, tilt = phi_and_slope(inner)
        made = (inner * phi).astype(LOW)
        hidden[:, cols] = made
        slope[:, cols] = tilt.astype(LOW)
        total = total + nn(made, wdown[cols, :])
    result, normed_two, inverse = ln_forward(
        total, small[top_row : top_row + 1, :], small[top_row + 1 : top_row + 2, :]
    )
    out[...] = result.astype(LOW)
    normed_out[...] = normed_two
    inverse_out[...] = jnp.broadcast_to(inverse, inverse_out.shape)


def ffn_forward(plan, normed, wup, wup_spec, wdown, wdown_spec, small, mid_row, top_row, inner, name):
    number, width = normed.shape
    return call(
        functools.partial(ffn_kernel, mid_row=mid_row, top_row=top_row),
        (number // TILE,),
        [rows_of(width), wup_spec, wdown_spec, whole(small.shape)],
        [rows_of(inner), rows_of(inner), rows_of(width), rows_of(width), rows_of(LANES)],
        [
            shaped((number, inner), LOW),
            shaped((number, inner), LOW),
            shaped((number, width), LOW),
            shaped((number, width), F32),
            shaped((number, LANES), F32),
        ],
        [],
        4 * number * width * inner,
        20 * number * width,
        name,
    )(plan, normed, wup, wdown, small)


def ffn_back_kernel(plan, *refs, summed, mid_row, top_row):
    if summed:
        (cot, extra, normed_top, inverse_top, slope, normed_mid, inverse_mid, wup, wdown, wo, small,
         d_inner, d_down, d_sum, d_product, d_context, sums) = refs
    else:
        (cot, normed_top, inverse_top, slope, normed_mid, inverse_mid, wup, wdown, wo, small,
         d_inner, d_down, d_sum, d_product, d_context, sums) = refs
    i = pl.program_id(0)

    @pl.when(i == 0)
    def _():
        sums[...] = jnp.zeros_like(sums)

    upstream = cot[...].astype(F32)
    if summed:
        upstream = upstream + extra[...]
    width = upstream.shape[1]
    top = normed_top[...]
    sums[2:3, :] += jnp.sum(upstream * top, axis=0, keepdims=True)
    sums[3:4, :] += jnp.sum(upstream, axis=0, keepdims=True)
    d_top = ln_backward(upstream, top, inverse_top[:, 0:1], small[top_row : top_row + 1, :])
    low = d_top.astype(LOW)
    d_down[...] = low
    d_mid = d_top
    for j in range(slope.shape[1] // width):
        cols = slice(j * width, j * width + width)
        part = (nt(low, wdown[cols, :]) * slope[:, cols].astype(F32)).astype(LOW)
        d_inner[:, cols] = part
        d_mid = d_mid + nt(part, block_of(wup, j))
    normed = normed_mid[...]
    sums[0:1, :] += jnp.sum(d_mid * normed, axis=0, keepdims=True)
    sums[1:2, :] += jnp.sum(d_mid, axis=0, keepdims=True)
    total = ln_backward(d_mid, normed, inverse_mid[:, 0:1], small[mid_row : mid_row + 1, :])
    d_sum[...] = total
    place = lax.broadcasted_iota(jnp.int32, (TILE, 1), 0) + i * TILE
    live = (place < plan[2, 0]).astype(F32)
    product = (total * live).astype(LOW)
    d_product[...] = product
    d_context[...] = nt(product, wo[...]).astype(LOW)


def ffn_backward(plan, cots, top, slope, mid, weights, weight_specs, small, mid_row, top_row, name):
    number, width = mid[0].shape
    inner = slope.shape[1]
    return call(
        functools.partial(
            ffn_back_kernel, summed=len(cots) == 2, mid_row=mid_row, top_row=top_row
        ),
        (number // TILE,),
        [rows_of(width)] * len(cots)
        + [rows_of(width), rows_of(LANES), rows_of(inner), rows_of(width), rows_of(LANES)]
        + weight_specs
        + [whole(small.shape)],
        [
            rows_of(inner),
            rows_of(width),
            rows_of(width),
            rows_of(width),
            rows_of(width),
            whole((8, width)),
        ],
        [
            shaped((number, inner), LOW),
            shaped((number, width), LOW),
            shaped((number, width), F32),
            shaped((number, width), LOW),
            shaped((number, width), LOW),
            shaped((8, width), F32),
        ],
        [],
        4 * number * width * inner,
        26 * number * width,
        name,
    )(plan, *cots, *top, slope, *mid, *weights, small)


def ffn_weights_kernel(plan, normed, d_inner, d_down, hidden, context, d_product, small, up, down, wo, turn, *, mid_row):
    i = pl.program_id(0)

    @pl.when(i == 0)
    def _():
        mid = normed[...] * small[mid_row : mid_row + 1, :] + small[mid_row + 1 : mid_row + 2, :]
        turn[...] = mid.T.astype(LOW)
        wo[...] = nn(turned(context[...]), d_product[...]).astype(LOW)

    put_block(up, 0, nn(turn[...], d_inner[...]).astype(LOW))
    down[...] = nn(turned(hidden[...]), d_down[...]).astype(LOW)


def ffn_weights(plan, normed, d_inner, d_down, hidden, context, d_product, small, mid_row, name):
    number, width = normed.shape
    blocks = d_inner.shape[1] // width
    full = whole((number, width))
    column = pl.BlockSpec((number, width), lambda i, *_: (0, i))
    return call(
        functools.partial(ffn_weights_kernel, mid_row=mid_row),
        (blocks,),
        [full, column, full, column, full, full, whole(small.shape)],
        [
            pl.BlockSpec((width // 16, 1, 16, width), lambda i, *_: (0, i, 0, 0)),
            pl.BlockSpec((width, width), lambda i, *_: (i, 0)),
            whole((width, width)),
        ],
        [
            shaped((width // 16, blocks, 16, width), LOW),
            shaped((blocks * width, width), LOW),
            shaped((width, width), LOW),
        ],
        [pltpu.VMEM((width, number), LOW)],
        4 * number * width * width * blocks,
        24 * number * width,
        name,
    )(plan, normed, d_inner, d_down, hidden, context, d_product, small)


def attention_back_kernel(plan, q_ref, k_ref, v_ref, do_ref, lse, owner_q, owner_k, dq, dk, dv,
                          kt, key_owner, masked_q, masked_do, dqt, dk_sum, dv_sum, weights, d_weights, dots):
    i = pl.program_id(0)

    @pl.when(i == 0)
    def _():
        key_owner[...] = jnp.broadcast_to(owner_k[...], (8, owner_k.shape[1])).T
        kt[...] = turned(k_ref[...])
        dk_sum[...] = jnp.zeros_like(dk_sum)
        dv_sum[...] = jnp.zeros_like(dv_sum)

    query = q_ref[...] * jnp.asarray(HEAD**-0.5, LOW)
    upstream = do_ref[...]
    for h in range(HEADS):
        masked_q[h] = one_head(query[:, pair_columns(h)], h)
        masked_do[h] = one_head(upstream[:, pair_columns(h)], h)
    dqt[...] = jnp.zeros_like(dqt)
    dots[...] = jnp.zeros_like(dots)
    owner_row = owner_q[...]
    lo = plan[0, i]
    hi = plan[1, i]

    def weigh_tile(j, carry):
        rows = pl.ds(pl.multiple_of(j * TILE, TILE), TILE)
        bias = jnp.where(key_owner[rows, 0:1] == owner_row, 0.0, floor_value)
        sums = []
        for h in range(HEADS):
            s = nt(k_ref[rows, pair_columns(h)], masked_q[h])
            p = jnp.exp((s - lse[h : h + 1, :]) + bias)
            dp = nt(v_ref[rows, pair_columns(h)], masked_do[h])
            weights[j, h] = p
            d_weights[j, h] = dp
            sums.append(jnp.sum(p * dp, axis=0, keepdims=True))
        dots[...] += jnp.concatenate(sums, axis=0)
        return carry

    lax.fori_loop(lo, hi, weigh_tile, 0)

    def grad_tile(j, carry):
        rows = pl.ds(pl.multiple_of(j * TILE, TILE), TILE)
        for pair in range(HEADS // 2):
            cols = pair_columns(2 * pair)
            dv_part = dv_sum[rows, cols]
            dk_part = dk_sum[rows, cols]
            for h in (2 * pair, 2 * pair + 1):
                p = weights[j, h]
                ds = (p * (d_weights[j, h] - dots[h : h + 1, :])).astype(LOW)
                dv_part = dv_part + nn(p.astype(LOW), masked_do[h])
                dk_part = dk_part + nn(ds, masked_q[h])
                dqt[head_rows(h), :] += nn(kt[head_rows(h), rows], ds)
            dv_sum[rows, cols] = dv_part
            dk_sum[rows, cols] = dk_part
        return carry

    lax.fori_loop(lo, hi, grad_tile, 0)
    dq[...] = (dqt[...] * HEAD**-0.5).T.astype(LOW)

    @pl.when(i == pl.num_programs(0) - 1)
    def _():
        dk[...] = dk_sum[...].astype(LOW)
        dv[...] = dv_sum[...].astype(LOW)


def attention_backward(plan, q, kv, d_context, lse, owner, key_owner, name):
    number, width = q.shape
    keys = kv.shape[0]
    return call(
        attention_back_kernel,
        (number // TILE,),
        [
            rows_of(width),
            at_block((keys, width), 0, 0),
            at_block((keys, width), 0, 1),
            rows_of(width),
            pl.BlockSpec((HEADS, TILE), lambda i, *_: (0, i)),
        ]
        + owner_specs(keys),
        [rows_of(width), whole((keys, width)), whole((keys, width))],
        [shaped((number, width), LOW), shaped((keys, width), LOW), shaped((keys, width), LOW)],
        [
            pltpu.VMEM((width, keys), LOW),
            pltpu.VMEM((keys, 8), F32),
            pltpu.VMEM((HEADS, TILE, LANES), LOW),
            pltpu.VMEM((HEADS, TILE, LANES), LOW),
            pltpu.VMEM((width, TILE), F32),
            pltpu.VMEM((keys, width), F32),
            pltpu.VMEM((keys, width), F32),
            pltpu.VMEM((keys // TILE, HEADS, TILE, TILE), F32),
            pltpu.VMEM((keys // TILE, HEADS, TILE, TILE), F32),
            pltpu.VMEM((HEADS, TILE), F32),
        ],
        number * keys * width * 4,
        12 * number * width,
        name,
    )(plan, q, kv, kv, d_context, lse, owner, key_owner)


def cross_back_kernel(plan, d_query, dk, dv, normed, inverse, d_above, memory, context, wq, wk_a, wk_b, wo, small,
                      d_memory, d_sum, d_context, g_query, g_pair, g_out, sums, d_product):
    i = pl.program_id(0)
    mine = pl.ds(pl.multiple_of(i * TILE, TILE), TILE)

    @pl.when(i == 0)
    def _():
        sums[...] = jnp.zeros_like(sums)
        low = normed[...] * small[4:5, :] + small[5:6, :]
        g_query[...] = nn(low.T.astype(LOW), d_query[...]).astype(LOW)

    wk = jnp.concatenate([block_of(wk_a, 0), block_of(wk_b, 0)], axis=0)
    wv = jnp.concatenate([block_of(wk_a, 1), block_of(wk_b, 1)], axis=0)
    d_memory[...] = nt(dk[mine, :], wk) + nt(dv[mine, :], wv)
    d_one = d_above[...] + nt(d_query[mine, :], wq[...])
    hat = normed[mine, :]
    sums[0:1, :] += jnp.sum(d_one * hat, axis=0, keepdims=True)
    sums[1:2, :] += jnp.sum(d_one, axis=0, keepdims=True)
    total = ln_backward(d_one, hat, inverse[:, 0:1], small[4:5, :])
    d_sum[...] = total
    place = lax.broadcasted_iota(jnp.int32, (TILE, 1), 0) + i * TILE
    live = (place < plan[2, 0]).astype(F32)
    product = (total * live).astype(LOW)
    d_product[mine, :] = product
    d_context[...] = nt(product, wo[...]).astype(LOW)

    @pl.when(i == 1)
    def _():
        turn = turned(memory[...])
        put_block(g_pair, 0, nn(turn, dk[...]).astype(LOW))

    @pl.when(i == 2)
    def _():
        turn = turned(memory[...])
        put_block(g_pair, 1, nn(turn, dv[...]).astype(LOW))

    @pl.when(i == pl.num_programs(0) - 1)
    def _():
        g_out[...] = nn(turned(context[...]), d_product[...]).astype(LOW)


def cross_projections_back(plan, d_query, dk, dv, normed, inverse, d_above, memory, context, dec_rows, wk_two, small):
    number, width = normed.shape
    full = whole((number, width))
    square = whole((width, width))
    half = (width // 32, 2, 16, width)
    return call(
        cross_back_kernel,
        (number // TILE,),
        [full, full, full, full, rows_of(LANES), rows_of(width), full, full,
         at_block((width, width), 4, 0), at_block(half, 5, 0, 0, 0), at_block(half, 6, 0, 0, 0),
         at_block((width, width), 3, 0), whole(small.shape)],
        [rows_of(width), rows_of(width), rows_of(width), square, whole((width // 16, 2, 16, width)), square,
         whole((8, width))],
        [shaped((number, width), F32), shaped((number, width), F32), shaped((number, width), LOW),
         shaped((width, width), LOW), shaped((width // 16, 2, 16, width), LOW), shaped((width, width), LOW),
         shaped((8, width), F32)],
        [pltpu.VMEM((number, width), LOW)],
        16 * number * width * width,
        24 * number * width,
        "cross_projections_back",
    )(plan, d_query, dk, dv, normed, inverse, d_above, memory, context, dec_rows, wk_two, wk_two, dec_rows, small)


def self_back_kernel(plan, *refs, masked):
    if masked:
        dq, dk, dv, d_above, x, wqkv, flags, d_x, g_qkv, mask_sum, turn = refs
    else:
        dq, dk, dv, d_above, x, wqkv, d_x, g_qkv, turn = refs
    i = pl.program_id(0)
    mine = pl.ds(pl.multiple_of(i * TILE, TILE), TILE)

    @pl.when(i == 0)
    def _():
        turn[...] = turned(x[...])
        if masked:
            mask_sum[...] = jnp.zeros_like(mask_sum)

    pieces = jnp.concatenate([ref[mine, :] for ref in (dq, dk, dv)], axis=1)
    weights = jnp.concatenate([block_of(wqkv, j) for j in range(3)], axis=1)
    total = nt(pieces, weights)
    if masked:
        total = total + d_above[...]
    for j, ref in enumerate((dq, dk, dv)):

        @pl.when(i == j)
        def _(ref=ref):
            put_block(g_qkv, 0, nn(turn[...], ref[...]).astype(LOW))

    if masked:
        hit = column_of(flags[...]) == 1.0
        d_x[...] = jnp.where(hit, 0.0, total)
        mask_sum[0:1, :] += jnp.sum(jnp.where(hit, total, 0.0), axis=0, keepdims=True)
    else:
        d_x[...] = d_above[...]
        d_x[...] += total


def self_projections_back(plan, dq, dk, dv, d_above, x, wqkv, wqkv_spec, flags, units, name):
    number, width = x.shape
    full = whole((number, width))
    masked = flags is not None
    if units:
        g_shape = (width // 16, 3, 16, width)
        g_spec = pl.BlockSpec((width // 16, 1, 16, width), lambda i, *_: (0, jnp.minimum(i, 2), 0, 0))
    else:
        g_shape = (3, width, width)
        g_spec = pl.BlockSpec((1, width, width), lambda i, *_: (jnp.minimum(i, 2), 0, 0))
    in_specs = [full, full, full, rows_of(width), full, wqkv_spec]
    out_specs = [rows_of(width), g_spec]
    out_shape = [shaped((number, width), F32), shaped(g_shape, LOW)]
    operands = [dq, dk, dv, d_above, x, wqkv]
    if masked:
        in_specs.append(pl.BlockSpec((1, TILE), lambda i, *_: (0, i)))
        out_specs.append(whole((8, width)))
        out_shape.append(shaped((8, width), F32))
        operands.append(flags)
    return call(
        functools.partial(self_back_kernel, masked=masked),
        (number // TILE,),
        in_specs,
        out_specs,
        out_shape,
        [pltpu.VMEM((width, number), LOW)],
        12 * number * width * width,
        20 * number * width,
        name,
    )(plan, *operands)


def enc_regions(width, inner):
    return ((0, 3 * width, 3), (4 * width, 4 * width + inner, inner // width))


def dec_regions(width, inner):
    return ((5 * width, 7 * width, 2), (8 * width, 8 * width + inner, inner // width))


def to_units(rows, k):
    return rows.reshape(-1, 16, k, rows.shape[1]).transpose(0, 2, 1, 3).reshape(rows.shape)


def from_units(rows, k):
    return rows.reshape(-1, k, 16, rows.shape[1]).transpose(0, 2, 1, 3).reshape(rows.shape)


def fits(size, region):
    return size % (16 * region[2]) == 0


def arrange_own(rows, first, regions, arrange):
    place = first + lax.broadcasted_iota(jnp.int32, (rows.shape[0], 1), 0)
    result = rows
    for region in regions:
        if fits(rows.shape[0], region):
            inside = (place >= region[0]) & (place < region[1])
            result = jnp.where(inside, arrange(rows, region[2]), result)
    return result


def arrange_all(rows, size, regions, arrange):
    for region in regions:
        if not fits(size, region):
            part = arrange(rows[region[0] : region[1]], region[2])
            rows = jnp.concatenate([rows[: region[0]], part, rows[region[1] :]], axis=0)
    return rows


def owners_of(lengths, number):
    bounds = jnp.cumsum(lengths)
    places = jnp.arange(number, dtype=jnp.int32)
    owners = jnp.sum((places[:, None] >= bounds[None, :]).astype(jnp.int32), axis=1)
    filled = places < bounds[-1]
    for_queries = jnp.where(filled, owners, -2).astype(F32)[None, :]
    for_keys = jnp.where(filled, owners, -1).astype(F32)[None, :]
    return for_queries, for_keys, bounds


def plan_of(query_bounds, key_bounds, key_lengths, number):
    firsts = jnp.arange(8, dtype=jnp.int32) * TILE
    filled = query_bounds[-1]
    lasts = jnp.minimum(firsts + TILE, filled) - 1

    def pair_of(places):
        found = jnp.sum((places[:, None] >= query_bounds[None, :]).astype(jnp.int32), axis=1)
        return jnp.minimum(found, key_lengths.shape[0] - 1)

    def pick(values, pairs):
        chosen = pairs[:, None] == jnp.arange(values.shape[0])[None, :]
        return jnp.sum(jnp.where(chosen, values[None, :], 0), axis=1)

    begin = pick(key_bounds - key_lengths, pair_of(firsts))
    end = pick(key_bounds, pair_of(lasts))
    some = firsts < filled
    lo = jnp.where(some, begin // TILE, 0)
    hi = jnp.where(some, (end + TILE - 1) // TILE, 0)
    return jnp.stack([lo, hi, jnp.full_like(lo, filled)]).astype(jnp.int32)


def moments(gradient, first, second):
    first_new = beta_one * first + (1.0 - beta_one) * gradient
    second_new = beta_two * second + (1.0 - beta_two) * gradient * gradient
    return (first_new, second_new)


def adamw(weight, gradient, first, second):
    first_new, second_new = moments(gradient, first, second)
    moved = weight - rate * (
        first_new
        / (1.0 - beta_one**STEPS)
        / (jnp.sqrt(second_new / (1.0 - beta_two**STEPS)) + epsilon)
        + decay * weight
    )
    return (moved, first_new, second_new)


def on_device(
    devices,
    src_in,
    tgt_in,
    src_len,
    tgt_len,
    tgt_mask,
    enc_cot,
    dec_cot,
    enc_master,
    enc_first,
    enc_second,
    dec_master,
    dec_first,
    dec_second,
    small_master,
    small_first,
    small_second,
):
    width = src_in.shape[1]
    number = src_in.shape[0]
    me = lax.axis_index("fsdp")
    enc_size, dec_size = enc_master.shape[0], dec_master.shape[0]
    enc_count, dec_count = enc_size * devices, dec_size * devices
    inner = (enc_count - 4 * width) // 2
    ups = inner // width
    enc_map, dec_map = enc_regions(width, inner), dec_regions(width, inner)

    enc_own = arrange_own(enc_master.astype(LOW), me * enc_size, enc_map, to_units)
    dec_own = arrange_own(dec_master.astype(LOW), me * dec_size, dec_map, to_units)
    enc_rows = lax.all_gather(enc_own, "fsdp", axis=0, tiled=True)
    dec_rows = lax.all_gather(dec_own, "fsdp", axis=0, tiled=True)
    small_rows = lax.all_gather(small_master.astype(LOW), "fsdp", axis=1, tiled=True)

    src_owner, src_key, src_bounds = owners_of(src_len[0], number)
    tgt_owner, tgt_key, tgt_bounds = owners_of(tgt_len[0], number)
    enc_plan = plan_of(src_bounds, src_bounds, src_len[0], number)
    dec_plan = plan_of(tgt_bounds, tgt_bounds, tgt_len[0], number)
    cross_plan = plan_of(tgt_bounds, src_bounds, src_len[0], number)

    smalls = jnp.pad(small_rows.astype(F32), ((0, 5), (0, 0)))
    masked = tgt_mask[:, None] == 1
    start = jnp.where(masked, small_rows[10][None, :], tgt_in)
    flags = tgt_mask.astype(F32)[None, :]

    enc_rows = arrange_all(enc_rows, enc_size, enc_map, to_units)
    dec_rows = arrange_all(dec_rows, dec_size, dec_map, to_units)
    enc_three = enc_rows.reshape(-1, 3, 16, width)
    enc_four = enc_rows.reshape(-1, ups, 16, width)
    dec_two = dec_rows.reshape(-1, 2, 16, width)
    dec_four = dec_rows.reshape(-1, ups, 16, width)
    dec_three = dec_rows[: 3 * width].reshape(width, 3, width).transpose(1, 0, 2)
    units = width // 16
    three_spec = at_block((units, 3, 16, width), 0, 0, 0, 0)
    enc_up = at_block((units, ups, 16, width), 1, 0, 0, 0)
    enc_down = at_block((inner, width), 2, 0)
    enc_wo = at_block((width, width), 3, 0)
    dec_up = at_block((units, ups, 16, width), 2, 0, 0, 0)
    dec_down = at_block((inner, width), 3, 0)

    e_q, e_kv, e_ctx, e_lse, e_hat, e_inv = self_block(
        enc_plan, src_in, enc_three, three_spec, enc_rows, enc_wo, smalls, 0, src_owner, src_key, "enc_block"
    )
    e_hidden, e_slope, memory, t_hat, t_inv = ffn_forward(
        enc_plan, e_hat, enc_four, enc_up, enc_rows, enc_down, smalls, 0, 2, inner, "enc_ffn"
    )
    s_q, s_kv, s_ctx, s_lse, s_hat, s_inv = self_block(
        dec_plan, start, dec_three, whole(dec_three.shape), dec_rows, at_block((width, width), 3, 0), smalls, 4,
        tgt_owner, tgt_key, "dec_block",
    )
    c_q, c_kv, c_ctx, c_lse, c_hat, c_inv = cross_block(
        cross_plan, s_hat, memory, dec_rows, dec_two, smalls, tgt_owner, src_key
    )
    d_hidden, d_slope, decoded, f_hat, f_inv = ffn_forward(
        dec_plan, c_hat, dec_four, dec_up, dec_rows, dec_down, smalls, 6, 8, inner, "dec_ffn"
    )

    dd_inner, dd_down, d_two, d_cross, d_cctx, sums_d = ffn_backward(
        dec_plan, [dec_cot], (f_hat, f_inv), d_slope, (c_hat, c_inv), (dec_four, dec_rows, dec_rows),
        [dec_up, dec_down, at_block((width, width), 7, 0)], smalls, 6, 8, "dec_ffn_back",
    )
    g_dup, g_ddown, g_cout = ffn_weights(
        dec_plan, c_hat, dd_inner, dd_down, d_hidden, c_ctx, d_cross, smalls, 6, "dec_ffn_weights"
    )
    dcq, dck, dcv = attention_backward(cross_plan, c_q, c_kv, d_cctx, c_lse, tgt_owner, src_key, "cross_back")
    d_memory, d_one, d_sctx, g_cq, g_ckv, g_sout, sums_c = cross_projections_back(
        dec_plan, dcq, dck, dcv, s_hat, s_inv, d_two, memory, s_ctx, dec_rows, dec_two, smalls
    )
    dsq, dsk, dsv = attention_backward(dec_plan, s_q, s_kv, d_sctx, s_lse, tgt_owner, tgt_key, "dec_back")
    tgt_grad, g_sqkv, mask_sum = self_projections_back(
        dec_plan, dsq, dsk, dsv, d_one, start, dec_three, whole(dec_three.shape), flags, False, "dec_proj_back"
    )
    de_inner, de_down, d_mid, d_eattn, d_ectx, sums_e = ffn_backward(
        enc_plan, [enc_cot, d_memory], (t_hat, t_inv), e_slope, (e_hat, e_inv), (enc_four, enc_rows, enc_rows),
        [enc_up, enc_down, enc_wo], smalls, 0, 2, "enc_ffn_back",
    )
    g_up, g_down, g_out = ffn_weights(
        enc_plan, e_hat, de_inner, de_down, e_hidden, e_ctx, d_eattn, smalls, 0, "enc_ffn_weights"
    )
    deq, dek, dev = attention_backward(enc_plan, e_q, e_kv, d_ectx, e_lse, src_owner, src_key, "enc_back")
    src_grad, g_qkv = self_projections_back(
        enc_plan, deq, dek, dev, d_mid, src_in, enc_three, three_spec, None, True, "enc_proj_back"
    )

    dec_grad = jnp.concatenate(
        [
            g_sqkv.transpose(1, 0, 2).reshape(-1, width),
            g_sout,
            g_cq,
            g_ckv.reshape(-1, width),
            g_cout,
            g_dup.reshape(-1, width),
            g_ddown,
        ],
        axis=0,
    )
    enc_grad = jnp.concatenate(
        [g_qkv.reshape(-1, width), g_out, g_up.reshape(-1, width), g_down], axis=0
    )
    small_grad = jnp.concatenate([sums_e[:4], sums_c[:2], sums_d[:4], mask_sum[:1]], axis=0)
    dec_grad = arrange_all(dec_grad, dec_size, dec_map, from_units)
    enc_grad = arrange_all(enc_grad, enc_size, enc_map, from_units)
    share = small_master.shape[1]
    small_wire = small_grad.reshape(-1, devices, share).transpose(1, 0, 2).reshape(devices, -1).astype(LOW)
    held = small_wire.shape[1]
    small_wire = jnp.pad(small_wire, ((0, 0), (0, 16 * width - held))).reshape(devices, 16, width)
    enc_wire = jnp.concatenate([enc_grad.reshape(devices, enc_size, width), small_wire], axis=1)
    dec_summed = lax.psum_scatter(dec_grad, "fsdp", scatter_dimension=0, tiled=True)
    enc_summed = lax.psum_scatter(enc_wire.reshape(-1, width), "fsdp", scatter_dimension=0, tiled=True)
    small_summed = enc_summed[enc_size:].reshape(-1)[:held].reshape(-1, share).astype(F32)
    enc_summed = arrange_own(enc_summed[:enc_size].astype(F32), me * enc_size, enc_map, from_units)
    dec_summed = arrange_own(dec_summed.astype(F32), me * dec_size, dec_map, from_units)

    part = 1.0 / devices
    enc_summed = enc_summed * part
    dec_summed = dec_summed * part
    small_summed = small_summed * part
    enc_new, enc_first_new, encoder_second_moment_updated = adamw(
        enc_master, enc_summed, enc_first, enc_second
    )
    dec_new, dec_first_new, dec_second_new = adamw(dec_master, dec_summed, dec_first, dec_second)
    small_first_new, small_second_new = moments(small_summed, small_first, small_second)
    return (
        memory,
        decoded,
        src_grad,
        tgt_grad,
        enc_new,
        enc_first_new,
        encoder_second_moment_updated,
        enc_new.astype(LOW),
        dec_new,
        dec_first_new,
        dec_second_new,
        dec_new.astype(LOW),
        small_summed,
        small_first_new,
        small_second_new,
    )


def solution(mesh):
    rows = P("fsdp", None)
    columns = P(None, "fsdp")
    return jax.shard_map(
        functools.partial(on_device, mesh.shape["fsdp"]),
        mesh=mesh,
        in_specs=(rows,) * 4 + (P("fsdp"),) + (rows,) * 8 + (columns,) * 3,
        out_specs=(rows,) * 12 + (columns,) * 3,
        check_vma=False,
    )
```

```python
import functools

import jax
import jax.numpy as jnp
from jax import lax
from jax.experimental import pallas as pl
from jax.experimental.pallas import tpu as pltpu
from jax.sharding import PartitionSpec as P

HEADS = 8
HEAD = 64
STEPS = 7
TILE = 256
LANES = 128

rate = 0.02
beta_one = 0.9
beta_two = 0.98
epsilon = 1e-06
decay = 0.01
floor_value = -1000000000.0
root_half = 0.7071067811865476
inverse_root_tau = 0.3989422804014327

F32 = jnp.float32
LOW = jnp.bfloat16
VMEM_BYTES = 56 * 2**20


def nn(former, latter):
    return lax.dot_general(
        former, latter, (((1,), (0,)), ((), ())), preferred_element_type=F32
    )


def nt(former, latter):
    return lax.dot_general(
        former, latter, (((1,), (1,)), ((), ())), preferred_element_type=F32
    )


def turned(values):
    return values.astype(F32).T.astype(LOW)


def column_of(row):
    return jnp.broadcast_to(row, (8, row.shape[1])).T[:, 0:1]


def ln_forward(values, gain, shift):
    centered = values - jnp.mean(values, axis=-1, keepdims=True)
    spread = jnp.mean(centered * centered, axis=-1, keepdims=True)
    inverse = lax.rsqrt(spread + 1e-05)
    normed = centered * inverse
    return normed * gain + shift, normed, inverse


def ln_backward(upstream, normed, inverse, gain):
    scaled = upstream * gain
    first = jnp.mean(scaled, axis=-1, keepdims=True)
    second = jnp.mean(scaled * normed, axis=-1, keepdims=True)
    return inverse * (scaled - first - normed * second)


def phi_and_slope(values):
    size = jnp.abs(values)
    bell = jnp.exp(-0.5 * (values * values))
    part = 1.0 / (1.0 + (0.3275911 * root_half) * size)
    series = part * (
        0.254829592
        + part
        * (-0.284496736 + part * (1.421413741 + part * (-1.453152027 + part * 1.061405429)))
    )
    half_tail = (0.5 * series) * bell
    phi = jnp.where(values >= 0, 1.0 - half_tail, half_tail)
    return phi, phi + values * (bell * inverse_root_tau)


def one_head(pair, head):
    lane = lax.broadcasted_iota(jnp.int32, pair.shape, 1)
    keep = lane < HEAD if head % 2 == 0 else lane >= HEAD
    return jnp.where(keep, pair, jnp.zeros_like(pair))


def pair_columns(head):
    return slice(LANES * (head // 2), LANES * (head // 2) + LANES)


def head_rows(head):
    return slice(HEAD * head, HEAD * head + HEAD)


def block_of(ref, j):
    if len(ref.shape) == 4:
        return ref[:, j].reshape(ref.shape[0] * ref.shape[2], ref.shape[3])
    return ref[j]


def put_block(ref, j, values):
    if len(ref.shape) == 4:
        ref[:, j] = values.reshape(ref.shape[0], ref.shape[2], ref.shape[3])
    else:
        ref[j] = values


def call(kernel, grid, in_specs, out_specs, out_shape, scratch, flops, moved, name):
    return pl.pallas_call(
        kernel,
        grid_spec=pltpu.PrefetchScalarGridSpec(
            num_scalar_prefetch=1,
            grid=grid,
            in_specs=in_specs,
            out_specs=out_specs,
            scratch_shapes=scratch,
        ),
        out_shape=out_shape,
        compiler_params=pltpu.CompilerParams(vmem_limit_bytes=VMEM_BYTES),
        cost_estimate=pl.CostEstimate(
            flops=flops, bytes_accessed=moved, transcendentals=0
        ),
        name=name,
    )


def whole(shape):
    zeros = (0,) * len(shape)
    return pl.BlockSpec(shape, lambda i, *_: zeros)


def rows_of(width):
    return pl.BlockSpec((TILE, width), lambda i, *_: (i, 0))


def at_block(shape, *index):
    return pl.BlockSpec(shape, lambda i, *_: index)


def shaped(shape, kind):
    return jax.ShapeDtypeStruct(shape, kind)


def attend_tile(plan, i, keys, key_cols, query, owner_row, key_owner, vt, sc):
    scores, acc, top, total, masked_q = sc
    query = query * jnp.asarray(HEAD**-0.5, LOW)
    for h in range(HEADS):
        masked_q[h] = one_head(query[:, pair_columns(h)], h)
    top[...] = jnp.full_like(top, -1e30)
    total[...] = jnp.zeros_like(total)
    acc[...] = jnp.zeros_like(acc)
    lo = plan[0, i]
    hi = plan[1, i]

    def score_tile(j, carry):
        rows = pl.ds(pl.multiple_of(j * TILE, TILE), TILE)
        bias = jnp.where(key_owner[rows, 0:1] == owner_row, 0.0, floor_value)
        tops = []
        for h in range(HEADS):
            cols = pl.ds(key_cols + LANES * (h // 2), LANES)
            s = nt(keys[rows, cols], masked_q[h]) + bias
            scores[j, h] = s
            tops.append(jnp.max(s, axis=0, keepdims=True))
        top[...] = jnp.maximum(top[...], jnp.concatenate(tops, axis=0))
        return carry

    lax.fori_loop(lo, hi, score_tile, 0)

    def weigh_tile(j, carry):
        rows = pl.ds(pl.multiple_of(j * TILE, TILE), TILE)
        sums = []
        for h in range(HEADS):
            p = jnp.exp(scores[j, h] - top[h : h + 1, :])
            sums.append(jnp.sum(p, axis=0, keepdims=True))
            acc[head_rows(h), :] += nn(vt[head_rows(h), rows], p.astype(LOW))
        total[...] += jnp.concatenate(sums, axis=0)
        return carry

    lax.fori_loop(lo, hi, weigh_tile, 0)


def fwd_block_kernel(plan, *refs, cross, gain_row):
    if cross:
        (normed_in, memory, wq, wk_a, wk_b, wo, small, owner_q, owner_k,
         q_out, kv_out, ctx_out, lse_out, normed_out, inverse_out,
         kv, vt, mean_v, key_owner, scores, acc, top, total, masked_q) = refs
    else:
        (x_all, wqkv, wo, small, owner_q, owner_k,
         q_out, kv_out, ctx_out, lse_out, normed_out, inverse_out,
         kv, vt, mean_v, key_owner, scores, acc, top, total, masked_q, q_all) = refs
    i = pl.program_id(0)
    width = kv.shape[1] // 2

    @pl.when(i == 0)
    def _():
        key_owner[...] = jnp.broadcast_to(owner_k[...], (8, owner_k.shape[1])).T
        if cross:
            wk = jnp.concatenate([block_of(wk_a, 0), block_of(wk_b, 0)], axis=0)
            wv = jnp.concatenate([block_of(wk_a, 1), block_of(wk_b, 1)], axis=0)
        else:
            wq_all = block_of(wqkv, 0)
            wk = block_of(wqkv, 1)
            wv = block_of(wqkv, 2)
        sums = jnp.zeros((1, width), F32)
        for t in range(kv.shape[0] // TILE):
            rows = slice(t * TILE, t * TILE + TILE)
            x = memory[rows, :] if cross else x_all[rows, :]
            if not cross:
                q_all[rows, :] = nn(x, wq_all).astype(LOW)
            kv[rows, :width] = nn(x, wk).astype(LOW)
            v = nn(x, wv).astype(LOW)
            kv[rows, width:] = v
            v = v.astype(F32)
            vt[:, rows] = v.T.astype(LOW)
            sums = sums + jnp.sum(v, axis=0, keepdims=True)
        mean_v[...] = sums * (1.0 / kv.shape[0])

    mine = pl.ds(pl.multiple_of(i * TILE, TILE), TILE)
    if cross:
        resid = normed_in[...] * small[4:5, :] + small[5:6, :]
        query = nn(resid.astype(LOW), wq[...]).astype(LOW)
        q_out[...] = query
    else:
        resid = x_all[mine, :].astype(F32)
        query = q_all[mine, :]
        q_out[...] = query
    kv_out[...] = kv[mine, :]
    owner_row = owner_q[...]
    attend_tile(plan, i, kv, 0, query, owner_row, key_owner, vt, (scores, acc, top, total, masked_q))
    dead = owner_row < 0
    sums = jnp.where(dead, 1.0, total[...])
    share = 1.0 / sums
    lse_out[...] = jnp.where(dead, 0.0, top[...] + jnp.log(sums))
    for h in range(HEADS):
        acc[head_rows(h), :] = acc[head_rows(h), :] * share[h : h + 1, :]
    live = column_of(owner_row) >= 0
    context = jnp.where(live, acc[...].T, mean_v[...]).astype(LOW)
    ctx_out[...] = context
    added = nn(context, wo[...]) * live.astype(F32)
    _, normed, inverse = ln_forward(
        resid + added, small[gain_row : gain_row + 1, :], small[gain_row + 1 : gain_row + 2, :]
    )
    normed_out[...] = normed
    inverse_out[...] = jnp.broadcast_to(inverse, inverse_out.shape)


def attention_scratch(keys, width):
    return [
        pltpu.VMEM((keys, 2 * width), LOW),
        pltpu.VMEM((width, keys), LOW),
        pltpu.VMEM((1, width), F32),
        pltpu.VMEM((keys, 8), F32),
        pltpu.VMEM((keys // TILE, HEADS, TILE, TILE), F32),
        pltpu.VMEM((width, TILE), F32),
        pltpu.VMEM((HEADS, TILE), F32),
        pltpu.VMEM((HEADS, TILE), F32),
        pltpu.VMEM((HEADS, TILE, LANES), LOW),
    ]


def block_outs(queries, width):
    specs = [
        rows_of(width),
        rows_of(2 * width),
        rows_of(width),
        pl.BlockSpec((HEADS, TILE), lambda i, *_: (0, i)),
        rows_of(width),
        rows_of(LANES),
    ]
    shapes = [
        shaped((queries, width), LOW),
        shaped((queries, 2 * width), LOW),
        shaped((queries, width), LOW),
        shaped((HEADS, queries), F32),
        shaped((queries, width), F32),
        shaped((queries, LANES), F32),
    ]
    return specs, shapes


def owner_specs(keys):
    return [pl.BlockSpec((1, TILE), lambda i, *_: (0, i)), whole((1, keys))]


def self_block(plan, x, wqkv, wqkv_spec, wo, wo_spec, small, gain_row, owner, key_owner, name):
    number, width = x.shape
    specs, shapes = block_outs(number, width)
    return call(
        functools.partial(fwd_block_kernel, cross=False, gain_row=gain_row),
        (number // TILE,),
        [whole(x.shape), wqkv_spec, wo_spec, whole(small.shape)] + owner_specs(number),
        specs,
        shapes,
        attention_scratch(number, width) + [pltpu.VMEM((number, width), LOW)],
        8 * number * width * width + number * number * width * 2,
        16 * number * width,
        name,
    )(plan, x, wqkv, wo, small, owner, key_owner)


def cross_block(plan, normed, memory, dec_rows, wk_two, small, owner, key_owner):
    number, width = normed.shape
    specs, shapes = block_outs(number, width)
    half = (width // 32, 2, 16, width)
    return call(
        functools.partial(fwd_block_kernel, cross=True, gain_row=6),
        (number // TILE,),
        [
            rows_of(width),
            whole(memory.shape),
            at_block((width, width), 4, 0),
            at_block(half, 5, 0, 0, 0),
            at_block(half, 6, 0, 0, 0),
            at_block((width, width), 7, 0),
            whole(small.shape),
        ]
        + owner_specs(number),
        specs,
        shapes,
        attention_scratch(number, width),
        8 * number * width * width + number * number * width * 2,
        16 * number * width,
        "cross_block",
    )(plan, normed, memory, dec_rows, wk_two, wk_two, dec_rows, small, owner, key_owner)


def ffn_kernel(plan, normed, wup, wdown, small, hidden, slope, out, normed_out, inverse_out, *, mid_row, top_row):
    mid = normed[...] * small[mid_row : mid_row + 1, :] + small[mid_row + 1 : mid_row + 2, :]
    low = mid.astype(LOW)
    width = mid.shape[1]
    total = mid
    for j in range(hidden.shape[1] // width):
        cols = slice(j * width, j * width + width)
        inner = nn(low, block_of(wup, j))
        phi, tilt = phi_and_slope(inner)
        made = (inner * phi).astype(LOW)
        hidden[:, cols] = made
        slope[:, cols] = tilt.astype(LOW)
        total = total + nn(made, wdown[cols, :])
    result, normed_two, inverse = ln_forward(
        total, small[top_row : top_row + 1, :], small[top_row + 1 : top_row + 2, :]
    )
    out[...] = result.astype(LOW)
    normed_out[...] = normed_two
    inverse_out[...] = jnp.broadcast_to(inverse, inverse_out.shape)


def ffn_forward(plan, normed, wup, wup_spec, wdown, wdown_spec, small, mid_row, top_row, inner, name):
    number, width = normed.shape
    return call(
        functools.partial(ffn_kernel, mid_row=mid_row, top_row=top_row),
        (number // TILE,),
        [rows_of(width), wup_spec, wdown_spec, whole(small.shape)],
        [rows_of(inner), rows_of(inner), rows_of(width), rows_of(width), rows_of(LANES)],
        [
            shaped((number, inner), LOW),
            shaped((number, inner), LOW),
            shaped((number, width), LOW),
            shaped((number, width), F32),
            shaped((number, LANES), F32),
        ],
        [],
        4 * number * width * inner,
        20 * number * width,
        name,
    )(plan, normed, wup, wdown, small)


def ffn_back_kernel(plan, *refs, summed, mid_row, top_row):
    if summed:
        (cot, extra, normed_top, inverse_top, slope, normed_mid, inverse_mid, wup, wdown, wo, small,
         d_inner, d_down, d_sum, d_product, d_context, sums) = refs
    else:
        (cot, normed_top, inverse_top, slope, normed_mid, inverse_mid, wup, wdown, wo, small,
         d_inner, d_down, d_sum, d_product, d_context, sums) = refs
    i = pl.program_id(0)

    @pl.when(i == 0)
    def _():
        sums[...] = jnp.zeros_like(sums)

    upstream = cot[...].astype(F32)
    if summed:
        upstream = upstream + extra[...]
    width = upstream.shape[1]
    top = normed_top[...]
    sums[2:3, :] += jnp.sum(upstream * top, axis=0, keepdims=True)
    sums[3:4, :] += jnp.sum(upstream, axis=0, keepdims=True)
    d_top = ln_backward(upstream, top, inverse_top[:, 0:1], small[top_row : top_row + 1, :])
    low = d_top.astype(LOW)
    d_down[...] = low
    d_mid = d_top
    for j in range(slope.shape[1] // width):
        cols = slice(j * width, j * width + width)
        part = (nt(low, wdown[cols, :]) * slope[:, cols].astype(F32)).astype(LOW)
        d_inner[:, cols] = part
        d_mid = d_mid + nt(part, block_of(wup, j))
    normed = normed_mid[...]
    sums[0:1, :] += jnp.sum(d_mid * normed, axis=0, keepdims=True)
    sums[1:2, :] += jnp.sum(d_mid, axis=0, keepdims=True)
    total = ln_backward(d_mid, normed, inverse_mid[:, 0:1], small[mid_row : mid_row + 1, :])
    d_sum[...] = total
    place = lax.broadcasted_iota(jnp.int32, (TILE, 1), 0) + i * TILE
    live = (place < plan[2, 0]).astype(F32)
    product = (total * live).astype(LOW)
    d_product[...] = product
    d_context[...] = nt(product, wo[...]).astype(LOW)


def ffn_backward(plan, cots, top, slope, mid, weights, weight_specs, small, mid_row, top_row, name):
    number, width = mid[0].shape
    inner = slope.shape[1]
    return call(
        functools.partial(
            ffn_back_kernel, summed=len(cots) == 2, mid_row=mid_row, top_row=top_row
        ),
        (number // TILE,),
        [rows_of(width)] * len(cots)
        + [rows_of(width), rows_of(LANES), rows_of(inner), rows_of(width), rows_of(LANES)]
        + weight_specs
        + [whole(small.shape)],
        [
            rows_of(inner),
            rows_of(width),
            rows_of(width),
            rows_of(width),
            rows_of(width),
            whole((8, width)),
        ],
        [
            shaped((number, inner), LOW),
            shaped((number, width), LOW),
            shaped((number, width), F32),
            shaped((number, width), LOW),
            shaped((number, width), LOW),
            shaped((8, width), F32),
        ],
        [],
        4 * number * width * inner,
        26 * number * width,
        name,
    )(plan, *cots, *top, slope, *mid, *weights, small)


def ffn_weights_kernel(plan, normed, d_inner, d_down, hidden, context, d_product, small, up, down, wo, turn, *, mid_row):
    i = pl.program_id(0)

    @pl.when(i == 0)
    def _():
        mid = normed[...] * small[mid_row : mid_row + 1, :] + small[mid_row + 1 : mid_row + 2, :]
        turn[...] = mid.T.astype(LOW)
        wo[...] = nn(turned(context[...]), d_product[...]).astype(LOW)

    put_block(up, 0, nn(turn[...], d_inner[...]).astype(LOW))
    down[...] = nn(turned(hidden[...]), d_down[...]).astype(LOW)


def ffn_weights(plan, normed, d_inner, d_down, hidden, context, d_product, small, mid_row, name):
    number, width = normed.shape
    blocks = d_inner.shape[1] // width
    full = whole((number, width))
    column = pl.BlockSpec((number, width), lambda i, *_: (0, i))
    return call(
        functools.partial(ffn_weights_kernel, mid_row=mid_row),
        (blocks,),
        [full, column, full, column, full, full, whole(small.shape)],
        [
            pl.BlockSpec((width // 16, 1, 16, width), lambda i, *_: (0, i, 0, 0)),
            pl.BlockSpec((width, width), lambda i, *_: (i, 0)),
            whole((width, width)),
        ],
        [
            shaped((width // 16, blocks, 16, width), LOW),
            shaped((blocks * width, width), LOW),
            shaped((width, width), LOW),
        ],
        [pltpu.VMEM((width, number), LOW)],
        4 * number * width * width * blocks,
        24 * number * width,
        name,
    )(plan, normed, d_inner, d_down, hidden, context, d_product, small)


def attention_back_kernel(plan, q_ref, k_ref, v_ref, do_ref, lse, owner_q, owner_k, dq, dk, dv,
                          kt, key_owner, masked_q, masked_do, dqt, dk_sum, dv_sum, weights, d_weights, dots):
    i = pl.program_id(0)

    @pl.when(i == 0)
    def _():
        key_owner[...] = jnp.broadcast_to(owner_k[...], (8, owner_k.shape[1])).T
        kt[...] = turned(k_ref[...])
        dk_sum[...] = jnp.zeros_like(dk_sum)
        dv_sum[...] = jnp.zeros_like(dv_sum)

    query = q_ref[...] * jnp.asarray(HEAD**-0.5, LOW)
    upstream = do_ref[...]
    for h in range(HEADS):
        masked_q[h] = one_head(query[:, pair_columns(h)], h)
        masked_do[h] = one_head(upstream[:, pair_columns(h)], h)
    dqt[...] = jnp.zeros_like(dqt)
    dots[...] = jnp.zeros_like(dots)
    owner_row = owner_q[...]
    lo = plan[0, i]
    hi = plan[1, i]

    def weigh_tile(j, carry):
        rows = pl.ds(pl.multiple_of(j * TILE, TILE), TILE)
        bias = jnp.where(key_owner[rows, 0:1] == owner_row, 0.0, floor_value)
        sums = []
        for h in range(HEADS):
            s = nt(k_ref[rows, pair_columns(h)], masked_q[h])
            p = jnp.exp((s - lse[h : h + 1, :]) + bias)
            dp = nt(v_ref[rows, pair_columns(h)], masked_do[h])
            weights[j, h] = p
            d_weights[j, h] = dp
            sums.append(jnp.sum(p * dp, axis=0, keepdims=True))
        dots[...] += jnp.concatenate(sums, axis=0)
        return carry

    lax.fori_loop(lo, hi, weigh_tile, 0)

    def grad_tile(j, carry):
        rows = pl.ds(pl.multiple_of(j * TILE, TILE), TILE)
        for pair in range(HEADS // 2):
            cols = pair_columns(2 * pair)
            dv_part = dv_sum[rows, cols]
            dk_part = dk_sum[rows, cols]
            for h in (2 * pair, 2 * pair + 1):
                p = weights[j, h]
                ds = (p * (d_weights[j, h] - dots[h : h + 1, :])).astype(LOW)
                dv_part = dv_part + nn(p.astype(LOW), masked_do[h])
                dk_part = dk_part + nn(ds, masked_q[h])
                dqt[head_rows(h), :] += nn(kt[head_rows(h), rows], ds)
            dv_sum[rows, cols] = dv_part
            dk_sum[rows, cols] = dk_part
        return carry

    lax.fori_loop(lo, hi, grad_tile, 0)
    dq[...] = (dqt[...] * HEAD**-0.5).T.astype(LOW)

    @pl.when(i == pl.num_programs(0) - 1)
    def _():
        dk[...] = dk_sum[...].astype(LOW)
        dv[...] = dv_sum[...].astype(LOW)


def attention_backward(plan, q, kv, d_context, lse, owner, key_owner, name):
    number, width = q.shape
    keys = kv.shape[0]
    return call(
        attention_back_kernel,
        (number // TILE,),
        [
            rows_of(width),
            at_block((keys, width), 0, 0),
            at_block((keys, width), 0, 1),
            rows_of(width),
            pl.BlockSpec((HEADS, TILE), lambda i, *_: (0, i)),
        ]
        + owner_specs(keys),
        [rows_of(width), whole((keys, width)), whole((keys, width))],
        [shaped((number, width), LOW), shaped((keys, width), LOW), shaped((keys, width), LOW)],
        [
            pltpu.VMEM((width, keys), LOW),
            pltpu.VMEM((keys, 8), F32),
            pltpu.VMEM((HEADS, TILE, LANES), LOW),
            pltpu.VMEM((HEADS, TILE, LANES), LOW),
            pltpu.VMEM((width, TILE), F32),
            pltpu.VMEM((keys, width), F32),
            pltpu.VMEM((keys, width), F32),
            pltpu.VMEM((keys // TILE, HEADS, TILE, TILE), F32),
            pltpu.VMEM((keys // TILE, HEADS, TILE, TILE), F32),
            pltpu.VMEM((HEADS, TILE), F32),
        ],
        number * keys * width * 4,
        12 * number * width,
        name,
    )(plan, q, kv, kv, d_context, lse, owner, key_owner)


def cross_back_kernel(plan, d_query, dk, dv, normed, inverse, d_above, memory, context, wq, wk_a, wk_b, wo, small,
                      d_memory, d_sum, d_context, g_query, g_pair, g_out, sums, d_product):
    i = pl.program_id(0)
    mine = pl.ds(pl.multiple_of(i * TILE, TILE), TILE)

    @pl.when(i == 0)
    def _():
        sums[...] = jnp.zeros_like(sums)
        low = normed[...] * small[4:5, :] + small[5:6, :]
        g_query[...] = nn(low.T.astype(LOW), d_query[...]).astype(LOW)

    wk = jnp.concatenate([block_of(wk_a, 0), block_of(wk_b, 0)], axis=0)
    wv = jnp.concatenate([block_of(wk_a, 1), block_of(wk_b, 1)], axis=0)
    d_memory[...] = nt(dk[mine, :], wk) + nt(dv[mine, :], wv)
    d_one = d_above[...] + nt(d_query[mine, :], wq[...])
    hat = normed[mine, :]
    sums[0:1, :] += jnp.sum(d_one * hat, axis=0, keepdims=True)
    sums[1:2, :] += jnp.sum(d_one, axis=0, keepdims=True)
    total = ln_backward(d_one, hat, inverse[:, 0:1], small[4:5, :])
    d_sum[...] = total
    place = lax.broadcasted_iota(jnp.int32, (TILE, 1), 0) + i * TILE
    live = (place < plan[2, 0]).astype(F32)
    product = (total * live).astype(LOW)
    d_product[mine, :] = product
    d_context[...] = nt(product, wo[...]).astype(LOW)

    @pl.when(i == 1)
    def _():
        turn = turned(memory[...])
        put_block(g_pair, 0, nn(turn, dk[...]).astype(LOW))

    @pl.when(i == 2)
    def _():
        turn = turned(memory[...])
        put_block(g_pair, 1, nn(turn, dv[...]).astype(LOW))

    @pl.when(i == pl.num_programs(0) - 1)
    def _():
        g_out[...] = nn(turned(context[...]), d_product[...]).astype(LOW)


def cross_projections_back(plan, d_query, dk, dv, normed, inverse, d_above, memory, context, dec_rows, wk_two, small):
    number, width = normed.shape
    full = whole((number, width))
    square = whole((width, width))
    half = (width // 32, 2, 16, width)
    return call(
        cross_back_kernel,
        (number // TILE,),
        [full, full, full, full, rows_of(LANES), rows_of(width), full, full,
         at_block((width, width), 4, 0), at_block(half, 5, 0, 0, 0), at_block(half, 6, 0, 0, 0),
         at_block((width, width), 3, 0), whole(small.shape)],
        [rows_of(width), rows_of(width), rows_of(width), square, whole((width // 16, 2, 16, width)), square,
         whole((8, width))],
        [shaped((number, width), F32), shaped((number, width), F32), shaped((number, width), LOW),
         shaped((width, width), LOW), shaped((width // 16, 2, 16, width), LOW), shaped((width, width), LOW),
         shaped((8, width), F32)],
        [pltpu.VMEM((number, width), LOW)],
        16 * number * width * width,
        24 * number * width,
        "cross_projections_back",
    )(plan, d_query, dk, dv, normed, inverse, d_above, memory, context, dec_rows, wk_two, wk_two, dec_rows, small)


def qkv_weights_kernel(plan, x, dq, dk, dv, g_qkv, turn):
    i = pl.program_id(0)

    @pl.when(i == 0)
    def _():
        turn[...] = turned(x[...])

    for j, ref in enumerate((dq, dk, dv)):

        @pl.when(i == j)
        def _(ref=ref):
            put_block(g_qkv, 0, nn(turn[...], ref[...]).astype(LOW))


def qkv_weights(plan, x, dq, dk, dv, units, name):
    number, width = x.shape
    full = whole((number, width))
    if units:
        shape = (width // 16, 3, 16, width)
        spec = pl.BlockSpec((width // 16, 1, 16, width), lambda i, *_: (0, i, 0, 0))
    else:
        shape = (3, width, width)
        spec = pl.BlockSpec((1, width, width), lambda i, *_: (i, 0, 0))
    return call(
        qkv_weights_kernel,
        (3,),
        [full] * 4,
        spec,
        shaped(shape, LOW),
        [pltpu.VMEM((width, number), LOW)],
        6 * number * width * width,
        12 * number * width,
        name,
    )(plan, x, dq, dk, dv)


def qkv_inputs_kernel(plan, *refs, masked):
    if masked:
        dq, dk, dv, d_above, wqkv, flags, d_x, mask_sum = refs
    else:
        dq, dk, dv, d_above, wqkv, d_x = refs
    pieces = jnp.concatenate([dq[...], dk[...], dv[...]], axis=1)
    weights = jnp.concatenate([block_of(wqkv, j) for j in range(3)], axis=1)
    total = nt(pieces, weights)
    if masked:
        total = total + d_above[...]

        @pl.when(pl.program_id(0) == 0)
        def _():
            mask_sum[...] = jnp.zeros_like(mask_sum)

        hit = column_of(flags[...]) == 1.0
        d_x[...] = jnp.where(hit, 0.0, total)
        mask_sum[0:1, :] += jnp.sum(jnp.where(hit, total, 0.0), axis=0, keepdims=True)
    else:
        d_x[...] = d_above[...]
        d_x[...] += total


def qkv_inputs(plan, dq, dk, dv, d_above, wqkv, wqkv_spec, flags, name):
    number, width = dq.shape
    masked = flags is not None
    in_specs = [rows_of(width)] * 4 + [wqkv_spec]
    out_specs = [rows_of(width)]
    out_shape = [shaped((number, width), F32)]
    operands = [dq, dk, dv, d_above, wqkv]
    if masked:
        in_specs.append(pl.BlockSpec((1, TILE), lambda i, *_: (0, i)))
        out_specs.append(whole((8, width)))
        out_shape.append(shaped((8, width), F32))
        operands.append(flags)
    return call(
        functools.partial(qkv_inputs_kernel, masked=masked),
        (number // TILE,),
        in_specs,
        out_specs,
        out_shape,
        [],
        6 * number * width * width,
        16 * number * width,
        name,
    )(plan, *operands)


def enc_regions(width, inner):
    return ((0, 3 * width, 3), (4 * width, 4 * width + inner, inner // width))


def dec_regions(width, inner):
    return ((5 * width, 7 * width, 2), (8 * width, 8 * width + inner, inner // width))


def to_units(rows, k):
    return rows.reshape(-1, 16, k, rows.shape[1]).transpose(0, 2, 1, 3).reshape(rows.shape)


def from_units(rows, k):
    return rows.reshape(-1, k, 16, rows.shape[1]).transpose(0, 2, 1, 3).reshape(rows.shape)


def fits(size, region):
    return size % (16 * region[2]) == 0


def arrange_own(rows, first, regions, arrange):
    place = first + lax.broadcasted_iota(jnp.int32, (rows.shape[0], 1), 0)
    result = rows
    for region in regions:
        if fits(rows.shape[0], region):
            inside = (place >= region[0]) & (place < region[1])
            result = jnp.where(inside, arrange(rows, region[2]), result)
    return result


def arrange_all(rows, size, regions, arrange):
    for region in regions:
        if not fits(size, region):
            part = arrange(rows[region[0] : region[1]], region[2])
            rows = jnp.concatenate([rows[: region[0]], part, rows[region[1] :]], axis=0)
    return rows


def owners_of(lengths, number):
    bounds = jnp.cumsum(lengths)
    places = jnp.arange(number, dtype=jnp.int32)
    owners = jnp.sum((places[:, None] >= bounds[None, :]).astype(jnp.int32), axis=1)
    filled = places < bounds[-1]
    for_queries = jnp.where(filled, owners, -2).astype(F32)[None, :]
    for_keys = jnp.where(filled, owners, -1).astype(F32)[None, :]
    return for_queries, for_keys, bounds


def plan_of(query_bounds, key_bounds, key_lengths, number):
    firsts = jnp.arange(8, dtype=jnp.int32) * TILE
    filled = query_bounds[-1]
    lasts = jnp.minimum(firsts + TILE, filled) - 1

    def pair_of(places):
        found = jnp.sum((places[:, None] >= query_bounds[None, :]).astype(jnp.int32), axis=1)
        return jnp.minimum(found, key_lengths.shape[0] - 1)

    def pick(values, pairs):
        chosen = pairs[:, None] == jnp.arange(values.shape[0])[None, :]
        return jnp.sum(jnp.where(chosen, values[None, :], 0), axis=1)

    begin = pick(key_bounds - key_lengths, pair_of(firsts))
    end = pick(key_bounds, pair_of(lasts))
    some = firsts < filled
    lo = jnp.where(some, begin // TILE, 0)
    hi = jnp.where(some, (end + TILE - 1) // TILE, 0)
    return jnp.stack([lo, hi, jnp.full_like(lo, filled)]).astype(jnp.int32)


def moments(gradient, first, second):
    first_new = beta_one * first + (1.0 - beta_one) * gradient
    second_new = beta_two * second + (1.0 - beta_two) * gradient * gradient
    return (first_new, second_new)


def adamw(weight, gradient, first, second):
    first_new, second_new = moments(gradient, first, second)
    moved = weight - rate * (
        first_new
        / (1.0 - beta_one**STEPS)
        / (jnp.sqrt(second_new / (1.0 - beta_two**STEPS)) + epsilon)
        + decay * weight
    )
    return (moved, first_new, second_new)


CORE, X, Y, Z_LOW, Z_HIGH = 0, 1, 2, 3, 4
BITS = 5


def partner(bit):
    return [(i, i ^ (1 << bit)) for i in range(1 << BITS)]


def bit_of(me, bit):
    return (me >> bit) & 1


def take(values, axis, index):
    return lax.dynamic_index_in_dim(values, index, axis, keepdims=False)


def overlaps(sizes, own):
    found = []
    first = 0
    for piece, size in enumerate(sizes):
        at = first
        while at < first + size:
            owner = at // own
            end = min(first + size, (owner + 1) * own)
            found.append((piece, at - first, owner, at - owner * own, end - at))
            at = end
        first += size
    return found


def pack_kernel(core, *refs, copies, number):
    pieces, send, keep, semaphores = refs[:number], refs[number], refs[number + 1], refs[number + 2]
    for side in (0, 1):

        @pl.when(core[0] == side)
        def _():
            handles = []
            for n, (piece, at, owner, to, rows) in enumerate(copies):
                target = keep if owner % 2 == side else send
                handles.append(
                    pltpu.make_async_copy(
                        pieces[piece].at[pl.ds(at, rows)],
                        target.at[owner // 2, pl.ds(to, rows)],
                        semaphores.at[n],
                    )
                )
            for handle in handles:
                handle.start()
            for handle in handles:
                handle.wait()


def pack(core, pieces, copies, block, name):
    width = pieces[0].shape[1]
    shape = shaped((1 << (BITS - 1), block, width), LOW)
    anywhere = pl.BlockSpec(memory_space=pl.ANY)
    total = sum(piece.size for piece in pieces)
    return call(
        functools.partial(pack_kernel, copies=copies, number=len(pieces)),
        (1,),
        [whole(piece.shape) for piece in pieces],
        [anywhere, anywhere],
        [shape, shape],
        [pltpu.SemaphoreType.DMA((len(copies),))],
        0,
        4 * total,
        name,
    )(core, *pieces)


def add_low(former, latter):
    return (former.astype(F32) + latter.astype(F32)).astype(LOW)


def swap(values, bit):
    return lax.ppermute(values, "fsdp", partner(bit))


def reduce_owned(me, send, keep, cut):
    rows, width = send.shape[1:]
    x, y, low, high = (bit_of(me, b) for b in (X, Y, Z_LOW, Z_HIGH))
    (send,) = yield (send,)
    chips = add_low(keep, swap(send, CORE)).reshape(2, 2, 2, 2, rows, width)
    first, second = chips[..., :cut, :], chips[..., cut:, :]
    for_y, for_x = yield (take(first, 2, 1 - y), take(second, 3, 1 - x))
    first = add_low(take(first, 2, y), swap(for_y, Y))
    second = add_low(take(second, 3, x), swap(for_x, X))
    for_x, for_y = yield (take(first, 2, 1 - x), take(second, 2, 1 - y))
    first = add_low(take(first, 2, x), swap(for_x, X))
    second = add_low(take(second, 2, y), swap(for_y, Y))
    column = jnp.concatenate([first, second], axis=2)
    (for_z,) = yield (take(column, 1, 1 - low),)
    column = add_low(take(column, 1, low), swap(for_z, Z_LOW))
    (for_z,) = yield (take(column, 0, 1 - high),)
    return take(column, 0, high).astype(F32) + swap(for_z, Z_HIGH).astype(F32)


class Rounds:
    def __init__(self, steps):
        self.steps = steps
        self.sent = next(steps)
        self.result = None

    def before(self, *operands):
        sent, operands = lax.optimization_barrier((self.sent, operands))
        self.move(sent)
        return operands[0] if len(operands) == 1 else operands

    def move(self, sent):
        try:
            self.sent = self.steps.send(sent)
        except StopIteration as stop:
            self.sent, self.result = None, stop.value

    def finish(self):
        while self.result is None:
            self.move(self.sent)
        return self.result


def on_device(
    devices,
    src_in,
    tgt_in,
    src_len,
    tgt_len,
    tgt_mask,
    enc_cot,
    dec_cot,
    enc_master,
    enc_first,
    enc_second,
    dec_master,
    dec_first,
    dec_second,
    small_master,
    small_first,
    small_second,
):
    width = src_in.shape[1]
    number = src_in.shape[0]
    me = lax.axis_index("fsdp")
    enc_size, dec_size = enc_master.shape[0], dec_master.shape[0]
    enc_count, dec_count = enc_size * devices, dec_size * devices
    inner = (enc_count - 4 * width) // 2
    ups = inner // width
    enc_map, dec_map = enc_regions(width, inner), dec_regions(width, inner)

    enc_own = arrange_own(enc_master.astype(LOW), me * enc_size, enc_map, to_units)
    dec_own = arrange_own(dec_master.astype(LOW), me * dec_size, dec_map, to_units)
    enc_rows = lax.all_gather(enc_own, "fsdp", axis=0, tiled=True)
    dec_rows = lax.all_gather(dec_own, "fsdp", axis=0, tiled=True)
    small_rows = lax.all_gather(small_master.astype(LOW), "fsdp", axis=1, tiled=True)

    src_owner, src_key, src_bounds = owners_of(src_len[0], number)
    tgt_owner, tgt_key, tgt_bounds = owners_of(tgt_len[0], number)
    enc_plan = plan_of(src_bounds, src_bounds, src_len[0], number)
    dec_plan = plan_of(tgt_bounds, tgt_bounds, tgt_len[0], number)
    cross_plan = plan_of(tgt_bounds, src_bounds, src_len[0], number)

    smalls = jnp.pad(small_rows.astype(F32), ((0, 5), (0, 0)))
    masked = tgt_mask[:, None] == 1
    start = jnp.where(masked, small_rows[10][None, :], tgt_in)
    flags = tgt_mask.astype(F32)[None, :]

    enc_rows = arrange_all(enc_rows, enc_size, enc_map, to_units)
    dec_rows = arrange_all(dec_rows, dec_size, dec_map, to_units)
    enc_three = enc_rows.reshape(-1, 3, 16, width)
    enc_four = enc_rows.reshape(-1, ups, 16, width)
    dec_two = dec_rows.reshape(-1, 2, 16, width)
    dec_four = dec_rows.reshape(-1, ups, 16, width)
    dec_three = dec_rows[: 3 * width].reshape(width, 3, width).transpose(1, 0, 2)
    units = width // 16
    three_spec = at_block((units, 3, 16, width), 0, 0, 0, 0)
    enc_up = at_block((units, ups, 16, width), 1, 0, 0, 0)
    enc_down = at_block((inner, width), 2, 0)
    enc_wo = at_block((width, width), 3, 0)
    dec_up = at_block((units, ups, 16, width), 2, 0, 0, 0)
    dec_down = at_block((inner, width), 3, 0)

    e_q, e_kv, e_ctx, e_lse, e_hat, e_inv = self_block(
        enc_plan, src_in, enc_three, three_spec, enc_rows, enc_wo, smalls, 0, src_owner, src_key, "enc_block"
    )
    e_hidden, e_slope, memory, t_hat, t_inv = ffn_forward(
        enc_plan, e_hat, enc_four, enc_up, enc_rows, enc_down, smalls, 0, 2, inner, "enc_ffn"
    )
    s_q, s_kv, s_ctx, s_lse, s_hat, s_inv = self_block(
        dec_plan, start, dec_three, whole(dec_three.shape), dec_rows, at_block((width, width), 3, 0), smalls, 4,
        tgt_owner, tgt_key, "dec_block",
    )
    c_q, c_kv, c_ctx, c_lse, c_hat, c_inv = cross_block(
        cross_plan, s_hat, memory, dec_rows, dec_two, smalls, tgt_owner, src_key
    )
    d_hidden, d_slope, decoded, f_hat, f_inv = ffn_forward(
        dec_plan, c_hat, dec_four, dec_up, dec_rows, dec_down, smalls, 6, 8, inner, "dec_ffn"
    )

    dd_inner, dd_down, d_two, d_cross, d_cctx, sums_d = ffn_backward(
        dec_plan, [dec_cot], (f_hat, f_inv), d_slope, (c_hat, c_inv), (dec_four, dec_rows, dec_rows),
        [dec_up, dec_down, at_block((width, width), 7, 0)], smalls, 6, 8, "dec_ffn_back",
    )
    g_dup, g_ddown, g_cout = ffn_weights(
        dec_plan, c_hat, dd_inner, dd_down, d_hidden, c_ctx, d_cross, smalls, 6, "dec_ffn_weights"
    )
    dcq, dck, dcv = attention_backward(cross_plan, c_q, c_kv, d_cctx, c_lse, tgt_owner, src_key, "cross_back")
    d_memory, d_one, d_sctx, g_cq, g_ckv, g_sout, sums_c = cross_projections_back(
        dec_plan, dcq, dck, dcv, s_hat, s_inv, d_two, memory, s_ctx, dec_rows, dec_two, smalls
    )
    dsq, dsk, dsv = attention_backward(dec_plan, s_q, s_kv, d_sctx, s_lse, tgt_owner, tgt_key, "dec_back")
    g_sqkv = qkv_weights(dec_plan, start, dsq, dsk, dsv, False, "dec_qkv_weights")
    dec_pieces = [
        g_sqkv.transpose(1, 0, 2).reshape(-1, width),
        g_sout,
        g_cq,
        g_ckv.reshape(-1, width),
        g_cout,
        g_dup.reshape(-1, width),
        g_ddown,
    ]
    by_rounds = devices == 1 << BITS
    rounds = None
    if by_rounds:
        core = bit_of(me, CORE)[None].astype(jnp.int32)
        copies = overlaps([p.shape[0] for p in dec_pieces], dec_size)
        send, keep = pack(core, dec_pieces, copies, dec_size, "dec_pack")
        rounds = Rounds(reduce_owned(me, send, keep, dec_size // 2))
        dsq, dsk, dsv = rounds.before(dsq, dsk, dsv)
    tgt_grad, mask_sum = qkv_inputs(
        dec_plan, dsq, dsk, dsv, d_one, dec_three, whole(dec_three.shape), flags, "dec_qkv_inputs"
    )
    if by_rounds:
        d_memory, mask_sum = rounds.before(d_memory, mask_sum)
    de_inner, de_down, d_mid, d_eattn, d_ectx, sums_e = ffn_backward(
        enc_plan, [enc_cot, d_memory], (t_hat, t_inv), e_slope, (e_hat, e_inv), (enc_four, enc_rows, enc_rows),
        [enc_up, enc_down, enc_wo], smalls, 0, 2, "enc_ffn_back",
    )
    if by_rounds:
        de_inner, d_ectx = rounds.before(de_inner, d_ectx)
    g_up, g_down, g_out = ffn_weights(
        enc_plan, e_hat, de_inner, de_down, e_hidden, e_ctx, d_eattn, smalls, 0, "enc_ffn_weights"
    )
    if by_rounds:
        d_ectx, g_up = rounds.before(d_ectx, g_up)
    deq, dek, dev = attention_backward(enc_plan, e_q, e_kv, d_ectx, e_lse, src_owner, src_key, "enc_back")
    if by_rounds:
        deq, dek, dev = rounds.before(deq, dek, dev)
    g_qkv = qkv_weights(enc_plan, src_in, deq, dek, dev, True, "enc_qkv_weights")

    enc_pieces = [g_qkv.reshape(-1, width), g_out, g_up.reshape(-1, width), g_down]
    small_grad = jnp.concatenate([sums_e[:4], sums_c[:2], sums_d[:4], mask_sum[:1]], axis=0)
    share = small_master.shape[1]
    small_wire = small_grad.reshape(-1, devices, share).transpose(1, 0, 2).reshape(devices, -1).astype(LOW)
    held = small_wire.shape[1]
    small_wire = jnp.pad(small_wire, ((0, 0), (0, 16 * width - held))).reshape(devices * 16, width)
    if by_rounds:
        dec_summed = rounds.finish()
        copies = overlaps([p.shape[0] for p in enc_pieces], enc_size)
        copies += [(len(enc_pieces), 16 * i, i, enc_size, 16) for i in range(devices)]
        send, keep = pack(core, enc_pieces + [small_wire], copies, enc_size + 16, "enc_pack")
        rounds = Rounds(reduce_owned(me, send, keep, enc_size // 2 + 16))
        deq, dek, dev = rounds.before(deq, dek, dev)
    src_grad = qkv_inputs(enc_plan, deq, dek, dev, d_mid, enc_three, three_spec, None, "enc_qkv_inputs")[0]
    if by_rounds:
        enc_summed = rounds.finish()
    else:
        dec_grad = arrange_all(jnp.concatenate(dec_pieces, axis=0), dec_size, dec_map, from_units)
        enc_grad = arrange_all(jnp.concatenate(enc_pieces, axis=0), enc_size, enc_map, from_units)
        enc_wire = jnp.concatenate(
            [enc_grad.reshape(devices, enc_size, width), small_wire.reshape(devices, 16, width)], axis=1
        )
        dec_summed = lax.psum_scatter(dec_grad, "fsdp", scatter_dimension=0, tiled=True).astype(F32)
        enc_summed = lax.psum_scatter(
            enc_wire.reshape(-1, width), "fsdp", scatter_dimension=0, tiled=True
        ).astype(F32)
    small_summed = enc_summed[enc_size:].reshape(-1)[:held].reshape(-1, share)
    enc_summed = arrange_own(enc_summed[:enc_size], me * enc_size, enc_map, from_units)
    dec_summed = arrange_own(dec_summed, me * dec_size, dec_map, from_units)

    part = 1.0 / devices
    enc_summed = enc_summed * part
    dec_summed = dec_summed * part
    small_summed = small_summed * part
    enc_new, enc_first_new, encoder_second_moment_updated = adamw(
        enc_master, enc_summed, enc_first, enc_second
    )
    dec_new, dec_first_new, dec_second_new = adamw(dec_master, dec_summed, dec_first, dec_second)
    small_first_new, small_second_new = moments(small_summed, small_first, small_second)
    return (
        memory,
        decoded,
        src_grad,
        tgt_grad,
        enc_new,
        enc_first_new,
        encoder_second_moment_updated,
        enc_new.astype(LOW),
        dec_new,
        dec_first_new,
        dec_second_new,
        dec_new.astype(LOW),
        small_summed,
        small_first_new,
        small_second_new,
    )


def solution(mesh):
    rows = P("fsdp", None)
    columns = P(None, "fsdp")
    return jax.shard_map(
        functools.partial(on_device, mesh.shape["fsdp"]),
        mesh=mesh,
        in_specs=(rows,) * 4 + (P("fsdp"),) + (rows,) * 8 + (columns,) * 3,
        out_specs=(rows,) * 12 + (columns,) * 3,
        check_vma=False,
    )
```

```python
import functools

import jax
import jax.numpy as jnp
from jax import lax
from jax.experimental import pallas as pl
from jax.experimental.pallas import tpu as pltpu
from jax.sharding import PartitionSpec as P

HEADS = 8
HEAD = 64
STEPS = 7
TILE = 256
LANES = 128

rate = 0.02
beta_one = 0.9
beta_two = 0.98
epsilon = 1e-06
decay = 0.01
floor_value = -1000000000.0
root_half = 0.7071067811865476
inverse_root_tau = 0.3989422804014327

F32 = jnp.float32
LOW = jnp.bfloat16
MIB = 2**20


def nn(former, latter):
    return lax.dot_general(
        former, latter, (((1,), (0,)), ((), ())), preferred_element_type=F32
    )


def nt(former, latter):
    return lax.dot_general(
        former, latter, (((1,), (1,)), ((), ())), preferred_element_type=F32
    )


def turned(values):
    return values.astype(F32).T.astype(LOW)


def column_of(row):
    return jnp.broadcast_to(row, (8, row.shape[1])).T[:, 0:1]


def ln_forward(values, gain, shift):
    centered = values - jnp.mean(values, axis=-1, keepdims=True)
    spread = jnp.mean(centered * centered, axis=-1, keepdims=True)
    inverse = lax.rsqrt(spread + 1e-05)
    normed = centered * inverse
    return normed * gain + shift, normed, inverse


def ln_backward(upstream, normed, inverse, gain):
    scaled = upstream * gain
    first = jnp.mean(scaled, axis=-1, keepdims=True)
    second = jnp.mean(scaled * normed, axis=-1, keepdims=True)
    return inverse * (scaled - first - normed * second)


def phi_and_slope(values):
    phi = 0.5 + 0.5 * lax.erf(values * root_half)
    return phi, phi + values * (jnp.exp(-0.5 * (values * values)) * inverse_root_tau)


def one_head(pair, head):
    lane = lax.broadcasted_iota(jnp.int32, pair.shape, 1)
    keep = lane < HEAD if head % 2 == 0 else lane >= HEAD
    return jnp.where(keep, pair, jnp.zeros_like(pair))


def pair_columns(head):
    return slice(LANES * (head // 2), LANES * (head // 2) + LANES)


def head_rows(head):
    return slice(HEAD * head, HEAD * head + HEAD)


def block_of(ref, j, count):
    if count == 1:
        return ref[...]
    return jnp.concatenate(
        [ref[first + 16 * j : first + 16 * j + 16, :] for first in range(0, ref.shape[0], 16 * count)], axis=0
    )


def spread(wide, values):
    for n in range(wide.shape[0]):
        wide[n] = values[:, LANES * n : LANES * n + LANES].astype(F32)


def third_rows(wide, j):
    rows = pl.ds(j, wide.shape[1] // 3, stride=3)
    return jnp.concatenate([wide[n, rows, :] for n in range(wide.shape[0])], axis=1).astype(LOW)


def put_third_rows(wide, j, values):
    rows = pl.ds(j, wide.shape[1] // 3, stride=3)
    for n in range(wide.shape[0]):
        wide[n, rows, :] = values[:, LANES * n : LANES * n + LANES]


def wide_scratch(width):
    return pltpu.VMEM((width // LANES, 3 * width, LANES), F32)


def put_block(ref, j, values):
    ref[:, j] = values.reshape(ref.shape[0], ref.shape[2], ref.shape[3])


OWNERS = 32


def row_copies(first, last, own, base):
    found = []
    at = first
    while at < last:
        owner = at // own
        end = min(last, (owner + 1) * own)
        found.append((owner, base + at - owner * own, end - at, at - first))
        at = end
    return found


class Fetch:
    def __init__(self, far, copies, near, semaphores, used):
        self.handles = [
            pltpu.make_async_copy(
                far.at[owner, pl.ds(row, rows)], near.at[pl.ds(to, rows)], semaphores.at[used + n]
            )
            for n, (owner, row, rows, to) in enumerate(copies)
        ]

    def start(self):
        for handle in self.handles:
            handle.start()

    def wait(self):
        for handle in self.handles:
            handle.wait()


def fetches(far, wanted, nears, semaphores):
    used = 0
    made = []
    for copies, near in zip(wanted, nears):
        made.append(Fetch(far, copies, near, semaphores, used))
        used += len(copies)
    return made


def fetch_scratch(wanted, width):
    return [pltpu.VMEM((sum(c[2] for c in copies), width), LOW) for copies in wanted] + [
        pltpu.SemaphoreType.DMA((sum(len(copies) for copies in wanted),))
    ]


FAR = pl.BlockSpec(memory_space=pl.ANY)


def call(kernel, grid, in_specs, out_specs, out_shape, scratch, flops, moved, name, room=24, near=(), keep=()):
    single = not isinstance(out_shape, list)
    shapes = [
        (pltpu.VMEM if keep is True or n in keep else pltpu.HBM)(*made)
        for n, made in enumerate([out_shape] if single else out_shape)
    ]
    made = pl.pallas_call(
        kernel,
        grid_spec=pltpu.PrefetchScalarGridSpec(
            num_scalar_prefetch=1,
            grid=grid,
            in_specs=in_specs,
            out_specs=out_specs,
            scratch_shapes=scratch,
        ),
        out_shape=shapes[0] if single else shapes,
        compiler_params=pltpu.CompilerParams(vmem_limit_bytes=room * MIB),
        cost_estimate=pl.CostEstimate(
            flops=flops, bytes_accessed=moved, transcendentals=0
        ),
        name=name,
    )

    def run(plan, *operands):
        placed = [
            operand
            if near is True or n in near
            else pltpu.with_memory_space_constraint(operand, pltpu.HBM)
            for n, operand in enumerate(operands)
        ]
        return made(plan, *placed)

    return run


def whole(shape):
    zeros = (0,) * len(shape)
    return pl.BlockSpec(shape, lambda i, *_: zeros)


def rows_of(width):
    return pl.BlockSpec((TILE, width), lambda i, *_: (i, 0))


def at_block(shape, *index):
    return pl.BlockSpec(shape, lambda i, *_: index)


def shaped(shape, kind):
    return (shape, kind)


def attend_tile(plan, i, keys, key_cols, query, owner_row, key_owner, vt, sc):
    scores, acc, top, total, masked_q = sc
    query = query * jnp.asarray(HEAD**-0.5, LOW)
    for h in range(HEADS):
        masked_q[h] = one_head(query[:, pair_columns(h)], h)
    top[...] = jnp.full_like(top, -1e30)
    total[...] = jnp.zeros_like(total)
    acc[...] = jnp.zeros_like(acc)
    lo = plan[0, i]
    hi = plan[1, i]

    def score_tile(j, carry):
        rows = pl.ds(pl.multiple_of(j * TILE, TILE), TILE)
        bias = jnp.where(key_owner[rows, 0:1] == owner_row, 0.0, floor_value)
        tops = []
        for h in range(HEADS):
            cols = pl.ds(key_cols + LANES * (h // 2), LANES)
            s = nt(keys[rows, cols], masked_q[h]) + bias
            scores[j, h] = s
            tops.append(jnp.max(s, axis=0, keepdims=True))
        top[...] = jnp.maximum(top[...], jnp.concatenate(tops, axis=0))
        return carry

    lax.fori_loop(lo, hi, score_tile, 0)

    def weigh_tile(j, carry):
        rows = pl.ds(pl.multiple_of(j * TILE, TILE), TILE)
        sums = []
        for h in range(HEADS):
            p = jnp.exp(scores[j, h] - top[h : h + 1, :])
            sums.append(jnp.sum(p, axis=0, keepdims=True))
            acc[head_rows(h), :] += nn(vt[head_rows(h), rows], p.astype(LOW))
        total[...] += jnp.concatenate(sums, axis=0)
        return carry

    lax.fori_loop(lo, hi, weigh_tile, 0)


def fwd_block_kernel(plan, *refs, cross, gain_row, wanted, packed, ffn):
    refs = list(refs)

    def next_refs(count):
        taken = refs[:count]
        del refs[:count]
        return taken

    if cross:
        normed_in, memory, far, small, owner_q, owner_k = next_refs(6)
    else:
        x_all, far, small, owner_q, owner_k = next_refs(5)
    q_out, kv_out, ctx_out, lse_out, normed_out, inverse_out = next_refs(6)
    if ffn:
        out, normed_last, inverse_last = next_refs(3)
    kv, vt, mean_v, key_owner, scores, acc, top, total, masked_q, q_all = next_refs(10)
    nears = next_refs(len(wanted))
    semaphores = refs.pop(0)
    loads = fetches(far, wanted, nears, semaphores)
    i = pl.program_id(0)
    width = kv.shape[1] // 2

    @pl.when(i == 0)
    def _():
        for load in loads:
            load.start()
        key_owner[...] = jnp.broadcast_to(owner_k[...], (8, owner_k.shape[1])).T
        loads[0].wait()
        if cross:
            wk, wv = block_of(nears[0], 0, 2), block_of(nears[0], 1, 2)
        elif packed:
            wq, wk, wv = (block_of(nears[0], j, 3) for j in range(3))
        else:
            wide = refs[0]
            spread(wide, nears[0][...])
            wq, wk, wv = (third_rows(wide, j) for j in range(3))
        sums = jnp.zeros((1, width), F32)
        for t in range(kv.shape[0] // TILE):
            rows = slice(t * TILE, t * TILE + TILE)
            x = memory[rows, :] if cross else x_all[rows, :]
            if not cross:
                q_all[rows, :] = nn(x, wq).astype(LOW)
            kv[rows, :width] = nn(x, wk).astype(LOW)
            v = nn(x, wv).astype(LOW)
            kv[rows, width:] = v
            v = v.astype(F32)
            vt[:, rows] = v.T.astype(LOW)
            sums = sums + jnp.sum(v, axis=0, keepdims=True)
        mean_v[...] = sums * (1.0 / kv.shape[0])
        for load in loads[1:]:
            load.wait()

    wo = nears[1]
    mine = pl.ds(pl.multiple_of(i * TILE, TILE), TILE)
    if cross:
        resid = normed_in[...] * small[4:5, :] + small[5:6, :]
        query = nn(resid.astype(LOW), nears[2][...]).astype(LOW)
        q_out[...] = query
    else:
        resid = x_all[mine, :].astype(F32)
        query = q_all[mine, :]
        q_out[...] = query
    kv_out[...] = kv[mine, :]
    owner_row = owner_q[...]
    attend_tile(plan, i, kv, 0, query, owner_row, key_owner, vt, (scores, acc, top, total, masked_q))
    dead = owner_row < 0
    sums = jnp.where(dead, 1.0, total[...])
    share = 1.0 / sums
    lse_out[...] = jnp.where(dead, 0.0, top[...] + jnp.log(sums))
    for h in range(HEADS):
        acc[head_rows(h), :] = acc[head_rows(h), :] * share[h : h + 1, :]
    live = column_of(owner_row) >= 0
    context = jnp.where(live, acc[...].T, mean_v[...]).astype(LOW)
    ctx_out[...] = context
    added = nn(context, wo[...]) * live.astype(F32)
    mid, normed, inverse = ln_forward(
        resid + added, small[gain_row : gain_row + 1, :], small[gain_row + 1 : gain_row + 2, :]
    )
    normed_out[...] = normed
    inverse_out[...] = jnp.broadcast_to(inverse, inverse_out.shape)
    if ffn:
        wup, wdown = nears[-2:]
        blocks = wdown.shape[0] // width
        low = mid.astype(LOW)
        result = mid
        for j in range(blocks):
            inner = nn(low, block_of(wup, j, blocks))
            phi = 0.5 + 0.5 * lax.erf(inner * root_half)
            result = result + nn((inner * phi).astype(LOW), wdown[j * width : j * width + width, :])
        result, normed, inverse = ln_forward(
            result, small[gain_row + 2 : gain_row + 3, :], small[gain_row + 3 : gain_row + 4, :]
        )
        out[...] = result.astype(LOW)
        normed_last[...] = normed
        inverse_last[...] = jnp.broadcast_to(inverse, inverse_last.shape)


def attention_scratch(keys, width):
    return [
        pltpu.VMEM((keys, 2 * width), LOW),
        pltpu.VMEM((width, keys), LOW),
        pltpu.VMEM((1, width), F32),
        pltpu.VMEM((keys, 8), F32),
        pltpu.VMEM((keys // TILE, HEADS, TILE, TILE), F32),
        pltpu.VMEM((width, TILE), F32),
        pltpu.VMEM((HEADS, TILE), F32),
        pltpu.VMEM((HEADS, TILE), F32),
        pltpu.VMEM((HEADS, TILE, LANES), LOW),
        pltpu.VMEM((keys, width), LOW),
    ]


def block_outs(queries, width):
    specs = [
        rows_of(width),
        rows_of(2 * width),
        rows_of(width),
        pl.BlockSpec((HEADS, TILE), lambda i, *_: (0, i)),
        rows_of(width),
        rows_of(LANES),
    ]
    shapes = [
        shaped((queries, width), LOW),
        shaped((queries, 2 * width), LOW),
        shaped((queries, width), LOW),
        shaped((HEADS, queries), F32),
        shaped((queries, width), F32),
        shaped((queries, LANES), F32),
    ]
    return specs, shapes


def owner_specs(keys):
    return [pl.BlockSpec((1, TILE), lambda i, *_: (0, i)), whole((1, keys))]


def fwd_block(plan, x, memory, far, wanted, packed, small, gain_row, owner, key_owner, ffn, name):
    cross = memory is not None
    number, width = x.shape
    specs, shapes = block_outs(number, width)
    if ffn:
        specs += [rows_of(width), rows_of(width), rows_of(LANES)]
        shapes += [shaped((number, width), LOW), shaped((number, width), F32), shaped((number, LANES), F32)]
    scratch = attention_scratch(number, width) + fetch_scratch(wanted, width)
    if not cross and not packed:
        scratch.append(wide_scratch(width))
    return call(
        functools.partial(
            fwd_block_kernel, cross=cross, gain_row=gain_row, wanted=wanted, packed=packed, ffn=ffn
        ),
        (number // TILE,),
        ([rows_of(width), whole(memory.shape)] if cross else [whole(x.shape)])
        + [FAR, whole(small.shape)]
        + owner_specs(number),
        specs,
        shapes,
        scratch,
        8 * number * width * width + number * number * width * 2,
        16 * number * width,
        name,
        room=44,
    )(plan, *([x, memory] if cross else [x]), far, small, owner, key_owner)


def ffn_back_kernel(plan, *refs, tiles, summed, gain_row, wanted):
    refs = list(refs)
    cot = refs.pop(0)
    extra = refs.pop(0) if summed else None
    (normed_top, inverse_top, normed_mid, inverse_mid, context, far, small,
     d_sum, d_context, g_up, g_down, g_out, sums, hidden, d_inner, mid_low, d_down, d_product,
     wup, wdown, wo, semaphores) = refs
    loads = fetches(far, wanted, (wup, wdown, wo), semaphores)
    i = pl.program_id(0)
    width = small.shape[1]
    blocks = wdown.shape[0] // width

    @pl.when(i == 0)
    def _():
        for load in loads:
            load.start()
        sums[...] = jnp.zeros_like(sums)
        for load in loads:
            load.wait()

    @pl.when(i < tiles)
    def _():
        mine = pl.ds(pl.multiple_of(i * TILE, TILE), TILE)
        upstream = cot[...].astype(F32)
        if summed:
            upstream = upstream + extra[...]
        top = normed_top[...]
        sums[2:3, :] += jnp.sum(upstream * top, axis=0, keepdims=True)
        sums[3:4, :] += jnp.sum(upstream, axis=0, keepdims=True)
        d_mid = ln_backward(upstream, top, inverse_top[:, 0:1], small[gain_row + 2 : gain_row + 3, :])
        low = d_mid.astype(LOW)
        d_down[mine, :] = low
        normed = normed_mid[...]
        mid = (normed * small[gain_row : gain_row + 1, :] + small[gain_row + 1 : gain_row + 2, :]).astype(LOW)
        mid_low[mine, :] = mid
        for j in range(blocks):
            cols = slice(j * width, j * width + width)
            up = block_of(wup, j, blocks)
            inner = nn(mid, up)
            phi, slope = phi_and_slope(inner)
            hidden[j, mine, :] = (inner * phi).astype(LOW)
            part = (nt(low, wdown[cols, :]) * slope).astype(LOW)
            d_inner[j, mine, :] = part
            d_mid = d_mid + nt(part, up)
        sums[0:1, :] += jnp.sum(d_mid * normed, axis=0, keepdims=True)
        sums[1:2, :] += jnp.sum(d_mid, axis=0, keepdims=True)
        total = ln_backward(d_mid, normed, inverse_mid[:, 0:1], small[gain_row : gain_row + 1, :])
        d_sum[...] = total
        place = lax.broadcasted_iota(jnp.int32, (TILE, 1), 0) + i * TILE
        live = (place < plan[2, 0]).astype(F32)
        product = (total * live).astype(LOW)
        d_product[mine, :] = product
        d_context[...] = nt(product, wo[...]).astype(LOW)

    @pl.when(i >= tiles)
    def _():
        j = i - tiles
        put_block(g_up, 0, nn(turned(mid_low[...]), d_inner[j]).astype(LOW))
        g_down[...] = nn(turned(hidden[j]), d_down[...]).astype(LOW)

    @pl.when(i == tiles)
    def _():
        g_out[...] = nn(turned(context[...]), d_product[...]).astype(LOW)


def ffn_backward(plan, cots, top, mid, context, far, wanted, small, gain_row, inner, name):
    number, width = mid[0].shape
    tiles, blocks = number // TILE, inner // width

    def tile_of(columns):
        return pl.BlockSpec((TILE, columns), lambda i, *_: (jnp.minimum(i, tiles - 1), 0))

    return call(
        functools.partial(
            ffn_back_kernel, tiles=tiles, summed=len(cots) == 2, gain_row=gain_row, wanted=wanted
        ),
        (tiles + blocks,),
        [tile_of(width)] * len(cots)
        + [tile_of(width), tile_of(LANES), tile_of(width), tile_of(LANES), whole((number, width))]
        + [FAR, whole(small.shape)],
        [
            tile_of(width),
            tile_of(width),
            pl.BlockSpec((width // 16, 1, 16, width), lambda i, *_: (0, jnp.maximum(i - tiles, 0), 0, 0)),
            pl.BlockSpec((width, width), lambda i, *_: (jnp.maximum(i - tiles, 0), 0)),
            pl.BlockSpec((width, width), lambda i, *_: (0, 0)),
            pl.BlockSpec((8, width), lambda i, *_: (0, 0)),
        ],
        [
            shaped((number, width), F32),
            shaped((number, width), LOW),
            shaped((width // 16, blocks, 16, width), LOW),
            shaped((inner, width), LOW),
            shaped((width, width), LOW),
            shaped((8, width), F32),
        ],
        [
            pltpu.VMEM((blocks, number, width), LOW),
            pltpu.VMEM((blocks, number, width), LOW),
            pltpu.VMEM((number, width), LOW),
            pltpu.VMEM((number, width), LOW),
            pltpu.VMEM((number, width), LOW),
        ]
        + fetch_scratch(wanted, width),
        10 * number * width * inner,
        30 * number * width,
        name,
        room=44,
    )(plan, *cots, *top, *mid, context, far, small)


def attention_back_kernel(plan, q_ref, k_ref, v_ref, do_ref, lse, owner_q, owner_k, dq, dk, dv,
                          kt, key_owner, masked_q, masked_do, dqt, dk_sum, dv_sum, weights, d_weights, dots):
    i = pl.program_id(0)

    @pl.when(i == 0)
    def _():
        key_owner[...] = jnp.broadcast_to(owner_k[...], (8, owner_k.shape[1])).T
        kt[...] = turned(k_ref[...])
        dk_sum[...] = jnp.zeros_like(dk_sum)
        dv_sum[...] = jnp.zeros_like(dv_sum)

    query = q_ref[...] * jnp.asarray(HEAD**-0.5, LOW)
    upstream = do_ref[...]
    for h in range(HEADS):
        masked_q[h] = one_head(query[:, pair_columns(h)], h)
        masked_do[h] = one_head(upstream[:, pair_columns(h)], h)
    dqt[...] = jnp.zeros_like(dqt)
    dots[...] = jnp.zeros_like(dots)
    owner_row = owner_q[...]
    lo = plan[0, i]
    hi = plan[1, i]

    def weigh_tile(j, carry):
        rows = pl.ds(pl.multiple_of(j * TILE, TILE), TILE)
        bias = jnp.where(key_owner[rows, 0:1] == owner_row, 0.0, floor_value)
        sums = []
        for h in range(HEADS):
            s = nt(k_ref[rows, pair_columns(h)], masked_q[h])
            p = jnp.exp((s - lse[h : h + 1, :]) + bias)
            dp = nt(v_ref[rows, pair_columns(h)], masked_do[h])
            weights[j, h] = p
            d_weights[j, h] = dp
            sums.append(jnp.sum(p * dp, axis=0, keepdims=True))
        dots[...] += jnp.concatenate(sums, axis=0)
        return carry

    lax.fori_loop(lo, hi, weigh_tile, 0)

    def grad_tile(j, carry):
        rows = pl.ds(pl.multiple_of(j * TILE, TILE), TILE)
        for pair in range(HEADS // 2):
            cols = pair_columns(2 * pair)
            dv_part = dv_sum[rows, cols]
            dk_part = dk_sum[rows, cols]
            for h in (2 * pair, 2 * pair + 1):
                p = weights[j, h]
                ds = (p * (d_weights[j, h] - dots[h : h + 1, :])).astype(LOW)
                dv_part = dv_part + nn(p.astype(LOW), masked_do[h])
                dk_part = dk_part + nn(ds, masked_q[h])
                dqt[head_rows(h), :] += nn(kt[head_rows(h), rows], ds)
            dv_sum[rows, cols] = dv_part
            dk_sum[rows, cols] = dk_part
        return carry

    lax.fori_loop(lo, hi, grad_tile, 0)
    dq[...] = (dqt[...] * HEAD**-0.5).T.astype(LOW)

    @pl.when(i == pl.num_programs(0) - 1)
    def _():
        dk[...] = dk_sum[...].astype(LOW)
        dv[...] = dv_sum[...].astype(LOW)


def attention_backward(plan, q, kv, d_context, lse, owner, key_owner, name):
    number, width = q.shape
    keys = kv.shape[0]
    return call(
        attention_back_kernel,
        (number // TILE,),
        [
            rows_of(width),
            at_block((keys, width), 0, 0),
            at_block((keys, width), 0, 1),
            rows_of(width),
            pl.BlockSpec((HEADS, TILE), lambda i, *_: (0, i)),
        ]
        + owner_specs(keys),
        [rows_of(width), whole((keys, width)), whole((keys, width))],
        [shaped((number, width), LOW), shaped((keys, width), LOW), shaped((keys, width), LOW)],
        [
            pltpu.VMEM((width, keys), LOW),
            pltpu.VMEM((keys, 8), F32),
            pltpu.VMEM((HEADS, TILE, LANES), LOW),
            pltpu.VMEM((HEADS, TILE, LANES), LOW),
            pltpu.VMEM((width, TILE), F32),
            pltpu.VMEM((keys, width), F32),
            pltpu.VMEM((keys, width), F32),
            pltpu.VMEM((keys // TILE, HEADS, TILE, TILE), F32),
            pltpu.VMEM((keys // TILE, HEADS, TILE, TILE), F32),
            pltpu.VMEM((HEADS, TILE), F32),
        ],
        number * keys * width * 4,
        12 * number * width,
        name,
        room=44,
    )(plan, q, kv, kv, d_context, lse, owner, key_owner)


def cross_back_kernel(plan, d_query, dk, dv, normed, inverse, d_above, memory, context, far, small,
                      d_memory, d_sum, d_context, g_query, g_pair, g_out, sums, d_product, wkv, wq, wo, semaphores,
                      *, wanted):
    i = pl.program_id(0)
    mine = pl.ds(pl.multiple_of(i * TILE, TILE), TILE)

    loads = fetches(far, wanted, (wkv, wq, wo), semaphores)

    @pl.when(i == 0)
    def _():
        for load in loads:
            load.start()
        sums[...] = jnp.zeros_like(sums)
        low = normed[...] * small[4:5, :] + small[5:6, :]
        g_query[...] = nn(low.T.astype(LOW), d_query[...]).astype(LOW)
        for load in loads:
            load.wait()

    wk, wv = block_of(wkv, 0, 2), block_of(wkv, 1, 2)
    d_memory[...] = nt(dk[mine, :], wk) + nt(dv[mine, :], wv)
    d_one = d_above[...] + nt(d_query[mine, :], wq[...])
    hat = normed[mine, :]
    sums[0:1, :] += jnp.sum(d_one * hat, axis=0, keepdims=True)
    sums[1:2, :] += jnp.sum(d_one, axis=0, keepdims=True)
    total = ln_backward(d_one, hat, inverse[:, 0:1], small[4:5, :])
    d_sum[...] = total
    place = lax.broadcasted_iota(jnp.int32, (TILE, 1), 0) + i * TILE
    live = (place < plan[2, 0]).astype(F32)
    product = (total * live).astype(LOW)
    d_product[mine, :] = product
    d_context[...] = nt(product, wo[...]).astype(LOW)

    @pl.when(i == 1)
    def _():
        turn = turned(memory[...])
        put_block(g_pair, 0, nn(turn, dk[...]).astype(LOW))

    @pl.when(i == 2)
    def _():
        turn = turned(memory[...])
        put_block(g_pair, 1, nn(turn, dv[...]).astype(LOW))

    @pl.when(i == pl.num_programs(0) - 1)
    def _():
        g_out[...] = nn(turned(context[...]), d_product[...]).astype(LOW)


def cross_projections_back(plan, d_query, dk, dv, normed, inverse, d_above, memory, context, far, wanted, small):
    number, width = normed.shape
    full = whole((number, width))
    square = whole((width, width))
    return call(
        functools.partial(cross_back_kernel, wanted=wanted),
        (number // TILE,),
        [full, full, full, full, rows_of(LANES), rows_of(width), full, full, FAR, whole(small.shape)],
        [rows_of(width), rows_of(width), rows_of(width), square, whole((width // 16, 2, 16, width)), square,
         whole((8, width))],
        [shaped((number, width), F32), shaped((number, width), F32), shaped((number, width), LOW),
         shaped((width, width), LOW), shaped((width // 16, 2, 16, width), LOW), shaped((width, width), LOW),
         shaped((8, width), F32)],
        [pltpu.VMEM((number, width), LOW)] + fetch_scratch(wanted, width),
        16 * number * width * width,
        24 * number * width,
        "cross_projections_back",
    )(plan, d_query, dk, dv, normed, inverse, d_above, memory, context, far, small)


def qkv_weights_kernel(plan, x, dq, dk, dv, g_qkv, turn, *wide):
    i = pl.program_id(0)
    width = turn.shape[0]

    @pl.when(i == 0)
    def _():
        turn[...] = turned(x[...])

    for j, ref in enumerate((dq, dk, dv)):

        @pl.when(i == j)
        def _(j=j, ref=ref):
            made = nn(turn[...], ref[...])
            if not wide:
                put_block(g_qkv, 0, made.astype(LOW))
            else:
                put_third_rows(wide[0], j, made)

    if wide:

        @pl.when(i == 2)
        def _():
            for n in range(width // LANES):
                g_qkv[:, LANES * n : LANES * n + LANES] = wide[0][n].astype(LOW)


def qkv_weights(plan, x, dq, dk, dv, packed, name):
    number, width = x.shape
    full = whole((number, width))
    scratch = [pltpu.VMEM((width, number), LOW)]
    if packed:
        shape = (width // 16, 3, 16, width)
        spec = pl.BlockSpec((width // 16, 1, 16, width), lambda i, *_: (0, i, 0, 0))
    else:
        shape = (3 * width, width)
        spec = whole(shape)
        scratch.append(wide_scratch(width))
    return call(
        qkv_weights_kernel,
        (3,),
        [full] * 4,
        spec,
        shaped(shape, LOW),
        scratch,
        6 * number * width * width,
        12 * number * width,
        name,
    )(plan, x, dq, dk, dv)


def qkv_inputs_kernel(plan, *refs, masked, wanted):
    if masked:
        dq, dk, dv, d_above, far, flags, d_x, mask_sum, near, semaphores, blocks, wide = refs
    else:
        dq, dk, dv, d_above, far, d_x, near, semaphores, blocks = refs
    width = dq.shape[1]

    @pl.when(pl.program_id(0) == 0)
    def _():
        (load,) = fetches(far, wanted, (near,), semaphores)
        load.start()
        load.wait()
        if masked:
            mask_sum[...] = jnp.zeros_like(mask_sum)
            spread(wide, near[...])
        for j in range(3):
            if masked:
                blocks[:, j * width : j * width + width] = third_rows(wide, j)
            else:
                blocks[:, j * width : j * width + width] = block_of(near, j, 3)

    pieces = jnp.concatenate([dq[...], dk[...], dv[...]], axis=1)
    total = nt(pieces, blocks[...])
    if masked:
        total = total + d_above[...]
        hit = column_of(flags[...]) == 1.0
        d_x[...] = jnp.where(hit, 0.0, total)
        mask_sum[0:1, :] += jnp.sum(jnp.where(hit, total, 0.0), axis=0, keepdims=True)
    else:
        d_x[...] = d_above[...]
        d_x[...] += total


def qkv_inputs(plan, dq, dk, dv, d_above, far, wanted, flags, name):
    number, width = dq.shape
    masked = flags is not None
    in_specs = [rows_of(width)] * 4 + [FAR]
    out_specs = [rows_of(width)]
    out_shape = [shaped((number, width), F32)]
    operands = [dq, dk, dv, d_above, far]
    scratch = fetch_scratch(wanted, width) + [pltpu.VMEM((width, 3 * width), LOW)]
    if masked:
        in_specs.append(pl.BlockSpec((1, TILE), lambda i, *_: (0, i)))
        out_specs.append(whole((8, width)))
        out_shape.append(shaped((8, width), F32))
        operands.append(flags)
        scratch.append(wide_scratch(width))
    return call(
        functools.partial(qkv_inputs_kernel, masked=masked, wanted=wanted),
        (number // TILE,),
        in_specs,
        out_specs,
        out_shape,
        scratch,
        6 * number * width * width,
        16 * number * width,
        name,
    )(plan, *operands)


def enc_regions(width, inner):
    return ((0, 3 * width, 3), (4 * width, 4 * width + inner, inner // width))


def dec_regions(width, inner):
    return ((5 * width, 7 * width, 2), (8 * width, 8 * width + inner, inner // width))


def to_units(rows, k):
    return rows.reshape(-1, 16, k, rows.shape[1]).transpose(0, 2, 1, 3).reshape(rows.shape)


def from_units(rows, k):
    return rows.reshape(-1, k, 16, rows.shape[1]).transpose(0, 2, 1, 3).reshape(rows.shape)


def fits(size, region):
    return size % (16 * region[2]) == 0


def arrange_own(rows, first, regions, arrange):
    place = first + lax.broadcasted_iota(jnp.int32, (rows.shape[0], 1), 0)
    result = rows
    for region in regions:
        if fits(rows.shape[0], region):
            inside = (place >= region[0]) & (place < region[1])
            result = jnp.where(inside, arrange(rows, region[2]), result)
    return result


def arrange_all(rows, size, regions, arrange):
    for region in regions:
        if not fits(size, region):
            part = arrange(rows[region[0] : region[1]], region[2])
            rows = jnp.concatenate([rows[: region[0]], part, rows[region[1] :]], axis=0)
    return rows


def owners_of(lengths, number):
    bounds = jnp.cumsum(lengths)
    places = jnp.arange(number, dtype=jnp.int32)
    owners = jnp.sum((places[:, None] >= bounds[None, :]).astype(jnp.int32), axis=1)
    filled = places < bounds[-1]
    for_queries = jnp.where(filled, owners, -2).astype(F32)[None, :]
    for_keys = jnp.where(filled, owners, -1).astype(F32)[None, :]
    return for_queries, for_keys, bounds


def plan_of(query_bounds, key_bounds, key_lengths, number):
    firsts = jnp.arange(8, dtype=jnp.int32) * TILE
    filled = query_bounds[-1]
    lasts = jnp.minimum(firsts + TILE, filled) - 1

    def pair_of(places):
        found = jnp.sum((places[:, None] >= query_bounds[None, :]).astype(jnp.int32), axis=1)
        return jnp.minimum(found, key_lengths.shape[0] - 1)

    def pick(values, pairs):
        chosen = pairs[:, None] == jnp.arange(values.shape[0])[None, :]
        return jnp.sum(jnp.where(chosen, values[None, :], 0), axis=1)

    begin = pick(key_bounds - key_lengths, pair_of(firsts))
    end = pick(key_bounds, pair_of(lasts))
    some = firsts < filled
    lo = jnp.where(some, begin // TILE, 0)
    hi = jnp.where(some, (end + TILE - 1) // TILE, 0)
    return jnp.stack([lo, hi, jnp.full_like(lo, filled)]).astype(jnp.int32)


def moments(gradient, first, second):
    first_new = beta_one * first + (1.0 - beta_one) * gradient
    second_new = beta_two * second + (1.0 - beta_two) * gradient * gradient
    return (first_new, second_new)


def adamw(weight, gradient, first, second):
    first_new, second_new = moments(gradient, first, second)
    moved = weight - rate * (
        first_new
        / (1.0 - beta_one**STEPS)
        / (jnp.sqrt(second_new / (1.0 - beta_two**STEPS)) + epsilon)
        + decay * weight
    )
    return (moved, first_new, second_new)


CORE, X, Y, Z_LOW, Z_HIGH = 0, 1, 2, 3, 4
BITS = 5


def partner(bit):
    return [(i, i ^ (1 << bit)) for i in range(1 << BITS)]


def bit_of(me, bit):
    return (me >> bit) & 1


def take(values, axis, index):
    return lax.dynamic_index_in_dim(values, index, axis, keepdims=False)


def overlaps(sizes, own):
    found = []
    first = 0
    for piece, size in enumerate(sizes):
        at = first
        while at < first + size:
            owner = at // own
            end = min(first + size, (owner + 1) * own)
            found.append((piece, at - first, owner, at - owner * own, end - at))
            at = end
        first += size
    return found


def pack_kernel(core, *refs, copies, number):
    pieces, send, keep, semaphores = refs[:number], refs[number], refs[number + 1], refs[number + 2]
    for side in (0, 1):

        @pl.when(core[0] == side)
        def _():
            handles = []
            for n, (piece, at, owner, to, rows) in enumerate(copies):
                target = keep if owner % 2 == side else send
                handles.append(
                    pltpu.make_async_copy(
                        pieces[piece].at[pl.ds(at, rows)],
                        target.at[owner // 2, pl.ds(to, rows)],
                        semaphores.at[n],
                    )
                )
            for handle in handles:
                handle.start()
            for handle in handles:
                handle.wait()


def pack(core, pieces, copies, block, name):
    width = pieces[0].shape[1]
    shape = shaped((1 << (BITS - 1), block, width), LOW)
    anywhere = pl.BlockSpec(memory_space=pl.ANY)
    total = sum(piece.size for piece in pieces)
    return call(
        functools.partial(pack_kernel, copies=copies, number=len(pieces)),
        (1,),
        [pl.BlockSpec(memory_space=pltpu.VMEM)] * len(pieces),
        [anywhere, anywhere],
        [shape, shape],
        [pltpu.SemaphoreType.DMA((len(copies),))],
        0,
        4 * total,
        name,
        near=True,
    )(core, *pieces)


def add_low(former, latter):
    return (former.astype(F32) + latter.astype(F32)).astype(LOW)


def swap(values, bit):
    return lax.ppermute(values, "fsdp", partner(bit))


def reduce_owned(me, send, keep, cut):
    rows, width = send.shape[1:]
    x, y, low, high = (bit_of(me, b) for b in (X, Y, Z_LOW, Z_HIGH))
    (send,) = yield (send,)
    chips = add_low(keep, swap(send, CORE)).reshape(2, 2, 2, 2, rows, width)
    first, second = chips[..., :cut, :], chips[..., cut:, :]
    for_y, for_x = yield (take(first, 2, 1 - y), take(second, 3, 1 - x))
    first = add_low(take(first, 2, y), swap(for_y, Y))
    second = add_low(take(second, 3, x), swap(for_x, X))
    for_x, for_y = yield (take(first, 2, 1 - x), take(second, 2, 1 - y))
    first = add_low(take(first, 2, x), swap(for_x, X))
    second = add_low(take(second, 2, y), swap(for_y, Y))
    column = jnp.concatenate([first, second], axis=2)
    (for_z,) = yield (take(column, 1, 1 - low),)
    column = add_low(take(column, 1, low), swap(for_z, Z_LOW))
    (for_z,) = yield (take(column, 0, 1 - high),)
    return take(column, 0, high).astype(F32) + swap(for_z, Z_HIGH).astype(F32)


class Rounds:
    def __init__(self, steps):
        self.steps = steps
        self.sent = next(steps)
        self.result = None

    def before(self, *operands):
        sent, operands = lax.optimization_barrier((self.sent, operands))
        self.move(sent)
        return operands[0] if len(operands) == 1 else operands

    def move(self, sent):
        try:
            self.sent = self.steps.send(sent)
        except StopIteration as stop:
            self.sent, self.result = None, stop.value

    def finish(self):
        while self.result is None:
            self.move(self.sent)
        return self.result


def on_device(
    devices,
    src_in,
    tgt_in,
    src_len,
    tgt_len,
    tgt_mask,
    enc_cot,
    dec_cot,
    enc_master,
    enc_first,
    enc_second,
    dec_master,
    dec_first,
    dec_second,
    small_master,
    small_first,
    small_second,
):
    width = src_in.shape[1]
    number = src_in.shape[0]
    me = lax.axis_index("fsdp")
    enc_size, dec_size = enc_master.shape[0], dec_master.shape[0]
    enc_count, dec_count = enc_size * devices, dec_size * devices
    inner = (enc_count - 4 * width) // 2
    ups = inner // width
    enc_map, dec_map = enc_regions(width, inner), dec_regions(width, inner)

    enc_own = arrange_own(enc_master.astype(LOW), me * enc_size, enc_map, to_units)
    dec_own = arrange_own(dec_master.astype(LOW), me * dec_size, dec_map, to_units)
    by_rounds = devices == 1 << BITS
    share = small_master.shape[1]
    held = small_master.size
    own = jnp.pad(small_master.astype(LOW).reshape(-1), (0, 16 * width - held)).reshape(16, width)
    far = lax.all_gather(jnp.concatenate([enc_own, dec_own, own], axis=0), "fsdp", axis=0, tiled=False)
    small_rows = far[:, enc_size + dec_size, :held].reshape(devices, -1, share)
    small_rows = small_rows.transpose(1, 0, 2).reshape(-1, width)
    if devices != OWNERS:
        enc_rows = arrange_all(far[:, :enc_size].reshape(-1, width), enc_size, enc_map, to_units)
        dec_rows = arrange_all(far[:, enc_size : enc_size + dec_size].reshape(-1, width), dec_size, dec_map, to_units)
        far = jnp.concatenate(
            [enc_rows.reshape(OWNERS, -1, width), dec_rows.reshape(OWNERS, -1, width)], axis=1
        )
    enc_share, dec_share = enc_count // OWNERS, dec_count // OWNERS

    def enc_part(first, last):
        return row_copies(first, last, enc_share, 0)

    def dec_part(first, last):
        return row_copies(first, last, dec_share, enc_share)

    enc_qkv = enc_part(0, 3 * width)
    enc_wo = enc_part(3 * width, 4 * width)
    enc_up = enc_part(4 * width, 4 * width + inner)
    enc_down = enc_part(4 * width + inner, enc_count)
    self_qkv = dec_part(0, 3 * width)
    self_wo = dec_part(3 * width, 4 * width)
    cross_q = dec_part(4 * width, 5 * width)
    cross_kv = dec_part(5 * width, 7 * width)
    cross_wo = dec_part(7 * width, 8 * width)
    dec_up = dec_part(8 * width, 8 * width + inner)
    dec_down = dec_part(8 * width + inner, dec_count)

    src_owner, src_key, src_bounds = owners_of(src_len[0], number)
    tgt_owner, tgt_key, tgt_bounds = owners_of(tgt_len[0], number)
    enc_plan = plan_of(src_bounds, src_bounds, src_len[0], number)
    dec_plan = plan_of(tgt_bounds, tgt_bounds, tgt_len[0], number)
    cross_plan = plan_of(tgt_bounds, src_bounds, src_len[0], number)

    smalls = jnp.pad(small_rows.astype(F32), ((0, 5), (0, 0)))
    masked = tgt_mask[:, None] == 1
    start = jnp.where(masked, small_rows[10][None, :], tgt_in)
    flags = tgt_mask.astype(F32)[None, :]

    e_q, e_kv, e_ctx, e_lse, e_hat, e_inv, memory, t_hat, t_inv = fwd_block(
        enc_plan, src_in, None, far, (enc_qkv, enc_wo, enc_up, enc_down), True, smalls, 0, src_owner, src_key, True,
        "enc_layer",
    )
    s_q, s_kv, s_ctx, s_lse, s_hat, s_inv = fwd_block(
        dec_plan, start, None, far, (self_qkv, self_wo), False, smalls, 4, tgt_owner, tgt_key, False, "dec_block"
    )
    c_q, c_kv, c_ctx, c_lse, c_hat, c_inv, decoded, f_hat, f_inv = fwd_block(
        cross_plan, s_hat, memory, far, (cross_kv, cross_wo, cross_q, dec_up, dec_down), True, smalls, 6,
        tgt_owner, src_key, True, "cross_layer",
    )

    d_two, d_cctx, g_dup, g_ddown, g_cout, sums_d = ffn_backward(
        dec_plan, [dec_cot], (f_hat, f_inv), (c_hat, c_inv), c_ctx, far, (dec_up, dec_down, cross_wo), smalls, 6,
        inner, "dec_ffn_back",
    )
    dcq, dck, dcv = attention_backward(cross_plan, c_q, c_kv, d_cctx, c_lse, tgt_owner, src_key, "cross_back")
    d_memory, d_one, d_sctx, g_cq, g_ckv, g_sout, sums_c = cross_projections_back(
        dec_plan, dcq, dck, dcv, s_hat, s_inv, d_two, memory, s_ctx, far, (cross_kv, cross_q, self_wo), smalls,
    )
    dsq, dsk, dsv = attention_backward(dec_plan, s_q, s_kv, d_sctx, s_lse, tgt_owner, tgt_key, "dec_back")
    g_sqkv = qkv_weights(dec_plan, start, dsq, dsk, dsv, False, "dec_qkv_weights")
    dec_pieces = [
        g_sqkv,
        g_sout,
        g_cq,
        g_ckv.reshape(-1, width),
        g_cout,
        g_dup.reshape(-1, width),
        g_ddown,
    ]
    if by_rounds:
        core = bit_of(me, CORE)[None].astype(jnp.int32)
        copies = overlaps([p.shape[0] for p in dec_pieces], dec_size)
        send, keep = pack(core, dec_pieces, copies, dec_size, "dec_pack")
        rounds = Rounds(reduce_owned(me, send, keep, dec_size // 2))
        dsq, dsk, dsv = rounds.before(dsq, dsk, dsv)
    tgt_grad, mask_sum = qkv_inputs(
        dec_plan, dsq, dsk, dsv, d_one, far, (self_qkv,), flags, "dec_qkv_inputs"
    )
    if by_rounds:
        d_memory, mask_sum = rounds.before(d_memory, mask_sum)
    d_mid, d_ectx, g_up, g_down, g_out, sums_e = ffn_backward(
        enc_plan, [enc_cot, d_memory], (t_hat, t_inv), (e_hat, e_inv), e_ctx, far,
        (enc_up, enc_down, enc_wo), smalls, 0, inner, "enc_ffn_back",
    )
    if by_rounds:
        d_ectx, g_up = rounds.before(d_ectx, g_up)
    deq, dek, dev = attention_backward(enc_plan, e_q, e_kv, d_ectx, e_lse, src_owner, src_key, "enc_back")
    if by_rounds:
        deq, dek, dev = rounds.before(deq, dek, dev)
    g_qkv = qkv_weights(enc_plan, src_in, deq, dek, dev, True, "enc_qkv_weights")

    enc_pieces = [g_qkv.reshape(-1, width), g_out, g_up.reshape(-1, width), g_down]
    small_grad = jnp.concatenate([sums_e[:4], sums_c[:2], sums_d[:4], mask_sum[:1]], axis=0)
    small_wire = small_grad.reshape(-1, devices, share).transpose(1, 0, 2).reshape(devices, -1).astype(LOW)
    small_wire = jnp.pad(small_wire, ((0, 0), (0, 16 * width - held))).reshape(devices * 16, width)
    if by_rounds:
        dec_summed = rounds.finish()
        copies = overlaps([p.shape[0] for p in enc_pieces], enc_size)
        copies += [(len(enc_pieces), 16 * i, i, enc_size, 16) for i in range(devices)]
        send, keep = pack(core, enc_pieces + [small_wire], copies, enc_size + 16, "enc_pack")
        rounds = Rounds(reduce_owned(me, send, keep, enc_size // 2 + 16))
        deq, dek, dev = rounds.before(deq, dek, dev)
    src_grad = qkv_inputs(enc_plan, deq, dek, dev, d_mid, far, (enc_qkv,), None, "enc_qkv_inputs")[0]
    if by_rounds:
        enc_summed = rounds.finish()
    else:
        dec_grad = arrange_all(jnp.concatenate(dec_pieces, axis=0), dec_size, dec_map, from_units)
        enc_grad = arrange_all(jnp.concatenate(enc_pieces, axis=0), enc_size, enc_map, from_units)
        enc_wire = jnp.concatenate(
            [enc_grad.reshape(devices, enc_size, width), small_wire.reshape(devices, 16, width)], axis=1
        )
        dec_summed = lax.psum_scatter(dec_grad, "fsdp", scatter_dimension=0, tiled=True).astype(F32)
        enc_summed = lax.psum_scatter(
            enc_wire.reshape(-1, width), "fsdp", scatter_dimension=0, tiled=True
        ).astype(F32)
    small_summed = enc_summed[enc_size:].reshape(-1)[:held].reshape(-1, share)
    enc_summed = arrange_own(enc_summed[:enc_size], me * enc_size, enc_map, from_units)
    dec_summed = arrange_own(dec_summed, me * dec_size, dec_map, from_units)

    part = 1.0 / devices
    enc_summed = enc_summed * part
    dec_summed = dec_summed * part
    small_summed = small_summed * part
    enc_new, enc_first_new, encoder_second_moment_updated = adamw(
        enc_master, enc_summed, enc_first, enc_second
    )
    dec_new, dec_first_new, dec_second_new = adamw(dec_master, dec_summed, dec_first, dec_second)
    small_first_new, small_second_new = moments(small_summed, small_first, small_second)
    return (
        memory,
        decoded,
        src_grad,
        tgt_grad,
        enc_new,
        enc_first_new,
        encoder_second_moment_updated,
        enc_new.astype(LOW),
        dec_new,
        dec_first_new,
        dec_second_new,
        dec_new.astype(LOW),
        small_summed,
        small_first_new,
        small_second_new,
    )


def solution(mesh):
    rows = P("fsdp", None)
    columns = P(None, "fsdp")
    return jax.shard_map(
        functools.partial(on_device, mesh.shape["fsdp"]),
        mesh=mesh,
        in_specs=(rows,) * 4 + (P("fsdp"),) + (rows,) * 8 + (columns,) * 3,
        out_specs=(rows,) * 12 + (columns,) * 3,
        check_vma=False,
    )
```

```python
import functools

import jax
import jax.numpy as jnp
from jax import lax
from jax.experimental import pallas as pl
from jax.experimental.pallas import tpu as pltpu
from jax.sharding import PartitionSpec as P

HEADS = 8
HEAD = 64
STEPS = 7
TILE = 256
LANES = 128

rate = 0.02
beta_one = 0.9
beta_two = 0.98
epsilon = 1e-06
decay = 0.01
floor_value = -1000000000.0
root_half = 0.7071067811865476
inverse_root_tau = 0.3989422804014327

F32 = jnp.float32
LOW = jnp.bfloat16
MIB = 2**20


def nn(former, latter):
    return lax.dot_general(
        former, latter, (((1,), (0,)), ((), ())), preferred_element_type=F32
    )


def nt(former, latter):
    return lax.dot_general(
        former, latter, (((1,), (1,)), ((), ())), preferred_element_type=F32
    )


def turned(values):
    return values.astype(F32).T.astype(LOW)


def column_of(row):
    return jnp.broadcast_to(row, (8, row.shape[1])).T[:, 0:1]


def ln_forward(values, gain, shift):
    centered = values - jnp.mean(values, axis=-1, keepdims=True)
    spread = jnp.mean(centered * centered, axis=-1, keepdims=True)
    inverse = lax.rsqrt(spread + 1e-05)
    normed = centered * inverse
    return normed * gain + shift, normed, inverse


def ln_backward(upstream, normed, inverse, gain):
    scaled = upstream * gain
    first = jnp.mean(scaled, axis=-1, keepdims=True)
    second = jnp.mean(scaled * normed, axis=-1, keepdims=True)
    return inverse * (scaled - first - normed * second)


def phi_and_slope(values):
    phi = 0.5 + 0.5 * lax.erf(values * root_half)
    return phi, phi + values * (jnp.exp(-0.5 * (values * values)) * inverse_root_tau)


def one_head(pair, head):
    lane = lax.broadcasted_iota(jnp.int32, pair.shape, 1)
    keep = lane < HEAD if head % 2 == 0 else lane >= HEAD
    return jnp.where(keep, pair, jnp.zeros_like(pair))


def pair_columns(head):
    return slice(LANES * (head // 2), LANES * (head // 2) + LANES)


def head_rows(head):
    return slice(HEAD * head, HEAD * head + HEAD)


def block_of(ref, j, count):
    if count == 1:
        return ref[...]
    return jnp.concatenate(
        [ref[first + 16 * j : first + 16 * j + 16, :] for first in range(0, ref.shape[0], 16 * count)], axis=0
    )


def spread(wide, values):
    for n in range(wide.shape[0]):
        wide[n] = values[:, LANES * n : LANES * n + LANES].astype(F32)


def third_rows(wide, j):
    rows = pl.ds(j, wide.shape[1] // 3, stride=3)
    return jnp.concatenate([wide[n, rows, :] for n in range(wide.shape[0])], axis=1).astype(LOW)


def put_third_rows(wide, j, values):
    rows = pl.ds(j, wide.shape[1] // 3, stride=3)
    for n in range(wide.shape[0]):
        wide[n, rows, :] = values[:, LANES * n : LANES * n + LANES]


def wide_scratch(width):
    return pltpu.VMEM((width // LANES, 3 * width, LANES), F32)


def put_block(ref, j, values):
    ref[:, j] = values.reshape(ref.shape[0], ref.shape[2], ref.shape[3])


OWNERS = 32


def row_copies(first, last, own, paired):
    found = []
    at = first
    while at < last:
        owner = at // own
        end = min(last, (owner + 1) * own)
        half = OWNERS // 4
        place = (2 * (owner // 2 // half) + owner % 2, owner // 2 % half) if paired else (0, owner)
        found.append((*place, at - owner * own, end - at, at - first))
        at = end
    return found


class Fetch:
    def __init__(self, far, core, copies, near, semaphores, used):
        self.core = core

        def handles(side):
            return [
                pltpu.make_async_copy(
                    far[source ^ side].at[owner, pl.ds(row, rows)], near.at[pl.ds(to, rows)], semaphores.at[used + n]
                )
                for n, (source, owner, row, rows, to) in enumerate(copies)
            ]

        self.handles = handles

    def start(self):
        if self.core is None:
            for handle in self.handles(0):
                handle.start()
            return
        for side in (0, 1):

            @pl.when(self.core == side)
            def _(side=side):
                for handle in self.handles(side):
                    handle.start()

    def wait(self):
        for handle in self.handles(0):
            handle.wait()


def fetches(far, plan, wanted, nears, semaphores):
    used = 0
    made = []
    core = plan[2, 1] if len(far) > 1 else None
    for copies, near in zip(wanted, nears):
        made.append(Fetch(far, core, copies, near, semaphores, used))
        used += len(copies)
    return made


def fetch_scratch(wanted, width):
    return [pltpu.VMEM((sum(c[3] for c in copies), width), LOW) for copies in wanted] + [
        pltpu.SemaphoreType.DMA((sum(len(copies) for copies in wanted),))
    ]


FAR = pl.BlockSpec(memory_space=pl.ANY)


def sources_of(wanted):
    last = max(copy[0] for copies in wanted for copy in copies)
    return 1 if last == 0 else 2 * (last // 2) + 2


def call(kernel, grid, in_specs, out_specs, out_shape, scratch, flops, moved, name, room=24, near=(), keep=()):
    single = not isinstance(out_shape, list)
    shapes = [
        (pltpu.VMEM if keep is True or n in keep else pltpu.HBM)(*made)
        for n, made in enumerate([out_shape] if single else out_shape)
    ]
    made = pl.pallas_call(
        kernel,
        grid_spec=pltpu.PrefetchScalarGridSpec(
            num_scalar_prefetch=1,
            grid=grid,
            in_specs=in_specs,
            out_specs=out_specs,
            scratch_shapes=scratch,
        ),
        out_shape=shapes[0] if single else shapes,
        compiler_params=pltpu.CompilerParams(vmem_limit_bytes=room * MIB),
        cost_estimate=pl.CostEstimate(
            flops=flops, bytes_accessed=moved, transcendentals=0
        ),
        name=name,
    )

    def run(plan, *operands):
        placed = [
            operand
            if near is True or n in near
            else pltpu.with_memory_space_constraint(operand, pltpu.HBM)
            for n, operand in enumerate(operands)
        ]
        return made(plan, *placed)

    return run


def whole(shape):
    zeros = (0,) * len(shape)
    return pl.BlockSpec(shape, lambda i, *_: zeros)


def rows_of(width):
    return pl.BlockSpec((TILE, width), lambda i, *_: (i, 0))


def at_block(shape, *index):
    return pl.BlockSpec(shape, lambda i, *_: index)


def shaped(shape, kind):
    return (shape, kind)


def attend_tile(plan, i, keys, key_cols, query, owner_row, key_owner, vt, sc):
    scores, acc, top, total, masked_q = sc
    query = query * jnp.asarray(HEAD**-0.5, LOW)
    for h in range(HEADS):
        masked_q[h] = one_head(query[:, pair_columns(h)], h)
    top[...] = jnp.full_like(top, -1e30)
    total[...] = jnp.zeros_like(total)
    acc[...] = jnp.zeros_like(acc)
    begin = plan[0, i]
    chunks = plan[1, i]

    def score_tile(j, carry):
        rows = pl.ds(pl.multiple_of(begin + j * TILE, LANES), TILE)
        bias = jnp.where(key_owner[rows, 0:1] == owner_row, 0.0, floor_value)
        tops = []
        for h in range(HEADS):
            cols = pl.ds(key_cols + LANES * (h // 2), LANES)
            s = nt(keys[rows, cols], masked_q[h]) + bias
            scores[j, h] = s
            tops.append(jnp.max(s, axis=0, keepdims=True))
        top[...] = jnp.maximum(top[...], jnp.concatenate(tops, axis=0))
        return carry

    lax.fori_loop(0, chunks, score_tile, 0)

    def weigh_tile(j, carry):
        rows = pl.ds(pl.multiple_of(begin + j * TILE, LANES), TILE)
        sums = []
        for h in range(HEADS):
            p = jnp.exp(scores[j, h] - top[h : h + 1, :])
            sums.append(jnp.sum(p, axis=0, keepdims=True))
            acc[head_rows(h), :] += nn(vt[head_rows(h), rows], p.astype(LOW))
        total[...] += jnp.concatenate(sums, axis=0)
        return carry

    lax.fori_loop(0, chunks, weigh_tile, 0)


def fwd_block_kernel(plan, *refs, cross, gain_row, wanted, packed, ffn):
    refs = list(refs)

    def next_refs(count):
        taken = refs[:count]
        del refs[:count]
        return taken

    if cross:
        normed_in, memory = next_refs(2)
    else:
        (x_all,) = next_refs(1)
    far = next_refs(sources_of(wanted))
    small, owner_q, owner_k = next_refs(3)
    q_out, kv_out, ctx_out, lse_out, normed_out, inverse_out = next_refs(6)
    if ffn:
        out, normed_last, inverse_last = next_refs(3)
    kv, vt, mean_v, key_owner, scores, acc, top, total, masked_q, q_all = next_refs(10)
    nears = next_refs(len(wanted))
    semaphores = refs.pop(0)
    loads = fetches(far, plan, wanted, nears, semaphores)
    i = pl.program_id(0)
    width = kv.shape[1] // 2

    @pl.when(i == 0)
    def _():
        for load in loads:
            load.start()
        key_owner[...] = jnp.broadcast_to(owner_k[...], (8, owner_k.shape[1])).T
        loads[0].wait()
        if cross:
            wk, wv = block_of(nears[0], 0, 2), block_of(nears[0], 1, 2)
        elif packed:
            wq, wk, wv = (block_of(nears[0], j, 3) for j in range(3))
        else:
            wide = refs[0]
            spread(wide, nears[0][...])
            wq, wk, wv = (third_rows(wide, j) for j in range(3))
        sums = jnp.zeros((1, width), F32)
        for t in range(kv.shape[0] // TILE):
            rows = slice(t * TILE, t * TILE + TILE)
            x = memory[rows, :] if cross else x_all[rows, :]
            if not cross:
                q_all[rows, :] = nn(x, wq).astype(LOW)
            kv[rows, :width] = nn(x, wk).astype(LOW)
            v = nn(x, wv).astype(LOW)
            kv[rows, width:] = v
            v = v.astype(F32)
            vt[:, rows] = v.T.astype(LOW)
            sums = sums + jnp.sum(v, axis=0, keepdims=True)
        mean_v[...] = sums * (1.0 / kv.shape[0])
        for load in loads[1:]:
            load.wait()

    wo = nears[1]
    mine = pl.ds(pl.multiple_of(i * TILE, TILE), TILE)
    if cross:
        resid = normed_in[...] * small[4:5, :] + small[5:6, :]
        query = nn(resid.astype(LOW), nears[2][...]).astype(LOW)
        q_out[...] = query
    else:
        resid = x_all[mine, :].astype(F32)
        query = q_all[mine, :]
        q_out[...] = query
    kv_out[...] = kv[mine, :]
    owner_row = owner_q[...]
    attend_tile(plan, i, kv, 0, query, owner_row, key_owner, vt, (scores, acc, top, total, masked_q))
    dead = owner_row < 0
    sums = jnp.where(dead, 1.0, total[...])
    share = 1.0 / sums
    lse_out[...] = jnp.where(dead, 0.0, top[...] + jnp.log(sums))
    for h in range(HEADS):
        acc[head_rows(h), :] = acc[head_rows(h), :] * share[h : h + 1, :]
    live = column_of(owner_row) >= 0
    context = jnp.where(live, acc[...].T, mean_v[...]).astype(LOW)
    ctx_out[...] = context
    added = nn(context, wo[...]) * live.astype(F32)
    mid, normed, inverse = ln_forward(
        resid + added, small[gain_row : gain_row + 1, :], small[gain_row + 1 : gain_row + 2, :]
    )
    normed_out[...] = normed
    inverse_out[...] = jnp.broadcast_to(inverse, inverse_out.shape)
    if ffn:
        wup, wdown = nears[-2:]
        blocks = wdown.shape[0] // width
        low = mid.astype(LOW)
        result = mid
        for j in range(blocks):
            inner = nn(low, block_of(wup, j, blocks))
            phi = 0.5 + 0.5 * lax.erf(inner * root_half)
            result = result + nn((inner * phi).astype(LOW), wdown[j * width : j * width + width, :])
        result, normed, inverse = ln_forward(
            result, small[gain_row + 2 : gain_row + 3, :], small[gain_row + 3 : gain_row + 4, :]
        )
        out[...] = result.astype(LOW)
        normed_last[...] = normed
        inverse_last[...] = jnp.broadcast_to(inverse, inverse_last.shape)


def attention_scratch(keys, width):
    return [
        pltpu.VMEM((keys, 2 * width), LOW),
        pltpu.VMEM((width, keys), LOW),
        pltpu.VMEM((1, width), F32),
        pltpu.VMEM((keys, 8), F32),
        pltpu.VMEM((keys // TILE, HEADS, TILE, TILE), F32),
        pltpu.VMEM((width, TILE), F32),
        pltpu.VMEM((HEADS, TILE), F32),
        pltpu.VMEM((HEADS, TILE), F32),
        pltpu.VMEM((HEADS, TILE, LANES), LOW),
        pltpu.VMEM((keys, width), LOW),
    ]


def block_outs(queries, width):
    specs = [
        rows_of(width),
        rows_of(2 * width),
        rows_of(width),
        pl.BlockSpec((HEADS, TILE), lambda i, *_: (0, i)),
        rows_of(width),
        rows_of(LANES),
    ]
    shapes = [
        shaped((queries, width), LOW),
        shaped((queries, 2 * width), LOW),
        shaped((queries, width), LOW),
        shaped((HEADS, queries), F32),
        shaped((queries, width), F32),
        shaped((queries, LANES), F32),
    ]
    return specs, shapes


def owner_specs(keys):
    return [pl.BlockSpec((1, TILE), lambda i, *_: (0, i)), whole((1, keys))]


def fwd_block(plan, x, memory, far, wanted, packed, small, gain_row, owner, key_owner, ffn, name):
    cross = memory is not None
    number, width = x.shape
    specs, shapes = block_outs(number, width)
    if ffn:
        specs += [rows_of(width), rows_of(width), rows_of(LANES)]
        shapes += [shaped((number, width), LOW), shaped((number, width), F32), shaped((number, LANES), F32)]
    scratch = attention_scratch(number, width) + fetch_scratch(wanted, width)
    if not cross and not packed:
        scratch.append(wide_scratch(width))
    return call(
        functools.partial(
            fwd_block_kernel, cross=cross, gain_row=gain_row, wanted=wanted, packed=packed, ffn=ffn
        ),
        (number // TILE,),
        ([rows_of(width), whole(memory.shape)] if cross else [whole(x.shape)])
        + [FAR] * sources_of(wanted)
        + [whole(small.shape)]
        + owner_specs(number),
        specs,
        shapes,
        scratch,
        8 * number * width * width + number * number * width * 2,
        16 * number * width,
        name,
        room=44,
    )(plan, *([x, memory] if cross else [x]), *far[: sources_of(wanted)], small, owner, key_owner)


def ffn_back_kernel(plan, *refs, tiles, summed, gain_row, wanted):
    refs = list(refs)
    cot = refs.pop(0)
    extra = refs.pop(0) if summed else None
    normed_top, inverse_top, normed_mid, inverse_mid, context = refs[:5]
    far = refs[5 : 5 + sources_of(wanted)]
    (small,
     d_sum, d_context, g_up, g_down, g_out, sums, hidden, d_inner, mid_low, d_down, d_product,
     wup, wdown, wo, semaphores) = refs[5 + sources_of(wanted) :]
    loads = fetches(far, plan, wanted, (wup, wdown, wo), semaphores)
    i = pl.program_id(0)
    width = small.shape[1]
    blocks = wdown.shape[0] // width

    @pl.when(i == 0)
    def _():
        for load in loads:
            load.start()
        sums[...] = jnp.zeros_like(sums)
        for load in loads:
            load.wait()

    @pl.when(i < tiles)
    def _():
        mine = pl.ds(pl.multiple_of(i * TILE, TILE), TILE)
        upstream = cot[...].astype(F32)
        if summed:
            upstream = upstream + extra[...]
        top = normed_top[...]
        sums[2:3, :] += jnp.sum(upstream * top, axis=0, keepdims=True)
        sums[3:4, :] += jnp.sum(upstream, axis=0, keepdims=True)
        d_mid = ln_backward(upstream, top, inverse_top[:, 0:1], small[gain_row + 2 : gain_row + 3, :])
        low = d_mid.astype(LOW)
        d_down[mine, :] = low
        normed = normed_mid[...]
        mid = (normed * small[gain_row : gain_row + 1, :] + small[gain_row + 1 : gain_row + 2, :]).astype(LOW)
        mid_low[mine, :] = mid
        for j in range(blocks):
            cols = slice(j * width, j * width + width)
            up = block_of(wup, j, blocks)
            inner = nn(mid, up)
            phi, slope = phi_and_slope(inner)
            hidden[j, mine, :] = (inner * phi).astype(LOW)
            part = (nt(low, wdown[cols, :]) * slope).astype(LOW)
            d_inner[j, mine, :] = part
            d_mid = d_mid + nt(part, up)
        sums[0:1, :] += jnp.sum(d_mid * normed, axis=0, keepdims=True)
        sums[1:2, :] += jnp.sum(d_mid, axis=0, keepdims=True)
        total = ln_backward(d_mid, normed, inverse_mid[:, 0:1], small[gain_row : gain_row + 1, :])
        d_sum[...] = total
        place = lax.broadcasted_iota(jnp.int32, (TILE, 1), 0) + i * TILE
        live = (place < plan[2, 0]).astype(F32)
        product = (total * live).astype(LOW)
        d_product[mine, :] = product
        d_context[...] = nt(product, wo[...]).astype(LOW)

    @pl.when(i >= tiles)
    def _():
        j = i - tiles
        put_block(g_up, 0, nn(turned(mid_low[...]), d_inner[j]).astype(LOW))
        g_down[...] = nn(turned(hidden[j]), d_down[...]).astype(LOW)

    @pl.when(i == tiles)
    def _():
        g_out[...] = nn(turned(context[...]), d_product[...]).astype(LOW)


def ffn_backward(plan, cots, top, mid, context, far, wanted, small, gain_row, inner, name):
    number, width = mid[0].shape
    tiles, blocks = number // TILE, inner // width

    def tile_of(columns):
        return pl.BlockSpec((TILE, columns), lambda i, *_: (jnp.minimum(i, tiles - 1), 0))

    return call(
        functools.partial(
            ffn_back_kernel, tiles=tiles, summed=len(cots) == 2, gain_row=gain_row, wanted=wanted
        ),
        (tiles + blocks,),
        [tile_of(width)] * len(cots)
        + [tile_of(width), tile_of(LANES), tile_of(width), tile_of(LANES), whole((number, width))]
        + [FAR] * sources_of(wanted)
        + [whole(small.shape)],
        [
            tile_of(width),
            tile_of(width),
            pl.BlockSpec((width // 16, 1, 16, width), lambda i, *_: (0, jnp.maximum(i - tiles, 0), 0, 0)),
            pl.BlockSpec((width, width), lambda i, *_: (jnp.maximum(i - tiles, 0), 0)),
            pl.BlockSpec((width, width), lambda i, *_: (0, 0)),
            pl.BlockSpec((8, width), lambda i, *_: (0, 0)),
        ],
        [
            shaped((number, width), F32),
            shaped((number, width), LOW),
            shaped((width // 16, blocks, 16, width), LOW),
            shaped((inner, width), LOW),
            shaped((width, width), LOW),
            shaped((8, width), F32),
        ],
        [
            pltpu.VMEM((blocks, number, width), LOW),
            pltpu.VMEM((blocks, number, width), LOW),
            pltpu.VMEM((number, width), LOW),
            pltpu.VMEM((number, width), LOW),
            pltpu.VMEM((number, width), LOW),
        ]
        + fetch_scratch(wanted, width),
        10 * number * width * inner,
        30 * number * width,
        name,
        room=44,
    )(plan, *cots, *top, *mid, context, *far[: sources_of(wanted)], small)


def attention_back_kernel(plan, q_ref, k_ref, v_ref, do_ref, lse, owner_q, owner_k, dq, dk, dv,
                          kt, key_owner, masked_q, masked_do, dqt, dk_sum, dv_sum, weights, d_weights, dots):
    i = pl.program_id(0)

    @pl.when(i == 0)
    def _():
        key_owner[...] = jnp.broadcast_to(owner_k[...], (8, owner_k.shape[1])).T
        kt[...] = turned(k_ref[...])
        dk_sum[...] = jnp.zeros_like(dk_sum)
        dv_sum[...] = jnp.zeros_like(dv_sum)

    query = q_ref[...] * jnp.asarray(HEAD**-0.5, LOW)
    upstream = do_ref[...]
    for h in range(HEADS):
        masked_q[h] = one_head(query[:, pair_columns(h)], h)
        masked_do[h] = one_head(upstream[:, pair_columns(h)], h)
    dqt[...] = jnp.zeros_like(dqt)
    dots[...] = jnp.zeros_like(dots)
    owner_row = owner_q[...]
    begin = plan[0, i]
    chunks = plan[1, i]

    def weigh_tile(j, carry):
        rows = pl.ds(pl.multiple_of(begin + j * TILE, LANES), TILE)
        bias = jnp.where(key_owner[rows, 0:1] == owner_row, 0.0, floor_value)
        sums = []
        for h in range(HEADS):
            s = nt(k_ref[rows, pair_columns(h)], masked_q[h])
            p = jnp.exp((s - lse[h : h + 1, :]) + bias)
            dp = nt(v_ref[rows, pair_columns(h)], masked_do[h])
            weights[j, h] = p
            d_weights[j, h] = dp
            sums.append(jnp.sum(p * dp, axis=0, keepdims=True))
        dots[...] += jnp.concatenate(sums, axis=0)
        return carry

    lax.fori_loop(0, chunks, weigh_tile, 0)

    def grad_tile(j, carry):
        rows = pl.ds(pl.multiple_of(begin + j * TILE, LANES), TILE)
        for pair in range(HEADS // 2):
            cols = pair_columns(2 * pair)
            dv_part = dv_sum[rows, cols]
            dk_part = dk_sum[rows, cols]
            for h in (2 * pair, 2 * pair + 1):
                p = weights[j, h]
                ds = (p * (d_weights[j, h] - dots[h : h + 1, :])).astype(LOW)
                dv_part = dv_part + nn(p.astype(LOW), masked_do[h])
                dk_part = dk_part + nn(ds, masked_q[h])
                dqt[head_rows(h), :] += nn(kt[head_rows(h), rows], ds)
            dv_sum[rows, cols] = dv_part
            dk_sum[rows, cols] = dk_part
        return carry

    lax.fori_loop(0, chunks, grad_tile, 0)
    dq[...] = (dqt[...] * HEAD**-0.5).T.astype(LOW)

    @pl.when(i == pl.num_programs(0) - 1)
    def _():
        dk[...] = dk_sum[...].astype(LOW)
        dv[...] = dv_sum[...].astype(LOW)


def attention_backward(plan, q, kv, d_context, lse, owner, key_owner, name):
    number, width = q.shape
    keys = kv.shape[0]
    return call(
        attention_back_kernel,
        (number // TILE,),
        [
            rows_of(width),
            at_block((keys, width), 0, 0),
            at_block((keys, width), 0, 1),
            rows_of(width),
            pl.BlockSpec((HEADS, TILE), lambda i, *_: (0, i)),
        ]
        + owner_specs(keys),
        [rows_of(width), whole((keys, width)), whole((keys, width))],
        [shaped((number, width), LOW), shaped((keys, width), LOW), shaped((keys, width), LOW)],
        [
            pltpu.VMEM((width, keys), LOW),
            pltpu.VMEM((keys, 8), F32),
            pltpu.VMEM((HEADS, TILE, LANES), LOW),
            pltpu.VMEM((HEADS, TILE, LANES), LOW),
            pltpu.VMEM((width, TILE), F32),
            pltpu.VMEM((keys, width), F32),
            pltpu.VMEM((keys, width), F32),
            pltpu.VMEM((keys // TILE, HEADS, TILE, TILE), F32),
            pltpu.VMEM((keys // TILE, HEADS, TILE, TILE), F32),
            pltpu.VMEM((HEADS, TILE), F32),
        ],
        number * keys * width * 4,
        12 * number * width,
        name,
        room=44,
    )(plan, q, kv, kv, d_context, lse, owner, key_owner)


def cross_back_kernel(plan, *refs, wanted):
    d_query, dk, dv, normed, inverse, d_above, memory, context = refs[:8]
    far = refs[8 : 8 + sources_of(wanted)]
    (small, d_memory, d_sum, d_context, g_query, g_pair, g_out, sums, d_product,
     wkv, wq, wo, semaphores) = refs[8 + sources_of(wanted) :]
    i = pl.program_id(0)
    mine = pl.ds(pl.multiple_of(i * TILE, TILE), TILE)

    loads = fetches(far, plan, wanted, (wkv, wq, wo), semaphores)

    @pl.when(i == 0)
    def _():
        for load in loads:
            load.start()
        sums[...] = jnp.zeros_like(sums)
        low = normed[...] * small[4:5, :] + small[5:6, :]
        g_query[...] = nn(low.T.astype(LOW), d_query[...]).astype(LOW)
        for load in loads:
            load.wait()

    wk, wv = block_of(wkv, 0, 2), block_of(wkv, 1, 2)
    d_memory[...] = nt(dk[mine, :], wk) + nt(dv[mine, :], wv)
    d_one = d_above[...] + nt(d_query[mine, :], wq[...])
    hat = normed[mine, :]
    sums[0:1, :] += jnp.sum(d_one * hat, axis=0, keepdims=True)
    sums[1:2, :] += jnp.sum(d_one, axis=0, keepdims=True)
    total = ln_backward(d_one, hat, inverse[:, 0:1], small[4:5, :])
    d_sum[...] = total
    place = lax.broadcasted_iota(jnp.int32, (TILE, 1), 0) + i * TILE
    live = (place < plan[2, 0]).astype(F32)
    product = (total * live).astype(LOW)
    d_product[mine, :] = product
    d_context[...] = nt(product, wo[...]).astype(LOW)

    @pl.when(i == 1)
    def _():
        turn = turned(memory[...])
        put_block(g_pair, 0, nn(turn, dk[...]).astype(LOW))

    @pl.when(i == 2)
    def _():
        turn = turned(memory[...])
        put_block(g_pair, 1, nn(turn, dv[...]).astype(LOW))

    @pl.when(i == pl.num_programs(0) - 1)
    def _():
        g_out[...] = nn(turned(context[...]), d_product[...]).astype(LOW)


def cross_projections_back(plan, d_query, dk, dv, normed, inverse, d_above, memory, context, far, wanted, small):
    number, width = normed.shape
    full = whole((number, width))
    square = whole((width, width))
    return call(
        functools.partial(cross_back_kernel, wanted=wanted),
        (number // TILE,),
        [full, full, full, full, rows_of(LANES), rows_of(width), full, full]
        + [FAR] * sources_of(wanted)
        + [whole(small.shape)],
        [rows_of(width), rows_of(width), rows_of(width), square, whole((width // 16, 2, 16, width)), square,
         whole((8, width))],
        [shaped((number, width), F32), shaped((number, width), F32), shaped((number, width), LOW),
         shaped((width, width), LOW), shaped((width // 16, 2, 16, width), LOW), shaped((width, width), LOW),
         shaped((8, width), F32)],
        [pltpu.VMEM((number, width), LOW)] + fetch_scratch(wanted, width),
        16 * number * width * width,
        24 * number * width,
        "cross_projections_back",
    )(plan, d_query, dk, dv, normed, inverse, d_above, memory, context, *far[: sources_of(wanted)], small)


def qkv_weights_kernel(plan, x, dq, dk, dv, g_qkv, turn, *wide):
    i = pl.program_id(0)
    width = turn.shape[0]

    @pl.when(i == 0)
    def _():
        turn[...] = turned(x[...])

    for j, ref in enumerate((dq, dk, dv)):

        @pl.when(i == j)
        def _(j=j, ref=ref):
            made = nn(turn[...], ref[...])
            if not wide:
                put_block(g_qkv, 0, made.astype(LOW))
            else:
                put_third_rows(wide[0], j, made)

    if wide:

        @pl.when(i == 2)
        def _():
            for n in range(width // LANES):
                g_qkv[:, LANES * n : LANES * n + LANES] = wide[0][n].astype(LOW)


def qkv_weights(plan, x, dq, dk, dv, packed, name):
    number, width = x.shape
    full = whole((number, width))
    scratch = [pltpu.VMEM((width, number), LOW)]
    if packed:
        shape = (width // 16, 3, 16, width)
        spec = pl.BlockSpec((width // 16, 1, 16, width), lambda i, *_: (0, i, 0, 0))
    else:
        shape = (3 * width, width)
        spec = whole(shape)
        scratch.append(wide_scratch(width))
    return call(
        qkv_weights_kernel,
        (3,),
        [full] * 4,
        spec,
        shaped(shape, LOW),
        scratch,
        6 * number * width * width,
        12 * number * width,
        name,
    )(plan, x, dq, dk, dv)


def qkv_inputs_kernel(plan, *refs, masked, wanted):
    if masked:
        dq, dk, dv, d_above, flags, *refs = refs
        far = refs[: sources_of(wanted)]
        d_x, mask_sum, near, semaphores, blocks, wide = refs[sources_of(wanted) :]
    else:
        dq, dk, dv, d_above, *refs = refs
        far = refs[: sources_of(wanted)]
        d_x, near, semaphores, blocks = refs[sources_of(wanted) :]
    width = dq.shape[1]

    @pl.when(pl.program_id(0) == 0)
    def _():
        (load,) = fetches(far, plan, wanted, (near,), semaphores)
        load.start()
        load.wait()
        if masked:
            mask_sum[...] = jnp.zeros_like(mask_sum)
            spread(wide, near[...])
        for j in range(3):
            if masked:
                blocks[:, j * width : j * width + width] = third_rows(wide, j)
            else:
                blocks[:, j * width : j * width + width] = block_of(near, j, 3)

    pieces = jnp.concatenate([dq[...], dk[...], dv[...]], axis=1)
    total = nt(pieces, blocks[...])
    if masked:
        total = total + d_above[...]
        hit = column_of(flags[...]) == 1.0
        d_x[...] = jnp.where(hit, 0.0, total)
        mask_sum[0:1, :] += jnp.sum(jnp.where(hit, total, 0.0), axis=0, keepdims=True)
    else:
        d_x[...] = d_above[...]
        d_x[...] += total


def qkv_inputs(plan, dq, dk, dv, d_above, far, wanted, flags, name):
    number, width = dq.shape
    masked = flags is not None
    in_specs = [rows_of(width)] * 4
    out_specs = [rows_of(width)]
    out_shape = [shaped((number, width), F32)]
    operands = [dq, dk, dv, d_above]
    scratch = fetch_scratch(wanted, width) + [pltpu.VMEM((width, 3 * width), LOW)]
    if masked:
        in_specs.append(pl.BlockSpec((1, TILE), lambda i, *_: (0, i)))
        out_specs.append(whole((8, width)))
        out_shape.append(shaped((8, width), F32))
        operands.append(flags)
        scratch.append(wide_scratch(width))
    in_specs += [FAR] * sources_of(wanted)
    operands += far[: sources_of(wanted)]
    return call(
        functools.partial(qkv_inputs_kernel, masked=masked, wanted=wanted),
        (number // TILE,),
        in_specs,
        out_specs,
        out_shape,
        scratch,
        6 * number * width * width,
        16 * number * width,
        name,
    )(plan, *operands)


def enc_regions(width, inner):
    return ((0, 3 * width, 3), (4 * width, 4 * width + inner, inner // width))


def dec_regions(width, inner):
    return ((5 * width, 7 * width, 2), (8 * width, 8 * width + inner, inner // width))


def to_units(rows, k):
    return rows.reshape(-1, 16, k, rows.shape[1]).transpose(0, 2, 1, 3).reshape(rows.shape)


def from_units(rows, k):
    return rows.reshape(-1, k, 16, rows.shape[1]).transpose(0, 2, 1, 3).reshape(rows.shape)


def fits(size, region):
    return size % (16 * region[2]) == 0


def arrange_own(rows, first, regions, arrange):
    place = first + lax.broadcasted_iota(jnp.int32, (rows.shape[0], 1), 0)
    result = rows
    for region in regions:
        if fits(rows.shape[0], region):
            inside = (place >= region[0]) & (place < region[1])
            result = jnp.where(inside, arrange(rows, region[2]), result)
    return result


def arrange_all(rows, size, regions, arrange):
    for region in regions:
        if not fits(size, region):
            part = arrange(rows[region[0] : region[1]], region[2])
            rows = jnp.concatenate([rows[: region[0]], part, rows[region[1] :]], axis=0)
    return rows


def owners_of(lengths, number):
    bounds = jnp.cumsum(lengths)
    places = jnp.arange(number, dtype=jnp.int32)
    owners = jnp.sum((places[:, None] >= bounds[None, :]).astype(jnp.int32), axis=1)
    filled = places < bounds[-1]
    for_queries = jnp.where(filled, owners, -2).astype(F32)[None, :]
    for_keys = jnp.where(filled, owners, -1).astype(F32)[None, :]
    return for_queries, for_keys, bounds


def plan_of(query_bounds, key_bounds, key_lengths, number, core):
    firsts = jnp.arange(8, dtype=jnp.int32) * TILE
    filled = query_bounds[-1]
    lasts = jnp.minimum(firsts + TILE, filled) - 1

    def pair_of(places):
        found = jnp.sum((places[:, None] >= query_bounds[None, :]).astype(jnp.int32), axis=1)
        return jnp.minimum(found, key_lengths.shape[0] - 1)

    def pick(values, pairs):
        chosen = pairs[:, None] == jnp.arange(values.shape[0])[None, :]
        return jnp.sum(jnp.where(chosen, values[None, :], 0), axis=1)

    begin = pick(key_bounds - key_lengths, pair_of(firsts))
    end = pick(key_bounds, pair_of(lasts))
    some = firsts < filled
    begin = begin // LANES * LANES
    chunks = (end - begin + TILE - 1) // TILE
    begin = jnp.where(some, jnp.minimum(begin, number - chunks * TILE), 0)
    chunks = jnp.where(some, chunks, 0)
    rest = jnp.where(jnp.arange(8) == 1, core, filled)
    return jnp.stack([begin, chunks, rest]).astype(jnp.int32)


def moments(gradient, first, second):
    first_new = beta_one * first + (1.0 - beta_one) * gradient
    second_new = beta_two * second + (1.0 - beta_two) * gradient * gradient
    return (first_new, second_new)


def adamw(weight, gradient, first, second):
    first_new, second_new = moments(gradient, first, second)
    moved = weight - rate * (
        first_new
        / (1.0 - beta_one**STEPS)
        / (jnp.sqrt(second_new / (1.0 - beta_two**STEPS)) + epsilon)
        + decay * weight
    )
    return (moved, first_new, second_new)


CORE, X, Y, Z_LOW, Z_HIGH = 0, 1, 2, 3, 4
BITS = 5


def partner(bit):
    return [(i, i ^ (1 << bit)) for i in range(1 << BITS)]


def bit_of(me, bit):
    return (me >> bit) & 1


def take(values, axis, index):
    return lax.dynamic_index_in_dim(values, index, axis, keepdims=False)


def overlaps(sizes, own):
    found = []
    first = 0
    for piece, size in enumerate(sizes):
        at = first
        while at < first + size:
            owner = at // own
            end = min(first + size, (owner + 1) * own)
            found.append((piece, at - first, owner, at - owner * own, end - at))
            at = end
        first += size
    return found


def pack_kernel(core, *refs, copies, number):
    pieces, send, keep, semaphores = refs[:number], refs[number], refs[number + 1], refs[number + 2]
    for side in (0, 1):

        @pl.when(core[0] == side)
        def _():
            handles = []
            for n, (piece, at, owner, to, rows) in enumerate(copies):
                target = keep if owner % 2 == side else send
                handles.append(
                    pltpu.make_async_copy(
                        pieces[piece].at[pl.ds(at, rows)],
                        target.at[owner // 2, pl.ds(to, rows)],
                        semaphores.at[n],
                    )
                )
            for handle in handles:
                handle.start()
            for handle in handles:
                handle.wait()


def pack(core, pieces, copies, block, name):
    width = pieces[0].shape[1]
    shape = shaped((1 << (BITS - 1), block, width), LOW)
    anywhere = pl.BlockSpec(memory_space=pl.ANY)
    total = sum(piece.size for piece in pieces)
    return call(
        functools.partial(pack_kernel, copies=copies, number=len(pieces)),
        (1,),
        [pl.BlockSpec(memory_space=pltpu.VMEM)] * len(pieces),
        [anywhere, anywhere],
        [shape, shape],
        [pltpu.SemaphoreType.DMA((len(copies),))],
        0,
        4 * total,
        name,
        near=True,
    )(core, *pieces)


def add_low(former, latter):
    return (former.astype(F32) + latter.astype(F32)).astype(LOW)


def swap(values, bit):
    return lax.ppermute(values, "fsdp", partner(bit))


def reduce_owned(me, send, keep, cut):
    rows, width = send.shape[1:]
    x, y, low, high = (bit_of(me, b) for b in (X, Y, Z_LOW, Z_HIGH))
    (send,) = yield (send,)
    chips = add_low(keep, swap(send, CORE)).reshape(2, 2, 2, 2, rows, width)
    first, second = chips[..., :cut, :], chips[..., cut:, :]
    for_y, for_x = yield (take(first, 2, 1 - y), take(second, 3, 1 - x))
    first = add_low(take(first, 2, y), swap(for_y, Y))
    second = add_low(take(second, 3, x), swap(for_x, X))
    for_x, for_y = yield (take(first, 2, 1 - x), take(second, 2, 1 - y))
    first = add_low(take(first, 2, x), swap(for_x, X))
    second = add_low(take(second, 2, y), swap(for_y, Y))
    column = jnp.concatenate([first, second], axis=2)
    (for_z,) = yield (take(column, 1, 1 - low),)
    column = add_low(take(column, 1, low), swap(for_z, Z_LOW))
    (for_z,) = yield (take(column, 0, 1 - high),)
    return take(column, 0, high).astype(F32) + swap(for_z, Z_HIGH).astype(F32)


def ordered(bit, mine, other, axis):
    first = bit == 0
    return jnp.stack([jnp.where(first, mine, other), jnp.where(first, other, mine)], axis=axis)


def gather_owned(me, own):
    x, y, low, high = (bit_of(me, b) for b in (X, Y, Z_LOW, Z_HIGH))
    rows, width = own.shape
    (own,) = yield (own,)
    column = ordered(high, own, swap(own, Z_HIGH), 0)
    (column,) = yield (column,)
    column = ordered(low, column, swap(column, Z_LOW), 1)
    below, above = yield (column[0], column[1])
    below = ordered(x, below, swap(below, X), 1)
    above = ordered(y, above, swap(above, Y), 1)
    below, above = yield (below, above)
    below = ordered(y, below, swap(below, Y), 1).reshape(-1, rows, width)
    above = ordered(x, above, swap(above, X), 2).reshape(-1, rows, width)
    below, above = yield (below, above)
    return [below, swap(below, CORE), above, swap(above, CORE)]


class Rounds:
    def __init__(self, steps):
        self.steps = steps
        self.sent = next(steps)
        self.result = None

    def before(self, *operands):
        sent, operands = lax.optimization_barrier((self.sent, operands))
        self.move(sent)
        return operands[0] if len(operands) == 1 else operands

    def move(self, sent):
        try:
            self.sent = self.steps.send(sent)
        except StopIteration as stop:
            self.sent, self.result = None, stop.value

    def finish(self):
        while self.result is None:
            self.move(self.sent)
        return self.result


def on_device(
    devices,
    src_in,
    tgt_in,
    src_len,
    tgt_len,
    tgt_mask,
    enc_cot,
    dec_cot,
    enc_master,
    enc_first,
    enc_second,
    dec_master,
    dec_first,
    dec_second,
    small_master,
    small_first,
    small_second,
):
    width = src_in.shape[1]
    number = src_in.shape[0]
    me = lax.axis_index("fsdp")
    enc_size, dec_size = enc_master.shape[0], dec_master.shape[0]
    enc_count, dec_count = enc_size * devices, dec_size * devices
    inner = (enc_count - 4 * width) // 2
    ups = inner // width
    enc_map, dec_map = enc_regions(width, inner), dec_regions(width, inner)

    enc_own = arrange_own(enc_master.astype(LOW), me * enc_size, enc_map, to_units)
    dec_own = arrange_own(dec_master.astype(LOW), me * dec_size, dec_map, to_units)
    by_rounds = devices == 1 << BITS
    share = small_master.shape[1]
    held = small_master.size
    own = jnp.zeros((16, width), LOW)
    own = lax.dynamic_update_slice(own, small_master.astype(LOW), (0, me * share))
    gathered = lax.all_gather(jnp.concatenate([enc_own, own], axis=0), "fsdp", axis=0, tiled=False)
    smalls = jnp.sum(gathered[:, enc_size:, :].astype(F32), axis=0)
    core = bit_of(me, CORE)
    src_owner, src_key, src_bounds = owners_of(src_len[0], number)
    tgt_owner, tgt_key, tgt_bounds = owners_of(tgt_len[0], number)
    enc_plan = plan_of(src_bounds, src_bounds, src_len[0], number, core)
    dec_plan = plan_of(tgt_bounds, tgt_bounds, tgt_len[0], number, core)
    cross_plan = plan_of(tgt_bounds, src_bounds, src_len[0], number, core)
    flags = tgt_mask.astype(F32)[None, :]
    if by_rounds:
        enc_far = [gathered]
        rounds = Rounds(gather_owned(me, dec_own))
        for _ in range(4):
            rounds.move(rounds.sent)
        early = (src_in, src_owner, src_key, tgt_owner, tgt_key, enc_plan, dec_plan, cross_plan, flags)
        src_in, src_owner, src_key, tgt_owner, tgt_key, enc_plan, dec_plan, cross_plan, flags = rounds.before(*early)
        dec_far = rounds.finish()
    else:
        enc_rows = arrange_all(gathered[:, :enc_size].reshape(-1, width), enc_size, enc_map, to_units)
        enc_far = [enc_rows.reshape(OWNERS, -1, width)]
        dec_rows = lax.all_gather(dec_own, "fsdp", axis=0, tiled=True)
        dec_rows = arrange_all(dec_rows, dec_size, dec_map, to_units).reshape(2, OWNERS // 4, 2, -1, width)
        first = core == 0
        dec_far = []
        for half in range(2):
            even, odd = dec_rows[half, :, 0], dec_rows[half, :, 1]
            dec_far += [jnp.where(first, even, odd), jnp.where(first, odd, even)]

    def enc_part(first, last):
        return row_copies(first, last, enc_count // OWNERS, False)

    def dec_part(first, last):
        return row_copies(first, last, dec_count // OWNERS, True)

    enc_qkv = enc_part(0, 3 * width)
    enc_wo = enc_part(3 * width, 4 * width)
    enc_up = enc_part(4 * width, 4 * width + inner)
    enc_down = enc_part(4 * width + inner, enc_count)
    self_qkv = dec_part(0, 3 * width)
    self_wo = dec_part(3 * width, 4 * width)
    cross_q = dec_part(4 * width, 5 * width)
    cross_kv = dec_part(5 * width, 7 * width)
    cross_wo = dec_part(7 * width, 8 * width)
    dec_up = dec_part(8 * width, 8 * width + inner)
    dec_down = dec_part(8 * width + inner, dec_count)

    start = jnp.where(tgt_mask[:, None] == 1, smalls[10].astype(LOW)[None, :], tgt_in)

    e_q, e_kv, e_ctx, e_lse, e_hat, e_inv, memory, t_hat, t_inv = fwd_block(
        enc_plan, src_in, None, enc_far, (enc_qkv, enc_wo, enc_up, enc_down), True, smalls, 0, src_owner, src_key, True,
        "enc_layer",
    )
    s_q, s_kv, s_ctx, s_lse, s_hat, s_inv = fwd_block(
        dec_plan, start, None, dec_far, (self_qkv, self_wo), False, smalls, 4, tgt_owner, tgt_key, False, "dec_block"
    )
    c_q, c_kv, c_ctx, c_lse, c_hat, c_inv, decoded, f_hat, f_inv = fwd_block(
        cross_plan, s_hat, memory, dec_far, (cross_kv, cross_wo, cross_q, dec_up, dec_down), True, smalls, 6,
        tgt_owner, src_key, True, "cross_layer",
    )

    d_two, d_cctx, g_dup, g_ddown, g_cout, sums_d = ffn_backward(
        dec_plan, [dec_cot], (f_hat, f_inv), (c_hat, c_inv), c_ctx, dec_far, (dec_up, dec_down, cross_wo), smalls, 6,
        inner, "dec_ffn_back",
    )
    dcq, dck, dcv = attention_backward(cross_plan, c_q, c_kv, d_cctx, c_lse, tgt_owner, src_key, "cross_back")
    d_memory, d_one, d_sctx, g_cq, g_ckv, g_sout, sums_c = cross_projections_back(
        dec_plan, dcq, dck, dcv, s_hat, s_inv, d_two, memory, s_ctx, dec_far, (cross_kv, cross_q, self_wo), smalls,
    )
    dsq, dsk, dsv = attention_backward(dec_plan, s_q, s_kv, d_sctx, s_lse, tgt_owner, tgt_key, "dec_back")
    g_sqkv = qkv_weights(dec_plan, start, dsq, dsk, dsv, False, "dec_qkv_weights")
    dec_pieces = [
        g_sqkv,
        g_sout,
        g_cq,
        g_ckv.reshape(-1, width),
        g_cout,
        g_dup.reshape(-1, width),
        g_ddown,
    ]
    if by_rounds:
        core = core[None].astype(jnp.int32)
        copies = overlaps([p.shape[0] for p in dec_pieces], dec_size)
        send, keep = pack(core, dec_pieces, copies, dec_size, "dec_pack")
        rounds = Rounds(reduce_owned(me, send, keep, dec_size // 2))
        dsq, dsk, dsv = rounds.before(dsq, dsk, dsv)
    tgt_grad, mask_sum = qkv_inputs(
        dec_plan, dsq, dsk, dsv, d_one, dec_far, (self_qkv,), flags, "dec_qkv_inputs"
    )
    if by_rounds:
        d_memory, mask_sum = rounds.before(d_memory, mask_sum)
    d_mid, d_ectx, g_up, g_down, g_out, sums_e = ffn_backward(
        enc_plan, [enc_cot, d_memory], (t_hat, t_inv), (e_hat, e_inv), e_ctx, enc_far,
        (enc_up, enc_down, enc_wo), smalls, 0, inner, "enc_ffn_back",
    )
    if by_rounds:
        d_ectx, g_up = rounds.before(d_ectx, g_up)
    deq, dek, dev = attention_backward(enc_plan, e_q, e_kv, d_ectx, e_lse, src_owner, src_key, "enc_back")
    if by_rounds:
        deq, dek, dev = rounds.before(deq, dek, dev)
    g_qkv = qkv_weights(enc_plan, src_in, deq, dek, dev, True, "enc_qkv_weights")

    enc_pieces = [g_qkv.reshape(-1, width), g_out, g_up.reshape(-1, width), g_down]
    small_grad = jnp.concatenate([sums_e[:4], sums_c[:2], sums_d[:4], mask_sum[:1]], axis=0)
    small_wire = small_grad.reshape(-1, devices, share).transpose(1, 0, 2).reshape(devices, -1).astype(LOW)
    small_wire = jnp.pad(small_wire, ((0, 0), (0, 16 * width - held))).reshape(devices * 16, width)
    if by_rounds:
        dec_summed = rounds.finish()
        copies = overlaps([p.shape[0] for p in enc_pieces], enc_size)
        copies += [(len(enc_pieces), 16 * i, i, enc_size, 16) for i in range(devices)]
        send, keep = pack(core, enc_pieces + [small_wire], copies, enc_size + 16, "enc_pack")
        rounds = Rounds(reduce_owned(me, send, keep, enc_size // 2 + 16))
        deq, dek, dev = rounds.before(deq, dek, dev)
    src_grad = qkv_inputs(enc_plan, deq, dek, dev, d_mid, enc_far, (enc_qkv,), None, "enc_qkv_inputs")[0]
    if by_rounds:
        enc_summed = rounds.finish()
    else:
        dec_grad = arrange_all(jnp.concatenate(dec_pieces, axis=0), dec_size, dec_map, from_units)
        enc_grad = arrange_all(jnp.concatenate(enc_pieces, axis=0), enc_size, enc_map, from_units)
        enc_wire = jnp.concatenate(
            [enc_grad.reshape(devices, enc_size, width), small_wire.reshape(devices, 16, width)], axis=1
        )
        dec_summed = lax.psum_scatter(dec_grad, "fsdp", scatter_dimension=0, tiled=True).astype(F32)
        enc_summed = lax.psum_scatter(
            enc_wire.reshape(-1, width), "fsdp", scatter_dimension=0, tiled=True
        ).astype(F32)
    small_summed = enc_summed[enc_size:].reshape(-1)[:held].reshape(-1, share)
    enc_summed = arrange_own(enc_summed[:enc_size], me * enc_size, enc_map, from_units)
    dec_summed = arrange_own(dec_summed, me * dec_size, dec_map, from_units)

    part = 1.0 / devices
    enc_summed = enc_summed * part
    dec_summed = dec_summed * part
    small_summed = small_summed * part
    enc_new, enc_first_new, encoder_second_moment_updated = adamw(
        enc_master, enc_summed, enc_first, enc_second
    )
    dec_new, dec_first_new, dec_second_new = adamw(dec_master, dec_summed, dec_first, dec_second)
    small_first_new, small_second_new = moments(small_summed, small_first, small_second)
    return (
        memory,
        decoded,
        src_grad,
        tgt_grad,
        enc_new,
        enc_first_new,
        encoder_second_moment_updated,
        enc_new.astype(LOW),
        dec_new,
        dec_first_new,
        dec_second_new,
        dec_new.astype(LOW),
        small_summed,
        small_first_new,
        small_second_new,
    )


def solution(mesh):
    rows = P("fsdp", None)
    columns = P(None, "fsdp")
    return jax.shard_map(
        functools.partial(on_device, mesh.shape["fsdp"]),
        mesh=mesh,
        in_specs=(rows,) * 4 + (P("fsdp"),) + (rows,) * 8 + (columns,) * 3,
        out_specs=(rows,) * 12 + (columns,) * 3,
        check_vma=False,
    )
```

```python
import functools

import jax
import jax.numpy as jnp
from jax import lax
from jax.experimental import pallas as pl
from jax.experimental.pallas import tpu as pltpu
from jax.sharding import PartitionSpec as P

HEADS = 8
HEAD = 64
STEPS = 7
TILE = 256
LANES = 128

rate = 0.02
beta_one = 0.9
beta_two = 0.98
epsilon = 1e-06
decay = 0.01
floor_value = -1000000000.0
root_half = 0.7071067811865476
inverse_root_tau = 0.3989422804014327

F32 = jnp.float32
LOW = jnp.bfloat16
MIB = 2**20


def nn(former, latter):
    return lax.dot_general(
        former, latter, (((1,), (0,)), ((), ())), preferred_element_type=F32
    )


def nt(former, latter):
    return lax.dot_general(
        former, latter, (((1,), (1,)), ((), ())), preferred_element_type=F32
    )


def turned(values):
    return values.astype(F32).T.astype(LOW)


def column_of(row):
    return jnp.broadcast_to(row, (8, row.shape[1])).T[:, 0:1]


def ln_forward(values, gain, shift):
    centered = values - jnp.mean(values, axis=-1, keepdims=True)
    spread = jnp.mean(centered * centered, axis=-1, keepdims=True)
    inverse = lax.rsqrt(spread + 1e-05)
    normed = centered * inverse
    return normed * gain + shift, normed, inverse


def ln_backward(upstream, normed, inverse, gain):
    scaled = upstream * gain
    first = jnp.mean(scaled, axis=-1, keepdims=True)
    second = jnp.mean(scaled * normed, axis=-1, keepdims=True)
    return inverse * (scaled - first - normed * second)


def phi_and_slope(values):
    phi = 0.5 + 0.5 * lax.erf(values * root_half)
    return phi, phi + values * (jnp.exp(-0.5 * (values * values)) * inverse_root_tau)


def one_head(pair, head):
    lane = lax.broadcasted_iota(jnp.int32, pair.shape, 1)
    keep = lane < HEAD if head % 2 == 0 else lane >= HEAD
    return jnp.where(keep, pair, jnp.zeros_like(pair))


def pair_columns(head):
    return slice(LANES * (head // 2), LANES * (head // 2) + LANES)


def head_rows(head):
    return slice(HEAD * head, HEAD * head + HEAD)


def block_of(ref, j, count):
    if count == 1:
        return ref[...]
    return jnp.concatenate(
        [ref[first + 16 * j : first + 16 * j + 16, :] for first in range(0, ref.shape[0], 16 * count)], axis=0
    )


def spread(wide, values):
    for n in range(wide.shape[0]):
        wide[n] = values[:, LANES * n : LANES * n + LANES].astype(F32)


def third_rows(wide, j):
    rows = pl.ds(j, wide.shape[1] // 3, stride=3)
    return jnp.concatenate([wide[n, rows, :] for n in range(wide.shape[0])], axis=1).astype(LOW)


def put_third_rows(wide, j, values):
    rows = pl.ds(j, wide.shape[1] // 3, stride=3)
    for n in range(wide.shape[0]):
        wide[n, rows, :] = values[:, LANES * n : LANES * n + LANES]


def wide_scratch(width):
    return pltpu.VMEM((width // LANES, 3 * width, LANES), F32)


def put_block(ref, j, values):
    ref[:, j] = values.reshape(ref.shape[0], ref.shape[2], ref.shape[3])


OWNERS = 32


def row_copies(first, last, own, paired):
    found = []
    at = first
    while at < last:
        owner = at // own
        end = min(last, (owner + 1) * own)
        half = OWNERS // 4
        place = (2 * (owner // 2 // half) + owner % 2, owner // 2 % half) if paired else (0, owner)
        found.append((*place, at - owner * own, end - at, at - first))
        at = end
    return found


class Fetch:
    def __init__(self, far, core, copies, near, semaphores, used):
        self.core = core

        def handles(side):
            return [
                pltpu.make_async_copy(
                    far[source ^ side].at[owner, pl.ds(row, rows)], near.at[pl.ds(to, rows)], semaphores.at[used + n]
                )
                for n, (source, owner, row, rows, to) in enumerate(copies)
            ]

        self.handles = handles

    def start(self):
        if self.core is None:
            for handle in self.handles(0):
                handle.start()
            return
        for side in (0, 1):

            @pl.when(self.core == side)
            def _(side=side):
                for handle in self.handles(side):
                    handle.start()

    def wait(self):
        for handle in self.handles(0):
            handle.wait()


def fetches(far, plan, wanted, nears, semaphores):
    used = 0
    made = []
    core = plan[2, 1] if len(far) > 1 else None
    for copies, near in zip(wanted, nears):
        made.append(Fetch(far, core, copies, near, semaphores, used))
        used += len(copies)
    return made


def wait_first(i, loads):
    @pl.when(i == 0)
    def _():
        for load in loads:
            load.wait()


def fetch_scratch(wanted, width):
    return [pltpu.VMEM((sum(c[3] for c in copies), width), LOW) for copies in wanted] + [
        pltpu.SemaphoreType.DMA((sum(len(copies) for copies in wanted),))
    ]


FAR = pl.BlockSpec(memory_space=pl.ANY)


def sources_of(wanted):
    last = max(copy[0] for copies in wanted for copy in copies)
    return 1 if last == 0 else 2 * (last // 2) + 2


def call(kernel, grid, in_specs, out_specs, out_shape, scratch, flops, moved, name, room=24, near=(), keep=()):
    single = not isinstance(out_shape, list)
    shapes = [
        (pltpu.VMEM if keep is True or n in keep else pltpu.HBM)(*made)
        for n, made in enumerate([out_shape] if single else out_shape)
    ]
    made = pl.pallas_call(
        kernel,
        grid_spec=pltpu.PrefetchScalarGridSpec(
            num_scalar_prefetch=1,
            grid=grid,
            in_specs=in_specs,
            out_specs=out_specs,
            scratch_shapes=scratch,
        ),
        out_shape=shapes[0] if single else shapes,
        compiler_params=pltpu.CompilerParams(vmem_limit_bytes=room * MIB),
        cost_estimate=pl.CostEstimate(
            flops=flops, bytes_accessed=moved, transcendentals=0
        ),
        name=name,
    )

    def run(plan, *operands):
        placed = [
            operand
            if near is True or n in near
            else pltpu.with_memory_space_constraint(operand, pltpu.HBM)
            for n, operand in enumerate(operands)
        ]
        return made(plan, *placed)

    return run


def whole(shape):
    zeros = (0,) * len(shape)
    return pl.BlockSpec(shape, lambda i, *_: zeros)


def rows_of(width):
    return pl.BlockSpec((TILE, width), lambda i, *_: (i, 0))


def at_block(shape, *index):
    return pl.BlockSpec(shape, lambda i, *_: index)


def shaped(shape, kind):
    return (shape, kind)


def attend_tile(plan, i, keys, key_cols, query, owner_row, key_owner, vt, sc):
    scores, acc, top, total, masked_q = sc
    query = query * jnp.asarray(HEAD**-0.5, LOW)
    for h in range(HEADS):
        masked_q[h] = one_head(query[:, pair_columns(h)], h)
    top[...] = jnp.full_like(top, -1e30)
    total[...] = jnp.zeros_like(total)
    acc[...] = jnp.zeros_like(acc)
    begin = plan[0, i]
    chunks = plan[1, i]

    def score_tile(j, carry):
        rows = pl.ds(pl.multiple_of(begin + j * TILE, LANES), TILE)
        bias = jnp.where(key_owner[rows, 0:1] == owner_row, 0.0, floor_value)
        tops = []
        for h in range(HEADS):
            cols = pl.ds(key_cols + LANES * (h // 2), LANES)
            s = nt(keys[rows, cols], masked_q[h]) + bias
            scores[j, h] = s
            tops.append(jnp.max(s, axis=0, keepdims=True))
        top[...] = jnp.maximum(top[...], jnp.concatenate(tops, axis=0))
        return carry

    lax.fori_loop(0, chunks, score_tile, 0)

    def weigh_tile(j, carry):
        rows = pl.ds(pl.multiple_of(begin + j * TILE, LANES), TILE)
        sums = []
        for h in range(HEADS):
            p = jnp.exp(scores[j, h] - top[h : h + 1, :])
            sums.append(jnp.sum(p, axis=0, keepdims=True))
            acc[head_rows(h), :] += nn(vt[head_rows(h), rows], p.astype(LOW))
        total[...] += jnp.concatenate(sums, axis=0)
        return carry

    lax.fori_loop(0, chunks, weigh_tile, 0)


def fwd_block_kernel(plan, *refs, cross, gain_row, wanted, packed, ffn):
    refs = list(refs)

    def next_refs(count):
        taken = refs[:count]
        del refs[:count]
        return taken

    if cross:
        normed_in, memory = next_refs(2)
    else:
        (x_all,) = next_refs(1)
    far = next_refs(sources_of(wanted))
    small, owner_q, owner_k = next_refs(3)
    q_out, kv_out, ctx_out, lse_out, normed_out, inverse_out = next_refs(6)
    if ffn:
        out, normed_last, inverse_last = next_refs(3)
    kv, vt, mean_v, key_owner, scores, acc, top, total, masked_q, q_all = next_refs(10)
    nears = next_refs(len(wanted))
    semaphores = refs.pop(0)
    loads = fetches(far, plan, wanted, nears, semaphores)
    i = pl.program_id(0)
    width = kv.shape[1] // 2

    @pl.when(i == 0)
    def _():
        for load in loads:
            load.start()
        key_owner[...] = jnp.broadcast_to(owner_k[...], (8, owner_k.shape[1])).T
        loads[0].wait()
        if cross:
            wk, wv = block_of(nears[0], 0, 2), block_of(nears[0], 1, 2)
        elif packed:
            wq, wk, wv = (block_of(nears[0], j, 3) for j in range(3))
        else:
            wide = refs[0]
            spread(wide, nears[0][...])
            wq, wk, wv = (third_rows(wide, j) for j in range(3))
        sums = jnp.zeros((1, width), F32)
        for t in range(kv.shape[0] // TILE):
            rows = slice(t * TILE, t * TILE + TILE)
            x = memory[rows, :] if cross else x_all[rows, :]
            if not cross:
                q_all[rows, :] = nn(x, wq).astype(LOW)
            kv[rows, :width] = nn(x, wk).astype(LOW)
            v = nn(x, wv).astype(LOW)
            kv[rows, width:] = v
            v = v.astype(F32)
            vt[:, rows] = v.T.astype(LOW)
            sums = sums + jnp.sum(v, axis=0, keepdims=True)
        mean_v[...] = sums * (1.0 / kv.shape[0])
        for load in loads[1 : 3 if cross else 2]:
            load.wait()

    wo = nears[1]
    mine = pl.ds(pl.multiple_of(i * TILE, TILE), TILE)
    if cross:
        resid = normed_in[...] * small[4:5, :] + small[5:6, :]
        query = nn(resid.astype(LOW), nears[2][...]).astype(LOW)
        q_out[...] = query
    else:
        resid = x_all[mine, :].astype(F32)
        query = q_all[mine, :]
        q_out[...] = query
    kv_out[...] = kv[mine, :]
    owner_row = owner_q[...]
    attend_tile(plan, i, kv, 0, query, owner_row, key_owner, vt, (scores, acc, top, total, masked_q))
    dead = owner_row < 0
    sums = jnp.where(dead, 1.0, total[...])
    share = 1.0 / sums
    lse_out[...] = jnp.where(dead, 0.0, top[...] + jnp.log(sums))
    for h in range(HEADS):
        acc[head_rows(h), :] = acc[head_rows(h), :] * share[h : h + 1, :]
    live = column_of(owner_row) >= 0
    context = jnp.where(live, acc[...].T, mean_v[...]).astype(LOW)
    ctx_out[...] = context
    added = nn(context, wo[...]) * live.astype(F32)
    mid, normed, inverse = ln_forward(
        resid + added, small[gain_row : gain_row + 1, :], small[gain_row + 1 : gain_row + 2, :]
    )
    normed_out[...] = normed
    inverse_out[...] = jnp.broadcast_to(inverse, inverse_out.shape)
    if ffn:
        wup, wdown = nears[-2:]
        wait_first(i, loads[-2:])
        blocks = wdown.shape[0] // width
        low = mid.astype(LOW)
        result = mid
        for j in range(blocks):
            inner = nn(low, block_of(wup, j, blocks))
            phi = 0.5 + 0.5 * lax.erf(inner * root_half)
            result = result + nn((inner * phi).astype(LOW), wdown[j * width : j * width + width, :])
        result, normed, inverse = ln_forward(
            result, small[gain_row + 2 : gain_row + 3, :], small[gain_row + 3 : gain_row + 4, :]
        )
        out[...] = result.astype(LOW)
        normed_last[...] = normed
        inverse_last[...] = jnp.broadcast_to(inverse, inverse_last.shape)


def attention_scratch(keys, width):
    return [
        pltpu.VMEM((keys, 2 * width), LOW),
        pltpu.VMEM((width, keys), LOW),
        pltpu.VMEM((1, width), F32),
        pltpu.VMEM((keys, 8), F32),
        pltpu.VMEM((keys // TILE, HEADS, TILE, TILE), F32),
        pltpu.VMEM((width, TILE), F32),
        pltpu.VMEM((HEADS, TILE), F32),
        pltpu.VMEM((HEADS, TILE), F32),
        pltpu.VMEM((HEADS, TILE, LANES), LOW),
        pltpu.VMEM((keys, width), LOW),
    ]


def block_outs(queries, width):
    specs = [
        rows_of(width),
        rows_of(2 * width),
        rows_of(width),
        pl.BlockSpec((HEADS, TILE), lambda i, *_: (0, i)),
        rows_of(width),
        rows_of(LANES),
    ]
    shapes = [
        shaped((queries, width), LOW),
        shaped((queries, 2 * width), LOW),
        shaped((queries, width), LOW),
        shaped((HEADS, queries), F32),
        shaped((queries, width), F32),
        shaped((queries, LANES), F32),
    ]
    return specs, shapes


def owner_specs(keys):
    return [pl.BlockSpec((1, TILE), lambda i, *_: (0, i)), whole((1, keys))]


def fwd_block(plan, x, memory, far, wanted, packed, small, gain_row, owner, key_owner, ffn, name):
    cross = memory is not None
    number, width = x.shape
    specs, shapes = block_outs(number, width)
    if ffn:
        specs += [rows_of(width), rows_of(width), rows_of(LANES)]
        shapes += [shaped((number, width), LOW), shaped((number, width), F32), shaped((number, LANES), F32)]
    scratch = attention_scratch(number, width) + fetch_scratch(wanted, width)
    if not cross and not packed:
        scratch.append(wide_scratch(width))
    return call(
        functools.partial(
            fwd_block_kernel, cross=cross, gain_row=gain_row, wanted=wanted, packed=packed, ffn=ffn
        ),
        (number // TILE,),
        ([rows_of(width), whole(memory.shape)] if cross else [whole(x.shape)])
        + [FAR] * sources_of(wanted)
        + [whole(small.shape)]
        + owner_specs(number),
        specs,
        shapes,
        scratch,
        8 * number * width * width + number * number * width * 2,
        16 * number * width,
        name,
        room=44,
    )(plan, *([x, memory] if cross else [x]), *far[: sources_of(wanted)], small, owner, key_owner)


def ffn_back_kernel(plan, *refs, tiles, summed, gain_row, wanted):
    refs = list(refs)
    cot = refs.pop(0)
    extra = refs.pop(0) if summed else None
    normed_top, inverse_top, normed_mid, inverse_mid, context = refs[:5]
    far = refs[5 : 5 + sources_of(wanted)]
    (small,
     d_sum, d_context, g_up, g_down, g_out, sums, hidden, d_inner, mid_low, d_down, d_product,
     wup, wdown, wo, semaphores) = refs[5 + sources_of(wanted) :]
    loads = fetches(far, plan, wanted, (wup, wdown, wo), semaphores)
    i = pl.program_id(0)
    width = small.shape[1]
    blocks = wdown.shape[0] // width

    @pl.when(i == 0)
    def _():
        for load in loads:
            load.start()
        sums[...] = jnp.zeros_like(sums)

    @pl.when(i < tiles)
    def _():
        mine = pl.ds(pl.multiple_of(i * TILE, TILE), TILE)
        upstream = cot[...].astype(F32)
        if summed:
            upstream = upstream + extra[...]
        top = normed_top[...]
        sums[2:3, :] += jnp.sum(upstream * top, axis=0, keepdims=True)
        sums[3:4, :] += jnp.sum(upstream, axis=0, keepdims=True)
        d_mid = ln_backward(upstream, top, inverse_top[:, 0:1], small[gain_row + 2 : gain_row + 3, :])
        low = d_mid.astype(LOW)
        d_down[mine, :] = low
        normed = normed_mid[...]
        mid = (normed * small[gain_row : gain_row + 1, :] + small[gain_row + 1 : gain_row + 2, :]).astype(LOW)
        mid_low[mine, :] = mid
        wait_first(i, loads)
        for j in range(blocks):
            cols = slice(j * width, j * width + width)
            up = block_of(wup, j, blocks)
            inner = nn(mid, up)
            phi, slope = phi_and_slope(inner)
            hidden[j, mine, :] = (inner * phi).astype(LOW)
            part = (nt(low, wdown[cols, :]) * slope).astype(LOW)
            d_inner[j, mine, :] = part
            d_mid = d_mid + nt(part, up)
        sums[0:1, :] += jnp.sum(d_mid * normed, axis=0, keepdims=True)
        sums[1:2, :] += jnp.sum(d_mid, axis=0, keepdims=True)
        total = ln_backward(d_mid, normed, inverse_mid[:, 0:1], small[gain_row : gain_row + 1, :])
        d_sum[...] = total
        place = lax.broadcasted_iota(jnp.int32, (TILE, 1), 0) + i * TILE
        live = (place < plan[2, 0]).astype(F32)
        product = (total * live).astype(LOW)
        d_product[mine, :] = product
        d_context[...] = nt(product, wo[...]).astype(LOW)

    @pl.when(i >= tiles)
    def _():
        j = i - tiles
        put_block(g_up, 0, nn(turned(mid_low[...]), d_inner[j]).astype(LOW))
        g_down[...] = nn(turned(hidden[j]), d_down[...]).astype(LOW)

    @pl.when(i == tiles)
    def _():
        g_out[...] = nn(turned(context[...]), d_product[...]).astype(LOW)


def ffn_backward(plan, cots, top, mid, context, far, wanted, small, gain_row, inner, name):
    number, width = mid[0].shape
    tiles, blocks = number // TILE, inner // width

    def tile_of(columns):
        return pl.BlockSpec((TILE, columns), lambda i, *_: (jnp.minimum(i, tiles - 1), 0))

    return call(
        functools.partial(
            ffn_back_kernel, tiles=tiles, summed=len(cots) == 2, gain_row=gain_row, wanted=wanted
        ),
        (tiles + blocks,),
        [tile_of(width)] * len(cots)
        + [tile_of(width), tile_of(LANES), tile_of(width), tile_of(LANES), whole((number, width))]
        + [FAR] * sources_of(wanted)
        + [whole(small.shape)],
        [
            tile_of(width),
            tile_of(width),
            pl.BlockSpec((width // 16, 1, 16, width), lambda i, *_: (0, jnp.maximum(i - tiles, 0), 0, 0)),
            pl.BlockSpec((width, width), lambda i, *_: (jnp.maximum(i - tiles, 0), 0)),
            pl.BlockSpec((width, width), lambda i, *_: (0, 0)),
            pl.BlockSpec((8, width), lambda i, *_: (0, 0)),
        ],
        [
            shaped((number, width), F32),
            shaped((number, width), LOW),
            shaped((width // 16, blocks, 16, width), LOW),
            shaped((inner, width), LOW),
            shaped((width, width), LOW),
            shaped((8, width), F32),
        ],
        [
            pltpu.VMEM((blocks, number, width), LOW),
            pltpu.VMEM((blocks, number, width), LOW),
            pltpu.VMEM((number, width), LOW),
            pltpu.VMEM((number, width), LOW),
            pltpu.VMEM((number, width), LOW),
        ]
        + fetch_scratch(wanted, width),
        10 * number * width * inner,
        30 * number * width,
        name,
        room=44,
    )(plan, *cots, *top, *mid, context, *far[: sources_of(wanted)], small)


def attend_back(plan, i, q_ref, k_ref, v_ref, do_ref, lse, owner_q, owner_k, scratch):
    kt, key_owner, masked_q, masked_do, dqt, dk_sum, dv_sum, weights, d_weights, dots = scratch

    @pl.when(i == 0)
    def _():
        key_owner[...] = jnp.broadcast_to(owner_k[...], (8, owner_k.shape[1])).T
        kt[...] = turned(k_ref[...])
        dk_sum[...] = jnp.zeros_like(dk_sum)
        dv_sum[...] = jnp.zeros_like(dv_sum)

    query = q_ref[...] * jnp.asarray(HEAD**-0.5, LOW)
    upstream = do_ref[...]
    for h in range(HEADS):
        masked_q[h] = one_head(query[:, pair_columns(h)], h)
        masked_do[h] = one_head(upstream[:, pair_columns(h)], h)
    dqt[...] = jnp.zeros_like(dqt)
    dots[...] = jnp.zeros_like(dots)
    owner_row = owner_q[...]
    begin = plan[0, i]
    chunks = plan[1, i]

    def weigh_tile(j, carry):
        rows = pl.ds(pl.multiple_of(begin + j * TILE, LANES), TILE)
        bias = jnp.where(key_owner[rows, 0:1] == owner_row, 0.0, floor_value)
        sums = []
        for h in range(HEADS):
            s = nt(k_ref[rows, pair_columns(h)], masked_q[h])
            p = jnp.exp((s - lse[h : h + 1, :]) + bias)
            dp = nt(v_ref[rows, pair_columns(h)], masked_do[h])
            weights[j, h] = p
            d_weights[j, h] = dp
            sums.append(jnp.sum(p * dp, axis=0, keepdims=True))
        dots[...] += jnp.concatenate(sums, axis=0)
        return carry

    lax.fori_loop(0, chunks, weigh_tile, 0)

    def grad_tile(j, carry):
        rows = pl.ds(pl.multiple_of(begin + j * TILE, LANES), TILE)
        for pair in range(HEADS // 2):
            cols = pair_columns(2 * pair)
            dv_part = dv_sum[rows, cols]
            dk_part = dk_sum[rows, cols]
            for h in (2 * pair, 2 * pair + 1):
                p = weights[j, h]
                ds = (p * (d_weights[j, h] - dots[h : h + 1, :])).astype(LOW)
                dv_part = dv_part + nn(p.astype(LOW), masked_do[h])
                dk_part = dk_part + nn(ds, masked_q[h])
                dqt[head_rows(h), :] += nn(kt[head_rows(h), rows], ds)
            dv_sum[rows, cols] = dv_part
            dk_sum[rows, cols] = dk_part
        return carry

    lax.fori_loop(0, chunks, grad_tile, 0)
    return (dqt[...] * HEAD**-0.5).T.astype(LOW)


def attention_back_kernel(plan, *refs, made):
    q_ref, k_ref, v_ref, do_ref, lse, owner_q, owner_k, *refs = refs
    x = refs.pop(0) if made else None
    dq, dk, dv, *refs = refs
    g_qkv = refs.pop(0) if made else None
    scratch, more = refs[:10], refs[10:]
    dk_sum, dv_sum = scratch[5:7]
    i = pl.program_id(0)
    dq_tile = attend_back(plan, i, q_ref, k_ref, v_ref, do_ref, lse, owner_q, owner_k, scratch)
    dq[...] = dq_tile
    if made:
        dq_all = more[0]
        dq_all[pl.ds(pl.multiple_of(i * TILE, TILE), TILE), :] = dq_tile

    @pl.when(i == pl.num_programs(0) - 1)
    def _():
        dk[...] = dk_sum[...].astype(LOW)
        dv[...] = dv_sum[...].astype(LOW)
        if made:
            turn = turned(x[...])
            for j, ref in enumerate((dq_all, dk, dv)):
                grad = nn(turn, ref[...])
                if made == "units":
                    put_block(g_qkv, j, grad.astype(LOW))
                else:
                    put_third_rows(more[1], j, grad)
        if made == "rows":
            for n in range(more[1].shape[0]):
                g_qkv[:, LANES * n : LANES * n + LANES] = more[1][n].astype(LOW)


def attend_back_scratch(keys, width):
    return [
        pltpu.VMEM((width, keys), LOW),
        pltpu.VMEM((keys, 8), F32),
        pltpu.VMEM((HEADS, TILE, LANES), LOW),
        pltpu.VMEM((HEADS, TILE, LANES), LOW),
        pltpu.VMEM((width, TILE), F32),
        pltpu.VMEM((keys, width), F32),
        pltpu.VMEM((keys, width), F32),
        pltpu.VMEM((keys // TILE, HEADS, TILE, TILE), F32),
        pltpu.VMEM((keys // TILE, HEADS, TILE, TILE), F32),
        pltpu.VMEM((HEADS, TILE), F32),
    ]


def attention_backward(plan, q, kv, d_context, lse, owner, key_owner, x, made, name):
    number, width = q.shape
    keys = kv.shape[0]
    in_specs = [
        rows_of(width),
        at_block((keys, width), 0, 0),
        at_block((keys, width), 0, 1),
        rows_of(width),
        pl.BlockSpec((HEADS, TILE), lambda i, *_: (0, i)),
    ] + owner_specs(keys)
    out_specs = [rows_of(width), whole((keys, width)), whole((keys, width))]
    out_shape = [shaped((number, width), LOW), shaped((keys, width), LOW), shaped((keys, width), LOW)]
    operands = [q, kv, kv, d_context, lse, owner, key_owner]
    scratch = attend_back_scratch(keys, width)
    if made:
        shape = (width // 16, 3, 16, width) if made == "units" else (3 * width, width)
        in_specs.append(whole(x.shape))
        operands.append(x)
        out_specs.append(whole(shape))
        out_shape.append(shaped(shape, LOW))
        scratch.append(pltpu.VMEM((number, width), LOW))
        if made == "rows":
            scratch.append(wide_scratch(width))
    return call(
        functools.partial(attention_back_kernel, made=made),
        (number // TILE,),
        in_specs,
        out_specs,
        out_shape,
        scratch,
        number * keys * width * 4 + (6 * number * width * width if made else 0),
        12 * number * width,
        name,
        room=52,
    )(plan, *operands)


def cross_back_kernel(plan, *refs, wanted, tiles):
    attention, refs = refs[:7], refs[7:]
    normed, inverse, d_above, memory, context = refs[:5]
    far = refs[5 : 5 + sources_of(wanted)]
    small, d_memory, d_sum, d_context, g_query, g_pair, g_out, sums, *refs = refs[5 + sources_of(wanted) :]
    scratch, refs = refs[:10], refs[10:]
    d_query, dk, dv, d_product, wkv, wq, wo, semaphores = refs
    dk_sum, dv_sum = scratch[5:7]
    loads = fetches(far, plan, wanted, (wkv, wq, wo), semaphores)
    i = pl.program_id(0)

    @pl.when(i == 0)
    def _():
        for load in loads:
            load.start()
        sums[...] = jnp.zeros_like(sums)

    @pl.when(i < tiles)
    def _():
        d_query[pl.ds(pl.multiple_of(i * TILE, TILE), TILE), :] = attend_back(plan, i, *attention, scratch)

    @pl.when(i == tiles)
    def _():
        dk[...] = dk_sum[...].astype(LOW)
        dv[...] = dv_sum[...].astype(LOW)
        for load in loads:
            load.wait()
        low = normed[...] * small[4:5, :] + small[5:6, :]
        g_query[...] = nn(low.T.astype(LOW), d_query[...]).astype(LOW)

    @pl.when(i >= tiles)
    def _():
        row = pl.multiple_of((i - tiles) * TILE, TILE)
        mine = pl.ds(row, TILE)
        wk, wv = block_of(wkv, 0, 2), block_of(wkv, 1, 2)
        d_memory[...] = nt(dk[mine, :], wk) + nt(dv[mine, :], wv)
        d_one = d_above[...] + nt(d_query[mine, :], wq[...])
        hat = normed[mine, :]
        sums[0:1, :] += jnp.sum(d_one * hat, axis=0, keepdims=True)
        sums[1:2, :] += jnp.sum(d_one, axis=0, keepdims=True)
        total = ln_backward(d_one, hat, inverse[:, 0:1], small[4:5, :])
        d_sum[...] = total
        place = lax.broadcasted_iota(jnp.int32, (TILE, 1), 0) + row
        live = (place < plan[2, 0]).astype(F32)
        product = (total * live).astype(LOW)
        d_product[mine, :] = product
        d_context[...] = nt(product, wo[...]).astype(LOW)

    @pl.when(i == tiles + 1)
    def _():
        put_block(g_pair, 0, nn(turned(memory[...]), dk[...]).astype(LOW))

    @pl.when(i == tiles + 2)
    def _():
        put_block(g_pair, 1, nn(turned(memory[...]), dv[...]).astype(LOW))

    @pl.when(i == 2 * tiles - 1)
    def _():
        g_out[...] = nn(turned(context[...]), d_product[...]).astype(LOW)


def cross_backward(plan, q, kv, d_context, lse, owner, key_owner, normed, inverse, d_above, memory, context, far,
                   wanted, small):
    number, width = normed.shape
    keys = kv.shape[0]
    tiles = number // TILE
    full = whole((number, width))

    def first_rows(columns):
        return pl.BlockSpec((TILE, columns), lambda i, *_: (jnp.minimum(i, tiles - 1), 0))

    def first_columns(rows):
        return pl.BlockSpec((rows, TILE), lambda i, *_: (0, jnp.minimum(i, tiles - 1)))

    def later_rows(columns):
        return pl.BlockSpec((TILE, columns), lambda i, *_: (jnp.maximum(i - tiles, 0), 0))

    return call(
        functools.partial(cross_back_kernel, wanted=wanted, tiles=tiles),
        (2 * tiles,),
        [first_rows(width), at_block((keys, width), 0, 0), at_block((keys, width), 0, 1), first_rows(width),
         first_columns(HEADS), first_columns(1), whole((1, keys)),
         full, later_rows(LANES), later_rows(width), whole(memory.shape), full]
        + [FAR] * sources_of(wanted)
        + [whole(small.shape)],
        [later_rows(width), later_rows(width), later_rows(width), whole((width, width)),
         whole((width // 16, 2, 16, width)), whole((width, width)), whole((8, width))],
        [shaped((number, width), F32), shaped((number, width), F32), shaped((number, width), LOW),
         shaped((width, width), LOW), shaped((width // 16, 2, 16, width), LOW), shaped((width, width), LOW),
         shaped((8, width), F32)],
        attend_back_scratch(keys, width)
        + [pltpu.VMEM((number, width), LOW), pltpu.VMEM((keys, width), LOW), pltpu.VMEM((keys, width), LOW),
           pltpu.VMEM((number, width), LOW)]
        + fetch_scratch(wanted, width),
        16 * number * width * width + number * keys * width * 4,
        24 * number * width,
        "cross_back",
        room=58,
    )(plan, q, kv, kv, d_context, lse, owner, key_owner, normed, inverse, d_above, memory, context,
      *far[: sources_of(wanted)], small)


def qkv_inputs_kernel(plan, *refs, masked, wanted):
    if masked:
        dq, dk, dv, d_above, flags, *refs = refs
        far = refs[: sources_of(wanted)]
        d_x, mask_sum, near, semaphores, blocks, wide = refs[sources_of(wanted) :]
    else:
        dq, dk, dv, d_above, *refs = refs
        far = refs[: sources_of(wanted)]
        d_x, near, semaphores, blocks = refs[sources_of(wanted) :]
    width = dq.shape[1]

    @pl.when(pl.program_id(0) == 0)
    def _():
        (load,) = fetches(far, plan, wanted, (near,), semaphores)
        load.start()
        load.wait()
        if masked:
            mask_sum[...] = jnp.zeros_like(mask_sum)
            spread(wide, near[...])
        for j in range(3):
            if masked:
                blocks[:, j * width : j * width + width] = third_rows(wide, j)
            else:
                blocks[:, j * width : j * width + width] = block_of(near, j, 3)

    pieces = jnp.concatenate([dq[...], dk[...], dv[...]], axis=1)
    total = nt(pieces, blocks[...])
    if masked:
        total = total + d_above[...]
        hit = column_of(flags[...]) == 1.0
        d_x[...] = jnp.where(hit, 0.0, total)
        mask_sum[0:1, :] += jnp.sum(jnp.where(hit, total, 0.0), axis=0, keepdims=True)
    else:
        d_x[...] = d_above[...]
        d_x[...] += total


def qkv_inputs(plan, dq, dk, dv, d_above, far, wanted, flags, name):
    number, width = dq.shape
    masked = flags is not None
    in_specs = [rows_of(width)] * 4
    out_specs = [rows_of(width)]
    out_shape = [shaped((number, width), F32)]
    operands = [dq, dk, dv, d_above]
    scratch = fetch_scratch(wanted, width) + [pltpu.VMEM((width, 3 * width), LOW)]
    if masked:
        in_specs.append(pl.BlockSpec((1, TILE), lambda i, *_: (0, i)))
        out_specs.append(whole((8, width)))
        out_shape.append(shaped((8, width), F32))
        operands.append(flags)
        scratch.append(wide_scratch(width))
    in_specs += [FAR] * sources_of(wanted)
    operands += far[: sources_of(wanted)]
    return call(
        functools.partial(qkv_inputs_kernel, masked=masked, wanted=wanted),
        (number // TILE,),
        in_specs,
        out_specs,
        out_shape,
        scratch,
        6 * number * width * width,
        16 * number * width,
        name,
    )(plan, *operands)


def enc_regions(width, inner):
    return ((0, 3 * width, 3), (4 * width, 4 * width + inner, inner // width))


def dec_regions(width, inner):
    return ((5 * width, 7 * width, 2), (8 * width, 8 * width + inner, inner // width))


def to_units(rows, k):
    return rows.reshape(-1, 16, k, rows.shape[1]).transpose(0, 2, 1, 3).reshape(rows.shape)


def from_units(rows, k):
    return rows.reshape(-1, k, 16, rows.shape[1]).transpose(0, 2, 1, 3).reshape(rows.shape)


def fits(size, region):
    return size % (16 * region[2]) == 0


def arrange_own(rows, first, regions, arrange):
    place = first + lax.broadcasted_iota(jnp.int32, (rows.shape[0], 1), 0)
    result = rows
    for region in regions:
        if fits(rows.shape[0], region):
            inside = (place >= region[0]) & (place < region[1])
            result = jnp.where(inside, arrange(rows, region[2]), result)
    return result


def arrange_all(rows, size, regions, arrange):
    for region in regions:
        if not fits(size, region):
            part = arrange(rows[region[0] : region[1]], region[2])
            rows = jnp.concatenate([rows[: region[0]], part, rows[region[1] :]], axis=0)
    return rows


def owners_of(lengths, number):
    bounds = jnp.cumsum(lengths)
    places = jnp.arange(number, dtype=jnp.int32)
    owners = jnp.sum((places[:, None] >= bounds[None, :]).astype(jnp.int32), axis=1)
    filled = places < bounds[-1]
    for_queries = jnp.where(filled, owners, -2).astype(F32)[None, :]
    for_keys = jnp.where(filled, owners, -1).astype(F32)[None, :]
    return for_queries, for_keys, bounds


def plan_of(query_bounds, key_bounds, key_lengths, number, core):
    firsts = jnp.arange(8, dtype=jnp.int32) * TILE
    filled = query_bounds[-1]
    lasts = jnp.minimum(firsts + TILE, filled) - 1

    def pair_of(places):
        found = jnp.sum((places[:, None] >= query_bounds[None, :]).astype(jnp.int32), axis=1)
        return jnp.minimum(found, key_lengths.shape[0] - 1)

    def pick(values, pairs):
        chosen = pairs[:, None] == jnp.arange(values.shape[0])[None, :]
        return jnp.sum(jnp.where(chosen, values[None, :], 0), axis=1)

    begin = pick(key_bounds - key_lengths, pair_of(firsts))
    end = pick(key_bounds, pair_of(lasts))
    some = firsts < filled
    begin = begin // LANES * LANES
    chunks = (end - begin + TILE - 1) // TILE
    begin = jnp.where(some, jnp.minimum(begin, number - chunks * TILE), 0)
    chunks = jnp.where(some, chunks, 0)
    rest = jnp.where(jnp.arange(8) == 1, core, filled)
    return jnp.stack([begin, chunks, rest]).astype(jnp.int32)


def moments(gradient, first, second):
    first_new = beta_one * first + (1.0 - beta_one) * gradient
    second_new = beta_two * second + (1.0 - beta_two) * gradient * gradient
    return (first_new, second_new)


def adamw(weight, gradient, first, second):
    first_new, second_new = moments(gradient, first, second)
    moved = weight - rate * (
        first_new
        / (1.0 - beta_one**STEPS)
        / (jnp.sqrt(second_new / (1.0 - beta_two**STEPS)) + epsilon)
        + decay * weight
    )
    return (moved, first_new, second_new)


CORE, X, Y, Z_LOW, Z_HIGH = 0, 1, 2, 3, 4
BITS = 5


def partner(bit):
    return [(i, i ^ (1 << bit)) for i in range(1 << BITS)]


def bit_of(me, bit):
    return (me >> bit) & 1


def take(values, axis, index):
    return lax.dynamic_index_in_dim(values, index, axis, keepdims=False)


def overlaps(sizes, own):
    found = []
    first = 0
    for piece, size in enumerate(sizes):
        at = first
        while at < first + size:
            owner = at // own
            end = min(first + size, (owner + 1) * own)
            found.append((piece, at - first, owner, at - owner * own, end - at))
            at = end
        first += size
    return found


def pack_kernel(core, *refs, copies, number):
    pieces, send, keep, semaphores = refs[:number], refs[number], refs[number + 1], refs[number + 2]
    for side in (0, 1):

        @pl.when(core[0] == side)
        def _():
            handles = []
            for n, (piece, at, owner, to, rows) in enumerate(copies):
                target = keep if owner % 2 == side else send
                handles.append(
                    pltpu.make_async_copy(
                        pieces[piece].at[pl.ds(at, rows)],
                        target.at[owner // 2, pl.ds(to, rows)],
                        semaphores.at[n],
                    )
                )
            for handle in handles:
                handle.start()
            for handle in handles:
                handle.wait()


def pack(core, pieces, copies, block, name):
    width = pieces[0].shape[1]
    shape = shaped((1 << (BITS - 1), block, width), LOW)
    anywhere = pl.BlockSpec(memory_space=pl.ANY)
    total = sum(piece.size for piece in pieces)
    return call(
        functools.partial(pack_kernel, copies=copies, number=len(pieces)),
        (1,),
        [pl.BlockSpec(memory_space=pltpu.VMEM)] * len(pieces),
        [anywhere, anywhere],
        [shape, shape],
        [pltpu.SemaphoreType.DMA((len(copies),))],
        0,
        4 * total,
        name,
        near=True,
    )(core, *pieces)


def add_low(former, latter):
    return (former.astype(F32) + latter.astype(F32)).astype(LOW)


def swap(values, bit):
    return lax.ppermute(values, "fsdp", partner(bit))


def reduce_owned(me, send, keep, cut):
    rows, width = send.shape[1:]
    x, y, low, high = (bit_of(me, b) for b in (X, Y, Z_LOW, Z_HIGH))
    (send,) = yield (send,)
    chips = add_low(keep, swap(send, CORE)).reshape(2, 2, 2, 2, rows, width)
    first, second = chips[..., :cut, :], chips[..., cut:, :]
    for_y, for_x = yield (take(first, 2, 1 - y), take(second, 3, 1 - x))
    first = add_low(take(first, 2, y), swap(for_y, Y))
    second = add_low(take(second, 3, x), swap(for_x, X))
    for_x, for_y = yield (take(first, 2, 1 - x), take(second, 2, 1 - y))
    first = add_low(take(first, 2, x), swap(for_x, X))
    second = add_low(take(second, 2, y), swap(for_y, Y))
    column = jnp.concatenate([first, second], axis=2)
    (for_z,) = yield (take(column, 1, 1 - low),)
    column = add_low(take(column, 1, low), swap(for_z, Z_LOW))
    (for_z,) = yield (take(column, 0, 1 - high),)
    return take(column, 0, high).astype(F32) + swap(for_z, Z_HIGH).astype(F32)


def ordered(bit, mine, other, axis):
    first = bit == 0
    return jnp.stack([jnp.where(first, mine, other), jnp.where(first, other, mine)], axis=axis)


def gather_owned(me, own):
    x, y, low, high = (bit_of(me, b) for b in (X, Y, Z_LOW, Z_HIGH))
    rows, width = own.shape
    (own,) = yield (own,)
    column = ordered(high, own, swap(own, Z_HIGH), 0)
    (column,) = yield (column,)
    column = ordered(low, column, swap(column, Z_LOW), 1)
    below, above = yield (column[0], column[1])
    below = ordered(x, below, swap(below, X), 1)
    above = ordered(y, above, swap(above, Y), 1)
    below, above = yield (below, above)
    below = ordered(y, below, swap(below, Y), 1).reshape(-1, rows, width)
    above = ordered(x, above, swap(above, X), 2).reshape(-1, rows, width)
    below, above = yield (below, above)
    return [below, swap(below, CORE), above, swap(above, CORE)]


class Rounds:
    def __init__(self, steps):
        self.steps = steps
        self.sent = next(steps)
        self.result = None

    def before(self, *operands):
        sent, operands = lax.optimization_barrier((self.sent, operands))
        self.move(sent)
        return operands[0] if len(operands) == 1 else operands

    def move(self, sent):
        try:
            self.sent = self.steps.send(sent)
        except StopIteration as stop:
            self.sent, self.result = None, stop.value

    def finish(self):
        while self.result is None:
            self.move(self.sent)
        return self.result


def on_device(
    devices,
    src_in,
    tgt_in,
    src_len,
    tgt_len,
    tgt_mask,
    enc_cot,
    dec_cot,
    enc_master,
    enc_first,
    enc_second,
    dec_master,
    dec_first,
    dec_second,
    small_master,
    small_first,
    small_second,
):
    width = src_in.shape[1]
    number = src_in.shape[0]
    me = lax.axis_index("fsdp")
    enc_size, dec_size = enc_master.shape[0], dec_master.shape[0]
    enc_count, dec_count = enc_size * devices, dec_size * devices
    inner = (enc_count - 4 * width) // 2
    ups = inner // width
    enc_map, dec_map = enc_regions(width, inner), dec_regions(width, inner)

    enc_own = arrange_own(enc_master.astype(LOW), me * enc_size, enc_map, to_units)
    dec_own = arrange_own(dec_master.astype(LOW), me * dec_size, dec_map, to_units)
    by_rounds = devices == 1 << BITS
    share = small_master.shape[1]
    held = small_master.size
    own = jnp.zeros((16, width), LOW)
    own = lax.dynamic_update_slice(own, small_master.astype(LOW), (0, me * share))
    gathered = lax.all_gather(jnp.concatenate([enc_own, own], axis=0), "fsdp", axis=0, tiled=False)
    smalls = jnp.sum(gathered[:, enc_size:, :].astype(F32), axis=0)
    core = bit_of(me, CORE)
    src_owner, src_key, src_bounds = owners_of(src_len[0], number)
    tgt_owner, tgt_key, tgt_bounds = owners_of(tgt_len[0], number)
    enc_plan = plan_of(src_bounds, src_bounds, src_len[0], number, core)
    dec_plan = plan_of(tgt_bounds, tgt_bounds, tgt_len[0], number, core)
    cross_plan = plan_of(tgt_bounds, src_bounds, src_len[0], number, core)
    flags = tgt_mask.astype(F32)[None, :]
    if by_rounds:
        enc_far = [gathered]
        rounds = Rounds(gather_owned(me, dec_own))
        for _ in range(4):
            rounds.move(rounds.sent)
        early = (src_in, src_owner, src_key, tgt_owner, tgt_key, enc_plan, dec_plan, cross_plan, flags)
        src_in, src_owner, src_key, tgt_owner, tgt_key, enc_plan, dec_plan, cross_plan, flags = rounds.before(*early)
        dec_far = rounds.finish()
    else:
        enc_rows = arrange_all(gathered[:, :enc_size].reshape(-1, width), enc_size, enc_map, to_units)
        enc_far = [enc_rows.reshape(OWNERS, -1, width)]
        dec_rows = lax.all_gather(dec_own, "fsdp", axis=0, tiled=True)
        dec_rows = arrange_all(dec_rows, dec_size, dec_map, to_units).reshape(2, OWNERS // 4, 2, -1, width)
        first = core == 0
        dec_far = []
        for half in range(2):
            even, odd = dec_rows[half, :, 0], dec_rows[half, :, 1]
            dec_far += [jnp.where(first, even, odd), jnp.where(first, odd, even)]

    def enc_part(first, last):
        return row_copies(first, last, enc_count // OWNERS, False)

    def dec_part(first, last):
        return row_copies(first, last, dec_count // OWNERS, True)

    enc_qkv = enc_part(0, 3 * width)
    enc_wo = enc_part(3 * width, 4 * width)
    enc_up = enc_part(4 * width, 4 * width + inner)
    enc_down = enc_part(4 * width + inner, enc_count)
    self_qkv = dec_part(0, 3 * width)
    self_wo = dec_part(3 * width, 4 * width)
    cross_q = dec_part(4 * width, 5 * width)
    cross_kv = dec_part(5 * width, 7 * width)
    cross_wo = dec_part(7 * width, 8 * width)
    dec_up = dec_part(8 * width, 8 * width + inner)
    dec_down = dec_part(8 * width + inner, dec_count)

    start = jnp.where(tgt_mask[:, None] == 1, smalls[10].astype(LOW)[None, :], tgt_in)

    e_q, e_kv, e_ctx, e_lse, e_hat, e_inv, memory, t_hat, t_inv = fwd_block(
        enc_plan, src_in, None, enc_far, (enc_qkv, enc_wo, enc_up, enc_down), True, smalls, 0, src_owner, src_key, True,
        "enc_layer",
    )
    s_q, s_kv, s_ctx, s_lse, s_hat, s_inv = fwd_block(
        dec_plan, start, None, dec_far, (self_qkv, self_wo), False, smalls, 4, tgt_owner, tgt_key, False, "dec_block"
    )
    c_q, c_kv, c_ctx, c_lse, c_hat, c_inv, decoded, f_hat, f_inv = fwd_block(
        cross_plan, s_hat, memory, dec_far, (cross_kv, cross_wo, cross_q, dec_up, dec_down), True, smalls, 6,
        tgt_owner, src_key, True, "cross_layer",
    )

    d_two, d_cctx, g_dup, g_ddown, g_cout, sums_d = ffn_backward(
        dec_plan, [dec_cot], (f_hat, f_inv), (c_hat, c_inv), c_ctx, dec_far, (dec_up, dec_down, cross_wo), smalls, 6,
        inner, "dec_ffn_back",
    )
    d_memory, d_one, d_sctx, g_cq, g_ckv, g_sout, sums_c = cross_backward(
        cross_plan, c_q, c_kv, d_cctx, c_lse, tgt_owner, src_key, s_hat, s_inv, d_two, memory, s_ctx, dec_far,
        (cross_kv, cross_q, self_wo), smalls,
    )
    dsq, dsk, dsv, g_sqkv = attention_backward(
        dec_plan, s_q, s_kv, d_sctx, s_lse, tgt_owner, tgt_key, start, "rows", "dec_back"
    )
    dec_pieces = [
        g_sqkv,
        g_sout,
        g_cq,
        g_ckv.reshape(-1, width),
        g_cout,
        g_dup.reshape(-1, width),
        g_ddown,
    ]
    if by_rounds:
        core = core[None].astype(jnp.int32)
        copies = overlaps([p.shape[0] for p in dec_pieces], dec_size)
        send, keep = pack(core, dec_pieces, copies, dec_size, "dec_pack")
        rounds = Rounds(reduce_owned(me, send, keep, dec_size // 2))
        dsq, dsk, dsv = rounds.before(dsq, dsk, dsv)
    tgt_grad, mask_sum = qkv_inputs(
        dec_plan, dsq, dsk, dsv, d_one, dec_far, (self_qkv,), flags, "dec_qkv_inputs"
    )
    if by_rounds:
        d_memory, mask_sum = rounds.before(d_memory, mask_sum)
    d_mid, d_ectx, g_up, g_down, g_out, sums_e = ffn_backward(
        enc_plan, [enc_cot, d_memory], (t_hat, t_inv), (e_hat, e_inv), e_ctx, enc_far,
        (enc_up, enc_down, enc_wo), smalls, 0, inner, "enc_ffn_back",
    )
    if by_rounds:
        d_ectx, g_up = rounds.before(d_ectx, g_up)
    deq, dek, dev, g_qkv = attention_backward(
        enc_plan, e_q, e_kv, d_ectx, e_lse, src_owner, src_key, src_in, "units", "enc_back"
    )

    enc_pieces = [g_qkv.reshape(-1, width), g_out, g_up.reshape(-1, width), g_down]
    small_grad = jnp.concatenate([sums_e[:4], sums_c[:2], sums_d[:4], mask_sum[:1]], axis=0)
    small_wire = small_grad.reshape(-1, devices, share).transpose(1, 0, 2).reshape(devices, -1).astype(LOW)
    small_wire = jnp.pad(small_wire, ((0, 0), (0, 16 * width - held))).reshape(devices * 16, width)
    if by_rounds:
        dec_summed = rounds.finish()
        copies = overlaps([p.shape[0] for p in enc_pieces], enc_size)
        copies += [(len(enc_pieces), 16 * i, i, enc_size, 16) for i in range(devices)]
        send, keep = pack(core, enc_pieces + [small_wire], copies, enc_size + 16, "enc_pack")
        rounds = Rounds(reduce_owned(me, send, keep, enc_size // 2 + 16))
        deq, dek, dev = rounds.before(deq, dek, dev)
    src_grad = qkv_inputs(enc_plan, deq, dek, dev, d_mid, enc_far, (enc_qkv,), None, "enc_qkv_inputs")[0]
    if by_rounds:
        enc_summed = rounds.finish()
    else:
        dec_grad = arrange_all(jnp.concatenate(dec_pieces, axis=0), dec_size, dec_map, from_units)
        enc_grad = arrange_all(jnp.concatenate(enc_pieces, axis=0), enc_size, enc_map, from_units)
        enc_wire = jnp.concatenate(
            [enc_grad.reshape(devices, enc_size, width), small_wire.reshape(devices, 16, width)], axis=1
        )
        dec_summed = lax.psum_scatter(dec_grad, "fsdp", scatter_dimension=0, tiled=True).astype(F32)
        enc_summed = lax.psum_scatter(
            enc_wire.reshape(-1, width), "fsdp", scatter_dimension=0, tiled=True
        ).astype(F32)
    small_summed = enc_summed[enc_size:].reshape(-1)[:held].reshape(-1, share)
    enc_summed = arrange_own(enc_summed[:enc_size], me * enc_size, enc_map, from_units)
    dec_summed = arrange_own(dec_summed, me * dec_size, dec_map, from_units)

    part = 1.0 / devices
    enc_summed = enc_summed * part
    dec_summed = dec_summed * part
    small_summed = small_summed * part
    enc_new, enc_first_new, encoder_second_moment_updated = adamw(
        enc_master, enc_summed, enc_first, enc_second
    )
    dec_new, dec_first_new, dec_second_new = adamw(dec_master, dec_summed, dec_first, dec_second)
    small_first_new, small_second_new = moments(small_summed, small_first, small_second)
    return (
        memory,
        decoded,
        src_grad,
        tgt_grad,
        enc_new,
        enc_first_new,
        encoder_second_moment_updated,
        enc_new.astype(LOW),
        dec_new,
        dec_first_new,
        dec_second_new,
        dec_new.astype(LOW),
        small_summed,
        small_first_new,
        small_second_new,
    )


def solution(mesh):
    rows = P("fsdp", None)
    columns = P(None, "fsdp")
    return jax.shard_map(
        functools.partial(on_device, mesh.shape["fsdp"]),
        mesh=mesh,
        in_specs=(rows,) * 4 + (P("fsdp"),) + (rows,) * 8 + (columns,) * 3,
        out_specs=(rows,) * 12 + (columns,) * 3,
        check_vma=False,
    )
```

```python
import functools

import jax
import jax.numpy as jnp
from jax import lax
from jax.experimental import pallas as pl
from jax.experimental.pallas import tpu as pltpu
from jax.sharding import PartitionSpec as P

HEADS = 8
HEAD = 64
STEPS = 7
TILE = 256
LANES = 128

rate = 0.02
beta_one = 0.9
beta_two = 0.98
epsilon = 1e-06
decay = 0.01
floor_value = -1000000000.0
root_half = 0.7071067811865476
inverse_root_tau = 0.3989422804014327

F32 = jnp.float32
LOW = jnp.bfloat16
MIB = 2**20


def nn(former, latter):
    return lax.dot_general(
        former, latter, (((1,), (0,)), ((), ())), preferred_element_type=F32
    )


def nt(former, latter):
    return lax.dot_general(
        former, latter, (((1,), (1,)), ((), ())), preferred_element_type=F32
    )


def turned(values):
    return values.astype(F32).T.astype(LOW)


def column_of(row):
    return jnp.broadcast_to(row, (8, row.shape[1])).T[:, 0:1]


def ln_forward(values, gain, shift):
    centered = values - jnp.mean(values, axis=-1, keepdims=True)
    spread = jnp.mean(centered * centered, axis=-1, keepdims=True)
    inverse = lax.rsqrt(spread + 1e-05)
    normed = centered * inverse
    return normed * gain + shift, normed, inverse


def ln_backward(upstream, normed, inverse, gain):
    scaled = upstream * gain
    first = jnp.mean(scaled, axis=-1, keepdims=True)
    second = jnp.mean(scaled * normed, axis=-1, keepdims=True)
    return inverse * (scaled - first - normed * second)


def phi_and_slope(values):
    phi = 0.5 + 0.5 * lax.erf(values * root_half)
    return phi, phi + values * (jnp.exp(-0.5 * (values * values)) * inverse_root_tau)


def one_head(pair, head):
    lane = lax.broadcasted_iota(jnp.int32, pair.shape, 1)
    keep = lane < HEAD if head % 2 == 0 else lane >= HEAD
    return jnp.where(keep, pair, jnp.zeros_like(pair))


def pair_columns(head):
    return slice(LANES * (head // 2), LANES * (head // 2) + LANES)


def head_rows(head):
    return slice(HEAD * head, HEAD * head + HEAD)


def block_of(ref, j, count):
    if count == 1:
        return ref[...]
    return jnp.concatenate(
        [ref[first + 16 * j : first + 16 * j + 16, :] for first in range(0, ref.shape[0], 16 * count)], axis=0
    )


def spread(wide, values):
    for n in range(wide.shape[0]):
        wide[n] = values[:, LANES * n : LANES * n + LANES].astype(F32)


def third_rows(wide, j):
    rows = pl.ds(j, wide.shape[1] // 3, stride=3)
    return jnp.concatenate([wide[n, rows, :] for n in range(wide.shape[0])], axis=1).astype(LOW)


def put_third_rows(wide, j, values):
    rows = pl.ds(j, wide.shape[1] // 3, stride=3)
    for n in range(wide.shape[0]):
        wide[n, rows, :] = values[:, LANES * n : LANES * n + LANES]


def wide_scratch(width):
    return pltpu.VMEM((width // LANES, 3 * width, LANES), F32)


def put_block(ref, j, values):
    ref[:, j] = values.reshape(ref.shape[0], ref.shape[2], ref.shape[3])


OWNERS = 32


def row_copies(first, last, own, paired):
    found = []
    at = first
    while at < last:
        owner = at // own
        end = min(last, (owner + 1) * own)
        half = OWNERS // 4
        place = (2 * (owner // 2 // half) + owner % 2, owner // 2 % half) if paired else (0, owner)
        found.append((*place, at - owner * own, end - at, at - first))
        at = end
    return found


class Fetch:
    def __init__(self, far, core, copies, near, semaphores, used):
        self.core = core

        def handles(side):
            return [
                pltpu.make_async_copy(
                    far[source ^ side].at[owner, pl.ds(row, rows)], near.at[pl.ds(to, rows)], semaphores.at[used + n]
                )
                for n, (source, owner, row, rows, to) in enumerate(copies)
            ]

        self.handles = handles

    def start(self):
        if self.core is None:
            for handle in self.handles(0):
                handle.start()
            return
        for side in (0, 1):

            @pl.when(self.core == side)
            def _(side=side):
                for handle in self.handles(side):
                    handle.start()

    def wait(self):
        for handle in self.handles(0):
            handle.wait()


def fetches(far, plan, wanted, nears, semaphores):
    used = 0
    made = []
    core = plan[2, 1] if len(far) > 1 else None
    for copies, near in zip(wanted, nears):
        made.append(Fetch(far, core, copies, near, semaphores, used))
        used += len(copies)
    return made


def wait_first(i, loads):
    @pl.when(i == 0)
    def _():
        for load in loads:
            load.wait()


def fetch_scratch(wanted, width):
    return [pltpu.VMEM((sum(c[3] for c in copies), width), LOW) for copies in wanted] + [
        pltpu.SemaphoreType.DMA((sum(len(copies) for copies in wanted),))
    ]


FAR = pl.BlockSpec(memory_space=pl.ANY)


def sources_of(wanted):
    last = max(copy[0] for copies in wanted for copy in copies)
    return 1 if last == 0 else 2 * (last // 2) + 2


def call(kernel, grid, in_specs, out_specs, out_shape, scratch, flops, moved, name, room=24, near=(), keep=()):
    single = not isinstance(out_shape, list)
    shapes = [
        (pltpu.VMEM if keep is True or n in keep else pltpu.HBM)(*made)
        for n, made in enumerate([out_shape] if single else out_shape)
    ]
    made = pl.pallas_call(
        kernel,
        grid_spec=pltpu.PrefetchScalarGridSpec(
            num_scalar_prefetch=1,
            grid=grid,
            in_specs=in_specs,
            out_specs=out_specs,
            scratch_shapes=scratch,
        ),
        out_shape=shapes[0] if single else shapes,
        compiler_params=pltpu.CompilerParams(vmem_limit_bytes=room * MIB),
        cost_estimate=pl.CostEstimate(
            flops=flops, bytes_accessed=moved, transcendentals=0
        ),
        name=name,
    )

    def run(plan, *operands):
        placed = [
            operand
            if near is True or n in near
            else pltpu.with_memory_space_constraint(operand, pltpu.HBM)
            for n, operand in enumerate(operands)
        ]
        return made(plan, *placed)

    return run


def whole(shape):
    zeros = (0,) * len(shape)
    return pl.BlockSpec(shape, lambda i, *_: zeros)


def rows_of(width):
    return pl.BlockSpec((TILE, width), lambda i, *_: (i, 0))


def at_block(shape, *index):
    return pl.BlockSpec(shape, lambda i, *_: index)


def shaped(shape, kind):
    return (shape, kind)


def attend_tile(plan, i, keys, key_cols, query, owner_row, key_owner, vt, sc):
    scores, acc, top, total, masked_q = sc
    query = query * jnp.asarray(HEAD**-0.5, LOW)
    for h in range(HEADS):
        masked_q[h] = one_head(query[:, pair_columns(h)], h)
    top[...] = jnp.full_like(top, -1e30)
    total[...] = jnp.zeros_like(total)
    acc[...] = jnp.zeros_like(acc)
    begin = plan[0, i]
    chunks = plan[1, i]

    def score_tile(j, carry):
        rows = pl.ds(pl.multiple_of(begin + j * TILE, LANES), TILE)
        bias = jnp.where(key_owner[rows, 0:1] == owner_row, 0.0, floor_value)
        tops = []
        for h in range(HEADS):
            cols = pl.ds(key_cols + LANES * (h // 2), LANES)
            s = nt(keys[rows, cols], masked_q[h]) + bias
            scores[j, h] = s
            tops.append(jnp.max(s, axis=0, keepdims=True))
        top[...] = jnp.maximum(top[...], jnp.concatenate(tops, axis=0))
        return carry

    lax.fori_loop(0, chunks, score_tile, 0)

    def weigh_tile(j, carry):
        rows = pl.ds(pl.multiple_of(begin + j * TILE, LANES), TILE)
        sums = []
        for h in range(HEADS):
            p = jnp.exp(scores[j, h] - top[h : h + 1, :])
            sums.append(jnp.sum(p, axis=0, keepdims=True))
            acc[head_rows(h), :] += nn(vt[head_rows(h), rows], p.astype(LOW))
        total[...] += jnp.concatenate(sums, axis=0)
        return carry

    lax.fori_loop(0, chunks, weigh_tile, 0)


def fwd_block_kernel(plan, *refs, cross, gain_row, wanted, packed, ffn):
    refs = list(refs)

    def next_refs(count):
        taken = refs[:count]
        del refs[:count]
        return taken

    if cross:
        normed_in, memory = next_refs(2)
    else:
        (x_all,) = next_refs(1)
    far = next_refs(sources_of(wanted))
    small, owner_q, owner_k = next_refs(3)
    q_out, kv_out, ctx_out, lse_out, normed_out, inverse_out = next_refs(6)
    if ffn:
        out, normed_last, inverse_last = next_refs(3)
    kv, vt, mean_v, key_owner, scores, acc, top, total, masked_q, q_all = next_refs(10)
    nears = next_refs(len(wanted))
    semaphores = refs.pop(0)
    loads = fetches(far, plan, wanted, nears, semaphores)
    i = pl.program_id(0)
    width = kv.shape[1] // 2

    @pl.when(i == 0)
    def _():
        for load in loads:
            load.start()
        key_owner[...] = jnp.broadcast_to(owner_k[...], (8, owner_k.shape[1])).T
        loads[0].wait()
        if cross:
            wk, wv = block_of(nears[0], 0, 2), block_of(nears[0], 1, 2)
        elif packed:
            wq, wk, wv = (block_of(nears[0], j, 3) for j in range(3))
        else:
            wide = refs[0]
            spread(wide, nears[0][...])
            wq, wk, wv = (third_rows(wide, j) for j in range(3))
        sums = jnp.zeros((1, width), F32)
        for t in range(kv.shape[0] // TILE):
            rows = slice(t * TILE, t * TILE + TILE)
            x = memory[rows, :] if cross else x_all[rows, :]
            if not cross:
                q_all[rows, :] = nn(x, wq).astype(LOW)
            kv[rows, :width] = nn(x, wk).astype(LOW)
            v = nn(x, wv).astype(LOW)
            kv[rows, width:] = v
            v = v.astype(F32)
            vt[:, rows] = v.T.astype(LOW)
            sums = sums + jnp.sum(v, axis=0, keepdims=True)
        mean_v[...] = sums * (1.0 / kv.shape[0])
        for load in loads[1 : 3 if cross else 2]:
            load.wait()

    wo = nears[1]
    mine = pl.ds(pl.multiple_of(i * TILE, TILE), TILE)
    if cross:
        resid = normed_in[...] * small[4:5, :] + small[5:6, :]
        query = nn(resid.astype(LOW), nears[2][...]).astype(LOW)
        q_out[...] = query
    else:
        resid = x_all[mine, :].astype(F32)
        query = q_all[mine, :]
        q_out[...] = query
    kv_out[...] = kv[mine, :]
    owner_row = owner_q[...]
    attend_tile(plan, i, kv, 0, query, owner_row, key_owner, vt, (scores, acc, top, total, masked_q))
    dead = owner_row < 0
    sums = jnp.where(dead, 1.0, total[...])
    share = 1.0 / sums
    lse_out[...] = jnp.where(dead, 0.0, top[...] + jnp.log(sums))
    for h in range(HEADS):
        acc[head_rows(h), :] = acc[head_rows(h), :] * share[h : h + 1, :]
    live = column_of(owner_row) >= 0
    context = jnp.where(live, acc[...].T, mean_v[...]).astype(LOW)
    ctx_out[...] = context
    added = nn(context, wo[...]) * live.astype(F32)
    mid, normed, inverse = ln_forward(
        resid + added, small[gain_row : gain_row + 1, :], small[gain_row + 1 : gain_row + 2, :]
    )
    normed_out[...] = normed
    inverse_out[...] = jnp.broadcast_to(inverse, inverse_out.shape)
    if ffn:
        wup, wdown = nears[-2:]
        wait_first(i, loads[-2:])
        blocks = wdown.shape[0] // width
        low = mid.astype(LOW)
        result = mid
        for j in range(blocks):
            inner = nn(low, block_of(wup, j, blocks))
            phi = 0.5 + 0.5 * lax.erf(inner * root_half)
            result = result + nn((inner * phi).astype(LOW), wdown[j * width : j * width + width, :])
        result, normed, inverse = ln_forward(
            result, small[gain_row + 2 : gain_row + 3, :], small[gain_row + 3 : gain_row + 4, :]
        )
        out[...] = result.astype(LOW)
        normed_last[...] = normed
        inverse_last[...] = jnp.broadcast_to(inverse, inverse_last.shape)


def attention_scratch(keys, width):
    return [
        pltpu.VMEM((keys, 2 * width), LOW),
        pltpu.VMEM((width, keys), LOW),
        pltpu.VMEM((1, width), F32),
        pltpu.VMEM((keys, 8), F32),
        pltpu.VMEM((keys // TILE, HEADS, TILE, TILE), F32),
        pltpu.VMEM((width, TILE), F32),
        pltpu.VMEM((HEADS, TILE), F32),
        pltpu.VMEM((HEADS, TILE), F32),
        pltpu.VMEM((HEADS, TILE, LANES), LOW),
        pltpu.VMEM((keys, width), LOW),
    ]


def block_outs(queries, width):
    specs = [
        rows_of(width),
        rows_of(2 * width),
        rows_of(width),
        pl.BlockSpec((HEADS, TILE), lambda i, *_: (0, i)),
        rows_of(width),
        rows_of(LANES),
    ]
    shapes = [
        shaped((queries, width), LOW),
        shaped((queries, 2 * width), LOW),
        shaped((queries, width), LOW),
        shaped((HEADS, queries), F32),
        shaped((queries, width), F32),
        shaped((queries, LANES), F32),
    ]
    return specs, shapes


def owner_specs(keys):
    return [pl.BlockSpec((1, TILE), lambda i, *_: (0, i)), whole((1, keys))]


def fwd_block(plan, x, memory, far, wanted, packed, small, gain_row, owner, key_owner, ffn, name):
    cross = memory is not None
    number, width = x.shape
    specs, shapes = block_outs(number, width)
    if ffn:
        specs += [rows_of(width), rows_of(width), rows_of(LANES)]
        shapes += [shaped((number, width), LOW), shaped((number, width), F32), shaped((number, LANES), F32)]
    scratch = attention_scratch(number, width) + fetch_scratch(wanted, width)
    if not cross and not packed:
        scratch.append(wide_scratch(width))
    return call(
        functools.partial(
            fwd_block_kernel, cross=cross, gain_row=gain_row, wanted=wanted, packed=packed, ffn=ffn
        ),
        (number // TILE,),
        ([rows_of(width), whole(memory.shape)] if cross else [whole(x.shape)])
        + [FAR] * sources_of(wanted)
        + [whole(small.shape)]
        + owner_specs(number),
        specs,
        shapes,
        scratch,
        8 * number * width * width + number * number * width * 2,
        16 * number * width,
        name,
        room=44,
    )(plan, *([x, memory] if cross else [x]), *far[: sources_of(wanted)], small, owner, key_owner)


def ffn_back_kernel(plan, *refs, tiles, summed, gain_row, wanted):
    refs = list(refs)
    cot = refs.pop(0)
    extra = refs.pop(0) if summed else None
    normed_top, inverse_top, normed_mid, inverse_mid, context = refs[:5]
    far = refs[5 : 5 + sources_of(wanted)]
    (small,
     d_sum, d_context, g_up, g_down, g_out, sums, hidden, d_inner, mid_low, d_down, d_product,
     wup, wdown, wo, semaphores) = refs[5 + sources_of(wanted) :]
    loads = fetches(far, plan, wanted, (wup, wdown, wo), semaphores)
    i = pl.program_id(0)
    width = small.shape[1]
    blocks = wdown.shape[0] // width

    @pl.when(i == 0)
    def _():
        for load in loads:
            load.start()
        sums[...] = jnp.zeros_like(sums)

    @pl.when(i < tiles)
    def _():
        mine = pl.ds(pl.multiple_of(i * TILE, TILE), TILE)
        upstream = cot[...].astype(F32)
        if summed:
            upstream = upstream + extra[...]
        top = normed_top[...]
        sums[2:3, :] += jnp.sum(upstream * top, axis=0, keepdims=True)
        sums[3:4, :] += jnp.sum(upstream, axis=0, keepdims=True)
        d_mid = ln_backward(upstream, top, inverse_top[:, 0:1], small[gain_row + 2 : gain_row + 3, :])
        low = d_mid.astype(LOW)
        d_down[mine, :] = low
        normed = normed_mid[...]
        mid = (normed * small[gain_row : gain_row + 1, :] + small[gain_row + 1 : gain_row + 2, :]).astype(LOW)
        mid_low[mine, :] = mid
        wait_first(i, loads)
        for j in range(blocks):
            cols = slice(j * width, j * width + width)
            up = block_of(wup, j, blocks)
            inner = nn(mid, up)
            phi, slope = phi_and_slope(inner)
            hidden[j, mine, :] = (inner * phi).astype(LOW)
            part = (nt(low, wdown[cols, :]) * slope).astype(LOW)
            d_inner[j, mine, :] = part
            d_mid = d_mid + nt(part, up)
        sums[0:1, :] += jnp.sum(d_mid * normed, axis=0, keepdims=True)
        sums[1:2, :] += jnp.sum(d_mid, axis=0, keepdims=True)
        total = ln_backward(d_mid, normed, inverse_mid[:, 0:1], small[gain_row : gain_row + 1, :])
        d_sum[...] = total
        place = lax.broadcasted_iota(jnp.int32, (TILE, 1), 0) + i * TILE
        live = (place < plan[2, 0]).astype(F32)
        product = (total * live).astype(LOW)
        d_product[mine, :] = product
        d_context[...] = nt(product, wo[...]).astype(LOW)

    @pl.when(i >= tiles)
    def _():
        j = i - tiles
        put_block(g_up, 0, nn(turned(mid_low[...]), d_inner[j]).astype(LOW))
        g_down[...] = nn(turned(hidden[j]), d_down[...]).astype(LOW)

    @pl.when(i == tiles)
    def _():
        g_out[...] = nn(turned(context[...]), d_product[...]).astype(LOW)


def ffn_backward(plan, cots, top, mid, context, far, wanted, small, gain_row, inner, name):
    number, width = mid[0].shape
    tiles, blocks = number // TILE, inner // width

    def tile_of(columns):
        return pl.BlockSpec((TILE, columns), lambda i, *_: (jnp.minimum(i, tiles - 1), 0))

    return call(
        functools.partial(
            ffn_back_kernel, tiles=tiles, summed=len(cots) == 2, gain_row=gain_row, wanted=wanted
        ),
        (tiles + blocks,),
        [tile_of(width)] * len(cots)
        + [tile_of(width), tile_of(LANES), tile_of(width), tile_of(LANES), whole((number, width))]
        + [FAR] * sources_of(wanted)
        + [whole(small.shape)],
        [
            tile_of(width),
            tile_of(width),
            pl.BlockSpec((width // 16, 1, 16, width), lambda i, *_: (0, jnp.maximum(i - tiles, 0), 0, 0)),
            pl.BlockSpec((width, width), lambda i, *_: (jnp.maximum(i - tiles, 0), 0)),
            pl.BlockSpec((width, width), lambda i, *_: (0, 0)),
            pl.BlockSpec((8, width), lambda i, *_: (0, 0)),
        ],
        [
            shaped((number, width), F32),
            shaped((number, width), LOW),
            shaped((width // 16, blocks, 16, width), LOW),
            shaped((inner, width), LOW),
            shaped((width, width), LOW),
            shaped((8, width), F32),
        ],
        [
            pltpu.VMEM((blocks, number, width), LOW),
            pltpu.VMEM((blocks, number, width), LOW),
            pltpu.VMEM((number, width), LOW),
            pltpu.VMEM((number, width), LOW),
            pltpu.VMEM((number, width), LOW),
        ]
        + fetch_scratch(wanted, width),
        10 * number * width * inner,
        30 * number * width,
        name,
        room=44,
    )(plan, *cots, *top, *mid, context, *far[: sources_of(wanted)], small)


def turn_kernel(plan, *refs, tiles, gain_row, wanted):
    normed_in, memory, cot = refs[:3]
    far = refs[3 : 3 + sources_of(wanted)]
    (small, owner_q, owner_k,
     q_out, kv_out, lse_out, out, d_sum, d_context, g_up, g_down, g_out, sums,
     kv, vt, mean_v, key_owner, scores, acc, top, total, masked_q,
     hidden, d_inner, mid_low, d_down, d_product, contexts, slopes,
     *nears, semaphores) = refs[3 + sources_of(wanted) :]
    wkv, wo, wq, wup, wdown = nears
    loads = fetches(far, plan, wanted, nears, semaphores)
    i = pl.program_id(0)
    width = small.shape[1]
    blocks = wdown.shape[0] // width

    @pl.when(i == 0)
    def _():
        for load in loads:
            load.start()
        sums[...] = jnp.zeros_like(sums)
        key_owner[...] = jnp.broadcast_to(owner_k[...], (8, owner_k.shape[1])).T
        loads[0].wait()
        wk, wv = block_of(wkv, 0, 2), block_of(wkv, 1, 2)
        means = jnp.zeros((1, width), F32)
        for t in range(kv.shape[0] // TILE):
            rows = slice(t * TILE, t * TILE + TILE)
            x = memory[rows, :]
            kv[rows, :width] = nn(x, wk).astype(LOW)
            v = nn(x, wv).astype(LOW)
            kv[rows, width:] = v
            v = v.astype(F32)
            vt[:, rows] = v.T.astype(LOW)
            means = means + jnp.sum(v, axis=0, keepdims=True)
        mean_v[...] = means * (1.0 / kv.shape[0])
        for load in loads[1:3]:
            load.wait()

    @pl.when(i < tiles)
    def _():
        mine = pl.ds(pl.multiple_of(i * TILE, TILE), TILE)
        resid = normed_in[...] * small[gain_row - 2 : gain_row - 1, :] + small[gain_row - 1 : gain_row, :]
        query = nn(resid.astype(LOW), wq[...]).astype(LOW)
        q_out[...] = query
        kv_out[...] = kv[mine, :]
        owner_row = owner_q[...]
        attend_tile(
            plan, i, kv, 0, query, owner_row, key_owner, vt, (scores, acc, top, total, masked_q)
        )
        dead = owner_row < 0
        weighed = jnp.where(dead, 1.0, total[...])
        share = 1.0 / weighed
        lse_out[...] = jnp.where(dead, 0.0, top[...] + jnp.log(weighed))
        for h in range(HEADS):
            acc[head_rows(h), :] = acc[head_rows(h), :] * share[h : h + 1, :]
        live = column_of(owner_row) >= 0
        context = jnp.where(live, acc[...].T, mean_v[...]).astype(LOW)
        contexts[mine, :] = context
        added = nn(context, wo[...]) * live.astype(F32)
        mid, normed_mid, inverse_mid = ln_forward(
            resid + added, small[gain_row : gain_row + 1, :], small[gain_row + 1 : gain_row + 2, :]
        )
        wait_first(i, loads[3:])
        low = mid.astype(LOW)
        mid_low[mine, :] = low
        result = mid
        for j in range(blocks):
            inner = nn(low, block_of(wup, j, blocks))
            phi, slope = phi_and_slope(inner)
            made = (inner * phi).astype(LOW)
            hidden[j, mine, :] = made
            slopes[j] = slope
            result = result + nn(made, wdown[j * width : j * width + width, :])
        result, normed, inverse = ln_forward(
            result, small[gain_row + 2 : gain_row + 3, :], small[gain_row + 3 : gain_row + 4, :]
        )
        out[...] = result.astype(LOW)

        upstream = cot[...].astype(F32)
        sums[2:3, :] += jnp.sum(upstream * normed, axis=0, keepdims=True)
        sums[3:4, :] += jnp.sum(upstream, axis=0, keepdims=True)
        d_mid = ln_backward(upstream, normed, inverse, small[gain_row + 2 : gain_row + 3, :])
        low = d_mid.astype(LOW)
        d_down[mine, :] = low
        for j in range(blocks):
            part = (nt(low, wdown[j * width : j * width + width, :]) * slopes[j]).astype(LOW)
            d_inner[j, mine, :] = part
            d_mid = d_mid + nt(part, block_of(wup, j, blocks))
        sums[0:1, :] += jnp.sum(d_mid * normed_mid, axis=0, keepdims=True)
        sums[1:2, :] += jnp.sum(d_mid, axis=0, keepdims=True)
        d_all = ln_backward(d_mid, normed_mid, inverse_mid, small[gain_row : gain_row + 1, :])
        d_sum[...] = d_all
        product = (d_all * live.astype(F32)).astype(LOW)
        d_product[mine, :] = product
        d_context[...] = nt(product, wo[...]).astype(LOW)

    @pl.when(i >= tiles)
    def _():
        j = i - tiles
        put_block(g_up, 0, nn(turned(mid_low[...]), d_inner[j]).astype(LOW))
        g_down[...] = nn(turned(hidden[j]), d_down[...]).astype(LOW)

    @pl.when(i == tiles)
    def _():
        g_out[...] = nn(turned(contexts[...]), d_product[...]).astype(LOW)


def cross_turn(plan, normed, memory, cot, far, wanted, small, gain_row, owner, key_owner, inner, name):
    number, width = normed.shape
    keys = memory.shape[0]
    tiles, blocks = number // TILE, inner // width

    def tile_of(columns):
        return pl.BlockSpec((TILE, columns), lambda i, *_: (jnp.minimum(i, tiles - 1), 0))

    def columns_of(rows):
        return pl.BlockSpec((rows, TILE), lambda i, *_: (0, jnp.minimum(i, tiles - 1)))

    return call(
        functools.partial(turn_kernel, tiles=tiles, gain_row=gain_row, wanted=wanted),
        (tiles + blocks,),
        [tile_of(width), whole(memory.shape), tile_of(width)]
        + [FAR] * sources_of(wanted)
        + [whole(small.shape), columns_of(1), whole((1, keys))],
        [
            tile_of(width),
            tile_of(2 * width),
            columns_of(HEADS),
            tile_of(width),
            tile_of(width),
            tile_of(width),
            pl.BlockSpec((width // 16, 1, 16, width), lambda i, *_: (0, jnp.maximum(i - tiles, 0), 0, 0)),
            pl.BlockSpec((width, width), lambda i, *_: (jnp.maximum(i - tiles, 0), 0)),
            whole((width, width)),
            whole((8, width)),
        ],
        [
            shaped((number, width), LOW),
            shaped((number, 2 * width), LOW),
            shaped((HEADS, number), F32),
            shaped((number, width), LOW),
            shaped((number, width), F32),
            shaped((number, width), LOW),
            shaped((width // 16, blocks, 16, width), LOW),
            shaped((inner, width), LOW),
            shaped((width, width), LOW),
            shaped((8, width), F32),
        ],
        attention_scratch(keys, width)[:-1]
        + [
            pltpu.VMEM((blocks, number, width), LOW),
            pltpu.VMEM((blocks, number, width), LOW),
            pltpu.VMEM((number, width), LOW),
            pltpu.VMEM((number, width), LOW),
            pltpu.VMEM((number, width), LOW),
            pltpu.VMEM((number, width), LOW),
            pltpu.VMEM((blocks, TILE, width), F32),
        ]
        + fetch_scratch(wanted, width),
        12 * number * width * inner + number * number * width * 2,
        30 * number * width,
        name,
        room=58,
    )(plan, normed, memory, cot, *far[: sources_of(wanted)], small, owner, key_owner)


def attend_back(plan, i, q_ref, k_ref, v_ref, do_ref, lse, owner_q, owner_k, scratch):
    kt, key_owner, masked_q, masked_do, dqt, dk_sum, dv_sum, weights, d_weights, dots = scratch

    @pl.when(i == 0)
    def _():
        key_owner[...] = jnp.broadcast_to(owner_k[...], (8, owner_k.shape[1])).T
        kt[...] = turned(k_ref[...])
        dk_sum[...] = jnp.zeros_like(dk_sum)
        dv_sum[...] = jnp.zeros_like(dv_sum)

    query = q_ref[...] * jnp.asarray(HEAD**-0.5, LOW)
    upstream = do_ref[...]
    for h in range(HEADS):
        masked_q[h] = one_head(query[:, pair_columns(h)], h)
        masked_do[h] = one_head(upstream[:, pair_columns(h)], h)
    dqt[...] = jnp.zeros_like(dqt)
    dots[...] = jnp.zeros_like(dots)
    owner_row = owner_q[...]
    begin = plan[0, i]
    chunks = plan[1, i]

    def weigh_tile(j, carry):
        rows = pl.ds(pl.multiple_of(begin + j * TILE, LANES), TILE)
        bias = jnp.where(key_owner[rows, 0:1] == owner_row, 0.0, floor_value)
        sums = []
        for h in range(HEADS):
            s = nt(k_ref[rows, pair_columns(h)], masked_q[h])
            p = jnp.exp((s - lse[h : h + 1, :]) + bias)
            dp = nt(v_ref[rows, pair_columns(h)], masked_do[h])
            weights[j, h] = p
            d_weights[j, h] = dp
            sums.append(jnp.sum(p * dp, axis=0, keepdims=True))
        dots[...] += jnp.concatenate(sums, axis=0)
        return carry

    lax.fori_loop(0, chunks, weigh_tile, 0)

    def grad_tile(j, carry):
        rows = pl.ds(pl.multiple_of(begin + j * TILE, LANES), TILE)
        for pair in range(HEADS // 2):
            cols = pair_columns(2 * pair)
            dv_part = dv_sum[rows, cols]
            dk_part = dk_sum[rows, cols]
            for h in (2 * pair, 2 * pair + 1):
                p = weights[j, h]
                ds = (p * (d_weights[j, h] - dots[h : h + 1, :])).astype(LOW)
                dv_part = dv_part + nn(p.astype(LOW), masked_do[h])
                dk_part = dk_part + nn(ds, masked_q[h])
                dqt[head_rows(h), :] += nn(kt[head_rows(h), rows], ds)
            dv_sum[rows, cols] = dv_part
            dk_sum[rows, cols] = dk_part
        return carry

    lax.fori_loop(0, chunks, grad_tile, 0)
    return (dqt[...] * HEAD**-0.5).T.astype(LOW)


def attention_back_kernel(plan, *refs, made):
    q_ref, k_ref, v_ref, do_ref, lse, owner_q, owner_k, *refs = refs
    x = refs.pop(0) if made else None
    dq, dk, dv, *refs = refs
    g_qkv = refs.pop(0) if made else None
    scratch, more = refs[:10], refs[10:]
    dk_sum, dv_sum = scratch[5:7]
    i = pl.program_id(0)
    dq_tile = attend_back(plan, i, q_ref, k_ref, v_ref, do_ref, lse, owner_q, owner_k, scratch)
    dq[...] = dq_tile
    if made:
        dq_all = more[0]
        dq_all[pl.ds(pl.multiple_of(i * TILE, TILE), TILE), :] = dq_tile

    @pl.when(i == pl.num_programs(0) - 1)
    def _():
        dk[...] = dk_sum[...].astype(LOW)
        dv[...] = dv_sum[...].astype(LOW)
        if made:
            turn = turned(x[...])
            for j, ref in enumerate((dq_all, dk, dv)):
                grad = nn(turn, ref[...])
                if made == "units":
                    put_block(g_qkv, j, grad.astype(LOW))
                else:
                    put_third_rows(more[1], j, grad)
        if made == "rows":
            for n in range(more[1].shape[0]):
                g_qkv[:, LANES * n : LANES * n + LANES] = more[1][n].astype(LOW)


def attend_back_scratch(keys, width):
    return [
        pltpu.VMEM((width, keys), LOW),
        pltpu.VMEM((keys, 8), F32),
        pltpu.VMEM((HEADS, TILE, LANES), LOW),
        pltpu.VMEM((HEADS, TILE, LANES), LOW),
        pltpu.VMEM((width, TILE), F32),
        pltpu.VMEM((keys, width), F32),
        pltpu.VMEM((keys, width), F32),
        pltpu.VMEM((keys // TILE, HEADS, TILE, TILE), F32),
        pltpu.VMEM((keys // TILE, HEADS, TILE, TILE), F32),
        pltpu.VMEM((HEADS, TILE), F32),
    ]


def attention_backward(plan, q, kv, d_context, lse, owner, key_owner, x, made, name):
    number, width = q.shape
    keys = kv.shape[0]
    in_specs = [
        rows_of(width),
        at_block((keys, width), 0, 0),
        at_block((keys, width), 0, 1),
        rows_of(width),
        pl.BlockSpec((HEADS, TILE), lambda i, *_: (0, i)),
    ] + owner_specs(keys)
    out_specs = [rows_of(width), whole((keys, width)), whole((keys, width))]
    out_shape = [shaped((number, width), LOW), shaped((keys, width), LOW), shaped((keys, width), LOW)]
    operands = [q, kv, kv, d_context, lse, owner, key_owner]
    scratch = attend_back_scratch(keys, width)
    if made:
        shape = (width // 16, 3, 16, width) if made == "units" else (3 * width, width)
        in_specs.append(whole(x.shape))
        operands.append(x)
        out_specs.append(whole(shape))
        out_shape.append(shaped(shape, LOW))
        scratch.append(pltpu.VMEM((number, width), LOW))
        if made == "rows":
            scratch.append(wide_scratch(width))
    return call(
        functools.partial(attention_back_kernel, made=made),
        (number // TILE,),
        in_specs,
        out_specs,
        out_shape,
        scratch,
        number * keys * width * 4 + (6 * number * width * width if made else 0),
        12 * number * width,
        name,
        room=52,
    )(plan, *operands)


def cross_back_kernel(plan, *refs, wanted, tiles):
    attention, refs = refs[:7], refs[7:]
    normed, inverse, d_above, memory, context = refs[:5]
    far = refs[5 : 5 + sources_of(wanted)]
    small, d_memory, d_sum, d_context, g_query, g_pair, g_out, sums, *refs = refs[5 + sources_of(wanted) :]
    scratch, refs = refs[:10], refs[10:]
    d_query, dk, dv, d_product, wkv, wq, wo, semaphores = refs
    dk_sum, dv_sum = scratch[5:7]
    loads = fetches(far, plan, wanted, (wkv, wq, wo), semaphores)
    i = pl.program_id(0)

    @pl.when(i == 0)
    def _():
        for load in loads:
            load.start()
        sums[...] = jnp.zeros_like(sums)

    @pl.when(i < tiles)
    def _():
        d_query[pl.ds(pl.multiple_of(i * TILE, TILE), TILE), :] = attend_back(plan, i, *attention, scratch)

    @pl.when(i == tiles)
    def _():
        dk[...] = dk_sum[...].astype(LOW)
        dv[...] = dv_sum[...].astype(LOW)
        for load in loads:
            load.wait()
        low = normed[...] * small[4:5, :] + small[5:6, :]
        g_query[...] = nn(low.T.astype(LOW), d_query[...]).astype(LOW)

    @pl.when(i >= tiles)
    def _():
        row = pl.multiple_of((i - tiles) * TILE, TILE)
        mine = pl.ds(row, TILE)
        wk, wv = block_of(wkv, 0, 2), block_of(wkv, 1, 2)
        d_memory[...] = nt(dk[mine, :], wk) + nt(dv[mine, :], wv)
        d_one = d_above[...] + nt(d_query[mine, :], wq[...])
        hat = normed[mine, :]
        sums[0:1, :] += jnp.sum(d_one * hat, axis=0, keepdims=True)
        sums[1:2, :] += jnp.sum(d_one, axis=0, keepdims=True)
        total = ln_backward(d_one, hat, inverse[:, 0:1], small[4:5, :])
        d_sum[...] = total
        place = lax.broadcasted_iota(jnp.int32, (TILE, 1), 0) + row
        live = (place < plan[2, 0]).astype(F32)
        product = (total * live).astype(LOW)
        d_product[mine, :] = product
        d_context[...] = nt(product, wo[...]).astype(LOW)

    @pl.when(i == tiles + 1)
    def _():
        put_block(g_pair, 0, nn(turned(memory[...]), dk[...]).astype(LOW))

    @pl.when(i == tiles + 2)
    def _():
        put_block(g_pair, 1, nn(turned(memory[...]), dv[...]).astype(LOW))

    @pl.when(i == 2 * tiles - 1)
    def _():
        g_out[...] = nn(turned(context[...]), d_product[...]).astype(LOW)


def cross_backward(plan, q, kv, d_context, lse, owner, key_owner, normed, inverse, d_above, memory, context, far,
                   wanted, small):
    number, width = normed.shape
    keys = kv.shape[0]
    tiles = number // TILE
    full = whole((number, width))

    def first_rows(columns):
        return pl.BlockSpec((TILE, columns), lambda i, *_: (jnp.minimum(i, tiles - 1), 0))

    def first_columns(rows):
        return pl.BlockSpec((rows, TILE), lambda i, *_: (0, jnp.minimum(i, tiles - 1)))

    def later_rows(columns):
        return pl.BlockSpec((TILE, columns), lambda i, *_: (jnp.maximum(i - tiles, 0), 0))

    return call(
        functools.partial(cross_back_kernel, wanted=wanted, tiles=tiles),
        (2 * tiles,),
        [first_rows(width), at_block((keys, width), 0, 0), at_block((keys, width), 0, 1), first_rows(width),
         first_columns(HEADS), first_columns(1), whole((1, keys)),
         full, later_rows(LANES), later_rows(width), whole(memory.shape), full]
        + [FAR] * sources_of(wanted)
        + [whole(small.shape)],
        [later_rows(width), later_rows(width), later_rows(width), whole((width, width)),
         whole((width // 16, 2, 16, width)), whole((width, width)), whole((8, width))],
        [shaped((number, width), F32), shaped((number, width), F32), shaped((number, width), LOW),
         shaped((width, width), LOW), shaped((width // 16, 2, 16, width), LOW), shaped((width, width), LOW),
         shaped((8, width), F32)],
        attend_back_scratch(keys, width)
        + [pltpu.VMEM((number, width), LOW), pltpu.VMEM((keys, width), LOW), pltpu.VMEM((keys, width), LOW),
           pltpu.VMEM((number, width), LOW)]
        + fetch_scratch(wanted, width),
        16 * number * width * width + number * keys * width * 4,
        24 * number * width,
        "cross_back",
        room=58,
    )(plan, q, kv, kv, d_context, lse, owner, key_owner, normed, inverse, d_above, memory, context,
      *far[: sources_of(wanted)], small)


def qkv_inputs_kernel(plan, *refs, masked, wanted):
    if masked:
        dq, dk, dv, d_above, flags, *refs = refs
        far = refs[: sources_of(wanted)]
        d_x, mask_sum, near, semaphores, blocks, wide = refs[sources_of(wanted) :]
    else:
        dq, dk, dv, d_above, *refs = refs
        far = refs[: sources_of(wanted)]
        d_x, near, semaphores, blocks = refs[sources_of(wanted) :]
    width = dq.shape[1]

    @pl.when(pl.program_id(0) == 0)
    def _():
        (load,) = fetches(far, plan, wanted, (near,), semaphores)
        load.start()
        load.wait()
        if masked:
            mask_sum[...] = jnp.zeros_like(mask_sum)
            spread(wide, near[...])
        for j in range(3):
            if masked:
                blocks[:, j * width : j * width + width] = third_rows(wide, j)
            else:
                blocks[:, j * width : j * width + width] = block_of(near, j, 3)

    pieces = jnp.concatenate([dq[...], dk[...], dv[...]], axis=1)
    total = nt(pieces, blocks[...])
    if masked:
        total = total + d_above[...]
        hit = column_of(flags[...]) == 1.0
        d_x[...] = jnp.where(hit, 0.0, total)
        mask_sum[0:1, :] += jnp.sum(jnp.where(hit, total, 0.0), axis=0, keepdims=True)
    else:
        d_x[...] = d_above[...]
        d_x[...] += total


def qkv_inputs(plan, dq, dk, dv, d_above, far, wanted, flags, name):
    number, width = dq.shape
    masked = flags is not None
    in_specs = [rows_of(width)] * 4
    out_specs = [rows_of(width)]
    out_shape = [shaped((number, width), F32)]
    operands = [dq, dk, dv, d_above]
    scratch = fetch_scratch(wanted, width) + [pltpu.VMEM((width, 3 * width), LOW)]
    if masked:
        in_specs.append(pl.BlockSpec((1, TILE), lambda i, *_: (0, i)))
        out_specs.append(whole((8, width)))
        out_shape.append(shaped((8, width), F32))
        operands.append(flags)
        scratch.append(wide_scratch(width))
    in_specs += [FAR] * sources_of(wanted)
    operands += far[: sources_of(wanted)]
    return call(
        functools.partial(qkv_inputs_kernel, masked=masked, wanted=wanted),
        (number // TILE,),
        in_specs,
        out_specs,
        out_shape,
        scratch,
        6 * number * width * width,
        16 * number * width,
        name,
    )(plan, *operands)


def enc_regions(width, inner):
    return ((0, 3 * width, 3), (4 * width, 4 * width + inner, inner // width))


def dec_regions(width, inner):
    return ((5 * width, 7 * width, 2), (8 * width, 8 * width + inner, inner // width))


def to_units(rows, k):
    return rows.reshape(-1, 16, k, rows.shape[1]).transpose(0, 2, 1, 3).reshape(rows.shape)


def from_units(rows, k):
    return rows.reshape(-1, k, 16, rows.shape[1]).transpose(0, 2, 1, 3).reshape(rows.shape)


def fits(size, region):
    return size % (16 * region[2]) == 0


def arrange_own(rows, first, regions, arrange):
    place = first + lax.broadcasted_iota(jnp.int32, (rows.shape[0], 1), 0)
    result = rows
    for region in regions:
        if fits(rows.shape[0], region):
            inside = (place >= region[0]) & (place < region[1])
            result = jnp.where(inside, arrange(rows, region[2]), result)
    return result


def arrange_all(rows, size, regions, arrange):
    for region in regions:
        if not fits(size, region):
            part = arrange(rows[region[0] : region[1]], region[2])
            rows = jnp.concatenate([rows[: region[0]], part, rows[region[1] :]], axis=0)
    return rows


def owners_of(lengths, number):
    bounds = jnp.cumsum(lengths)
    places = jnp.arange(number, dtype=jnp.int32)
    owners = jnp.sum((places[:, None] >= bounds[None, :]).astype(jnp.int32), axis=1)
    filled = places < bounds[-1]
    for_queries = jnp.where(filled, owners, -2).astype(F32)[None, :]
    for_keys = jnp.where(filled, owners, -1).astype(F32)[None, :]
    return for_queries, for_keys, bounds


def plan_of(query_bounds, key_bounds, key_lengths, number, core):
    firsts = jnp.arange(8, dtype=jnp.int32) * TILE
    filled = query_bounds[-1]
    lasts = jnp.minimum(firsts + TILE, filled) - 1

    def pair_of(places):
        found = jnp.sum((places[:, None] >= query_bounds[None, :]).astype(jnp.int32), axis=1)
        return jnp.minimum(found, key_lengths.shape[0] - 1)

    def pick(values, pairs):
        chosen = pairs[:, None] == jnp.arange(values.shape[0])[None, :]
        return jnp.sum(jnp.where(chosen, values[None, :], 0), axis=1)

    begin = pick(key_bounds - key_lengths, pair_of(firsts))
    end = pick(key_bounds, pair_of(lasts))
    some = firsts < filled
    begin = begin // LANES * LANES
    chunks = (end - begin + TILE - 1) // TILE
    begin = jnp.where(some, jnp.minimum(begin, number - chunks * TILE), 0)
    chunks = jnp.where(some, chunks, 0)
    rest = jnp.where(jnp.arange(8) == 1, core, filled)
    return jnp.stack([begin, chunks, rest]).astype(jnp.int32)


def moments(gradient, first, second):
    first_new = beta_one * first + (1.0 - beta_one) * gradient
    second_new = beta_two * second + (1.0 - beta_two) * gradient * gradient
    return (first_new, second_new)


def adamw(weight, gradient, first, second):
    first_new, second_new = moments(gradient, first, second)
    moved = weight - rate * (
        first_new
        / (1.0 - beta_one**STEPS)
        / (jnp.sqrt(second_new / (1.0 - beta_two**STEPS)) + epsilon)
        + decay * weight
    )
    return (moved, first_new, second_new)


CORE, X, Y, Z_LOW, Z_HIGH = 0, 1, 2, 3, 4
BITS = 5


def partner(bit):
    return [(i, i ^ (1 << bit)) for i in range(1 << BITS)]


def bit_of(me, bit):
    return (me >> bit) & 1


def take(values, axis, index):
    return lax.dynamic_index_in_dim(values, index, axis, keepdims=False)


def overlaps(sizes, own):
    found = []
    first = 0
    for piece, size in enumerate(sizes):
        at = first
        while at < first + size:
            owner = at // own
            end = min(first + size, (owner + 1) * own)
            found.append((piece, at - first, owner, at - owner * own, end - at))
            at = end
        first += size
    return found


def pack_kernel(core, *refs, copies, number):
    pieces, send, keep, semaphores = refs[:number], refs[number], refs[number + 1], refs[number + 2]
    for side in (0, 1):

        @pl.when(core[0] == side)
        def _():
            handles = []
            for n, (piece, at, owner, to, rows) in enumerate(copies):
                target = keep if owner % 2 == side else send
                handles.append(
                    pltpu.make_async_copy(
                        pieces[piece].at[pl.ds(at, rows)],
                        target.at[owner // 2, pl.ds(to, rows)],
                        semaphores.at[n],
                    )
                )
            for handle in handles:
                handle.start()
            for handle in handles:
                handle.wait()


def pack(core, pieces, copies, block, name):
    width = pieces[0].shape[1]
    shape = shaped((1 << (BITS - 1), block, width), LOW)
    anywhere = pl.BlockSpec(memory_space=pl.ANY)
    total = sum(piece.size for piece in pieces)
    return call(
        functools.partial(pack_kernel, copies=copies, number=len(pieces)),
        (1,),
        [pl.BlockSpec(memory_space=pltpu.VMEM)] * len(pieces),
        [anywhere, anywhere],
        [shape, shape],
        [pltpu.SemaphoreType.DMA((len(copies),))],
        0,
        4 * total,
        name,
        near=True,
    )(core, *pieces)


def add_low(former, latter):
    return (former.astype(F32) + latter.astype(F32)).astype(LOW)


def swap(values, bit):
    return lax.ppermute(values, "fsdp", partner(bit))


def reduce_owned(me, send, keep, cut):
    rows, width = send.shape[1:]
    x, y, low, high = (bit_of(me, b) for b in (X, Y, Z_LOW, Z_HIGH))
    (send,) = yield (send,)
    chips = add_low(keep, swap(send, CORE)).reshape(2, 2, 2, 2, rows, width)
    first, second = chips[..., :cut, :], chips[..., cut:, :]
    for_y, for_x = yield (take(first, 2, 1 - y), take(second, 3, 1 - x))
    first = add_low(take(first, 2, y), swap(for_y, Y))
    second = add_low(take(second, 3, x), swap(for_x, X))
    for_x, for_y = yield (take(first, 2, 1 - x), take(second, 2, 1 - y))
    first = add_low(take(first, 2, x), swap(for_x, X))
    second = add_low(take(second, 2, y), swap(for_y, Y))
    column = jnp.concatenate([first, second], axis=2)
    (for_z,) = yield (take(column, 1, 1 - low),)
    column = add_low(take(column, 1, low), swap(for_z, Z_LOW))
    (for_z,) = yield (take(column, 0, 1 - high),)
    return take(column, 0, high).astype(F32) + swap(for_z, Z_HIGH).astype(F32)


def ordered(bit, mine, other, axis):
    first = bit == 0
    return jnp.stack([jnp.where(first, mine, other), jnp.where(first, other, mine)], axis=axis)


def gather_owned(me, own):
    x, y, low, high = (bit_of(me, b) for b in (X, Y, Z_LOW, Z_HIGH))
    rows, width = own.shape
    (own,) = yield (own,)
    column = ordered(high, own, swap(own, Z_HIGH), 0)
    (column,) = yield (column,)
    column = ordered(low, column, swap(column, Z_LOW), 1)
    below, above = yield (column[0], column[1])
    below = ordered(x, below, swap(below, X), 1)
    above = ordered(y, above, swap(above, Y), 1)
    below, above = yield (below, above)
    below = ordered(y, below, swap(below, Y), 1).reshape(-1, rows, width)
    above = ordered(x, above, swap(above, X), 2).reshape(-1, rows, width)
    below, above = yield (below, above)
    return [below, swap(below, CORE), above, swap(above, CORE)]


class Rounds:
    def __init__(self, steps):
        self.steps = steps
        self.sent = next(steps)
        self.result = None

    def before(self, *operands):
        sent, operands = lax.optimization_barrier((self.sent, operands))
        self.move(sent)
        return operands[0] if len(operands) == 1 else operands

    def move(self, sent):
        try:
            self.sent = self.steps.send(sent)
        except StopIteration as stop:
            self.sent, self.result = None, stop.value

    def finish(self):
        while self.result is None:
            self.move(self.sent)
        return self.result


def on_device(
    devices,
    src_in,
    tgt_in,
    src_len,
    tgt_len,
    tgt_mask,
    enc_cot,
    dec_cot,
    enc_master,
    enc_first,
    enc_second,
    dec_master,
    dec_first,
    dec_second,
    small_master,
    small_first,
    small_second,
):
    width = src_in.shape[1]
    number = src_in.shape[0]
    me = lax.axis_index("fsdp")
    enc_size, dec_size = enc_master.shape[0], dec_master.shape[0]
    enc_count, dec_count = enc_size * devices, dec_size * devices
    inner = (enc_count - 4 * width) // 2
    ups = inner // width
    enc_map, dec_map = enc_regions(width, inner), dec_regions(width, inner)

    enc_own = arrange_own(enc_master.astype(LOW), me * enc_size, enc_map, to_units)
    dec_own = arrange_own(dec_master.astype(LOW), me * dec_size, dec_map, to_units)
    by_rounds = devices == 1 << BITS
    share = small_master.shape[1]
    held = small_master.size
    own = jnp.zeros((16, width), LOW)
    own = lax.dynamic_update_slice(own, small_master.astype(LOW), (0, me * share))
    gathered = lax.all_gather(jnp.concatenate([enc_own, own], axis=0), "fsdp", axis=0, tiled=False)
    smalls = jnp.sum(gathered[:, enc_size:, :].astype(F32), axis=0)
    core = bit_of(me, CORE)
    src_owner, src_key, src_bounds = owners_of(src_len[0], number)
    tgt_owner, tgt_key, tgt_bounds = owners_of(tgt_len[0], number)
    enc_plan = plan_of(src_bounds, src_bounds, src_len[0], number, core)
    dec_plan = plan_of(tgt_bounds, tgt_bounds, tgt_len[0], number, core)
    cross_plan = plan_of(tgt_bounds, src_bounds, src_len[0], number, core)
    flags = tgt_mask.astype(F32)[None, :]
    if by_rounds:
        enc_far = [gathered]
        rounds = Rounds(gather_owned(me, dec_own))
        for _ in range(4):
            rounds.move(rounds.sent)
        early = (src_in, src_owner, src_key, tgt_owner, tgt_key, enc_plan, dec_plan, cross_plan, flags)
        src_in, src_owner, src_key, tgt_owner, tgt_key, enc_plan, dec_plan, cross_plan, flags = rounds.before(*early)
        dec_far = rounds.finish()
    else:
        enc_rows = arrange_all(gathered[:, :enc_size].reshape(-1, width), enc_size, enc_map, to_units)
        enc_far = [enc_rows.reshape(OWNERS, -1, width)]
        dec_rows = lax.all_gather(dec_own, "fsdp", axis=0, tiled=True)
        dec_rows = arrange_all(dec_rows, dec_size, dec_map, to_units).reshape(2, OWNERS // 4, 2, -1, width)
        first = core == 0
        dec_far = []
        for half in range(2):
            even, odd = dec_rows[half, :, 0], dec_rows[half, :, 1]
            dec_far += [jnp.where(first, even, odd), jnp.where(first, odd, even)]

    def enc_part(first, last):
        return row_copies(first, last, enc_count // OWNERS, False)

    def dec_part(first, last):
        return row_copies(first, last, dec_count // OWNERS, True)

    enc_qkv = enc_part(0, 3 * width)
    enc_wo = enc_part(3 * width, 4 * width)
    enc_up = enc_part(4 * width, 4 * width + inner)
    enc_down = enc_part(4 * width + inner, enc_count)
    self_qkv = dec_part(0, 3 * width)
    self_wo = dec_part(3 * width, 4 * width)
    cross_q = dec_part(4 * width, 5 * width)
    cross_kv = dec_part(5 * width, 7 * width)
    cross_wo = dec_part(7 * width, 8 * width)
    dec_up = dec_part(8 * width, 8 * width + inner)
    dec_down = dec_part(8 * width + inner, dec_count)

    start = jnp.where(tgt_mask[:, None] == 1, smalls[10].astype(LOW)[None, :], tgt_in)

    e_q, e_kv, e_ctx, e_lse, e_hat, e_inv, memory, t_hat, t_inv = fwd_block(
        enc_plan, src_in, None, enc_far, (enc_qkv, enc_wo, enc_up, enc_down), True, smalls, 0, src_owner, src_key, True,
        "enc_layer",
    )
    s_q, s_kv, s_ctx, s_lse, s_hat, s_inv = fwd_block(
        dec_plan, start, None, dec_far, (self_qkv, self_wo), False, smalls, 4, tgt_owner, tgt_key, False, "dec_block"
    )
    c_q, c_kv, c_lse, decoded, d_two, d_cctx, g_dup, g_ddown, g_cout, sums_d = cross_turn(
        cross_plan, s_hat, memory, dec_cot, dec_far, (cross_kv, cross_wo, cross_q, dec_up, dec_down), smalls, 6,
        tgt_owner, src_key, inner, "cross_turn",
    )

    d_memory, d_one, d_sctx, g_cq, g_ckv, g_sout, sums_c = cross_backward(
        cross_plan, c_q, c_kv, d_cctx, c_lse, tgt_owner, src_key, s_hat, s_inv, d_two, memory, s_ctx, dec_far,
        (cross_kv, cross_q, self_wo), smalls,
    )
    dsq, dsk, dsv, g_sqkv = attention_backward(
        dec_plan, s_q, s_kv, d_sctx, s_lse, tgt_owner, tgt_key, start, "rows", "dec_back"
    )
    dec_pieces = [
        g_sqkv,
        g_sout,
        g_cq,
        g_ckv.reshape(-1, width),
        g_cout,
        g_dup.reshape(-1, width),
        g_ddown,
    ]
    if by_rounds:
        core = core[None].astype(jnp.int32)
        copies = overlaps([p.shape[0] for p in dec_pieces], dec_size)
        send, keep = pack(core, dec_pieces, copies, dec_size, "dec_pack")
        rounds = Rounds(reduce_owned(me, send, keep, dec_size // 2))
        dsq, dsk, dsv = rounds.before(dsq, dsk, dsv)
    tgt_grad, mask_sum = qkv_inputs(
        dec_plan, dsq, dsk, dsv, d_one, dec_far, (self_qkv,), flags, "dec_qkv_inputs"
    )
    if by_rounds:
        d_memory, mask_sum = rounds.before(d_memory, mask_sum)
    d_mid, d_ectx, g_up, g_down, g_out, sums_e = ffn_backward(
        enc_plan, [enc_cot, d_memory], (t_hat, t_inv), (e_hat, e_inv), e_ctx, enc_far,
        (enc_up, enc_down, enc_wo), smalls, 0, inner, "enc_ffn_back",
    )
    if by_rounds:
        d_ectx, g_up = rounds.before(d_ectx, g_up)
    deq, dek, dev, g_qkv = attention_backward(
        enc_plan, e_q, e_kv, d_ectx, e_lse, src_owner, src_key, src_in, "units", "enc_back"
    )

    enc_pieces = [g_qkv.reshape(-1, width), g_out, g_up.reshape(-1, width), g_down]
    small_grad = jnp.concatenate([sums_e[:4], sums_c[:2], sums_d[:4], mask_sum[:1]], axis=0)
    small_wire = small_grad.reshape(-1, devices, share).transpose(1, 0, 2).reshape(devices, -1).astype(LOW)
    small_wire = jnp.pad(small_wire, ((0, 0), (0, 16 * width - held))).reshape(devices * 16, width)
    if by_rounds:
        dec_summed = rounds.finish()
        copies = overlaps([p.shape[0] for p in enc_pieces], enc_size)
        copies += [(len(enc_pieces), 16 * i, i, enc_size, 16) for i in range(devices)]
        send, keep = pack(core, enc_pieces + [small_wire], copies, enc_size + 16, "enc_pack")
        rounds = Rounds(reduce_owned(me, send, keep, enc_size // 2 + 16))
        deq, dek, dev = rounds.before(deq, dek, dev)
    src_grad = qkv_inputs(enc_plan, deq, dek, dev, d_mid, enc_far, (enc_qkv,), None, "enc_qkv_inputs")[0]
    if by_rounds:
        enc_summed = rounds.finish()
    else:
        dec_grad = arrange_all(jnp.concatenate(dec_pieces, axis=0), dec_size, dec_map, from_units)
        enc_grad = arrange_all(jnp.concatenate(enc_pieces, axis=0), enc_size, enc_map, from_units)
        enc_wire = jnp.concatenate(
            [enc_grad.reshape(devices, enc_size, width), small_wire.reshape(devices, 16, width)], axis=1
        )
        dec_summed = lax.psum_scatter(dec_grad, "fsdp", scatter_dimension=0, tiled=True).astype(F32)
        enc_summed = lax.psum_scatter(
            enc_wire.reshape(-1, width), "fsdp", scatter_dimension=0, tiled=True
        ).astype(F32)
    small_summed = enc_summed[enc_size:].reshape(-1)[:held].reshape(-1, share)
    enc_summed = arrange_own(enc_summed[:enc_size], me * enc_size, enc_map, from_units)
    dec_summed = arrange_own(dec_summed, me * dec_size, dec_map, from_units)

    part = 1.0 / devices
    enc_summed = enc_summed * part
    dec_summed = dec_summed * part
    small_summed = small_summed * part
    enc_new, enc_first_new, encoder_second_moment_updated = adamw(
        enc_master, enc_summed, enc_first, enc_second
    )
    dec_new, dec_first_new, dec_second_new = adamw(dec_master, dec_summed, dec_first, dec_second)
    small_first_new, small_second_new = moments(small_summed, small_first, small_second)
    return (
        memory,
        decoded,
        src_grad,
        tgt_grad,
        enc_new,
        enc_first_new,
        encoder_second_moment_updated,
        enc_new.astype(LOW),
        dec_new,
        dec_first_new,
        dec_second_new,
        dec_new.astype(LOW),
        small_summed,
        small_first_new,
        small_second_new,
    )


def solution(mesh):
    rows = P("fsdp", None)
    columns = P(None, "fsdp")
    return jax.shard_map(
        functools.partial(on_device, mesh.shape["fsdp"]),
        mesh=mesh,
        in_specs=(rows,) * 4 + (P("fsdp"),) + (rows,) * 8 + (columns,) * 3,
        out_specs=(rows,) * 12 + (columns,) * 3,
        check_vma=False,
    )
```

```python
import functools

import jax
import jax.numpy as jnp
from jax import lax
from jax.experimental import pallas as pl
from jax.experimental.pallas import tpu as pltpu
from jax.sharding import PartitionSpec as P

HEADS = 8
HEAD = 64
STEPS = 7
TILE = 256
LANES = 128

rate = 0.02
beta_one = 0.9
beta_two = 0.98
epsilon = 1e-06
decay = 0.01
floor_value = -1000000000.0
root_half = 0.7071067811865476
inverse_root_tau = 0.3989422804014327

F32 = jnp.float32
LOW = jnp.bfloat16
MIB = 2**20


def nn(former, latter):
    return lax.dot_general(
        former, latter, (((1,), (0,)), ((), ())), preferred_element_type=F32
    )


def nt(former, latter):
    return lax.dot_general(
        former, latter, (((1,), (1,)), ((), ())), preferred_element_type=F32
    )


def turned(values):
    return values.astype(F32).T.astype(LOW)


def column_of(row):
    return jnp.broadcast_to(row, (8, row.shape[1])).T[:, 0:1]


def ln_forward(values, gain, shift):
    centered = values - jnp.mean(values, axis=-1, keepdims=True)
    spread = jnp.mean(centered * centered, axis=-1, keepdims=True)
    inverse = lax.rsqrt(spread + 1e-05)
    normed = centered * inverse
    return normed * gain + shift, normed, inverse


def ln_backward(upstream, normed, inverse, gain):
    scaled = upstream * gain
    first = jnp.mean(scaled, axis=-1, keepdims=True)
    second = jnp.mean(scaled * normed, axis=-1, keepdims=True)
    return inverse * (scaled - first - normed * second)


def phi_and_slope(values):
    phi = 0.5 + 0.5 * lax.erf(values * root_half)
    return phi, phi + values * (jnp.exp(-0.5 * (values * values)) * inverse_root_tau)


def one_head(pair, head):
    lane = lax.broadcasted_iota(jnp.int32, pair.shape, 1)
    keep = lane < HEAD if head % 2 == 0 else lane >= HEAD
    return jnp.where(keep, pair, jnp.zeros_like(pair))


def pair_columns(head):
    return slice(LANES * (head // 2), LANES * (head // 2) + LANES)


def head_rows(head):
    return slice(HEAD * head, HEAD * head + HEAD)


def block_of(ref, j, count):
    if count == 1:
        return ref[...]
    return jnp.concatenate(
        [ref[first + 16 * j : first + 16 * j + 16, :] for first in range(0, ref.shape[0], 16 * count)], axis=0
    )


def spread(wide, values):
    for n in range(wide.shape[0]):
        wide[n] = values[:, LANES * n : LANES * n + LANES].astype(F32)


def third_rows(wide, j):
    rows = pl.ds(j, wide.shape[1] // 3, stride=3)
    return jnp.concatenate([wide[n, rows, :] for n in range(wide.shape[0])], axis=1).astype(LOW)


def put_third_rows(wide, j, values):
    rows = pl.ds(j, wide.shape[1] // 3, stride=3)
    for n in range(wide.shape[0]):
        wide[n, rows, :] = values[:, LANES * n : LANES * n + LANES]


def wide_scratch(width):
    return pltpu.VMEM((width // LANES, 3 * width, LANES), F32)


def put_block(ref, j, values):
    ref[:, j] = values.reshape(ref.shape[0], ref.shape[2], ref.shape[3])


OWNERS = 32


def row_copies(first, last, own, paired):
    found = []
    at = first
    while at < last:
        owner = at // own
        end = min(last, (owner + 1) * own)
        half = OWNERS // 4
        place = (2 * (owner // 2 // half) + owner % 2, owner // 2 % half) if paired else (0, owner)
        found.append((*place, at - owner * own, end - at, at - first))
        at = end
    return found


class Fetch:
    def __init__(self, far, core, copies, near, semaphores, used):
        self.core = core

        def handles(side):
            return [
                pltpu.make_async_copy(
                    far[source ^ side].at[owner, pl.ds(row, rows)], near.at[pl.ds(to, rows)], semaphores.at[used + n]
                )
                for n, (source, owner, row, rows, to) in enumerate(copies)
            ]

        self.handles = handles

    def start(self):
        if self.core is None:
            for handle in self.handles(0):
                handle.start()
            return
        for side in (0, 1):

            @pl.when(self.core == side)
            def _(side=side):
                for handle in self.handles(side):
                    handle.start()

    def wait(self):
        for handle in self.handles(0):
            handle.wait()


def fetches(far, plan, wanted, nears, semaphores):
    used = 0
    made = []
    core = plan[2, 1] if len(far) > 1 else None
    for copies, near in zip(wanted, nears):
        made.append(Fetch(far, core, copies, near, semaphores, used))
        used += len(copies)
    return made


def wait_first(i, loads):
    @pl.when(i == 0)
    def _():
        for load in loads:
            load.wait()


def fetch_scratch(wanted, width):
    return [pltpu.VMEM((sum(c[3] for c in copies), width), LOW) for copies in wanted] + [
        pltpu.SemaphoreType.DMA((sum(len(copies) for copies in wanted),))
    ]


FAR = pl.BlockSpec(memory_space=pl.ANY)


def sources_of(wanted):
    last = max(copy[0] for copies in wanted for copy in copies)
    return 1 if last == 0 else 2 * (last // 2) + 2


def call(kernel, grid, in_specs, out_specs, out_shape, scratch, flops, moved, name, room=24, near=(), keep=()):
    single = not isinstance(out_shape, list)
    shapes = [
        (pltpu.VMEM if keep is True or n in keep else pltpu.HBM)(*made)
        for n, made in enumerate([out_shape] if single else out_shape)
    ]
    made = pl.pallas_call(
        kernel,
        grid_spec=pltpu.PrefetchScalarGridSpec(
            num_scalar_prefetch=1,
            grid=grid,
            in_specs=in_specs,
            out_specs=out_specs,
            scratch_shapes=scratch,
        ),
        out_shape=shapes[0] if single else shapes,
        compiler_params=pltpu.CompilerParams(vmem_limit_bytes=room * MIB),
        cost_estimate=pl.CostEstimate(
            flops=flops, bytes_accessed=moved, transcendentals=0
        ),
        name=name,
    )

    def run(plan, *operands):
        placed = [
            operand
            if near is True or n in near
            else pltpu.with_memory_space_constraint(operand, pltpu.HBM)
            for n, operand in enumerate(operands)
        ]
        return made(plan, *placed)

    return run


def whole(shape):
    zeros = (0,) * len(shape)
    return pl.BlockSpec(shape, lambda i, *_: zeros)


def rows_of(width):
    return pl.BlockSpec((TILE, width), lambda i, *_: (i, 0))


def at_block(shape, *index):
    return pl.BlockSpec(shape, lambda i, *_: index)


def shaped(shape, kind):
    return (shape, kind)


def attend_tile(plan, i, keys, key_cols, query, owner_row, key_owner, vt, sc):
    scores, acc, top, total, masked_q = sc
    query = query * jnp.asarray(HEAD**-0.5, LOW)
    for h in range(HEADS):
        masked_q[h] = one_head(query[:, pair_columns(h)], h)
    top[...] = jnp.full_like(top, -1e30)
    total[...] = jnp.zeros_like(total)
    acc[...] = jnp.zeros_like(acc)
    begin = plan[0, i]
    chunks = plan[1, i]

    def score_tile(j, carry):
        rows = pl.ds(pl.multiple_of(begin + j * TILE, LANES), TILE)
        bias = jnp.where(key_owner[rows, 0:1] == owner_row, 0.0, floor_value)
        tops = []
        for h in range(HEADS):
            cols = pl.ds(key_cols + LANES * (h // 2), LANES)
            s = nt(keys[rows, cols], masked_q[h]) + bias
            scores[j, h] = s
            tops.append(jnp.max(s, axis=0, keepdims=True))
        top[...] = jnp.maximum(top[...], jnp.concatenate(tops, axis=0))
        return carry

    lax.fori_loop(0, chunks, score_tile, 0)

    def weigh_tile(j, carry):
        rows = pl.ds(pl.multiple_of(begin + j * TILE, LANES), TILE)
        sums = []
        for h in range(HEADS):
            p = jnp.exp(scores[j, h] - top[h : h + 1, :])
            sums.append(jnp.sum(p, axis=0, keepdims=True))
            acc[head_rows(h), :] += nn(vt[head_rows(h), rows], p.astype(LOW))
        total[...] += jnp.concatenate(sums, axis=0)
        return carry

    lax.fori_loop(0, chunks, weigh_tile, 0)


def fwd_block_kernel(plan, *refs, cross, gain_row, wanted, packed, ffn):
    refs = list(refs)

    def next_refs(count):
        taken = refs[:count]
        del refs[:count]
        return taken

    if cross:
        normed_in, memory = next_refs(2)
    else:
        (x_all,) = next_refs(1)
    far = next_refs(sources_of(wanted))
    small, owner_q, owner_k = next_refs(3)
    q_out, kv_out, ctx_out, lse_out, normed_out, inverse_out = next_refs(6)
    if ffn:
        out, normed_last, inverse_last = next_refs(3)
    kv, vt, mean_v, key_owner, scores, acc, top, total, masked_q, q_all = next_refs(10)
    nears = next_refs(len(wanted))
    semaphores = refs.pop(0)
    loads = fetches(far, plan, wanted, nears, semaphores)
    i = pl.program_id(0)
    width = kv.shape[1] // 2

    @pl.when(i == 0)
    def _():
        for load in loads:
            load.start()
        key_owner[...] = jnp.broadcast_to(owner_k[...], (8, owner_k.shape[1])).T
        loads[0].wait()
        if cross:
            wk, wv = block_of(nears[0], 0, 2), block_of(nears[0], 1, 2)
        elif packed:
            wq, wk, wv = (block_of(nears[0], j, 3) for j in range(3))
        else:
            wide = refs[0]
            spread(wide, nears[0][...])
            wq, wk, wv = (third_rows(wide, j) for j in range(3))
        sums = jnp.zeros((1, width), F32)
        for t in range(kv.shape[0] // TILE):
            rows = slice(t * TILE, t * TILE + TILE)
            x = memory[rows, :] if cross else x_all[rows, :]
            if not cross:
                q_all[rows, :] = nn(x, wq).astype(LOW)
            kv[rows, :width] = nn(x, wk).astype(LOW)
            v = nn(x, wv).astype(LOW)
            kv[rows, width:] = v
            v = v.astype(F32)
            vt[:, rows] = v.T.astype(LOW)
            sums = sums + jnp.sum(v, axis=0, keepdims=True)
        mean_v[...] = sums * (1.0 / kv.shape[0])
        for load in loads[1 : 3 if cross else 2]:
            load.wait()

    wo = nears[1]
    mine = pl.ds(pl.multiple_of(i * TILE, TILE), TILE)
    if cross:
        resid = normed_in[...] * small[4:5, :] + small[5:6, :]
        query = nn(resid.astype(LOW), nears[2][...]).astype(LOW)
        q_out[...] = query
    else:
        resid = x_all[mine, :].astype(F32)
        query = q_all[mine, :]
        q_out[...] = query
    kv_out[...] = kv[mine, :]
    owner_row = owner_q[...]
    attend_tile(plan, i, kv, 0, query, owner_row, key_owner, vt, (scores, acc, top, total, masked_q))
    dead = owner_row < 0
    sums = jnp.where(dead, 1.0, total[...])
    share = 1.0 / sums
    lse_out[...] = jnp.where(dead, 0.0, top[...] + jnp.log(sums))
    for h in range(HEADS):
        acc[head_rows(h), :] = acc[head_rows(h), :] * share[h : h + 1, :]
    live = column_of(owner_row) >= 0
    context = jnp.where(live, acc[...].T, mean_v[...]).astype(LOW)
    ctx_out[...] = context
    added = nn(context, wo[...]) * live.astype(F32)
    mid, normed, inverse = ln_forward(
        resid + added, small[gain_row : gain_row + 1, :], small[gain_row + 1 : gain_row + 2, :]
    )
    normed_out[...] = normed
    inverse_out[...] = jnp.broadcast_to(inverse, inverse_out.shape)
    if ffn:
        wup, wdown = nears[-2:]
        wait_first(i, loads[-2:])
        blocks = wdown.shape[0] // width
        low = mid.astype(LOW)
        result = mid
        for j in range(blocks):
            inner = nn(low, block_of(wup, j, blocks))
            phi = 0.5 + 0.5 * lax.erf(inner * root_half)
            result = result + nn((inner * phi).astype(LOW), wdown[j * width : j * width + width, :])
        result, normed, inverse = ln_forward(
            result, small[gain_row + 2 : gain_row + 3, :], small[gain_row + 3 : gain_row + 4, :]
        )
        out[...] = result.astype(LOW)
        normed_last[...] = normed
        inverse_last[...] = jnp.broadcast_to(inverse, inverse_last.shape)


def attention_scratch(keys, width):
    return [
        pltpu.VMEM((keys, 2 * width), LOW),
        pltpu.VMEM((width, keys), LOW),
        pltpu.VMEM((1, width), F32),
        pltpu.VMEM((keys, 8), F32),
        pltpu.VMEM((keys // TILE, HEADS, TILE, TILE), F32),
        pltpu.VMEM((width, TILE), F32),
        pltpu.VMEM((HEADS, TILE), F32),
        pltpu.VMEM((HEADS, TILE), F32),
        pltpu.VMEM((HEADS, TILE, LANES), LOW),
        pltpu.VMEM((keys, width), LOW),
    ]


def block_outs(queries, width):
    specs = [
        rows_of(width),
        rows_of(2 * width),
        rows_of(width),
        pl.BlockSpec((HEADS, TILE), lambda i, *_: (0, i)),
        rows_of(width),
        rows_of(LANES),
    ]
    shapes = [
        shaped((queries, width), LOW),
        shaped((queries, 2 * width), LOW),
        shaped((queries, width), LOW),
        shaped((HEADS, queries), F32),
        shaped((queries, width), F32),
        shaped((queries, LANES), F32),
    ]
    return specs, shapes


def owner_specs(keys):
    return [pl.BlockSpec((1, TILE), lambda i, *_: (0, i)), whole((1, keys))]


def fwd_block(plan, x, memory, far, wanted, packed, small, gain_row, owner, key_owner, ffn, name):
    cross = memory is not None
    number, width = x.shape
    specs, shapes = block_outs(number, width)
    if ffn:
        specs += [rows_of(width), rows_of(width), rows_of(LANES)]
        shapes += [shaped((number, width), LOW), shaped((number, width), F32), shaped((number, LANES), F32)]
    scratch = attention_scratch(number, width) + fetch_scratch(wanted, width)
    if not cross and not packed:
        scratch.append(wide_scratch(width))
    return call(
        functools.partial(
            fwd_block_kernel, cross=cross, gain_row=gain_row, wanted=wanted, packed=packed, ffn=ffn
        ),
        (number // TILE,),
        ([rows_of(width), whole(memory.shape)] if cross else [whole(x.shape)])
        + [FAR] * sources_of(wanted)
        + [whole(small.shape)]
        + owner_specs(number),
        specs,
        shapes,
        scratch,
        8 * number * width * width + number * number * width * 2,
        16 * number * width,
        name,
        room=44,
    )(plan, *([x, memory] if cross else [x]), *far[: sources_of(wanted)], small, owner, key_owner)


def ffn_back_kernel(plan, *refs, tiles, summed, gain_row, wanted):
    refs = list(refs)
    cot = refs.pop(0)
    extra = refs.pop(0) if summed else None
    normed_top, inverse_top, normed_mid, inverse_mid, context = refs[:5]
    far = refs[5 : 5 + sources_of(wanted)]
    (small,
     d_sum, d_context, g_up, g_down, g_out, sums, hidden, d_inner, mid_low, d_down, d_product,
     wup, wdown, wo, semaphores) = refs[5 + sources_of(wanted) :]
    loads = fetches(far, plan, wanted, (wup, wdown, wo), semaphores)
    i = pl.program_id(0)
    width = small.shape[1]
    blocks = wdown.shape[0] // width

    @pl.when(i == 0)
    def _():
        for load in loads:
            load.start()
        sums[...] = jnp.zeros_like(sums)

    @pl.when(i < tiles)
    def _():
        mine = pl.ds(pl.multiple_of(i * TILE, TILE), TILE)
        upstream = cot[...].astype(F32)
        if summed:
            upstream = upstream + extra[...]
        top = normed_top[...]
        sums[2:3, :] += jnp.sum(upstream * top, axis=0, keepdims=True)
        sums[3:4, :] += jnp.sum(upstream, axis=0, keepdims=True)
        d_mid = ln_backward(upstream, top, inverse_top[:, 0:1], small[gain_row + 2 : gain_row + 3, :])
        low = d_mid.astype(LOW)
        d_down[mine, :] = low
        normed = normed_mid[...]
        mid = (normed * small[gain_row : gain_row + 1, :] + small[gain_row + 1 : gain_row + 2, :]).astype(LOW)
        mid_low[mine, :] = mid
        wait_first(i, loads)
        for j in range(blocks):
            cols = slice(j * width, j * width + width)
            up = block_of(wup, j, blocks)
            inner = nn(mid, up)
            phi, slope = phi_and_slope(inner)
            hidden[j, mine, :] = (inner * phi).astype(LOW)
            part = (nt(low, wdown[cols, :]) * slope).astype(LOW)
            d_inner[j, mine, :] = part
            d_mid = d_mid + nt(part, up)
        sums[0:1, :] += jnp.sum(d_mid * normed, axis=0, keepdims=True)
        sums[1:2, :] += jnp.sum(d_mid, axis=0, keepdims=True)
        total = ln_backward(d_mid, normed, inverse_mid[:, 0:1], small[gain_row : gain_row + 1, :])
        d_sum[...] = total
        place = lax.broadcasted_iota(jnp.int32, (TILE, 1), 0) + i * TILE
        live = (place < plan[2, 0]).astype(F32)
        product = (total * live).astype(LOW)
        d_product[mine, :] = product
        d_context[...] = nt(product, wo[...]).astype(LOW)

    @pl.when(i >= tiles)
    def _():
        j = i - tiles
        put_block(g_up, 0, nn(turned(mid_low[...]), d_inner[j]).astype(LOW))
        g_down[...] = nn(turned(hidden[j]), d_down[...]).astype(LOW)

    @pl.when(i == tiles)
    def _():
        g_out[...] = nn(turned(context[...]), d_product[...]).astype(LOW)


def ffn_backward(plan, cots, top, mid, context, far, wanted, small, gain_row, inner, name):
    number, width = mid[0].shape
    tiles, blocks = number // TILE, inner // width

    def tile_of(columns):
        return pl.BlockSpec((TILE, columns), lambda i, *_: (jnp.minimum(i, tiles - 1), 0))

    return call(
        functools.partial(
            ffn_back_kernel, tiles=tiles, summed=len(cots) == 2, gain_row=gain_row, wanted=wanted
        ),
        (tiles + blocks,),
        [tile_of(width)] * len(cots)
        + [tile_of(width), tile_of(LANES), tile_of(width), tile_of(LANES), whole((number, width))]
        + [FAR] * sources_of(wanted)
        + [whole(small.shape)],
        [
            tile_of(width),
            tile_of(width),
            pl.BlockSpec((width // 16, 1, 16, width), lambda i, *_: (0, jnp.maximum(i - tiles, 0), 0, 0)),
            pl.BlockSpec((width, width), lambda i, *_: (jnp.maximum(i - tiles, 0), 0)),
            pl.BlockSpec((width, width), lambda i, *_: (0, 0)),
            pl.BlockSpec((8, width), lambda i, *_: (0, 0)),
        ],
        [
            shaped((number, width), F32),
            shaped((number, width), LOW),
            shaped((width // 16, blocks, 16, width), LOW),
            shaped((inner, width), LOW),
            shaped((width, width), LOW),
            shaped((8, width), F32),
        ],
        [
            pltpu.VMEM((blocks, number, width), LOW),
            pltpu.VMEM((blocks, number, width), LOW),
            pltpu.VMEM((number, width), LOW),
            pltpu.VMEM((number, width), LOW),
            pltpu.VMEM((number, width), LOW),
        ]
        + fetch_scratch(wanted, width),
        10 * number * width * inner,
        30 * number * width,
        name,
        room=44,
    )(plan, *cots, *top, *mid, context, *far[: sources_of(wanted)], small)


def turn_kernel(plan, *refs, tiles, gain_row, wanted):
    normed_in, memory, cot = refs[:3]
    far = refs[3 : 3 + sources_of(wanted)]
    (small, owner_q, owner_k,
     q_out, kv_out, lse_out, out, d_sum, d_context, g_up, g_down, g_out, sums,
     kv, vt, mean_v, key_owner, scores, acc, top, total, masked_q,
     hidden, d_inner, mid_low, d_down, d_product, contexts, slopes,
     *nears, semaphores) = refs[3 + sources_of(wanted) :]
    wkv, wo, wq, wup, wdown = nears
    loads = fetches(far, plan, wanted, nears, semaphores)
    i = pl.program_id(0)
    width = small.shape[1]
    blocks = wdown.shape[0] // width

    @pl.when(i == 0)
    def _():
        for load in loads:
            load.start()
        sums[...] = jnp.zeros_like(sums)
        key_owner[...] = jnp.broadcast_to(owner_k[...], (8, owner_k.shape[1])).T
        loads[0].wait()
        wk, wv = block_of(wkv, 0, 2), block_of(wkv, 1, 2)
        means = jnp.zeros((1, width), F32)
        for t in range(kv.shape[0] // TILE):
            rows = slice(t * TILE, t * TILE + TILE)
            x = memory[rows, :]
            kv[rows, :width] = nn(x, wk).astype(LOW)
            v = nn(x, wv).astype(LOW)
            kv[rows, width:] = v
            v = v.astype(F32)
            vt[:, rows] = v.T.astype(LOW)
            means = means + jnp.sum(v, axis=0, keepdims=True)
        mean_v[...] = means * (1.0 / kv.shape[0])
        for load in loads[1:3]:
            load.wait()

    @pl.when(i < tiles)
    def _():
        mine = pl.ds(pl.multiple_of(i * TILE, TILE), TILE)
        resid = normed_in[...] * small[gain_row - 2 : gain_row - 1, :] + small[gain_row - 1 : gain_row, :]
        query = nn(resid.astype(LOW), wq[...]).astype(LOW)
        q_out[...] = query
        kv_out[...] = kv[mine, :]
        owner_row = owner_q[...]
        attend_tile(
            plan, i, kv, 0, query, owner_row, key_owner, vt, (scores, acc, top, total, masked_q)
        )
        dead = owner_row < 0
        weighed = jnp.where(dead, 1.0, total[...])
        share = 1.0 / weighed
        lse_out[...] = jnp.where(dead, 0.0, top[...] + jnp.log(weighed))
        for h in range(HEADS):
            acc[head_rows(h), :] = acc[head_rows(h), :] * share[h : h + 1, :]
        live = column_of(owner_row) >= 0
        context = jnp.where(live, acc[...].T, mean_v[...]).astype(LOW)
        contexts[mine, :] = context
        added = nn(context, wo[...]) * live.astype(F32)
        mid, normed_mid, inverse_mid = ln_forward(
            resid + added, small[gain_row : gain_row + 1, :], small[gain_row + 1 : gain_row + 2, :]
        )
        wait_first(i, loads[3:])
        low = mid.astype(LOW)
        mid_low[mine, :] = low
        result = mid
        for j in range(blocks):
            inner = nn(low, block_of(wup, j, blocks))
            phi, slope = phi_and_slope(inner)
            made = (inner * phi).astype(LOW)
            hidden[j, mine, :] = made
            slopes[j] = slope
            result = result + nn(made, wdown[j * width : j * width + width, :])
        result, normed, inverse = ln_forward(
            result, small[gain_row + 2 : gain_row + 3, :], small[gain_row + 3 : gain_row + 4, :]
        )
        out[...] = result.astype(LOW)

        upstream = cot[...].astype(F32)
        sums[2:3, :] += jnp.sum(upstream * normed, axis=0, keepdims=True)
        sums[3:4, :] += jnp.sum(upstream, axis=0, keepdims=True)
        d_mid = ln_backward(upstream, normed, inverse, small[gain_row + 2 : gain_row + 3, :])
        low = d_mid.astype(LOW)
        d_down[mine, :] = low
        for j in range(blocks):
            part = (nt(low, wdown[j * width : j * width + width, :]) * slopes[j]).astype(LOW)
            d_inner[j, mine, :] = part
            d_mid = d_mid + nt(part, block_of(wup, j, blocks))
        sums[0:1, :] += jnp.sum(d_mid * normed_mid, axis=0, keepdims=True)
        sums[1:2, :] += jnp.sum(d_mid, axis=0, keepdims=True)
        d_all = ln_backward(d_mid, normed_mid, inverse_mid, small[gain_row : gain_row + 1, :])
        d_sum[...] = d_all
        product = (d_all * live.astype(F32)).astype(LOW)
        d_product[mine, :] = product
        d_context[...] = nt(product, wo[...]).astype(LOW)

    @pl.when(i >= tiles)
    def _():
        j = i - tiles
        put_block(g_up, 0, nn(turned(mid_low[...]), d_inner[j]).astype(LOW))
        g_down[...] = nn(turned(hidden[j]), d_down[...]).astype(LOW)

    @pl.when(i == tiles)
    def _():
        g_out[...] = nn(turned(contexts[...]), d_product[...]).astype(LOW)


def cross_turn(plan, normed, memory, cot, far, wanted, small, gain_row, owner, key_owner, inner, name):
    number, width = normed.shape
    keys = memory.shape[0]
    tiles, blocks = number // TILE, inner // width

    def tile_of(columns):
        return pl.BlockSpec((TILE, columns), lambda i, *_: (jnp.minimum(i, tiles - 1), 0))

    def columns_of(rows):
        return pl.BlockSpec((rows, TILE), lambda i, *_: (0, jnp.minimum(i, tiles - 1)))

    return call(
        functools.partial(turn_kernel, tiles=tiles, gain_row=gain_row, wanted=wanted),
        (tiles + blocks,),
        [tile_of(width), whole(memory.shape), tile_of(width)]
        + [FAR] * sources_of(wanted)
        + [whole(small.shape), columns_of(1), whole((1, keys))],
        [
            tile_of(width),
            tile_of(2 * width),
            columns_of(HEADS),
            tile_of(width),
            tile_of(width),
            tile_of(width),
            pl.BlockSpec((width // 16, 1, 16, width), lambda i, *_: (0, jnp.maximum(i - tiles, 0), 0, 0)),
            pl.BlockSpec((width, width), lambda i, *_: (jnp.maximum(i - tiles, 0), 0)),
            whole((width, width)),
            whole((8, width)),
        ],
        [
            shaped((number, width), LOW),
            shaped((number, 2 * width), LOW),
            shaped((HEADS, number), F32),
            shaped((number, width), LOW),
            shaped((number, width), F32),
            shaped((number, width), LOW),
            shaped((width // 16, blocks, 16, width), LOW),
            shaped((inner, width), LOW),
            shaped((width, width), LOW),
            shaped((8, width), F32),
        ],
        attention_scratch(keys, width)[:-1]
        + [
            pltpu.VMEM((blocks, number, width), LOW),
            pltpu.VMEM((blocks, number, width), LOW),
            pltpu.VMEM((number, width), LOW),
            pltpu.VMEM((number, width), LOW),
            pltpu.VMEM((number, width), LOW),
            pltpu.VMEM((number, width), LOW),
            pltpu.VMEM((blocks, TILE, width), F32),
        ]
        + fetch_scratch(wanted, width),
        12 * number * width * inner + number * number * width * 2,
        30 * number * width,
        name,
        room=58,
    )(plan, normed, memory, cot, *far[: sources_of(wanted)], small, owner, key_owner)


def attend_back(plan, i, q_ref, k_ref, v_ref, do_ref, lse, owner_q, owner_k, scratch):
    kt, key_owner, masked_q, masked_do, dqt, dk_sum, dv_sum, weights, d_weights, dots = scratch

    @pl.when(i == 0)
    def _():
        key_owner[...] = jnp.broadcast_to(owner_k[...], (8, owner_k.shape[1])).T
        kt[...] = turned(k_ref[...])
        dk_sum[...] = jnp.zeros_like(dk_sum)
        dv_sum[...] = jnp.zeros_like(dv_sum)

    query = q_ref[...] * jnp.asarray(HEAD**-0.5, LOW)
    upstream = do_ref[...]
    for h in range(HEADS):
        masked_q[h] = one_head(query[:, pair_columns(h)], h)
        masked_do[h] = one_head(upstream[:, pair_columns(h)], h)
    dqt[...] = jnp.zeros_like(dqt)
    dots[...] = jnp.zeros_like(dots)
    owner_row = owner_q[...]
    begin = plan[0, i]
    chunks = plan[1, i]

    def weigh_tile(j, carry):
        rows = pl.ds(pl.multiple_of(begin + j * TILE, LANES), TILE)
        bias = jnp.where(key_owner[rows, 0:1] == owner_row, 0.0, floor_value)
        sums = []
        for h in range(HEADS):
            s = nt(k_ref[rows, pair_columns(h)], masked_q[h])
            p = jnp.exp((s - lse[h : h + 1, :]) + bias)
            dp = nt(v_ref[rows, pair_columns(h)], masked_do[h])
            weights[j, h] = p
            d_weights[j, h] = dp
            sums.append(jnp.sum(p * dp, axis=0, keepdims=True))
        dots[...] += jnp.concatenate(sums, axis=0)
        return carry

    lax.fori_loop(0, chunks, weigh_tile, 0)

    def grad_tile(j, carry):
        rows = pl.ds(pl.multiple_of(begin + j * TILE, LANES), TILE)
        for pair in range(HEADS // 2):
            cols = pair_columns(2 * pair)
            dv_part = dv_sum[rows, cols]
            dk_part = dk_sum[rows, cols]
            for h in (2 * pair, 2 * pair + 1):
                p = weights[j, h]
                ds = (p * (d_weights[j, h] - dots[h : h + 1, :])).astype(LOW)
                dv_part = dv_part + nn(p.astype(LOW), masked_do[h])
                dk_part = dk_part + nn(ds, masked_q[h])
                dqt[head_rows(h), :] += nn(kt[head_rows(h), rows], ds)
            dv_sum[rows, cols] = dv_part
            dk_sum[rows, cols] = dk_part
        return carry

    lax.fori_loop(0, chunks, grad_tile, 0)
    return (dqt[...] * HEAD**-0.5).T.astype(LOW)


def attention_back_kernel(plan, *refs, made):
    q_ref, k_ref, v_ref, do_ref, lse, owner_q, owner_k, *refs = refs
    x = refs.pop(0) if made else None
    dq, dk, dv, *refs = refs
    g_qkv = refs.pop(0) if made else None
    scratch, more = refs[:10], refs[10:]
    dk_sum, dv_sum = scratch[5:7]
    i = pl.program_id(0)
    dq_tile = attend_back(plan, i, q_ref, k_ref, v_ref, do_ref, lse, owner_q, owner_k, scratch)
    dq[...] = dq_tile
    if made:
        dq_all = more[0]
        dq_all[pl.ds(pl.multiple_of(i * TILE, TILE), TILE), :] = dq_tile

    @pl.when(i == pl.num_programs(0) - 1)
    def _():
        dk[...] = dk_sum[...].astype(LOW)
        dv[...] = dv_sum[...].astype(LOW)
        if made:
            turn = turned(x[...])
            for j, ref in enumerate((dq_all, dk, dv)):
                grad = nn(turn, ref[...])
                if made == "units":
                    put_block(g_qkv, j, grad.astype(LOW))
                else:
                    put_third_rows(more[1], j, grad)
        if made == "rows":
            for n in range(more[1].shape[0]):
                g_qkv[:, LANES * n : LANES * n + LANES] = more[1][n].astype(LOW)


def attend_back_scratch(keys, width):
    return [
        pltpu.VMEM((width, keys), LOW),
        pltpu.VMEM((keys, 8), F32),
        pltpu.VMEM((HEADS, TILE, LANES), LOW),
        pltpu.VMEM((HEADS, TILE, LANES), LOW),
        pltpu.VMEM((width, TILE), F32),
        pltpu.VMEM((keys, width), F32),
        pltpu.VMEM((keys, width), F32),
        pltpu.VMEM((keys // TILE, HEADS, TILE, TILE), F32),
        pltpu.VMEM((keys // TILE, HEADS, TILE, TILE), F32),
        pltpu.VMEM((HEADS, TILE), F32),
    ]


def attention_backward(plan, q, kv, d_context, lse, owner, key_owner, x, made, name):
    number, width = q.shape
    keys = kv.shape[0]
    in_specs = [
        rows_of(width),
        at_block((keys, width), 0, 0),
        at_block((keys, width), 0, 1),
        rows_of(width),
        pl.BlockSpec((HEADS, TILE), lambda i, *_: (0, i)),
    ] + owner_specs(keys)
    out_specs = [rows_of(width), whole((keys, width)), whole((keys, width))]
    out_shape = [shaped((number, width), LOW), shaped((keys, width), LOW), shaped((keys, width), LOW)]
    operands = [q, kv, kv, d_context, lse, owner, key_owner]
    scratch = attend_back_scratch(keys, width)
    if made:
        shape = (width // 16, 3, 16, width) if made == "units" else (3 * width, width)
        in_specs.append(whole(x.shape))
        operands.append(x)
        out_specs.append(whole(shape))
        out_shape.append(shaped(shape, LOW))
        scratch.append(pltpu.VMEM((number, width), LOW))
        if made == "rows":
            scratch.append(wide_scratch(width))
    return call(
        functools.partial(attention_back_kernel, made=made),
        (number // TILE,),
        in_specs,
        out_specs,
        out_shape,
        scratch,
        number * keys * width * 4 + (6 * number * width * width if made else 0),
        12 * number * width,
        name,
        room=52,
    )(plan, *operands)


def cross_back_kernel(plan, *refs, wanted, tiles):
    attention, refs = refs[:7], refs[7:]
    normed, inverse, d_above, memory, context = refs[:5]
    far = refs[5 : 5 + sources_of(wanted)]
    small, d_memory, d_sum, d_context, g_query, g_pair, g_out, sums, *refs = refs[5 + sources_of(wanted) :]
    scratch, refs = refs[:10], refs[10:]
    d_query, dk, dv, d_product, wkv, wq, wo, semaphores = refs
    dk_sum, dv_sum = scratch[5:7]
    loads = fetches(far, plan, wanted, (wkv, wq, wo), semaphores)
    i = pl.program_id(0)

    @pl.when(i == 0)
    def _():
        for load in loads:
            load.start()
        sums[...] = jnp.zeros_like(sums)

    @pl.when(i < tiles)
    def _():
        d_query[pl.ds(pl.multiple_of(i * TILE, TILE), TILE), :] = attend_back(plan, i, *attention, scratch)

    @pl.when(i == tiles)
    def _():
        dk[...] = dk_sum[...].astype(LOW)
        dv[...] = dv_sum[...].astype(LOW)
        for load in loads:
            load.wait()
        low = normed[...] * small[4:5, :] + small[5:6, :]
        g_query[...] = nn(low.T.astype(LOW), d_query[...]).astype(LOW)

    @pl.when(i >= tiles)
    def _():
        row = pl.multiple_of((i - tiles) * TILE, TILE)
        mine = pl.ds(row, TILE)
        wk, wv = block_of(wkv, 0, 2), block_of(wkv, 1, 2)
        d_memory[...] = nt(dk[mine, :], wk) + nt(dv[mine, :], wv)
        d_one = d_above[...] + nt(d_query[mine, :], wq[...])
        hat = normed[mine, :]
        sums[0:1, :] += jnp.sum(d_one * hat, axis=0, keepdims=True)
        sums[1:2, :] += jnp.sum(d_one, axis=0, keepdims=True)
        total = ln_backward(d_one, hat, inverse[:, 0:1], small[4:5, :])
        d_sum[...] = total
        place = lax.broadcasted_iota(jnp.int32, (TILE, 1), 0) + row
        live = (place < plan[2, 0]).astype(F32)
        product = (total * live).astype(LOW)
        d_product[mine, :] = product
        d_context[...] = nt(product, wo[...]).astype(LOW)

    @pl.when(i == tiles + 1)
    def _():
        put_block(g_pair, 0, nn(turned(memory[...]), dk[...]).astype(LOW))

    @pl.when(i == tiles + 2)
    def _():
        put_block(g_pair, 1, nn(turned(memory[...]), dv[...]).astype(LOW))

    @pl.when(i == 2 * tiles - 1)
    def _():
        g_out[...] = nn(turned(context[...]), d_product[...]).astype(LOW)


def cross_backward(plan, q, kv, d_context, lse, owner, key_owner, normed, inverse, d_above, memory, context, far,
                   wanted, small):
    number, width = normed.shape
    keys = kv.shape[0]
    tiles = number // TILE
    full = whole((number, width))

    def first_rows(columns):
        return pl.BlockSpec((TILE, columns), lambda i, *_: (jnp.minimum(i, tiles - 1), 0))

    def first_columns(rows):
        return pl.BlockSpec((rows, TILE), lambda i, *_: (0, jnp.minimum(i, tiles - 1)))

    def later_rows(columns):
        return pl.BlockSpec((TILE, columns), lambda i, *_: (jnp.maximum(i - tiles, 0), 0))

    return call(
        functools.partial(cross_back_kernel, wanted=wanted, tiles=tiles),
        (2 * tiles,),
        [first_rows(width), at_block((keys, width), 0, 0), at_block((keys, width), 0, 1), first_rows(width),
         first_columns(HEADS), first_columns(1), whole((1, keys)),
         full, later_rows(LANES), later_rows(width), whole(memory.shape), full]
        + [FAR] * sources_of(wanted)
        + [whole(small.shape)],
        [later_rows(width), later_rows(width), later_rows(width), whole((width, width)),
         whole((width // 16, 2, 16, width)), whole((width, width)), whole((8, width))],
        [shaped((number, width), F32), shaped((number, width), F32), shaped((number, width), LOW),
         shaped((width, width), LOW), shaped((width // 16, 2, 16, width), LOW), shaped((width, width), LOW),
         shaped((8, width), F32)],
        attend_back_scratch(keys, width)
        + [pltpu.VMEM((number, width), LOW), pltpu.VMEM((keys, width), LOW), pltpu.VMEM((keys, width), LOW),
           pltpu.VMEM((number, width), LOW)]
        + fetch_scratch(wanted, width),
        16 * number * width * width + number * keys * width * 4,
        24 * number * width,
        "cross_back",
        room=58,
    )(plan, q, kv, kv, d_context, lse, owner, key_owner, normed, inverse, d_above, memory, context,
      *far[: sources_of(wanted)], small)


def qkv_inputs_kernel(plan, *refs, masked, wanted):
    if masked:
        dq, dk, dv, d_above, flags, *refs = refs
        far = refs[: sources_of(wanted)]
        d_x, mask_sum, near, semaphores, blocks, wide = refs[sources_of(wanted) :]
    else:
        dq, dk, dv, d_above, *refs = refs
        far = refs[: sources_of(wanted)]
        d_x, near, semaphores, blocks = refs[sources_of(wanted) :]
    width = dq.shape[1]

    @pl.when(pl.program_id(0) == 0)
    def _():
        (load,) = fetches(far, plan, wanted, (near,), semaphores)
        load.start()
        load.wait()
        if masked:
            mask_sum[...] = jnp.zeros_like(mask_sum)
            spread(wide, near[...])
        for j in range(3):
            if masked:
                blocks[:, j * width : j * width + width] = third_rows(wide, j)
            else:
                blocks[:, j * width : j * width + width] = block_of(near, j, 3)

    pieces = jnp.concatenate([dq[...], dk[...], dv[...]], axis=1)
    total = nt(pieces, blocks[...])
    if masked:
        total = total + d_above[...]
        hit = column_of(flags[...]) == 1.0
        d_x[...] = jnp.where(hit, 0.0, total)
        mask_sum[0:1, :] += jnp.sum(jnp.where(hit, total, 0.0), axis=0, keepdims=True)
    else:
        d_x[...] = d_above[...]
        d_x[...] += total


def qkv_inputs(plan, dq, dk, dv, d_above, far, wanted, flags, name):
    number, width = dq.shape
    masked = flags is not None
    in_specs = [rows_of(width)] * 4
    out_specs = [rows_of(width)]
    out_shape = [shaped((number, width), F32)]
    operands = [dq, dk, dv, d_above]
    scratch = fetch_scratch(wanted, width) + [pltpu.VMEM((width, 3 * width), LOW)]
    if masked:
        in_specs.append(pl.BlockSpec((1, TILE), lambda i, *_: (0, i)))
        out_specs.append(whole((8, width)))
        out_shape.append(shaped((8, width), F32))
        operands.append(flags)
        scratch.append(wide_scratch(width))
    in_specs += [FAR] * sources_of(wanted)
    operands += far[: sources_of(wanted)]
    return call(
        functools.partial(qkv_inputs_kernel, masked=masked, wanted=wanted),
        (number // TILE,),
        in_specs,
        out_specs,
        out_shape,
        scratch,
        6 * number * width * width,
        16 * number * width,
        name,
    )(plan, *operands)


def enc_regions(width, inner):
    return ((0, 3 * width, 3), (4 * width, 4 * width + inner, inner // width))


def dec_regions(width, inner):
    return ((5 * width, 7 * width, 2), (8 * width, 8 * width + inner, inner // width))


def to_units(rows, k):
    return rows.reshape(-1, 16, k, rows.shape[1]).transpose(0, 2, 1, 3).reshape(rows.shape)


def from_units(rows, k):
    return rows.reshape(-1, k, 16, rows.shape[1]).transpose(0, 2, 1, 3).reshape(rows.shape)


def fits(size, region):
    return size % (16 * region[2]) == 0


def arrange_own(rows, first, regions, arrange):
    place = first + lax.broadcasted_iota(jnp.int32, (rows.shape[0], 1), 0)
    result = rows
    for region in regions:
        if fits(rows.shape[0], region):
            inside = (place >= region[0]) & (place < region[1])
            result = jnp.where(inside, arrange(rows, region[2]), result)
    return result


def arrange_all(rows, size, regions, arrange):
    for region in regions:
        if not fits(size, region):
            part = arrange(rows[region[0] : region[1]], region[2])
            rows = jnp.concatenate([rows[: region[0]], part, rows[region[1] :]], axis=0)
    return rows


def owners_of(lengths, number):
    bounds = jnp.cumsum(lengths)
    places = jnp.arange(number, dtype=jnp.int32)
    owners = jnp.sum((places[:, None] >= bounds[None, :]).astype(jnp.int32), axis=1)
    filled = places < bounds[-1]
    for_queries = jnp.where(filled, owners, -2).astype(F32)[None, :]
    for_keys = jnp.where(filled, owners, -1).astype(F32)[None, :]
    return for_queries, for_keys, bounds


def plan_of(query_bounds, key_bounds, key_lengths, number, core):
    firsts = jnp.arange(8, dtype=jnp.int32) * TILE
    filled = query_bounds[-1]
    lasts = jnp.minimum(firsts + TILE, filled) - 1

    def pair_of(places):
        found = jnp.sum((places[:, None] >= query_bounds[None, :]).astype(jnp.int32), axis=1)
        return jnp.minimum(found, key_lengths.shape[0] - 1)

    def pick(values, pairs):
        chosen = pairs[:, None] == jnp.arange(values.shape[0])[None, :]
        return jnp.sum(jnp.where(chosen, values[None, :], 0), axis=1)

    begin = pick(key_bounds - key_lengths, pair_of(firsts))
    end = pick(key_bounds, pair_of(lasts))
    some = firsts < filled
    begin = begin // LANES * LANES
    chunks = (end - begin + TILE - 1) // TILE
    begin = jnp.where(some, jnp.minimum(begin, number - chunks * TILE), 0)
    chunks = jnp.where(some, chunks, 0)
    rest = jnp.where(jnp.arange(8) == 1, core, filled)
    return jnp.stack([begin, chunks, rest]).astype(jnp.int32)


def moments(gradient, first, second):
    first_new = beta_one * first + (1.0 - beta_one) * gradient
    second_new = beta_two * second + (1.0 - beta_two) * gradient * gradient
    return (first_new, second_new)


def adamw(weight, gradient, first, second):
    first_new, second_new = moments(gradient, first, second)
    moved = weight - rate * (
        first_new
        / (1.0 - beta_one**STEPS)
        / (jnp.sqrt(second_new / (1.0 - beta_two**STEPS)) + epsilon)
        + decay * weight
    )
    return (moved, first_new, second_new)


CORE, X, Y, Z_LOW, Z_HIGH = 0, 1, 2, 3, 4
BITS = 5


def partner(bit):
    return [(i, i ^ (1 << bit)) for i in range(1 << BITS)]


def bit_of(me, bit):
    return (me >> bit) & 1


def take(values, axis, index):
    return lax.dynamic_index_in_dim(values, index, axis, keepdims=False)


def overlaps(sizes, own):
    found = []
    first = 0
    for piece, size in enumerate(sizes):
        at = first
        while at < first + size:
            owner = at // own
            end = min(first + size, (owner + 1) * own)
            found.append((piece, at - first, owner, at - owner * own, end - at))
            at = end
        first += size
    return found


def pack_kernel(core, *refs, copies, number):
    pieces, send, keep, semaphores = refs[:number], refs[number], refs[number + 1], refs[number + 2]
    for side in (0, 1):

        @pl.when(core[0] == side)
        def _():
            handles = []
            for n, (piece, at, owner, to, rows) in enumerate(copies):
                target = keep if owner % 2 == side else send
                handles.append(
                    pltpu.make_async_copy(
                        pieces[piece].at[pl.ds(at, rows)],
                        target.at[owner // 2, pl.ds(to, rows)],
                        semaphores.at[n],
                    )
                )
            for handle in handles:
                handle.start()
            for handle in handles:
                handle.wait()


def pack(core, pieces, copies, block, name):
    width = pieces[0].shape[1]
    shape = shaped((1 << (BITS - 1), block, width), LOW)
    anywhere = pl.BlockSpec(memory_space=pl.ANY)
    total = sum(piece.size for piece in pieces)
    return call(
        functools.partial(pack_kernel, copies=copies, number=len(pieces)),
        (1,),
        [pl.BlockSpec(memory_space=pltpu.VMEM)] * len(pieces),
        [anywhere, anywhere],
        [shape, shape],
        [pltpu.SemaphoreType.DMA((len(copies),))],
        0,
        4 * total,
        name,
        near=True,
    )(core, *pieces)


def add_low(former, latter):
    return (former.astype(F32) + latter.astype(F32)).astype(LOW)


def swap(values, bit):
    return lax.ppermute(values, "fsdp", partner(bit))


def reduce_owned(me, send, keep, cut):
    rows, width = send.shape[1:]
    x, y, low, high = (bit_of(me, b) for b in (X, Y, Z_LOW, Z_HIGH))
    (send,) = yield (send,)
    chips = add_low(keep, swap(send, CORE)).reshape(2, 2, 2, 2, rows, width)
    first, second = chips[..., :cut, :], chips[..., cut:, :]
    for_y, for_x = yield (take(first, 2, 1 - y), take(second, 3, 1 - x))
    first = add_low(take(first, 2, y), swap(for_y, Y))
    second = add_low(take(second, 3, x), swap(for_x, X))
    for_x, for_y = yield (take(first, 2, 1 - x), take(second, 2, 1 - y))
    first = add_low(take(first, 2, x), swap(for_x, X))
    second = add_low(take(second, 2, y), swap(for_y, Y))
    column = jnp.concatenate([first, second], axis=2)
    (for_z,) = yield (take(column, 1, 1 - low),)
    column = add_low(take(column, 1, low), swap(for_z, Z_LOW))
    (for_z,) = yield (take(column, 0, 1 - high),)
    return take(column, 0, high).astype(F32) + swap(for_z, Z_HIGH).astype(F32)


def ordered(bit, mine, other, axis):
    first = bit == 0
    return jnp.stack([jnp.where(first, mine, other), jnp.where(first, other, mine)], axis=axis)


def gather_owned(me, own):
    x, y, low, high = (bit_of(me, b) for b in (X, Y, Z_LOW, Z_HIGH))
    rows, width = own.shape
    (own,) = yield (own,)
    column = ordered(high, own, swap(own, Z_HIGH), 0)
    (column,) = yield (column,)
    column = ordered(low, column, swap(column, Z_LOW), 1)
    below, above = yield (column[0], column[1])
    below = ordered(x, below, swap(below, X), 1)
    above = ordered(y, above, swap(above, Y), 1)
    below, above = yield (below, above)
    below = ordered(y, below, swap(below, Y), 1).reshape(-1, rows, width)
    above = ordered(x, above, swap(above, X), 2).reshape(-1, rows, width)
    below, above = yield (below, above)
    return [below, swap(below, CORE), above, swap(above, CORE)]


class Rounds:
    def __init__(self, steps):
        self.steps = steps
        self.sent = next(steps)
        self.result = None

    def before(self, *operands):
        sent, operands = lax.optimization_barrier((self.sent, operands))
        self.move(sent)
        return operands[0] if len(operands) == 1 else operands

    def move(self, sent):
        try:
            self.sent = self.steps.send(sent)
        except StopIteration as stop:
            self.sent, self.result = None, stop.value

    def finish(self):
        while self.result is None:
            self.move(self.sent)
        return self.result


def on_device(
    devices,
    src_in,
    tgt_in,
    src_len,
    tgt_len,
    tgt_mask,
    enc_cot,
    dec_cot,
    enc_master,
    enc_first,
    enc_second,
    dec_master,
    dec_first,
    dec_second,
    small_master,
    small_first,
    small_second,
):
    width = src_in.shape[1]
    number = src_in.shape[0]
    me = lax.axis_index("fsdp")
    enc_size, dec_size = enc_master.shape[0], dec_master.shape[0]
    enc_count, dec_count = enc_size * devices, dec_size * devices
    inner = (enc_count - 4 * width) // 2
    ups = inner // width
    enc_map, dec_map = enc_regions(width, inner), dec_regions(width, inner)

    enc_own = arrange_own(enc_master.astype(LOW), me * enc_size, enc_map, to_units)
    dec_own = arrange_own(dec_master.astype(LOW), me * dec_size, dec_map, to_units)
    by_rounds = devices == 1 << BITS
    share = small_master.shape[1]
    held = small_master.size
    own = jnp.zeros((16, width), LOW)
    own = lax.dynamic_update_slice(own, small_master.astype(LOW), (0, me * share))
    core = bit_of(me, CORE)
    src_owner, src_key, src_bounds = owners_of(src_len[0], number)
    tgt_owner, tgt_key, tgt_bounds = owners_of(tgt_len[0], number)
    enc_plan = plan_of(src_bounds, src_bounds, src_len[0], number, core)
    dec_plan = plan_of(tgt_bounds, tgt_bounds, tgt_len[0], number, core)
    cross_plan = plan_of(tgt_bounds, src_bounds, src_len[0], number, core)
    flags = tgt_mask.astype(F32)[None, :]
    if by_rounds:
        ahead = Rounds(gather_owned(me, jnp.concatenate([enc_own, own], axis=0)))
        ahead.move(ahead.sent)
        ahead.move(ahead.sent)
        dec_own = ahead.before(dec_own)
        behind = Rounds(gather_owned(me, dec_own))
        behind.move(behind.sent)
        behind.sent = (ahead.before(*behind.sent),)
        behind.move(behind.sent)
        ahead.sent, behind.sent = lax.optimization_barrier((ahead.sent, behind.sent))
        behind.move(behind.sent)
        ahead.sent, behind.sent = lax.optimization_barrier((ahead.sent, behind.sent))
        enc_far, behind.sent = lax.optimization_barrier((ahead.finish(), behind.sent))
        smalls = sum(jnp.sum(part[:, enc_size:].astype(F32), axis=0) for part in enc_far)
        early = (src_in, src_owner, src_key, tgt_owner, tgt_key, enc_plan, dec_plan, cross_plan, flags)
        src_in, src_owner, src_key, tgt_owner, tgt_key, enc_plan, dec_plan, cross_plan, flags = behind.before(*early)
    else:
        first = core == 0

        def paired(own_rows, size, regions):
            rows = lax.all_gather(own_rows, "fsdp", axis=0, tiled=True)
            rows = arrange_all(rows, size, regions, to_units).reshape(2, OWNERS // 4, 2, -1, width)
            made = []
            for half in range(2):
                even, odd = rows[half, :, 0], rows[half, :, 1]
                made += [jnp.where(first, even, odd), jnp.where(first, odd, even)]
            return made

        enc_far, dec_far = paired(enc_own, enc_size, enc_map), paired(dec_own, dec_size, dec_map)
        smalls = lax.psum(own.astype(F32), "fsdp")

    def enc_part(first, last):
        return row_copies(first, last, enc_count // OWNERS, True)

    def dec_part(first, last):
        return row_copies(first, last, dec_count // OWNERS, True)

    enc_qkv = enc_part(0, 3 * width)
    enc_wo = enc_part(3 * width, 4 * width)
    enc_up = enc_part(4 * width, 4 * width + inner)
    enc_down = enc_part(4 * width + inner, enc_count)
    self_qkv = dec_part(0, 3 * width)
    self_wo = dec_part(3 * width, 4 * width)
    cross_q = dec_part(4 * width, 5 * width)
    cross_kv = dec_part(5 * width, 7 * width)
    cross_wo = dec_part(7 * width, 8 * width)
    dec_up = dec_part(8 * width, 8 * width + inner)
    dec_down = dec_part(8 * width + inner, dec_count)

    start = jnp.where(tgt_mask[:, None] == 1, smalls[10].astype(LOW)[None, :], tgt_in)

    e_q, e_kv, e_ctx, e_lse, e_hat, e_inv, memory, t_hat, t_inv = fwd_block(
        enc_plan, src_in, None, enc_far, (enc_qkv, enc_wo, enc_up, enc_down), True, smalls, 0, src_owner, src_key, True,
        "enc_layer",
    )
    if by_rounds:
        memory = behind.before(memory)
        dec_far = behind.finish()
    s_q, s_kv, s_ctx, s_lse, s_hat, s_inv = fwd_block(
        dec_plan, start, None, dec_far, (self_qkv, self_wo), False, smalls, 4, tgt_owner, tgt_key, False, "dec_block"
    )
    c_q, c_kv, c_lse, decoded, d_two, d_cctx, g_dup, g_ddown, g_cout, sums_d = cross_turn(
        cross_plan, s_hat, memory, dec_cot, dec_far, (cross_kv, cross_wo, cross_q, dec_up, dec_down), smalls, 6,
        tgt_owner, src_key, inner, "cross_turn",
    )

    d_memory, d_one, d_sctx, g_cq, g_ckv, g_sout, sums_c = cross_backward(
        cross_plan, c_q, c_kv, d_cctx, c_lse, tgt_owner, src_key, s_hat, s_inv, d_two, memory, s_ctx, dec_far,
        (cross_kv, cross_q, self_wo), smalls,
    )
    dsq, dsk, dsv, g_sqkv = attention_backward(
        dec_plan, s_q, s_kv, d_sctx, s_lse, tgt_owner, tgt_key, start, "rows", "dec_back"
    )
    dec_pieces = [
        g_sqkv,
        g_sout,
        g_cq,
        g_ckv.reshape(-1, width),
        g_cout,
        g_dup.reshape(-1, width),
        g_ddown,
    ]
    if by_rounds:
        core = core[None].astype(jnp.int32)
        copies = overlaps([p.shape[0] for p in dec_pieces], dec_size)
        send, keep = pack(core, dec_pieces, copies, dec_size, "dec_pack")
        rounds = Rounds(reduce_owned(me, send, keep, dec_size // 2))
        dsq, dsk, dsv = rounds.before(dsq, dsk, dsv)
    tgt_grad, mask_sum = qkv_inputs(
        dec_plan, dsq, dsk, dsv, d_one, dec_far, (self_qkv,), flags, "dec_qkv_inputs"
    )
    if by_rounds:
        d_memory, mask_sum = rounds.before(d_memory, mask_sum)
    d_mid, d_ectx, g_up, g_down, g_out, sums_e = ffn_backward(
        enc_plan, [enc_cot, d_memory], (t_hat, t_inv), (e_hat, e_inv), e_ctx, enc_far,
        (enc_up, enc_down, enc_wo), smalls, 0, inner, "enc_ffn_back",
    )
    if by_rounds:
        d_ectx, g_up = rounds.before(d_ectx, g_up)
    deq, dek, dev, g_qkv = attention_backward(
        enc_plan, e_q, e_kv, d_ectx, e_lse, src_owner, src_key, src_in, "units", "enc_back"
    )

    enc_pieces = [g_qkv.reshape(-1, width), g_out, g_up.reshape(-1, width), g_down]
    small_grad = jnp.concatenate([sums_e[:4], sums_c[:2], sums_d[:4], mask_sum[:1]], axis=0)
    small_wire = small_grad.reshape(-1, devices, share).transpose(1, 0, 2).reshape(devices, -1).astype(LOW)
    small_wire = jnp.pad(small_wire, ((0, 0), (0, 16 * width - held))).reshape(devices * 16, width)
    if by_rounds:
        dec_summed = rounds.finish()
        copies = overlaps([p.shape[0] for p in enc_pieces], enc_size)
        copies += [(len(enc_pieces), 16 * i, i, enc_size, 16) for i in range(devices)]
        send, keep = pack(core, enc_pieces + [small_wire], copies, enc_size + 16, "enc_pack")
        rounds = Rounds(reduce_owned(me, send, keep, enc_size // 2 + 16))
        deq, dek, dev = rounds.before(deq, dek, dev)
    src_grad = qkv_inputs(enc_plan, deq, dek, dev, d_mid, enc_far, (enc_qkv,), None, "enc_qkv_inputs")[0]
    if by_rounds:
        enc_summed = rounds.finish()
    else:
        dec_grad = arrange_all(jnp.concatenate(dec_pieces, axis=0), dec_size, dec_map, from_units)
        enc_grad = arrange_all(jnp.concatenate(enc_pieces, axis=0), enc_size, enc_map, from_units)
        enc_wire = jnp.concatenate(
            [enc_grad.reshape(devices, enc_size, width), small_wire.reshape(devices, 16, width)], axis=1
        )
        dec_summed = lax.psum_scatter(dec_grad, "fsdp", scatter_dimension=0, tiled=True).astype(F32)
        enc_summed = lax.psum_scatter(
            enc_wire.reshape(-1, width), "fsdp", scatter_dimension=0, tiled=True
        ).astype(F32)
    small_summed = enc_summed[enc_size:].reshape(-1)[:held].reshape(-1, share)
    enc_summed = arrange_own(enc_summed[:enc_size], me * enc_size, enc_map, from_units)
    dec_summed = arrange_own(dec_summed, me * dec_size, dec_map, from_units)

    part = 1.0 / devices
    enc_summed = enc_summed * part
    dec_summed = dec_summed * part
    small_summed = small_summed * part
    enc_new, enc_first_new, encoder_second_moment_updated = adamw(
        enc_master, enc_summed, enc_first, enc_second
    )
    dec_new, dec_first_new, dec_second_new = adamw(dec_master, dec_summed, dec_first, dec_second)
    small_first_new, small_second_new = moments(small_summed, small_first, small_second)
    return (
        memory,
        decoded,
        src_grad,
        tgt_grad,
        enc_new,
        enc_first_new,
        encoder_second_moment_updated,
        enc_new.astype(LOW),
        dec_new,
        dec_first_new,
        dec_second_new,
        dec_new.astype(LOW),
        small_summed,
        small_first_new,
        small_second_new,
    )


def solution(mesh):
    rows = P("fsdp", None)
    columns = P(None, "fsdp")
    return jax.shard_map(
        functools.partial(on_device, mesh.shape["fsdp"]),
        mesh=mesh,
        in_specs=(rows,) * 4 + (P("fsdp"),) + (rows,) * 8 + (columns,) * 3,
        out_specs=(rows,) * 12 + (columns,) * 3,
        check_vma=False,
    )
```

```python
import functools

import jax
import jax.numpy as jnp
from jax import lax
from jax.experimental import pallas as pl
from jax.experimental.pallas import tpu as pltpu
from jax.sharding import PartitionSpec as P

HEADS = 8
HEAD = 64
STEPS = 7
TILE = 256
LANES = 128

rate = 0.02
beta_one = 0.9
beta_two = 0.98
epsilon = 1e-06
decay = 0.01
floor_value = -1000000000.0
root_half = 0.7071067811865476
inverse_root_tau = 0.3989422804014327

F32 = jnp.float32
LOW = jnp.bfloat16
MIB = 2**20


def nn(former, latter):
    return lax.dot_general(
        former, latter, (((1,), (0,)), ((), ())), preferred_element_type=F32
    )


def nt(former, latter):
    return lax.dot_general(
        former, latter, (((1,), (1,)), ((), ())), preferred_element_type=F32
    )


def turned(values):
    return values.astype(F32).T.astype(LOW)


def column_of(row):
    return jnp.broadcast_to(row, (8, row.shape[1])).T[:, 0:1]


def ln_forward(values, gain, shift):
    centered = values - jnp.mean(values, axis=-1, keepdims=True)
    spread = jnp.mean(centered * centered, axis=-1, keepdims=True)
    inverse = lax.rsqrt(spread + 1e-05)
    normed = centered * inverse
    return normed * gain + shift, normed, inverse


def ln_backward(upstream, normed, inverse, gain):
    scaled = upstream * gain
    first = jnp.mean(scaled, axis=-1, keepdims=True)
    second = jnp.mean(scaled * normed, axis=-1, keepdims=True)
    return inverse * (scaled - first - normed * second)


def phi_and_slope(values):
    phi = 0.5 + 0.5 * lax.erf(values * root_half)
    return phi, phi + values * (jnp.exp(-0.5 * (values * values)) * inverse_root_tau)


def one_head(pair, head):
    lane = lax.broadcasted_iota(jnp.int32, pair.shape, 1)
    keep = lane < HEAD if head % 2 == 0 else lane >= HEAD
    return jnp.where(keep, pair, jnp.zeros_like(pair))


def pair_columns(head):
    return slice(LANES * (head // 2), LANES * (head // 2) + LANES)


def head_rows(head):
    return slice(HEAD * head, HEAD * head + HEAD)


def block_of(ref, j, count):
    if count == 1:
        return ref[...]
    return jnp.concatenate(
        [ref[first + 16 * j : first + 16 * j + 16, :] for first in range(0, ref.shape[0], 16 * count)], axis=0
    )


def spread(wide, values):
    for n in range(wide.shape[0]):
        wide[n] = values[:, LANES * n : LANES * n + LANES].astype(F32)


def third_rows(wide, j):
    rows = pl.ds(j, wide.shape[1] // 3, stride=3)
    return jnp.concatenate([wide[n, rows, :] for n in range(wide.shape[0])], axis=1).astype(LOW)


def put_third_rows(wide, j, values):
    rows = pl.ds(j, wide.shape[1] // 3, stride=3)
    for n in range(wide.shape[0]):
        wide[n, rows, :] = values[:, LANES * n : LANES * n + LANES]


def wide_scratch(width):
    return pltpu.VMEM((width // LANES, 3 * width, LANES), F32)


def put_block(ref, j, values):
    ref[:, j] = values.reshape(ref.shape[0], ref.shape[2], ref.shape[3])


OWNERS = 32


def row_copies(first, last, own, paired):
    found = []
    at = first
    while at < last:
        owner = at // own
        end = min(last, (owner + 1) * own)
        half = OWNERS // 4
        place = (2 * (owner // 2 // half) + owner % 2, owner // 2 % half) if paired else (0, owner)
        found.append((*place, at - owner * own, end - at, at - first))
        at = end
    return found


class Fetch:
    def __init__(self, far, core, copies, near, semaphores, used):
        self.core = core

        def handles(side):
            return [
                pltpu.make_async_copy(
                    far[source ^ side].at[owner, pl.ds(row, rows)], near.at[pl.ds(to, rows)], semaphores.at[used + n]
                )
                for n, (source, owner, row, rows, to) in enumerate(copies)
            ]

        self.handles = handles

    def start(self):
        if self.core is None:
            for handle in self.handles(0):
                handle.start()
            return
        for side in (0, 1):

            @pl.when(self.core == side)
            def _(side=side):
                for handle in self.handles(side):
                    handle.start()

    def wait(self):
        for handle in self.handles(0):
            handle.wait()


def fetches(far, plan, wanted, nears, semaphores):
    used = 0
    made = []
    core = plan[2, 1] if len(far) > 1 else None
    for copies, near in zip(wanted, nears):
        made.append(Fetch(far, core, copies, near, semaphores, used))
        used += len(copies)
    return made


def wait_first(i, loads):
    @pl.when(i == 0)
    def _():
        for load in loads:
            load.wait()


def fetch_scratch(wanted, width):
    return [pltpu.VMEM((sum(c[3] for c in copies), width), LOW) for copies in wanted] + [
        pltpu.SemaphoreType.DMA((sum(len(copies) for copies in wanted),))
    ]


FAR = pl.BlockSpec(memory_space=pl.ANY)


def sources_of(wanted):
    last = max(copy[0] for copies in wanted for copy in copies)
    return 1 if last == 0 else 2 * (last // 2) + 2


def call(kernel, grid, in_specs, out_specs, out_shape, scratch, flops, moved, name, room=24, near=(), keep=()):
    single = not isinstance(out_shape, list)
    shapes = [
        (pltpu.VMEM if keep is True or n in keep else pltpu.HBM)(*made)
        for n, made in enumerate([out_shape] if single else out_shape)
    ]
    made = pl.pallas_call(
        kernel,
        grid_spec=pltpu.PrefetchScalarGridSpec(
            num_scalar_prefetch=1,
            grid=grid,
            in_specs=in_specs,
            out_specs=out_specs,
            scratch_shapes=scratch,
        ),
        out_shape=shapes[0] if single else shapes,
        compiler_params=pltpu.CompilerParams(vmem_limit_bytes=room * MIB),
        cost_estimate=pl.CostEstimate(
            flops=flops, bytes_accessed=moved, transcendentals=0
        ),
        name=name,
    )

    def run(plan, *operands):
        placed = [
            operand
            if near is True or n in near
            else pltpu.with_memory_space_constraint(operand, pltpu.HBM)
            for n, operand in enumerate(operands)
        ]
        return made(plan, *placed)

    return run


def whole(shape):
    zeros = (0,) * len(shape)
    return pl.BlockSpec(shape, lambda i, *_: zeros)


def rows_of(width):
    return pl.BlockSpec((TILE, width), lambda i, *_: (i, 0))


def at_block(shape, *index):
    return pl.BlockSpec(shape, lambda i, *_: index)


def shaped(shape, kind):
    return (shape, kind)


def attend_tile(plan, i, keys, key_cols, query, owner_row, key_owner, vt, sc):
    scores, acc, top, total, masked_q = sc
    query = query * jnp.asarray(HEAD**-0.5, LOW)
    for h in range(HEADS):
        masked_q[h] = one_head(query[:, pair_columns(h)], h)
    top[...] = jnp.full_like(top, -1e30)
    total[...] = jnp.zeros_like(total)
    acc[...] = jnp.zeros_like(acc)
    begin = plan[0, i]
    chunks = plan[1, i]

    def score_tile(j, carry):
        rows = pl.ds(pl.multiple_of(begin + j * TILE, LANES), TILE)
        bias = jnp.where(key_owner[rows, 0:1] == owner_row, 0.0, floor_value)
        tops = []
        for h in range(HEADS):
            cols = pl.ds(key_cols + LANES * (h // 2), LANES)
            s = nt(keys[rows, cols], masked_q[h]) + bias
            scores[j, h] = s
            tops.append(jnp.max(s, axis=0, keepdims=True))
        top[...] = jnp.maximum(top[...], jnp.concatenate(tops, axis=0))
        return carry

    lax.fori_loop(0, chunks, score_tile, 0)

    def weigh_tile(j, carry):
        rows = pl.ds(pl.multiple_of(begin + j * TILE, LANES), TILE)
        sums = []
        for h in range(HEADS):
            p = jnp.exp(scores[j, h] - top[h : h + 1, :])
            sums.append(jnp.sum(p, axis=0, keepdims=True))
            acc[head_rows(h), :] += nn(vt[head_rows(h), rows], p.astype(LOW))
        total[...] += jnp.concatenate(sums, axis=0)
        return carry

    lax.fori_loop(0, chunks, weigh_tile, 0)


def fwd_block_kernel(plan, *refs, cross, gain_row, wanted, packed, ffn):
    refs = list(refs)

    def next_refs(count):
        taken = refs[:count]
        del refs[:count]
        return taken

    if cross:
        normed_in, memory = next_refs(2)
    else:
        (x_all,) = next_refs(1)
    far = next_refs(sources_of(wanted))
    small, owner_q, owner_k = next_refs(3)
    q_out, kv_out, ctx_out, lse_out, normed_out, inverse_out = next_refs(6)
    if ffn:
        out, normed_last, inverse_last = next_refs(3)
    kv, vt, mean_v, key_owner, scores, acc, top, total, masked_q, q_all = next_refs(10)
    nears = next_refs(len(wanted))
    semaphores = refs.pop(0)
    loads = fetches(far, plan, wanted, nears, semaphores)
    i = pl.program_id(0)
    width = kv.shape[1] // 2

    @pl.when(i == 0)
    def _():
        for load in loads:
            load.start()
        key_owner[...] = jnp.broadcast_to(owner_k[...], (8, owner_k.shape[1])).T
        loads[0].wait()
        if cross:
            wk, wv = block_of(nears[0], 0, 2), block_of(nears[0], 1, 2)
        elif packed:
            wq, wk, wv = (block_of(nears[0], j, 3) for j in range(3))
        else:
            wide = refs[0]
            spread(wide, nears[0][...])
            wq, wk, wv = (third_rows(wide, j) for j in range(3))
        sums = jnp.zeros((1, width), F32)
        for t in range(kv.shape[0] // TILE):
            rows = slice(t * TILE, t * TILE + TILE)
            x = memory[rows, :] if cross else x_all[rows, :]
            if not cross:
                q_all[rows, :] = nn(x, wq).astype(LOW)
            kv[rows, :width] = nn(x, wk).astype(LOW)
            v = nn(x, wv).astype(LOW)
            kv[rows, width:] = v
            v = v.astype(F32)
            vt[:, rows] = v.T.astype(LOW)
            sums = sums + jnp.sum(v, axis=0, keepdims=True)
        mean_v[...] = sums * (1.0 / kv.shape[0])
        for load in loads[1 : 3 if cross else 2]:
            load.wait()

    wo = nears[1]
    mine = pl.ds(pl.multiple_of(i * TILE, TILE), TILE)
    if cross:
        resid = normed_in[...] * small[4:5, :] + small[5:6, :]
        query = nn(resid.astype(LOW), nears[2][...]).astype(LOW)
        q_out[...] = query
    else:
        resid = x_all[mine, :].astype(F32)
        query = q_all[mine, :]
        q_out[...] = query
    kv_out[...] = kv[mine, :]
    owner_row = owner_q[...]
    attend_tile(plan, i, kv, 0, query, owner_row, key_owner, vt, (scores, acc, top, total, masked_q))
    dead = owner_row < 0
    sums = jnp.where(dead, 1.0, total[...])
    share = 1.0 / sums
    lse_out[...] = jnp.where(dead, 0.0, top[...] + jnp.log(sums))
    for h in range(HEADS):
        acc[head_rows(h), :] = acc[head_rows(h), :] * share[h : h + 1, :]
    live = column_of(owner_row) >= 0
    context = jnp.where(live, acc[...].T, mean_v[...]).astype(LOW)
    ctx_out[...] = context
    added = nn(context, wo[...]) * live.astype(F32)
    mid, normed, inverse = ln_forward(
        resid + added, small[gain_row : gain_row + 1, :], small[gain_row + 1 : gain_row + 2, :]
    )
    normed_out[...] = normed
    inverse_out[...] = jnp.broadcast_to(inverse, inverse_out.shape)
    if ffn:
        wup, wdown = nears[-2:]
        wait_first(i, loads[-2:])
        blocks = wdown.shape[0] // width
        low = mid.astype(LOW)
        result = mid
        for j in range(blocks):
            inner = nn(low, block_of(wup, j, blocks))
            phi = 0.5 + 0.5 * lax.erf(inner * root_half)
            result = result + nn((inner * phi).astype(LOW), wdown[j * width : j * width + width, :])
        result, normed, inverse = ln_forward(
            result, small[gain_row + 2 : gain_row + 3, :], small[gain_row + 3 : gain_row + 4, :]
        )
        out[...] = result.astype(LOW)
        normed_last[...] = normed
        inverse_last[...] = jnp.broadcast_to(inverse, inverse_last.shape)


def attention_scratch(keys, width):
    return [
        pltpu.VMEM((keys, 2 * width), LOW),
        pltpu.VMEM((width, keys), LOW),
        pltpu.VMEM((1, width), F32),
        pltpu.VMEM((keys, 8), F32),
        pltpu.VMEM((keys // TILE, HEADS, TILE, TILE), F32),
        pltpu.VMEM((width, TILE), F32),
        pltpu.VMEM((HEADS, TILE), F32),
        pltpu.VMEM((HEADS, TILE), F32),
        pltpu.VMEM((HEADS, TILE, LANES), LOW),
        pltpu.VMEM((keys, width), LOW),
    ]


def block_outs(queries, width):
    specs = [
        rows_of(width),
        rows_of(2 * width),
        rows_of(width),
        pl.BlockSpec((HEADS, TILE), lambda i, *_: (0, i)),
        rows_of(width),
        rows_of(LANES),
    ]
    shapes = [
        shaped((queries, width), LOW),
        shaped((queries, 2 * width), LOW),
        shaped((queries, width), LOW),
        shaped((HEADS, queries), F32),
        shaped((queries, width), F32),
        shaped((queries, LANES), F32),
    ]
    return specs, shapes


def owner_specs(keys):
    return [pl.BlockSpec((1, TILE), lambda i, *_: (0, i)), whole((1, keys))]


def fwd_block(plan, x, memory, far, wanted, packed, small, gain_row, owner, key_owner, ffn, name):
    cross = memory is not None
    number, width = x.shape
    specs, shapes = block_outs(number, width)
    if ffn:
        specs += [rows_of(width), rows_of(width), rows_of(LANES)]
        shapes += [shaped((number, width), LOW), shaped((number, width), F32), shaped((number, LANES), F32)]
    scratch = attention_scratch(number, width) + fetch_scratch(wanted, width)
    if not cross and not packed:
        scratch.append(wide_scratch(width))
    return call(
        functools.partial(
            fwd_block_kernel, cross=cross, gain_row=gain_row, wanted=wanted, packed=packed, ffn=ffn
        ),
        (number // TILE,),
        ([rows_of(width), whole(memory.shape)] if cross else [whole(x.shape)])
        + [FAR] * sources_of(wanted)
        + [whole(small.shape)]
        + owner_specs(number),
        specs,
        shapes,
        scratch,
        8 * number * width * width + number * number * width * 2,
        16 * number * width,
        name,
        room=44,
    )(plan, *([x, memory] if cross else [x]), *far[: sources_of(wanted)], small, owner, key_owner)


def ffn_back_kernel(plan, *refs, tiles, summed, gain_row, wanted):
    refs = list(refs)
    cot = refs.pop(0)
    extra = refs.pop(0) if summed else None
    normed_top, inverse_top, normed_mid, inverse_mid, context = refs[:5]
    far = refs[5 : 5 + sources_of(wanted)]
    (small,
     d_sum, d_context, g_up, g_down, g_out, sums, hidden, d_inner, mid_low, d_down, d_product,
     wup, wdown, wo, semaphores) = refs[5 + sources_of(wanted) :]
    loads = fetches(far, plan, wanted, (wup, wdown, wo), semaphores)
    i = pl.program_id(0)
    width = small.shape[1]
    blocks = wdown.shape[0] // width

    @pl.when(i == 0)
    def _():
        for load in loads:
            load.start()
        sums[...] = jnp.zeros_like(sums)

    @pl.when(i < tiles)
    def _():
        mine = pl.ds(pl.multiple_of(i * TILE, TILE), TILE)
        upstream = cot[...].astype(F32)
        if summed:
            upstream = upstream + extra[...]
        top = normed_top[...]
        sums[2:3, :] += jnp.sum(upstream * top, axis=0, keepdims=True)
        sums[3:4, :] += jnp.sum(upstream, axis=0, keepdims=True)
        d_mid = ln_backward(upstream, top, inverse_top[:, 0:1], small[gain_row + 2 : gain_row + 3, :])
        low = d_mid.astype(LOW)
        d_down[mine, :] = low
        normed = normed_mid[...]
        mid = (normed * small[gain_row : gain_row + 1, :] + small[gain_row + 1 : gain_row + 2, :]).astype(LOW)
        mid_low[mine, :] = mid
        wait_first(i, loads)
        for j in range(blocks):
            cols = slice(j * width, j * width + width)
            up = block_of(wup, j, blocks)
            inner = nn(mid, up)
            phi, slope = phi_and_slope(inner)
            hidden[j, mine, :] = (inner * phi).astype(LOW)
            part = (nt(low, wdown[cols, :]) * slope).astype(LOW)
            d_inner[j, mine, :] = part
            d_mid = d_mid + nt(part, up)
        sums[0:1, :] += jnp.sum(d_mid * normed, axis=0, keepdims=True)
        sums[1:2, :] += jnp.sum(d_mid, axis=0, keepdims=True)
        total = ln_backward(d_mid, normed, inverse_mid[:, 0:1], small[gain_row : gain_row + 1, :])
        d_sum[...] = total
        place = lax.broadcasted_iota(jnp.int32, (TILE, 1), 0) + i * TILE
        live = (place < plan[2, 0]).astype(F32)
        product = (total * live).astype(LOW)
        d_product[mine, :] = product
        d_context[...] = nt(product, wo[...]).astype(LOW)

    @pl.when(i >= tiles)
    def _():
        j = i - tiles
        put_block(g_up, 0, nn(turned(mid_low[...]), d_inner[j]).astype(LOW))
        g_down[...] = nn(turned(hidden[j]), d_down[...]).astype(LOW)

    @pl.when(i == tiles)
    def _():
        g_out[...] = nn(turned(context[...]), d_product[...]).astype(LOW)


def ffn_backward(plan, cots, top, mid, context, far, wanted, small, gain_row, inner, name):
    number, width = mid[0].shape
    tiles, blocks = number // TILE, inner // width

    def tile_of(columns):
        return pl.BlockSpec((TILE, columns), lambda i, *_: (jnp.minimum(i, tiles - 1), 0))

    return call(
        functools.partial(
            ffn_back_kernel, tiles=tiles, summed=len(cots) == 2, gain_row=gain_row, wanted=wanted
        ),
        (tiles + blocks,),
        [tile_of(width)] * len(cots)
        + [tile_of(width), tile_of(LANES), tile_of(width), tile_of(LANES), whole((number, width))]
        + [FAR] * sources_of(wanted)
        + [whole(small.shape)],
        [
            tile_of(width),
            tile_of(width),
            pl.BlockSpec((width // 16, 1, 16, width), lambda i, *_: (0, jnp.maximum(i - tiles, 0), 0, 0)),
            pl.BlockSpec((width, width), lambda i, *_: (jnp.maximum(i - tiles, 0), 0)),
            pl.BlockSpec((width, width), lambda i, *_: (0, 0)),
            pl.BlockSpec((8, width), lambda i, *_: (0, 0)),
        ],
        [
            shaped((number, width), F32),
            shaped((number, width), LOW),
            shaped((width // 16, blocks, 16, width), LOW),
            shaped((inner, width), LOW),
            shaped((width, width), LOW),
            shaped((8, width), F32),
        ],
        [
            pltpu.VMEM((blocks, number, width), LOW),
            pltpu.VMEM((blocks, number, width), LOW),
            pltpu.VMEM((number, width), LOW),
            pltpu.VMEM((number, width), LOW),
            pltpu.VMEM((number, width), LOW),
        ]
        + fetch_scratch(wanted, width),
        10 * number * width * inner,
        30 * number * width,
        name,
        room=44,
    )(plan, *cots, *top, *mid, context, *far[: sources_of(wanted)], small)


def turn_kernel(plan, *refs, tiles, gain_row, wanted):
    normed_in, memory, cot = refs[:3]
    far = refs[3 : 3 + sources_of(wanted)]
    (small, owner_q, owner_k,
     q_out, kv_out, lse_out, out, d_sum, d_context, g_up, g_down, g_out, sums,
     kv, vt, mean_v, key_owner, scores, acc, top, total, masked_q,
     hidden, d_inner, mid_low, d_down, d_product, contexts, slopes,
     *nears, semaphores) = refs[3 + sources_of(wanted) :]
    wkv, wo, wq, wup, wdown = nears
    loads = fetches(far, plan, wanted, nears, semaphores)
    i = pl.program_id(0)
    width = small.shape[1]
    blocks = wdown.shape[0] // width

    @pl.when(i == 0)
    def _():
        for load in loads:
            load.start()
        sums[...] = jnp.zeros_like(sums)
        key_owner[...] = jnp.broadcast_to(owner_k[...], (8, owner_k.shape[1])).T
        loads[0].wait()
        wk, wv = block_of(wkv, 0, 2), block_of(wkv, 1, 2)
        means = jnp.zeros((1, width), F32)
        for t in range(kv.shape[0] // TILE):
            rows = slice(t * TILE, t * TILE + TILE)
            x = memory[rows, :]
            kv[rows, :width] = nn(x, wk).astype(LOW)
            v = nn(x, wv).astype(LOW)
            kv[rows, width:] = v
            v = v.astype(F32)
            vt[:, rows] = v.T.astype(LOW)
            means = means + jnp.sum(v, axis=0, keepdims=True)
        mean_v[...] = means * (1.0 / kv.shape[0])
        for load in loads[1:3]:
            load.wait()

    @pl.when(i < tiles)
    def _():
        mine = pl.ds(pl.multiple_of(i * TILE, TILE), TILE)
        resid = normed_in[...] * small[gain_row - 2 : gain_row - 1, :] + small[gain_row - 1 : gain_row, :]
        query = nn(resid.astype(LOW), wq[...]).astype(LOW)
        q_out[...] = query
        kv_out[...] = kv[mine, :]
        owner_row = owner_q[...]
        attend_tile(
            plan, i, kv, 0, query, owner_row, key_owner, vt, (scores, acc, top, total, masked_q)
        )
        dead = owner_row < 0
        weighed = jnp.where(dead, 1.0, total[...])
        share = 1.0 / weighed
        lse_out[...] = jnp.where(dead, 0.0, top[...] + jnp.log(weighed))
        for h in range(HEADS):
            acc[head_rows(h), :] = acc[head_rows(h), :] * share[h : h + 1, :]
        live = column_of(owner_row) >= 0
        context = jnp.where(live, acc[...].T, mean_v[...]).astype(LOW)
        contexts[mine, :] = context
        added = nn(context, wo[...]) * live.astype(F32)
        mid, normed_mid, inverse_mid = ln_forward(
            resid + added, small[gain_row : gain_row + 1, :], small[gain_row + 1 : gain_row + 2, :]
        )
        wait_first(i, loads[3:])
        low = mid.astype(LOW)
        mid_low[mine, :] = low
        result = mid
        for j in range(blocks):
            inner = nn(low, block_of(wup, j, blocks))
            phi, slope = phi_and_slope(inner)
            made = (inner * phi).astype(LOW)
            hidden[j, mine, :] = made
            slopes[j] = slope
            result = result + nn(made, wdown[j * width : j * width + width, :])
        result, normed, inverse = ln_forward(
            result, small[gain_row + 2 : gain_row + 3, :], small[gain_row + 3 : gain_row + 4, :]
        )
        out[...] = result.astype(LOW)

        upstream = cot[...].astype(F32)
        sums[2:3, :] += jnp.sum(upstream * normed, axis=0, keepdims=True)
        sums[3:4, :] += jnp.sum(upstream, axis=0, keepdims=True)
        d_mid = ln_backward(upstream, normed, inverse, small[gain_row + 2 : gain_row + 3, :])
        low = d_mid.astype(LOW)
        d_down[mine, :] = low
        for j in range(blocks):
            part = (nt(low, wdown[j * width : j * width + width, :]) * slopes[j]).astype(LOW)
            d_inner[j, mine, :] = part
            d_mid = d_mid + nt(part, block_of(wup, j, blocks))
        sums[0:1, :] += jnp.sum(d_mid * normed_mid, axis=0, keepdims=True)
        sums[1:2, :] += jnp.sum(d_mid, axis=0, keepdims=True)
        d_all = ln_backward(d_mid, normed_mid, inverse_mid, small[gain_row : gain_row + 1, :])
        d_sum[...] = d_all
        product = (d_all * live.astype(F32)).astype(LOW)
        d_product[mine, :] = product
        d_context[...] = nt(product, wo[...]).astype(LOW)

    @pl.when(i >= tiles)
    def _():
        j = i - tiles
        put_block(g_up, 0, nn(turned(mid_low[...]), d_inner[j]).astype(LOW))
        g_down[...] = nn(turned(hidden[j]), d_down[...]).astype(LOW)

    @pl.when(i == tiles)
    def _():
        g_out[...] = nn(turned(contexts[...]), d_product[...]).astype(LOW)


def cross_turn(plan, normed, memory, cot, far, wanted, small, gain_row, owner, key_owner, inner, name):
    number, width = normed.shape
    keys = memory.shape[0]
    tiles, blocks = number // TILE, inner // width

    def tile_of(columns):
        return pl.BlockSpec((TILE, columns), lambda i, *_: (jnp.minimum(i, tiles - 1), 0))

    def columns_of(rows):
        return pl.BlockSpec((rows, TILE), lambda i, *_: (0, jnp.minimum(i, tiles - 1)))

    return call(
        functools.partial(turn_kernel, tiles=tiles, gain_row=gain_row, wanted=wanted),
        (tiles + blocks,),
        [tile_of(width), whole(memory.shape), tile_of(width)]
        + [FAR] * sources_of(wanted)
        + [whole(small.shape), columns_of(1), whole((1, keys))],
        [
            tile_of(width),
            tile_of(2 * width),
            columns_of(HEADS),
            tile_of(width),
            tile_of(width),
            tile_of(width),
            pl.BlockSpec((width // 16, 1, 16, width), lambda i, *_: (0, jnp.maximum(i - tiles, 0), 0, 0)),
            pl.BlockSpec((width, width), lambda i, *_: (jnp.maximum(i - tiles, 0), 0)),
            whole((width, width)),
            whole((8, width)),
        ],
        [
            shaped((number, width), LOW),
            shaped((number, 2 * width), LOW),
            shaped((HEADS, number), F32),
            shaped((number, width), LOW),
            shaped((number, width), F32),
            shaped((number, width), LOW),
            shaped((width // 16, blocks, 16, width), LOW),
            shaped((inner, width), LOW),
            shaped((width, width), LOW),
            shaped((8, width), F32),
        ],
        attention_scratch(keys, width)[:-1]
        + [
            pltpu.VMEM((blocks, number, width), LOW),
            pltpu.VMEM((blocks, number, width), LOW),
            pltpu.VMEM((number, width), LOW),
            pltpu.VMEM((number, width), LOW),
            pltpu.VMEM((number, width), LOW),
            pltpu.VMEM((number, width), LOW),
            pltpu.VMEM((blocks, TILE, width), F32),
        ]
        + fetch_scratch(wanted, width),
        12 * number * width * inner + number * number * width * 2,
        30 * number * width,
        name,
        room=58,
    )(plan, normed, memory, cot, *far[: sources_of(wanted)], small, owner, key_owner)


def attend_back(plan, i, q_ref, k_ref, v_ref, do_ref, lse, owner_q, owner_k, scratch):
    kt, key_owner, masked_q, masked_do, dqt, dk_sum, dv_sum, weights, d_weights, dots = scratch

    @pl.when(i == 0)
    def _():
        key_owner[...] = jnp.broadcast_to(owner_k[...], (8, owner_k.shape[1])).T
        kt[...] = turned(k_ref[...])
        dk_sum[...] = jnp.zeros_like(dk_sum)
        dv_sum[...] = jnp.zeros_like(dv_sum)

    query = q_ref[...] * jnp.asarray(HEAD**-0.5, LOW)
    upstream = do_ref[...]
    for h in range(HEADS):
        masked_q[h] = one_head(query[:, pair_columns(h)], h)
        masked_do[h] = one_head(upstream[:, pair_columns(h)], h)
    dqt[...] = jnp.zeros_like(dqt)
    dots[...] = jnp.zeros_like(dots)
    owner_row = owner_q[...]
    begin = plan[0, i]
    chunks = plan[1, i]

    def weigh_tile(j, carry):
        rows = pl.ds(pl.multiple_of(begin + j * TILE, LANES), TILE)
        bias = jnp.where(key_owner[rows, 0:1] == owner_row, 0.0, floor_value)
        sums = []
        for h in range(HEADS):
            s = nt(k_ref[rows, pair_columns(h)], masked_q[h])
            p = jnp.exp((s - lse[h : h + 1, :]) + bias)
            dp = nt(v_ref[rows, pair_columns(h)], masked_do[h])
            weights[j, h] = p
            d_weights[j, h] = dp
            sums.append(jnp.sum(p * dp, axis=0, keepdims=True))
        dots[...] += jnp.concatenate(sums, axis=0)
        return carry

    lax.fori_loop(0, chunks, weigh_tile, 0)

    def grad_tile(j, carry):
        rows = pl.ds(pl.multiple_of(begin + j * TILE, LANES), TILE)
        for pair in range(HEADS // 2):
            cols = pair_columns(2 * pair)
            dv_part = dv_sum[rows, cols]
            dk_part = dk_sum[rows, cols]
            for h in (2 * pair, 2 * pair + 1):
                p = weights[j, h]
                ds = (p * (d_weights[j, h] - dots[h : h + 1, :])).astype(LOW)
                dv_part = dv_part + nn(p.astype(LOW), masked_do[h])
                dk_part = dk_part + nn(ds, masked_q[h])
                dqt[head_rows(h), :] += nn(kt[head_rows(h), rows], ds)
            dv_sum[rows, cols] = dv_part
            dk_sum[rows, cols] = dk_part
        return carry

    lax.fori_loop(0, chunks, grad_tile, 0)
    return (dqt[...] * HEAD**-0.5).T.astype(LOW)


def attention_back_kernel(plan, *refs, made):
    q_ref, k_ref, v_ref, do_ref, lse, owner_q, owner_k, *refs = refs
    x = refs.pop(0) if made else None
    dq, dk, dv, *refs = refs
    g_qkv = refs.pop(0) if made else None
    scratch, more = refs[:10], refs[10:]
    dk_sum, dv_sum = scratch[5:7]
    i = pl.program_id(0)
    dq_tile = attend_back(plan, i, q_ref, k_ref, v_ref, do_ref, lse, owner_q, owner_k, scratch)
    dq[...] = dq_tile
    if made:
        dq_all = more[0]
        dq_all[pl.ds(pl.multiple_of(i * TILE, TILE), TILE), :] = dq_tile

    @pl.when(i == pl.num_programs(0) - 1)
    def _():
        dk[...] = dk_sum[...].astype(LOW)
        dv[...] = dv_sum[...].astype(LOW)
        if made:
            turn = turned(x[...])
            for j, ref in enumerate((dq_all, dk, dv)):
                grad = nn(turn, ref[...])
                if made == "units":
                    put_block(g_qkv, j, grad.astype(LOW))
                else:
                    put_third_rows(more[1], j, grad)
        if made == "rows":
            for n in range(more[1].shape[0]):
                g_qkv[:, LANES * n : LANES * n + LANES] = more[1][n].astype(LOW)


def attend_back_scratch(keys, width):
    return [
        pltpu.VMEM((width, keys), LOW),
        pltpu.VMEM((keys, 8), F32),
        pltpu.VMEM((HEADS, TILE, LANES), LOW),
        pltpu.VMEM((HEADS, TILE, LANES), LOW),
        pltpu.VMEM((width, TILE), F32),
        pltpu.VMEM((keys, width), F32),
        pltpu.VMEM((keys, width), F32),
        pltpu.VMEM((keys // TILE, HEADS, TILE, TILE), F32),
        pltpu.VMEM((keys // TILE, HEADS, TILE, TILE), F32),
        pltpu.VMEM((HEADS, TILE), F32),
    ]


def attention_backward(plan, q, kv, d_context, lse, owner, key_owner, x, made, name):
    number, width = q.shape
    keys = kv.shape[0]
    in_specs = [
        rows_of(width),
        at_block((keys, width), 0, 0),
        at_block((keys, width), 0, 1),
        rows_of(width),
        pl.BlockSpec((HEADS, TILE), lambda i, *_: (0, i)),
    ] + owner_specs(keys)
    out_specs = [rows_of(width), whole((keys, width)), whole((keys, width))]
    out_shape = [shaped((number, width), LOW), shaped((keys, width), LOW), shaped((keys, width), LOW)]
    operands = [q, kv, kv, d_context, lse, owner, key_owner]
    scratch = attend_back_scratch(keys, width)
    if made:
        shape = (width // 16, 3, 16, width) if made == "units" else (3 * width, width)
        in_specs.append(whole(x.shape))
        operands.append(x)
        out_specs.append(whole(shape))
        out_shape.append(shaped(shape, LOW))
        scratch.append(pltpu.VMEM((number, width), LOW))
        if made == "rows":
            scratch.append(wide_scratch(width))
    return call(
        functools.partial(attention_back_kernel, made=made),
        (number // TILE,),
        in_specs,
        out_specs,
        out_shape,
        scratch,
        number * keys * width * 4 + (6 * number * width * width if made else 0),
        12 * number * width,
        name,
        room=52,
    )(plan, *operands)


def cross_back_kernel(plan, *refs, wanted, tiles):
    attention, refs = refs[:7], refs[7:]
    normed, inverse, d_above, memory, context = refs[:5]
    far = refs[5 : 5 + sources_of(wanted)]
    small, d_memory, d_sum, d_context, g_query, g_pair, g_out, sums, *refs = refs[5 + sources_of(wanted) :]
    scratch, refs = refs[:10], refs[10:]
    d_query, dk, dv, d_product, wkv, wq, wo, semaphores = refs
    dk_sum, dv_sum = scratch[5:7]
    loads = fetches(far, plan, wanted, (wkv, wq, wo), semaphores)
    i = pl.program_id(0)

    @pl.when(i == 0)
    def _():
        for load in loads:
            load.start()
        sums[...] = jnp.zeros_like(sums)

    @pl.when(i < tiles)
    def _():
        d_query[pl.ds(pl.multiple_of(i * TILE, TILE), TILE), :] = attend_back(plan, i, *attention, scratch)

    @pl.when(i == tiles)
    def _():
        dk[...] = dk_sum[...].astype(LOW)
        dv[...] = dv_sum[...].astype(LOW)
        for load in loads:
            load.wait()
        low = normed[...] * small[4:5, :] + small[5:6, :]
        g_query[...] = nn(low.T.astype(LOW), d_query[...]).astype(LOW)

    @pl.when(i >= tiles)
    def _():
        row = pl.multiple_of((i - tiles) * TILE, TILE)
        mine = pl.ds(row, TILE)
        wk, wv = block_of(wkv, 0, 2), block_of(wkv, 1, 2)
        d_memory[...] = nt(dk[mine, :], wk) + nt(dv[mine, :], wv)
        d_one = d_above[...] + nt(d_query[mine, :], wq[...])
        hat = normed[mine, :]
        sums[0:1, :] += jnp.sum(d_one * hat, axis=0, keepdims=True)
        sums[1:2, :] += jnp.sum(d_one, axis=0, keepdims=True)
        total = ln_backward(d_one, hat, inverse[:, 0:1], small[4:5, :])
        d_sum[...] = total
        place = lax.broadcasted_iota(jnp.int32, (TILE, 1), 0) + row
        live = (place < plan[2, 0]).astype(F32)
        product = (total * live).astype(LOW)
        d_product[mine, :] = product
        d_context[...] = nt(product, wo[...]).astype(LOW)

    @pl.when(i == tiles + 1)
    def _():
        put_block(g_pair, 0, nn(turned(memory[...]), dk[...]).astype(LOW))

    @pl.when(i == tiles + 2)
    def _():
        put_block(g_pair, 1, nn(turned(memory[...]), dv[...]).astype(LOW))

    @pl.when(i == 2 * tiles - 1)
    def _():
        g_out[...] = nn(turned(context[...]), d_product[...]).astype(LOW)


def cross_backward(plan, q, kv, d_context, lse, owner, key_owner, normed, inverse, d_above, memory, context, far,
                   wanted, small):
    number, width = normed.shape
    keys = kv.shape[0]
    tiles = number // TILE
    full = whole((number, width))

    def first_rows(columns):
        return pl.BlockSpec((TILE, columns), lambda i, *_: (jnp.minimum(i, tiles - 1), 0))

    def first_columns(rows):
        return pl.BlockSpec((rows, TILE), lambda i, *_: (0, jnp.minimum(i, tiles - 1)))

    def later_rows(columns):
        return pl.BlockSpec((TILE, columns), lambda i, *_: (jnp.maximum(i - tiles, 0), 0))

    return call(
        functools.partial(cross_back_kernel, wanted=wanted, tiles=tiles),
        (2 * tiles,),
        [first_rows(width), at_block((keys, width), 0, 0), at_block((keys, width), 0, 1), first_rows(width),
         first_columns(HEADS), first_columns(1), whole((1, keys)),
         full, later_rows(LANES), later_rows(width), whole(memory.shape), full]
        + [FAR] * sources_of(wanted)
        + [whole(small.shape)],
        [later_rows(width), later_rows(width), later_rows(width), whole((width, width)),
         whole((width // 16, 2, 16, width)), whole((width, width)), whole((8, width))],
        [shaped((number, width), F32), shaped((number, width), F32), shaped((number, width), LOW),
         shaped((width, width), LOW), shaped((width // 16, 2, 16, width), LOW), shaped((width, width), LOW),
         shaped((8, width), F32)],
        attend_back_scratch(keys, width)
        + [pltpu.VMEM((number, width), LOW), pltpu.VMEM((keys, width), LOW), pltpu.VMEM((keys, width), LOW),
           pltpu.VMEM((number, width), LOW)]
        + fetch_scratch(wanted, width),
        16 * number * width * width + number * keys * width * 4,
        24 * number * width,
        "cross_back",
        room=58,
    )(plan, q, kv, kv, d_context, lse, owner, key_owner, normed, inverse, d_above, memory, context,
      *far[: sources_of(wanted)], small)


def qkv_inputs_kernel(plan, *refs, masked, wanted):
    if masked:
        dq, dk, dv, d_above, flags, *refs = refs
        far = refs[: sources_of(wanted)]
        d_x, mask_sum, near, semaphores, blocks, wide = refs[sources_of(wanted) :]
    else:
        dq, dk, dv, d_above, *refs = refs
        far = refs[: sources_of(wanted)]
        d_x, near, semaphores, blocks = refs[sources_of(wanted) :]
    width = dq.shape[1]

    @pl.when(pl.program_id(0) == 0)
    def _():
        (load,) = fetches(far, plan, wanted, (near,), semaphores)
        load.start()
        load.wait()
        if masked:
            mask_sum[...] = jnp.zeros_like(mask_sum)
            spread(wide, near[...])
        for j in range(3):
            if masked:
                blocks[:, j * width : j * width + width] = third_rows(wide, j)
            else:
                blocks[:, j * width : j * width + width] = block_of(near, j, 3)

    pieces = jnp.concatenate([dq[...], dk[...], dv[...]], axis=1)
    total = nt(pieces, blocks[...])
    if masked:
        total = total + d_above[...]
        hit = column_of(flags[...]) == 1.0
        d_x[...] = jnp.where(hit, 0.0, total)
        mask_sum[0:1, :] += jnp.sum(jnp.where(hit, total, 0.0), axis=0, keepdims=True)
    else:
        d_x[...] = d_above[...]
        d_x[...] += total


def qkv_inputs(plan, dq, dk, dv, d_above, far, wanted, flags, name):
    number, width = dq.shape
    masked = flags is not None
    in_specs = [rows_of(width)] * 4
    out_specs = [rows_of(width)]
    out_shape = [shaped((number, width), F32)]
    operands = [dq, dk, dv, d_above]
    scratch = fetch_scratch(wanted, width) + [pltpu.VMEM((width, 3 * width), LOW)]
    if masked:
        in_specs.append(pl.BlockSpec((1, TILE), lambda i, *_: (0, i)))
        out_specs.append(whole((8, width)))
        out_shape.append(shaped((8, width), F32))
        operands.append(flags)
        scratch.append(wide_scratch(width))
    in_specs += [FAR] * sources_of(wanted)
    operands += far[: sources_of(wanted)]
    return call(
        functools.partial(qkv_inputs_kernel, masked=masked, wanted=wanted),
        (number // TILE,),
        in_specs,
        out_specs,
        out_shape,
        scratch,
        6 * number * width * width,
        16 * number * width,
        name,
    )(plan, *operands)


def enc_regions(width, inner):
    return ((0, 3 * width, 3), (4 * width, 4 * width + inner, inner // width))


def dec_regions(width, inner):
    return ((5 * width, 7 * width, 2), (8 * width, 8 * width + inner, inner // width))


def to_units(rows, k):
    return rows.reshape(-1, 16, k, rows.shape[1]).transpose(0, 2, 1, 3).reshape(rows.shape)


def from_units(rows, k):
    return rows.reshape(-1, k, 16, rows.shape[1]).transpose(0, 2, 1, 3).reshape(rows.shape)


def fits(size, region):
    return size % (16 * region[2]) == 0


def arrange_own(rows, first, regions, arrange):
    place = first + lax.broadcasted_iota(jnp.int32, (rows.shape[0], 1), 0)
    result = rows
    for region in regions:
        if fits(rows.shape[0], region):
            inside = (place >= region[0]) & (place < region[1])
            result = jnp.where(inside, arrange(rows, region[2]), result)
    return result


def arrange_all(rows, size, regions, arrange):
    for region in regions:
        if not fits(size, region):
            part = arrange(rows[region[0] : region[1]], region[2])
            rows = jnp.concatenate([rows[: region[0]], part, rows[region[1] :]], axis=0)
    return rows


def owners_of(lengths, number):
    bounds = jnp.cumsum(lengths)
    places = jnp.arange(number, dtype=jnp.int32)
    owners = jnp.sum((places[:, None] >= bounds[None, :]).astype(jnp.int32), axis=1)
    filled = places < bounds[-1]
    for_queries = jnp.where(filled, owners, -2).astype(F32)[None, :]
    for_keys = jnp.where(filled, owners, -1).astype(F32)[None, :]
    return for_queries, for_keys, bounds


def plan_of(query_bounds, key_bounds, key_lengths, number, core):
    firsts = jnp.arange(8, dtype=jnp.int32) * TILE
    filled = query_bounds[-1]
    lasts = jnp.minimum(firsts + TILE, filled) - 1

    def pair_of(places):
        found = jnp.sum((places[:, None] >= query_bounds[None, :]).astype(jnp.int32), axis=1)
        return jnp.minimum(found, key_lengths.shape[0] - 1)

    def pick(values, pairs):
        chosen = pairs[:, None] == jnp.arange(values.shape[0])[None, :]
        return jnp.sum(jnp.where(chosen, values[None, :], 0), axis=1)

    begin = pick(key_bounds - key_lengths, pair_of(firsts))
    end = pick(key_bounds, pair_of(lasts))
    some = firsts < filled
    begin = begin // LANES * LANES
    chunks = (end - begin + TILE - 1) // TILE
    begin = jnp.where(some, jnp.minimum(begin, number - chunks * TILE), 0)
    chunks = jnp.where(some, chunks, 0)
    rest = jnp.where(jnp.arange(8) == 1, core, filled)
    return jnp.stack([begin, chunks, rest]).astype(jnp.int32)


def moments(gradient, first, second):
    first_new = beta_one * first + (1.0 - beta_one) * gradient
    second_new = beta_two * second + (1.0 - beta_two) * gradient * gradient
    return (first_new, second_new)


def adamw(weight, gradient, first, second):
    first_new, second_new = moments(gradient, first, second)
    moved = weight - rate * (
        first_new
        / (1.0 - beta_one**STEPS)
        / (jnp.sqrt(second_new / (1.0 - beta_two**STEPS)) + epsilon)
        + decay * weight
    )
    return (moved, first_new, second_new)


CORE, X, Y, Z_LOW, Z_HIGH = 0, 1, 2, 3, 4
BITS = 5


def partner(bits):
    mask = sum(1 << bit for bit in bits)
    return [(i, i ^ mask) for i in range(1 << BITS)]


def bit_of(me, bit):
    return (me >> bit) & 1


def take(values, axis, index):
    return lax.dynamic_index_in_dim(values, index, axis, keepdims=False)


def overlaps(sizes, own):
    found = []
    first = 0
    for piece, size in enumerate(sizes):
        at = first
        while at < first + size:
            owner = at // own
            end = min(first + size, (owner + 1) * own)
            found.append((piece, at - first, owner, at - owner * own, end - at))
            at = end
        first += size
    return found


def pack_kernel(core, *refs, copies, number):
    pieces, send, keep, semaphores = refs[:number], refs[number], refs[number + 1], refs[number + 2]
    for side in (0, 1):

        @pl.when(core[0] == side)
        def _():
            handles = []
            for n, (piece, at, owner, to, rows) in enumerate(copies):
                target = keep if owner % 2 == side else send
                handles.append(
                    pltpu.make_async_copy(
                        pieces[piece].at[pl.ds(at, rows)],
                        target.at[owner // 2, pl.ds(to, rows)],
                        semaphores.at[n],
                    )
                )
            for handle in handles:
                handle.start()
            for handle in handles:
                handle.wait()


def pack(core, pieces, copies, block, name):
    width = pieces[0].shape[1]
    shape = shaped((1 << (BITS - 1), block, width), LOW)
    anywhere = pl.BlockSpec(memory_space=pl.ANY)
    total = sum(piece.size for piece in pieces)
    return call(
        functools.partial(pack_kernel, copies=copies, number=len(pieces)),
        (1,),
        [pl.BlockSpec(memory_space=pltpu.VMEM)] * len(pieces),
        [anywhere, anywhere],
        [shape, shape],
        [pltpu.SemaphoreType.DMA((len(copies),))],
        0,
        4 * total,
        name,
        near=True,
    )(core, *pieces)


def add_low(former, latter):
    return (former.astype(F32) + latter.astype(F32)).astype(LOW)


def swap(values, *bits):
    return lax.ppermute(values, "fsdp", partner(bits))


def reduce_owned(me, send, keep, cut):
    rows, width = send.shape[1:]
    x, y, low, high = (bit_of(me, b) for b in (X, Y, Z_LOW, Z_HIGH))
    (send,) = yield (send,)
    chips = add_low(keep, swap(send, CORE)).reshape(2, 2, 2, 2, rows, width)
    first, second = chips[..., :cut, :], chips[..., cut:, :]
    for_y, for_x = yield (take(first, 2, 1 - y), take(second, 3, 1 - x))
    first = add_low(take(first, 2, y), swap(for_y, Y))
    second = add_low(take(second, 3, x), swap(for_x, X))
    for_x, for_y = yield (take(first, 2, 1 - x), take(second, 2, 1 - y))
    first = add_low(take(first, 2, x), swap(for_x, X))
    second = add_low(take(second, 2, y), swap(for_y, Y))
    column = jnp.concatenate([first, second], axis=2)

    def block(above, beside):
        return take(take(column, 0, above), 0, beside)

    near, far, across = yield (block(high, 1 - low), block(1 - high, low), block(1 - high, 1 - low))
    total = block(high, low).astype(F32)
    for values, bits in ((near, (Z_LOW,)), (far, (Z_HIGH,)), (across, (Z_LOW, Z_HIGH))):
        total = total + swap(values, *bits).astype(F32)
    return total


def ordered(bit, mine, other, axis):
    first = bit == 0
    return jnp.stack([jnp.where(first, mine, other), jnp.where(first, other, mine)], axis=axis)


def gather_owned(me, own):
    x, y, low, high = (bit_of(me, b) for b in (X, Y, Z_LOW, Z_HIGH))
    rows, width = own.shape
    (own,) = yield (own,)
    column = ordered(high, own, swap(own, Z_HIGH), 0)
    (column,) = yield (column,)
    column = ordered(low, column, swap(column, Z_LOW), 1)
    below, above = yield (column[0], column[1])
    below = ordered(x, below, swap(below, X), 1)
    above = ordered(y, above, swap(above, Y), 1)
    below, above = yield (below, above)
    below = ordered(y, below, swap(below, Y), 1).reshape(-1, rows, width)
    above = ordered(x, above, swap(above, X), 2).reshape(-1, rows, width)
    below, above = yield (below, above)
    return [below, swap(below, CORE), above, swap(above, CORE)]


class Rounds:
    def __init__(self, steps):
        self.steps = steps
        self.sent = next(steps)
        self.result = None

    def before(self, *operands):
        sent, operands = lax.optimization_barrier((self.sent, operands))
        self.move(sent)
        return operands[0] if len(operands) == 1 else operands

    def move(self, sent):
        try:
            self.sent = self.steps.send(sent)
        except StopIteration as stop:
            self.sent, self.result = None, stop.value

    def finish(self):
        while self.result is None:
            self.move(self.sent)
        return self.result


def on_device(
    devices,
    src_in,
    tgt_in,
    src_len,
    tgt_len,
    tgt_mask,
    enc_cot,
    dec_cot,
    enc_master,
    enc_first,
    enc_second,
    dec_master,
    dec_first,
    dec_second,
    small_master,
    small_first,
    small_second,
):
    width = src_in.shape[1]
    number = src_in.shape[0]
    me = lax.axis_index("fsdp")
    enc_size, dec_size = enc_master.shape[0], dec_master.shape[0]
    enc_count, dec_count = enc_size * devices, dec_size * devices
    inner = (enc_count - 4 * width) // 2
    ups = inner // width
    enc_map, dec_map = enc_regions(width, inner), dec_regions(width, inner)

    enc_own = arrange_own(enc_master.astype(LOW), me * enc_size, enc_map, to_units)
    dec_own = arrange_own(dec_master.astype(LOW), me * dec_size, dec_map, to_units)
    by_rounds = devices == 1 << BITS
    share = small_master.shape[1]
    held = small_master.size
    own = jnp.zeros((16, width), LOW)
    own = lax.dynamic_update_slice(own, small_master.astype(LOW), (0, me * share))
    core = bit_of(me, CORE)
    src_owner, src_key, src_bounds = owners_of(src_len[0], number)
    tgt_owner, tgt_key, tgt_bounds = owners_of(tgt_len[0], number)
    enc_plan = plan_of(src_bounds, src_bounds, src_len[0], number, core)
    dec_plan = plan_of(tgt_bounds, tgt_bounds, tgt_len[0], number, core)
    cross_plan = plan_of(tgt_bounds, src_bounds, src_len[0], number, core)
    flags = tgt_mask.astype(F32)[None, :]
    if by_rounds:
        ahead = Rounds(gather_owned(me, jnp.concatenate([enc_own, own], axis=0)))
        ahead.move(ahead.sent)
        ahead.move(ahead.sent)
        dec_own = ahead.before(dec_own)
        behind = Rounds(gather_owned(me, dec_own))
        behind.move(behind.sent)
        behind.sent = (ahead.before(*behind.sent),)
        behind.move(behind.sent)
        ahead.sent, behind.sent = lax.optimization_barrier((ahead.sent, behind.sent))
        behind.move(behind.sent)
        ahead.sent, behind.sent = lax.optimization_barrier((ahead.sent, behind.sent))
        enc_far, behind.sent = lax.optimization_barrier((ahead.finish(), behind.sent))
        smalls = sum(jnp.sum(part[:, enc_size:].astype(F32), axis=0) for part in enc_far)
        early = (src_in, src_owner, src_key, tgt_owner, tgt_key, enc_plan, dec_plan, cross_plan, flags)
        src_in, src_owner, src_key, tgt_owner, tgt_key, enc_plan, dec_plan, cross_plan, flags = behind.before(*early)
    else:
        first = core == 0

        def paired(own_rows, size, regions):
            rows = lax.all_gather(own_rows, "fsdp", axis=0, tiled=True)
            rows = arrange_all(rows, size, regions, to_units).reshape(2, OWNERS // 4, 2, -1, width)
            made = []
            for half in range(2):
                even, odd = rows[half, :, 0], rows[half, :, 1]
                made += [jnp.where(first, even, odd), jnp.where(first, odd, even)]
            return made

        enc_far, dec_far = paired(enc_own, enc_size, enc_map), paired(dec_own, dec_size, dec_map)
        smalls = lax.psum(own.astype(F32), "fsdp")

    def enc_part(first, last):
        return row_copies(first, last, enc_count // OWNERS, True)

    def dec_part(first, last):
        return row_copies(first, last, dec_count // OWNERS, True)

    enc_qkv = enc_part(0, 3 * width)
    enc_wo = enc_part(3 * width, 4 * width)
    enc_up = enc_part(4 * width, 4 * width + inner)
    enc_down = enc_part(4 * width + inner, enc_count)
    self_qkv = dec_part(0, 3 * width)
    self_wo = dec_part(3 * width, 4 * width)
    cross_q = dec_part(4 * width, 5 * width)
    cross_kv = dec_part(5 * width, 7 * width)
    cross_wo = dec_part(7 * width, 8 * width)
    dec_up = dec_part(8 * width, 8 * width + inner)
    dec_down = dec_part(8 * width + inner, dec_count)

    start = jnp.where(tgt_mask[:, None] == 1, smalls[10].astype(LOW)[None, :], tgt_in)

    e_q, e_kv, e_ctx, e_lse, e_hat, e_inv, memory, t_hat, t_inv = fwd_block(
        enc_plan, src_in, None, enc_far, (enc_qkv, enc_wo, enc_up, enc_down), True, smalls, 0, src_owner, src_key, True,
        "enc_layer",
    )
    if by_rounds:
        memory = behind.before(memory)
        dec_far = behind.finish()
    s_q, s_kv, s_ctx, s_lse, s_hat, s_inv = fwd_block(
        dec_plan, start, None, dec_far, (self_qkv, self_wo), False, smalls, 4, tgt_owner, tgt_key, False, "dec_block"
    )
    c_q, c_kv, c_lse, decoded, d_two, d_cctx, g_dup, g_ddown, g_cout, sums_d = cross_turn(
        cross_plan, s_hat, memory, dec_cot, dec_far, (cross_kv, cross_wo, cross_q, dec_up, dec_down), smalls, 6,
        tgt_owner, src_key, inner, "cross_turn",
    )

    d_memory, d_one, d_sctx, g_cq, g_ckv, g_sout, sums_c = cross_backward(
        cross_plan, c_q, c_kv, d_cctx, c_lse, tgt_owner, src_key, s_hat, s_inv, d_two, memory, s_ctx, dec_far,
        (cross_kv, cross_q, self_wo), smalls,
    )
    dsq, dsk, dsv, g_sqkv = attention_backward(
        dec_plan, s_q, s_kv, d_sctx, s_lse, tgt_owner, tgt_key, start, "rows", "dec_back"
    )
    dec_pieces = [
        g_sqkv,
        g_sout,
        g_cq,
        g_ckv.reshape(-1, width),
        g_cout,
        g_dup.reshape(-1, width),
        g_ddown,
    ]
    if by_rounds:
        core = core[None].astype(jnp.int32)
        copies = overlaps([p.shape[0] for p in dec_pieces], dec_size)
        send, keep = pack(core, dec_pieces, copies, dec_size, "dec_pack")
        rounds = Rounds(reduce_owned(me, send, keep, dec_size // 2))
        dsq, dsk, dsv = rounds.before(dsq, dsk, dsv)
    tgt_grad, mask_sum = qkv_inputs(
        dec_plan, dsq, dsk, dsv, d_one, dec_far, (self_qkv,), flags, "dec_qkv_inputs"
    )
    if by_rounds:
        d_memory, mask_sum = rounds.before(d_memory, mask_sum)
    d_mid, d_ectx, g_up, g_down, g_out, sums_e = ffn_backward(
        enc_plan, [enc_cot, d_memory], (t_hat, t_inv), (e_hat, e_inv), e_ctx, enc_far,
        (enc_up, enc_down, enc_wo), smalls, 0, inner, "enc_ffn_back",
    )
    if by_rounds:
        d_ectx, g_up = rounds.before(d_ectx, g_up)
    deq, dek, dev, g_qkv = attention_backward(
        enc_plan, e_q, e_kv, d_ectx, e_lse, src_owner, src_key, src_in, "units", "enc_back"
    )

    enc_pieces = [g_qkv.reshape(-1, width), g_out, g_up.reshape(-1, width), g_down]
    small_grad = jnp.concatenate([sums_e[:4], sums_c[:2], sums_d[:4], mask_sum[:1]], axis=0)
    small_wire = small_grad.reshape(-1, devices, share).transpose(1, 0, 2).reshape(devices, -1).astype(LOW)
    small_wire = jnp.pad(small_wire, ((0, 0), (0, 16 * width - held))).reshape(devices * 16, width)
    if by_rounds:
        dec_summed = rounds.finish()
        copies = overlaps([p.shape[0] for p in enc_pieces], enc_size)
        copies += [(len(enc_pieces), 16 * i, i, enc_size, 16) for i in range(devices)]
        send, keep = pack(core, enc_pieces + [small_wire], copies, enc_size + 16, "enc_pack")
        rounds = Rounds(reduce_owned(me, send, keep, enc_size // 2 + 16))
        deq, dek, dev = rounds.before(deq, dek, dev)
    src_grad = qkv_inputs(enc_plan, deq, dek, dev, d_mid, enc_far, (enc_qkv,), None, "enc_qkv_inputs")[0]
    if by_rounds:
        rounds.move(rounds.sent)
        rounds.move(rounds.sent)
        dec_summed = rounds.before(dec_summed)
        enc_summed = rounds.finish()
    else:
        dec_grad = arrange_all(jnp.concatenate(dec_pieces, axis=0), dec_size, dec_map, from_units)
        enc_grad = arrange_all(jnp.concatenate(enc_pieces, axis=0), enc_size, enc_map, from_units)
        enc_wire = jnp.concatenate(
            [enc_grad.reshape(devices, enc_size, width), small_wire.reshape(devices, 16, width)], axis=1
        )
        dec_summed = lax.psum_scatter(dec_grad, "fsdp", scatter_dimension=0, tiled=True).astype(F32)
        enc_summed = lax.psum_scatter(
            enc_wire.reshape(-1, width), "fsdp", scatter_dimension=0, tiled=True
        ).astype(F32)
    small_summed = enc_summed[enc_size:].reshape(-1)[:held].reshape(-1, share)
    enc_summed = arrange_own(enc_summed[:enc_size], me * enc_size, enc_map, from_units)
    dec_summed = arrange_own(dec_summed, me * dec_size, dec_map, from_units)

    part = 1.0 / devices
    enc_summed = enc_summed * part
    dec_summed = dec_summed * part
    small_summed = small_summed * part
    enc_new, enc_first_new, encoder_second_moment_updated = adamw(
        enc_master, enc_summed, enc_first, enc_second
    )
    dec_new, dec_first_new, dec_second_new = adamw(dec_master, dec_summed, dec_first, dec_second)
    small_first_new, small_second_new = moments(small_summed, small_first, small_second)
    return (
        memory,
        decoded,
        src_grad,
        tgt_grad,
        enc_new,
        enc_first_new,
        encoder_second_moment_updated,
        enc_new.astype(LOW),
        dec_new,
        dec_first_new,
        dec_second_new,
        dec_new.astype(LOW),
        small_summed,
        small_first_new,
        small_second_new,
    )


def solution(mesh):
    rows = P("fsdp", None)
    columns = P(None, "fsdp")
    return jax.shard_map(
        functools.partial(on_device, mesh.shape["fsdp"]),
        mesh=mesh,
        in_specs=(rows,) * 4 + (P("fsdp"),) + (rows,) * 8 + (columns,) * 3,
        out_specs=(rows,) * 12 + (columns,) * 3,
        check_vma=False,
    )
```

```python
import functools

import jax
import jax.numpy as jnp
from jax import lax
from jax.experimental import pallas as pl
from jax.experimental.pallas import tpu as pltpu
from jax.sharding import PartitionSpec as P

HEADS = 8
HEAD = 64
STEPS = 7
TILE = 256
LANES = 128

rate = 0.02
beta_one = 0.9
beta_two = 0.98
epsilon = 1e-06
decay = 0.01
floor_value = -1000000000.0
root_half = 0.7071067811865476
inverse_root_tau = 0.3989422804014327

F32 = jnp.float32
LOW = jnp.bfloat16
MIB = 2**20


def nn(former, latter):
    return lax.dot_general(
        former, latter, (((1,), (0,)), ((), ())), preferred_element_type=F32
    )


def nt(former, latter):
    return lax.dot_general(
        former, latter, (((1,), (1,)), ((), ())), preferred_element_type=F32
    )


def turned(values):
    return values.astype(F32).T.astype(LOW)


def column_of(row):
    return jnp.broadcast_to(row, (8, row.shape[1])).T[:, 0:1]


def ln_forward(values, gain, shift):
    centered = values - jnp.mean(values, axis=-1, keepdims=True)
    spread = jnp.mean(centered * centered, axis=-1, keepdims=True)
    inverse = lax.rsqrt(spread + 1e-05)
    normed = centered * inverse
    return normed * gain + shift, normed, inverse


def ln_backward(upstream, normed, inverse, gain):
    scaled = upstream * gain
    first = jnp.mean(scaled, axis=-1, keepdims=True)
    second = jnp.mean(scaled * normed, axis=-1, keepdims=True)
    return inverse * (scaled - first - normed * second)


def phi_and_slope(values):
    phi = 0.5 + 0.5 * lax.erf(values * root_half)
    return phi, phi + values * (jnp.exp(-0.5 * (values * values)) * inverse_root_tau)


def one_head(pair, head):
    lane = lax.broadcasted_iota(jnp.int32, pair.shape, 1)
    keep = lane < HEAD if head % 2 == 0 else lane >= HEAD
    return jnp.where(keep, pair, jnp.zeros_like(pair))


def pair_columns(head):
    return slice(LANES * (head // 2), LANES * (head // 2) + LANES)


def head_rows(head):
    return slice(HEAD * head, HEAD * head + HEAD)


def block_of(ref, j, count):
    if count == 1:
        return ref[...]
    return jnp.concatenate(
        [ref[first + 16 * j : first + 16 * j + 16, :] for first in range(0, ref.shape[0], 16 * count)], axis=0
    )


def spread(wide, values):
    for n in range(wide.shape[0]):
        wide[n] = values[:, LANES * n : LANES * n + LANES].astype(F32)


def third_rows(wide, j):
    rows = pl.ds(j, wide.shape[1] // 3, stride=3)
    return jnp.concatenate([wide[n, rows, :] for n in range(wide.shape[0])], axis=1).astype(LOW)


def put_third_rows(wide, j, values):
    rows = pl.ds(j, wide.shape[1] // 3, stride=3)
    for n in range(wide.shape[0]):
        wide[n, rows, :] = values[:, LANES * n : LANES * n + LANES]


def wide_scratch(width):
    return pltpu.VMEM((width // LANES, 3 * width, LANES), F32)


def put_block(ref, j, values):
    ref[:, j] = values.reshape(ref.shape[0], ref.shape[2], ref.shape[3])


OWNERS = 32


def row_copies(first, last, own, paired):
    found = []
    at = first
    while at < last:
        owner = at // own
        end = min(last, (owner + 1) * own)
        half = OWNERS // 4
        place = (2 * (owner // 2 // half) + owner % 2, owner // 2 % half) if paired else (0, owner)
        found.append((*place, at - owner * own, end - at, at - first))
        at = end
    return found


class Fetch:
    def __init__(self, far, core, copies, near, semaphores, used):
        self.core = core

        def handles(side):
            return [
                pltpu.make_async_copy(
                    far[source ^ side].at[owner, pl.ds(row, rows)], near.at[pl.ds(to, rows)], semaphores.at[used + n]
                )
                for n, (source, owner, row, rows, to) in enumerate(copies)
            ]

        self.handles = handles

    def start(self):
        if self.core is None:
            for handle in self.handles(0):
                handle.start()
            return
        for side in (0, 1):

            @pl.when(self.core == side)
            def _(side=side):
                for handle in self.handles(side):
                    handle.start()

    def wait(self):
        for handle in self.handles(0):
            handle.wait()


def fetches(far, plan, wanted, nears, semaphores):
    used = 0
    made = []
    core = plan[2, 1] if len(far) > 1 else None
    for copies, near in zip(wanted, nears):
        made.append(Fetch(far, core, copies, near, semaphores, used))
        used += len(copies)
    return made


def wait_first(i, loads):
    @pl.when(i == 0)
    def _():
        for load in loads:
            load.wait()


def fetch_scratch(wanted, width):
    return [pltpu.VMEM((sum(c[3] for c in copies), width), LOW) for copies in wanted] + [
        pltpu.SemaphoreType.DMA((sum(len(copies) for copies in wanted),))
    ]


FAR = pl.BlockSpec(memory_space=pl.ANY)


def sources_of(wanted):
    last = max(copy[0] for copies in wanted for copy in copies)
    return 1 if last == 0 else 2 * (last // 2) + 2


def call(kernel, grid, in_specs, out_specs, out_shape, scratch, flops, moved, name, room=24, near=(), keep=()):
    single = not isinstance(out_shape, list)
    shapes = [
        (pltpu.VMEM if keep is True or n in keep else pltpu.HBM)(*made)
        for n, made in enumerate([out_shape] if single else out_shape)
    ]
    made = pl.pallas_call(
        kernel,
        grid_spec=pltpu.PrefetchScalarGridSpec(
            num_scalar_prefetch=1,
            grid=grid,
            in_specs=in_specs,
            out_specs=out_specs,
            scratch_shapes=scratch,
        ),
        out_shape=shapes[0] if single else shapes,
        compiler_params=pltpu.CompilerParams(vmem_limit_bytes=room * MIB),
        cost_estimate=pl.CostEstimate(
            flops=flops, bytes_accessed=moved, transcendentals=0
        ),
        name=name,
    )

    def run(plan, *operands):
        placed = [
            operand
            if near is True or n in near
            else pltpu.with_memory_space_constraint(operand, pltpu.HBM)
            for n, operand in enumerate(operands)
        ]
        return made(plan, *placed)

    return run


def whole(shape):
    zeros = (0,) * len(shape)
    return pl.BlockSpec(shape, lambda i, *_: zeros)


def rows_of(width):
    return pl.BlockSpec((TILE, width), lambda i, *_: (i, 0))


def at_block(shape, *index):
    return pl.BlockSpec(shape, lambda i, *_: index)


def shaped(shape, kind):
    return (shape, kind)


def attend_tile(plan, i, keys, key_cols, query, owner_row, key_owner, vt, sc):
    scores, acc, top, total, masked_q = sc
    query = query * jnp.asarray(HEAD**-0.5, LOW)
    for h in range(HEADS):
        masked_q[h] = one_head(query[:, pair_columns(h)], h)
    top[...] = jnp.full_like(top, -1e30)
    total[...] = jnp.zeros_like(total)
    acc[...] = jnp.zeros_like(acc)
    begin = plan[0, i]
    chunks = plan[1, i]

    def score_tile(j, carry):
        rows = pl.ds(pl.multiple_of(begin + j * TILE, LANES), TILE)
        bias = jnp.where(key_owner[rows, 0:1] == owner_row, 0.0, floor_value)
        tops = []
        for h in range(HEADS):
            cols = pl.ds(key_cols + LANES * (h // 2), LANES)
            s = nt(keys[rows, cols], masked_q[h]) + bias
            scores[j, h] = s
            tops.append(jnp.max(s, axis=0, keepdims=True))
        top[...] = jnp.maximum(top[...], jnp.concatenate(tops, axis=0))
        return carry

    lax.fori_loop(0, chunks, score_tile, 0)

    def weigh_tile(j, carry):
        rows = pl.ds(pl.multiple_of(begin + j * TILE, LANES), TILE)
        sums = []
        for h in range(HEADS):
            p = jnp.exp(scores[j, h] - top[h : h + 1, :])
            sums.append(jnp.sum(p, axis=0, keepdims=True))
            acc[head_rows(h), :] += nn(vt[head_rows(h), rows], p.astype(LOW))
        total[...] += jnp.concatenate(sums, axis=0)
        return carry

    lax.fori_loop(0, chunks, weigh_tile, 0)


def fwd_block_kernel(plan, *refs, cross, gain_row, wanted, packed, ffn):
    refs = list(refs)

    def next_refs(count):
        taken = refs[:count]
        del refs[:count]
        return taken

    if cross:
        normed_in, memory = next_refs(2)
    else:
        (x_all,) = next_refs(1)
    far = next_refs(sources_of(wanted))
    small, owner_q, owner_k = next_refs(3)
    q_out, kv_out, ctx_out, lse_out, normed_out, inverse_out = next_refs(6)
    if ffn:
        out, normed_last, inverse_last = next_refs(3)
    kv, vt, mean_v, key_owner, scores, acc, top, total, masked_q, q_all = next_refs(10)
    nears = next_refs(len(wanted))
    semaphores = refs.pop(0)
    loads = fetches(far, plan, wanted, nears, semaphores)
    i = pl.program_id(0)
    width = kv.shape[1] // 2

    @pl.when(i == 0)
    def _():
        for load in loads:
            load.start()
        key_owner[...] = jnp.broadcast_to(owner_k[...], (8, owner_k.shape[1])).T
        loads[0].wait()
        if cross:
            wk, wv = block_of(nears[0], 0, 2), block_of(nears[0], 1, 2)
        elif packed:
            wq, wk, wv = (block_of(nears[0], j, 3) for j in range(3))
        else:
            wide = refs[0]
            spread(wide, nears[0][...])
            wq, wk, wv = (third_rows(wide, j) for j in range(3))
        sums = jnp.zeros((1, width), F32)
        for t in range(kv.shape[0] // TILE):
            rows = slice(t * TILE, t * TILE + TILE)
            x = memory[rows, :] if cross else x_all[rows, :]
            if not cross:
                q_all[rows, :] = nn(x, wq).astype(LOW)
            kv[rows, :width] = nn(x, wk).astype(LOW)
            v = nn(x, wv).astype(LOW)
            kv[rows, width:] = v
            v = v.astype(F32)
            vt[:, rows] = v.T.astype(LOW)
            sums = sums + jnp.sum(v, axis=0, keepdims=True)
        mean_v[...] = sums * (1.0 / kv.shape[0])
        for load in loads[1 : 3 if cross else 2]:
            load.wait()

    wo = nears[1]
    mine = pl.ds(pl.multiple_of(i * TILE, TILE), TILE)
    if cross:
        resid = normed_in[...] * small[4:5, :] + small[5:6, :]
        query = nn(resid.astype(LOW), nears[2][...]).astype(LOW)
        q_out[...] = query
    else:
        resid = x_all[mine, :].astype(F32)
        query = q_all[mine, :]
        q_out[...] = query
    kv_out[...] = kv[mine, :]
    owner_row = owner_q[...]
    attend_tile(plan, i, kv, 0, query, owner_row, key_owner, vt, (scores, acc, top, total, masked_q))
    dead = owner_row < 0
    sums = jnp.where(dead, 1.0, total[...])
    share = 1.0 / sums
    lse_out[...] = jnp.where(dead, 0.0, top[...] + jnp.log(sums))
    for h in range(HEADS):
        acc[head_rows(h), :] = acc[head_rows(h), :] * share[h : h + 1, :]
    live = column_of(owner_row) >= 0
    context = jnp.where(live, acc[...].T, mean_v[...]).astype(LOW)
    ctx_out[...] = context
    added = nn(context, wo[...]) * live.astype(F32)
    mid, normed, inverse = ln_forward(
        resid + added, small[gain_row : gain_row + 1, :], small[gain_row + 1 : gain_row + 2, :]
    )
    normed_out[...] = normed
    inverse_out[...] = jnp.broadcast_to(inverse, inverse_out.shape)
    if ffn:
        wup, wdown = nears[-2:]
        wait_first(i, loads[-2:])
        blocks = wdown.shape[0] // width
        low = mid.astype(LOW)
        result = mid
        for j in range(blocks):
            inner = nn(low, block_of(wup, j, blocks))
            phi = 0.5 + 0.5 * lax.erf(inner * root_half)
            result = result + nn((inner * phi).astype(LOW), wdown[j * width : j * width + width, :])
        result, normed, inverse = ln_forward(
            result, small[gain_row + 2 : gain_row + 3, :], small[gain_row + 3 : gain_row + 4, :]
        )
        out[...] = result.astype(LOW)
        normed_last[...] = normed
        inverse_last[...] = jnp.broadcast_to(inverse, inverse_last.shape)


def attention_scratch(keys, width):
    return [
        pltpu.VMEM((keys, 2 * width), LOW),
        pltpu.VMEM((width, keys), LOW),
        pltpu.VMEM((1, width), F32),
        pltpu.VMEM((keys, 8), F32),
        pltpu.VMEM((keys // TILE, HEADS, TILE, TILE), F32),
        pltpu.VMEM((width, TILE), F32),
        pltpu.VMEM((HEADS, TILE), F32),
        pltpu.VMEM((HEADS, TILE), F32),
        pltpu.VMEM((HEADS, TILE, LANES), LOW),
        pltpu.VMEM((keys, width), LOW),
    ]


def block_outs(queries, width):
    specs = [
        rows_of(width),
        rows_of(2 * width),
        rows_of(width),
        pl.BlockSpec((HEADS, TILE), lambda i, *_: (0, i)),
        rows_of(width),
        rows_of(LANES),
    ]
    shapes = [
        shaped((queries, width), LOW),
        shaped((queries, 2 * width), LOW),
        shaped((queries, width), LOW),
        shaped((HEADS, queries), F32),
        shaped((queries, width), F32),
        shaped((queries, LANES), F32),
    ]
    return specs, shapes


def owner_specs(keys):
    return [pl.BlockSpec((1, TILE), lambda i, *_: (0, i)), whole((1, keys))]


def fwd_block(plan, x, memory, far, wanted, packed, small, gain_row, owner, key_owner, ffn, name):
    cross = memory is not None
    number, width = x.shape
    specs, shapes = block_outs(number, width)
    if ffn:
        specs += [rows_of(width), rows_of(width), rows_of(LANES)]
        shapes += [shaped((number, width), LOW), shaped((number, width), F32), shaped((number, LANES), F32)]
    scratch = attention_scratch(number, width) + fetch_scratch(wanted, width)
    if not cross and not packed:
        scratch.append(wide_scratch(width))
    return call(
        functools.partial(
            fwd_block_kernel, cross=cross, gain_row=gain_row, wanted=wanted, packed=packed, ffn=ffn
        ),
        (number // TILE,),
        ([rows_of(width), whole(memory.shape)] if cross else [whole(x.shape)])
        + [FAR] * sources_of(wanted)
        + [whole(small.shape)]
        + owner_specs(number),
        specs,
        shapes,
        scratch,
        8 * number * width * width + number * number * width * 2,
        16 * number * width,
        name,
        room=44,
        near=() if packed else (0,),
    )(plan, *([x, memory] if cross else [x]), *far[: sources_of(wanted)], small, owner, key_owner)


def ffn_back_kernel(plan, *refs, tiles, summed, gain_row, wanted):
    refs = list(refs)
    cot = refs.pop(0)
    extra = refs.pop(0) if summed else None
    normed_top, inverse_top, normed_mid, inverse_mid, context = refs[:5]
    far = refs[5 : 5 + sources_of(wanted)]
    (small,
     d_sum, d_context, g_up, g_down, g_out, sums, hidden, d_inner, mid_low, d_down, d_product,
     wup, wdown, wo, semaphores) = refs[5 + sources_of(wanted) :]
    loads = fetches(far, plan, wanted, (wup, wdown, wo), semaphores)
    i = pl.program_id(0)
    width = small.shape[1]
    blocks = wdown.shape[0] // width

    @pl.when(i == 0)
    def _():
        for load in loads:
            load.start()
        sums[...] = jnp.zeros_like(sums)

    @pl.when(i < tiles)
    def _():
        mine = pl.ds(pl.multiple_of(i * TILE, TILE), TILE)
        upstream = cot[...].astype(F32)
        if summed:
            upstream = upstream + extra[...]
        top = normed_top[...]
        sums[2:3, :] += jnp.sum(upstream * top, axis=0, keepdims=True)
        sums[3:4, :] += jnp.sum(upstream, axis=0, keepdims=True)
        d_mid = ln_backward(upstream, top, inverse_top[:, 0:1], small[gain_row + 2 : gain_row + 3, :])
        low = d_mid.astype(LOW)
        d_down[mine, :] = low
        normed = normed_mid[...]
        mid = (normed * small[gain_row : gain_row + 1, :] + small[gain_row + 1 : gain_row + 2, :]).astype(LOW)
        mid_low[mine, :] = mid
        wait_first(i, loads)
        for j in range(blocks):
            cols = slice(j * width, j * width + width)
            up = block_of(wup, j, blocks)
            inner = nn(mid, up)
            phi, slope = phi_and_slope(inner)
            hidden[j, mine, :] = (inner * phi).astype(LOW)
            part = (nt(low, wdown[cols, :]) * slope).astype(LOW)
            d_inner[j, mine, :] = part
            d_mid = d_mid + nt(part, up)
        sums[0:1, :] += jnp.sum(d_mid * normed, axis=0, keepdims=True)
        sums[1:2, :] += jnp.sum(d_mid, axis=0, keepdims=True)
        total = ln_backward(d_mid, normed, inverse_mid[:, 0:1], small[gain_row : gain_row + 1, :])
        d_sum[...] = total
        place = lax.broadcasted_iota(jnp.int32, (TILE, 1), 0) + i * TILE
        live = (place < plan[2, 0]).astype(F32)
        product = (total * live).astype(LOW)
        d_product[mine, :] = product
        d_context[...] = nt(product, wo[...]).astype(LOW)

    @pl.when(i >= tiles)
    def _():
        j = i - tiles
        put_block(g_up, 0, nn(turned(mid_low[...]), d_inner[j]).astype(LOW))
        g_down[...] = nn(turned(hidden[j]), d_down[...]).astype(LOW)

    @pl.when(i == tiles)
    def _():
        g_out[...] = nn(turned(context[...]), d_product[...]).astype(LOW)


def ffn_backward(plan, cots, top, mid, context, far, wanted, small, gain_row, inner, name):
    number, width = mid[0].shape
    tiles, blocks = number // TILE, inner // width

    def tile_of(columns):
        return pl.BlockSpec((TILE, columns), lambda i, *_: (jnp.minimum(i, tiles - 1), 0))

    return call(
        functools.partial(
            ffn_back_kernel, tiles=tiles, summed=len(cots) == 2, gain_row=gain_row, wanted=wanted
        ),
        (tiles + blocks,),
        [tile_of(width)] * len(cots)
        + [tile_of(width), tile_of(LANES), tile_of(width), tile_of(LANES), whole((number, width))]
        + [FAR] * sources_of(wanted)
        + [whole(small.shape)],
        [
            tile_of(width),
            tile_of(width),
            pl.BlockSpec((width // 16, 1, 16, width), lambda i, *_: (0, jnp.maximum(i - tiles, 0), 0, 0)),
            pl.BlockSpec((width, width), lambda i, *_: (jnp.maximum(i - tiles, 0), 0)),
            pl.BlockSpec((width, width), lambda i, *_: (0, 0)),
            pl.BlockSpec((8, width), lambda i, *_: (0, 0)),
        ],
        [
            shaped((number, width), F32),
            shaped((number, width), LOW),
            shaped((width // 16, blocks, 16, width), LOW),
            shaped((inner, width), LOW),
            shaped((width, width), LOW),
            shaped((8, width), F32),
        ],
        [
            pltpu.VMEM((blocks, number, width), LOW),
            pltpu.VMEM((blocks, number, width), LOW),
            pltpu.VMEM((number, width), LOW),
            pltpu.VMEM((number, width), LOW),
            pltpu.VMEM((number, width), LOW),
        ]
        + fetch_scratch(wanted, width),
        10 * number * width * inner,
        30 * number * width,
        name,
        room=44,
    )(plan, *cots, *top, *mid, context, *far[: sources_of(wanted)], small)


def turn_kernel(plan, *refs, tiles, gain_row, wanted):
    normed_in, memory, cot = refs[:3]
    far = refs[3 : 3 + sources_of(wanted)]
    (small, owner_q, owner_k,
     q_out, kv_out, lse_out, out, d_sum, d_context, g_up, g_down, g_out, sums,
     kv, vt, mean_v, key_owner, scores, acc, top, total, masked_q,
     hidden, d_inner, mid_low, d_down, d_product, contexts, slopes,
     *nears, semaphores) = refs[3 + sources_of(wanted) :]
    wkv, wo, wq, wup, wdown = nears
    loads = fetches(far, plan, wanted, nears, semaphores)
    i = pl.program_id(0)
    width = small.shape[1]
    blocks = wdown.shape[0] // width

    @pl.when(i == 0)
    def _():
        for load in loads:
            load.start()
        sums[...] = jnp.zeros_like(sums)
        key_owner[...] = jnp.broadcast_to(owner_k[...], (8, owner_k.shape[1])).T
        loads[0].wait()
        wk, wv = block_of(wkv, 0, 2), block_of(wkv, 1, 2)
        means = jnp.zeros((1, width), F32)
        for t in range(kv.shape[0] // TILE):
            rows = slice(t * TILE, t * TILE + TILE)
            x = memory[rows, :]
            kv[rows, :width] = nn(x, wk).astype(LOW)
            v = nn(x, wv).astype(LOW)
            kv[rows, width:] = v
            v = v.astype(F32)
            vt[:, rows] = v.T.astype(LOW)
            means = means + jnp.sum(v, axis=0, keepdims=True)
        mean_v[...] = means * (1.0 / kv.shape[0])
        for load in loads[1:3]:
            load.wait()

    @pl.when(i < tiles)
    def _():
        mine = pl.ds(pl.multiple_of(i * TILE, TILE), TILE)
        resid = normed_in[...] * small[gain_row - 2 : gain_row - 1, :] + small[gain_row - 1 : gain_row, :]
        query = nn(resid.astype(LOW), wq[...]).astype(LOW)
        q_out[...] = query
        kv_out[...] = kv[mine, :]
        owner_row = owner_q[...]
        attend_tile(
            plan, i, kv, 0, query, owner_row, key_owner, vt, (scores, acc, top, total, masked_q)
        )
        dead = owner_row < 0
        weighed = jnp.where(dead, 1.0, total[...])
        share = 1.0 / weighed
        lse_out[...] = jnp.where(dead, 0.0, top[...] + jnp.log(weighed))
        for h in range(HEADS):
            acc[head_rows(h), :] = acc[head_rows(h), :] * share[h : h + 1, :]
        live = column_of(owner_row) >= 0
        context = jnp.where(live, acc[...].T, mean_v[...]).astype(LOW)
        contexts[mine, :] = context
        added = nn(context, wo[...]) * live.astype(F32)
        mid, normed_mid, inverse_mid = ln_forward(
            resid + added, small[gain_row : gain_row + 1, :], small[gain_row + 1 : gain_row + 2, :]
        )
        wait_first(i, loads[3:])
        low = mid.astype(LOW)
        mid_low[mine, :] = low
        result = mid
        for j in range(blocks):
            inner = nn(low, block_of(wup, j, blocks))
            phi, slope = phi_and_slope(inner)
            made = (inner * phi).astype(LOW)
            hidden[j, mine, :] = made
            slopes[j] = slope
            result = result + nn(made, wdown[j * width : j * width + width, :])
        result, normed, inverse = ln_forward(
            result, small[gain_row + 2 : gain_row + 3, :], small[gain_row + 3 : gain_row + 4, :]
        )
        out[...] = result.astype(LOW)

        upstream = cot[...].astype(F32)
        sums[2:3, :] += jnp.sum(upstream * normed, axis=0, keepdims=True)
        sums[3:4, :] += jnp.sum(upstream, axis=0, keepdims=True)
        d_mid = ln_backward(upstream, normed, inverse, small[gain_row + 2 : gain_row + 3, :])
        low = d_mid.astype(LOW)
        d_down[mine, :] = low
        for j in range(blocks):
            part = (nt(low, wdown[j * width : j * width + width, :]) * slopes[j]).astype(LOW)
            d_inner[j, mine, :] = part
            d_mid = d_mid + nt(part, block_of(wup, j, blocks))
        sums[0:1, :] += jnp.sum(d_mid * normed_mid, axis=0, keepdims=True)
        sums[1:2, :] += jnp.sum(d_mid, axis=0, keepdims=True)
        d_all = ln_backward(d_mid, normed_mid, inverse_mid, small[gain_row : gain_row + 1, :])
        d_sum[...] = d_all
        product = (d_all * live.astype(F32)).astype(LOW)
        d_product[mine, :] = product
        d_context[...] = nt(product, wo[...]).astype(LOW)

    @pl.when(i >= tiles)
    def _():
        j = i - tiles
        put_block(g_up, 0, nn(turned(mid_low[...]), d_inner[j]).astype(LOW))
        g_down[...] = nn(turned(hidden[j]), d_down[...]).astype(LOW)

    @pl.when(i == tiles)
    def _():
        g_out[...] = nn(turned(contexts[...]), d_product[...]).astype(LOW)


def cross_turn(plan, normed, memory, cot, far, wanted, small, gain_row, owner, key_owner, inner, name):
    number, width = normed.shape
    keys = memory.shape[0]
    tiles, blocks = number // TILE, inner // width

    def tile_of(columns):
        return pl.BlockSpec((TILE, columns), lambda i, *_: (jnp.minimum(i, tiles - 1), 0))

    def columns_of(rows):
        return pl.BlockSpec((rows, TILE), lambda i, *_: (0, jnp.minimum(i, tiles - 1)))

    return call(
        functools.partial(turn_kernel, tiles=tiles, gain_row=gain_row, wanted=wanted),
        (tiles + blocks,),
        [tile_of(width), whole(memory.shape), tile_of(width)]
        + [FAR] * sources_of(wanted)
        + [whole(small.shape), columns_of(1), whole((1, keys))],
        [
            tile_of(width),
            tile_of(2 * width),
            columns_of(HEADS),
            tile_of(width),
            tile_of(width),
            tile_of(width),
            pl.BlockSpec((width // 16, 1, 16, width), lambda i, *_: (0, jnp.maximum(i - tiles, 0), 0, 0)),
            pl.BlockSpec((width, width), lambda i, *_: (jnp.maximum(i - tiles, 0), 0)),
            whole((width, width)),
            whole((8, width)),
        ],
        [
            shaped((number, width), LOW),
            shaped((number, 2 * width), LOW),
            shaped((HEADS, number), F32),
            shaped((number, width), LOW),
            shaped((number, width), F32),
            shaped((number, width), LOW),
            shaped((width // 16, blocks, 16, width), LOW),
            shaped((inner, width), LOW),
            shaped((width, width), LOW),
            shaped((8, width), F32),
        ],
        attention_scratch(keys, width)[:-1]
        + [
            pltpu.VMEM((blocks, number, width), LOW),
            pltpu.VMEM((blocks, number, width), LOW),
            pltpu.VMEM((number, width), LOW),
            pltpu.VMEM((number, width), LOW),
            pltpu.VMEM((number, width), LOW),
            pltpu.VMEM((number, width), LOW),
            pltpu.VMEM((blocks, TILE, width), F32),
        ]
        + fetch_scratch(wanted, width),
        12 * number * width * inner + number * number * width * 2,
        30 * number * width,
        name,
        room=58,
    )(plan, normed, memory, cot, *far[: sources_of(wanted)], small, owner, key_owner)


def attend_back(plan, i, q_ref, k_ref, v_ref, do_ref, lse, owner_q, owner_k, scratch):
    kt, key_owner, masked_q, masked_do, dqt, dk_sum, dv_sum, weights, d_weights, dots = scratch

    @pl.when(i == 0)
    def _():
        key_owner[...] = jnp.broadcast_to(owner_k[...], (8, owner_k.shape[1])).T
        kt[...] = turned(k_ref[...])
        dk_sum[...] = jnp.zeros_like(dk_sum)
        dv_sum[...] = jnp.zeros_like(dv_sum)

    query = q_ref[...] * jnp.asarray(HEAD**-0.5, LOW)
    upstream = do_ref[...]
    for h in range(HEADS):
        masked_q[h] = one_head(query[:, pair_columns(h)], h)
        masked_do[h] = one_head(upstream[:, pair_columns(h)], h)
    dqt[...] = jnp.zeros_like(dqt)
    dots[...] = jnp.zeros_like(dots)
    owner_row = owner_q[...]
    begin = plan[0, i]
    chunks = plan[1, i]

    def weigh_tile(j, carry):
        rows = pl.ds(pl.multiple_of(begin + j * TILE, LANES), TILE)
        bias = jnp.where(key_owner[rows, 0:1] == owner_row, 0.0, floor_value)
        sums = []
        for h in range(HEADS):
            s = nt(k_ref[rows, pair_columns(h)], masked_q[h])
            p = jnp.exp((s - lse[h : h + 1, :]) + bias)
            dp = nt(v_ref[rows, pair_columns(h)], masked_do[h])
            weights[j, h] = p
            d_weights[j, h] = dp
            sums.append(jnp.sum(p * dp, axis=0, keepdims=True))
        dots[...] += jnp.concatenate(sums, axis=0)
        return carry

    lax.fori_loop(0, chunks, weigh_tile, 0)

    def grad_tile(j, carry):
        rows = pl.ds(pl.multiple_of(begin + j * TILE, LANES), TILE)
        for pair in range(HEADS // 2):
            cols = pair_columns(2 * pair)
            dv_part = dv_sum[rows, cols]
            dk_part = dk_sum[rows, cols]
            for h in (2 * pair, 2 * pair + 1):
                p = weights[j, h]
                ds = (p * (d_weights[j, h] - dots[h : h + 1, :])).astype(LOW)
                dv_part = dv_part + nn(p.astype(LOW), masked_do[h])
                dk_part = dk_part + nn(ds, masked_q[h])
                dqt[head_rows(h), :] += nn(kt[head_rows(h), rows], ds)
            dv_sum[rows, cols] = dv_part
            dk_sum[rows, cols] = dk_part
        return carry

    lax.fori_loop(0, chunks, grad_tile, 0)
    return (dqt[...] * HEAD**-0.5).T.astype(LOW)


def attention_back_kernel(plan, *refs, made):
    q_ref, k_ref, v_ref, do_ref, lse, owner_q, owner_k, *refs = refs
    x = refs.pop(0) if made else None
    dq, dk, dv, *refs = refs
    g_qkv = refs.pop(0) if made else None
    scratch, more = refs[:10], refs[10:]
    dk_sum, dv_sum = scratch[5:7]
    i = pl.program_id(0)
    dq_tile = attend_back(plan, i, q_ref, k_ref, v_ref, do_ref, lse, owner_q, owner_k, scratch)
    dq[...] = dq_tile
    if made:
        dq_all = more[0]
        dq_all[pl.ds(pl.multiple_of(i * TILE, TILE), TILE), :] = dq_tile

    @pl.when(i == pl.num_programs(0) - 1)
    def _():
        dk[...] = dk_sum[...].astype(LOW)
        dv[...] = dv_sum[...].astype(LOW)
        if made:
            turn = turned(x[...])
            for j, ref in enumerate((dq_all, dk, dv)):
                grad = nn(turn, ref[...])
                if made == "units":
                    put_block(g_qkv, j, grad.astype(LOW))
                else:
                    put_third_rows(more[1], j, grad)
        if made == "rows":
            for n in range(more[1].shape[0]):
                g_qkv[:, LANES * n : LANES * n + LANES] = more[1][n].astype(LOW)


def attend_back_scratch(keys, width):
    return [
        pltpu.VMEM((width, keys), LOW),
        pltpu.VMEM((keys, 8), F32),
        pltpu.VMEM((HEADS, TILE, LANES), LOW),
        pltpu.VMEM((HEADS, TILE, LANES), LOW),
        pltpu.VMEM((width, TILE), F32),
        pltpu.VMEM((keys, width), F32),
        pltpu.VMEM((keys, width), F32),
        pltpu.VMEM((keys // TILE, HEADS, TILE, TILE), F32),
        pltpu.VMEM((keys // TILE, HEADS, TILE, TILE), F32),
        pltpu.VMEM((HEADS, TILE), F32),
    ]


def attention_backward(plan, q, kv, d_context, lse, owner, key_owner, x, made, name):
    number, width = q.shape
    keys = kv.shape[0]
    in_specs = [
        rows_of(width),
        at_block((keys, width), 0, 0),
        at_block((keys, width), 0, 1),
        rows_of(width),
        pl.BlockSpec((HEADS, TILE), lambda i, *_: (0, i)),
    ] + owner_specs(keys)
    out_specs = [rows_of(width), whole((keys, width)), whole((keys, width))]
    out_shape = [shaped((number, width), LOW), shaped((keys, width), LOW), shaped((keys, width), LOW)]
    operands = [q, kv, kv, d_context, lse, owner, key_owner]
    scratch = attend_back_scratch(keys, width)
    if made:
        shape = (width // 16, 3, 16, width) if made == "units" else (3 * width, width)
        in_specs.append(whole(x.shape))
        operands.append(x)
        out_specs.append(whole(shape))
        out_shape.append(shaped(shape, LOW))
        scratch.append(pltpu.VMEM((number, width), LOW))
        if made == "rows":
            scratch.append(wide_scratch(width))
    return call(
        functools.partial(attention_back_kernel, made=made),
        (number // TILE,),
        in_specs,
        out_specs,
        out_shape,
        scratch,
        number * keys * width * 4 + (6 * number * width * width if made else 0),
        12 * number * width,
        name,
        room=52,
    )(plan, *operands)


def cross_back_kernel(plan, *refs, wanted, tiles):
    attention, refs = refs[:7], refs[7:]
    normed, inverse, d_above, memory, context = refs[:5]
    far = refs[5 : 5 + sources_of(wanted)]
    small, d_memory, d_sum, d_context, g_query, g_pair, g_out, sums, *refs = refs[5 + sources_of(wanted) :]
    scratch, refs = refs[:10], refs[10:]
    d_query, dk, dv, d_product, wkv, wq, wo, semaphores = refs
    dk_sum, dv_sum = scratch[5:7]
    loads = fetches(far, plan, wanted, (wkv, wq, wo), semaphores)
    i = pl.program_id(0)

    @pl.when(i == 0)
    def _():
        for load in loads:
            load.start()
        sums[...] = jnp.zeros_like(sums)

    @pl.when(i < tiles)
    def _():
        d_query[pl.ds(pl.multiple_of(i * TILE, TILE), TILE), :] = attend_back(plan, i, *attention, scratch)

    @pl.when(i == tiles)
    def _():
        dk[...] = dk_sum[...].astype(LOW)
        dv[...] = dv_sum[...].astype(LOW)
        for load in loads:
            load.wait()
        low = normed[...] * small[4:5, :] + small[5:6, :]
        g_query[...] = nn(low.T.astype(LOW), d_query[...]).astype(LOW)

    @pl.when(i >= tiles)
    def _():
        row = pl.multiple_of((i - tiles) * TILE, TILE)
        mine = pl.ds(row, TILE)
        wk, wv = block_of(wkv, 0, 2), block_of(wkv, 1, 2)
        d_memory[...] = nt(dk[mine, :], wk) + nt(dv[mine, :], wv)
        d_one = d_above[...] + nt(d_query[mine, :], wq[...])
        hat = normed[mine, :]
        sums[0:1, :] += jnp.sum(d_one * hat, axis=0, keepdims=True)
        sums[1:2, :] += jnp.sum(d_one, axis=0, keepdims=True)
        total = ln_backward(d_one, hat, inverse[:, 0:1], small[4:5, :])
        d_sum[...] = total
        place = lax.broadcasted_iota(jnp.int32, (TILE, 1), 0) + row
        live = (place < plan[2, 0]).astype(F32)
        product = (total * live).astype(LOW)
        d_product[mine, :] = product
        d_context[...] = nt(product, wo[...]).astype(LOW)

    @pl.when(i == tiles + 1)
    def _():
        put_block(g_pair, 0, nn(turned(memory[...]), dk[...]).astype(LOW))

    @pl.when(i == tiles + 2)
    def _():
        put_block(g_pair, 1, nn(turned(memory[...]), dv[...]).astype(LOW))

    @pl.when(i == 2 * tiles - 1)
    def _():
        g_out[...] = nn(turned(context[...]), d_product[...]).astype(LOW)


def cross_backward(plan, q, kv, d_context, lse, owner, key_owner, normed, inverse, d_above, memory, context, far,
                   wanted, small):
    number, width = normed.shape
    keys = kv.shape[0]
    tiles = number // TILE
    full = whole((number, width))

    def first_rows(columns):
        return pl.BlockSpec((TILE, columns), lambda i, *_: (jnp.minimum(i, tiles - 1), 0))

    def first_columns(rows):
        return pl.BlockSpec((rows, TILE), lambda i, *_: (0, jnp.minimum(i, tiles - 1)))

    def later_rows(columns):
        return pl.BlockSpec((TILE, columns), lambda i, *_: (jnp.maximum(i - tiles, 0), 0))

    return call(
        functools.partial(cross_back_kernel, wanted=wanted, tiles=tiles),
        (2 * tiles,),
        [first_rows(width), at_block((keys, width), 0, 0), at_block((keys, width), 0, 1), first_rows(width),
         first_columns(HEADS), first_columns(1), whole((1, keys)),
         full, later_rows(LANES), later_rows(width), whole(memory.shape), full]
        + [FAR] * sources_of(wanted)
        + [whole(small.shape)],
        [later_rows(width), later_rows(width), later_rows(width), whole((width, width)),
         whole((width // 16, 2, 16, width)), whole((width, width)), whole((8, width))],
        [shaped((number, width), F32), shaped((number, width), F32), shaped((number, width), LOW),
         shaped((width, width), LOW), shaped((width // 16, 2, 16, width), LOW), shaped((width, width), LOW),
         shaped((8, width), F32)],
        attend_back_scratch(keys, width)
        + [pltpu.VMEM((number, width), LOW), pltpu.VMEM((keys, width), LOW), pltpu.VMEM((keys, width), LOW),
           pltpu.VMEM((number, width), LOW)]
        + fetch_scratch(wanted, width),
        16 * number * width * width + number * keys * width * 4,
        24 * number * width,
        "cross_back",
        room=58,
    )(plan, q, kv, kv, d_context, lse, owner, key_owner, normed, inverse, d_above, memory, context,
      *far[: sources_of(wanted)], small)


def qkv_inputs_kernel(plan, *refs, masked, wanted):
    if masked:
        dq, dk, dv, d_above, flags, *refs = refs
        far = refs[: sources_of(wanted)]
        d_x, mask_sum, near, semaphores, blocks, wide = refs[sources_of(wanted) :]
    else:
        dq, dk, dv, d_above, *refs = refs
        far = refs[: sources_of(wanted)]
        d_x, near, semaphores, blocks = refs[sources_of(wanted) :]
    width = dq.shape[1]

    @pl.when(pl.program_id(0) == 0)
    def _():
        (load,) = fetches(far, plan, wanted, (near,), semaphores)
        load.start()
        load.wait()
        if masked:
            mask_sum[...] = jnp.zeros_like(mask_sum)
            spread(wide, near[...])
        for j in range(3):
            if masked:
                blocks[:, j * width : j * width + width] = third_rows(wide, j)
            else:
                blocks[:, j * width : j * width + width] = block_of(near, j, 3)

    pieces = jnp.concatenate([dq[...], dk[...], dv[...]], axis=1)
    total = nt(pieces, blocks[...])
    if masked:
        total = total + d_above[...]
        hit = column_of(flags[...]) == 1.0
        d_x[...] = jnp.where(hit, 0.0, total)
        mask_sum[0:1, :] += jnp.sum(jnp.where(hit, total, 0.0), axis=0, keepdims=True)
    else:
        d_x[...] = d_above[...]
        d_x[...] += total


def qkv_inputs(plan, dq, dk, dv, d_above, far, wanted, flags, name):
    number, width = dq.shape
    masked = flags is not None
    in_specs = [rows_of(width)] * 4
    out_specs = [rows_of(width)]
    out_shape = [shaped((number, width), F32)]
    operands = [dq, dk, dv, d_above]
    scratch = fetch_scratch(wanted, width) + [pltpu.VMEM((width, 3 * width), LOW)]
    if masked:
        in_specs.append(pl.BlockSpec((1, TILE), lambda i, *_: (0, i)))
        out_specs.append(whole((8, width)))
        out_shape.append(shaped((8, width), F32))
        operands.append(flags)
        scratch.append(wide_scratch(width))
    in_specs += [FAR] * sources_of(wanted)
    operands += far[: sources_of(wanted)]
    return call(
        functools.partial(qkv_inputs_kernel, masked=masked, wanted=wanted),
        (number // TILE,),
        in_specs,
        out_specs,
        out_shape,
        scratch,
        6 * number * width * width,
        16 * number * width,
        name,
    )(plan, *operands)


def enc_regions(width, inner):
    return ((0, 3 * width, 3), (4 * width, 4 * width + inner, inner // width))


def dec_regions(width, inner):
    return ((5 * width, 7 * width, 2), (8 * width, 8 * width + inner, inner // width))


def to_units(rows, k):
    return rows.reshape(-1, 16, k, rows.shape[1]).transpose(0, 2, 1, 3).reshape(rows.shape)


def from_units(rows, k):
    return rows.reshape(-1, k, 16, rows.shape[1]).transpose(0, 2, 1, 3).reshape(rows.shape)


def fits(size, region):
    return size % (16 * region[2]) == 0


def arrange_own(rows, first, regions, arrange):
    place = first + lax.broadcasted_iota(jnp.int32, (rows.shape[0], 1), 0)
    result = rows
    for region in regions:
        if fits(rows.shape[0], region):
            inside = (place >= region[0]) & (place < region[1])
            result = jnp.where(inside, arrange(rows, region[2]), result)
    return result


def arrange_all(rows, size, regions, arrange):
    for region in regions:
        if not fits(size, region):
            part = arrange(rows[region[0] : region[1]], region[2])
            rows = jnp.concatenate([rows[: region[0]], part, rows[region[1] :]], axis=0)
    return rows


def owners_of(lengths, number):
    bounds = jnp.cumsum(lengths)
    places = jnp.arange(number, dtype=jnp.int32)
    owners = jnp.sum((places[:, None] >= bounds[None, :]).astype(jnp.int32), axis=1)
    filled = places < bounds[-1]
    for_queries = jnp.where(filled, owners, -2).astype(F32)[None, :]
    for_keys = jnp.where(filled, owners, -1).astype(F32)[None, :]
    return for_queries, for_keys, bounds


def plan_of(query_bounds, key_bounds, key_lengths, number, core):
    firsts = jnp.arange(8, dtype=jnp.int32) * TILE
    filled = query_bounds[-1]
    lasts = jnp.minimum(firsts + TILE, filled) - 1

    def pair_of(places):
        found = jnp.sum((places[:, None] >= query_bounds[None, :]).astype(jnp.int32), axis=1)
        return jnp.minimum(found, key_lengths.shape[0] - 1)

    def pick(values, pairs):
        chosen = pairs[:, None] == jnp.arange(values.shape[0])[None, :]
        return jnp.sum(jnp.where(chosen, values[None, :], 0), axis=1)

    begin = pick(key_bounds - key_lengths, pair_of(firsts))
    end = pick(key_bounds, pair_of(lasts))
    some = firsts < filled
    begin = begin // LANES * LANES
    chunks = (end - begin + TILE - 1) // TILE
    begin = jnp.where(some, jnp.minimum(begin, number - chunks * TILE), 0)
    chunks = jnp.where(some, chunks, 0)
    rest = jnp.where(jnp.arange(8) == 1, core, filled)
    return jnp.stack([begin, chunks, rest]).astype(jnp.int32)


def moments(gradient, first, second):
    first_new = beta_one * first + (1.0 - beta_one) * gradient
    second_new = beta_two * second + (1.0 - beta_two) * gradient * gradient
    return (first_new, second_new)


def adamw(weight, gradient, first, second):
    first_new, second_new = moments(gradient, first, second)
    moved = weight - rate * (
        first_new
        / (1.0 - beta_one**STEPS)
        / (jnp.sqrt(second_new / (1.0 - beta_two**STEPS)) + epsilon)
        + decay * weight
    )
    return (moved, first_new, second_new)


CORE, X, Y, Z_LOW, Z_HIGH = 0, 1, 2, 3, 4
BITS = 5


def partner(bits):
    mask = sum(1 << bit for bit in bits)
    return [(i, i ^ mask) for i in range(1 << BITS)]


def bit_of(me, bit):
    return (me >> bit) & 1


def take(values, axis, index):
    return lax.dynamic_index_in_dim(values, index, axis, keepdims=False)


def overlaps(sizes, own):
    found = []
    first = 0
    for piece, size in enumerate(sizes):
        at = first
        while at < first + size:
            owner = at // own
            end = min(first + size, (owner + 1) * own)
            found.append((piece, at - first, owner, at - owner * own, end - at))
            at = end
        first += size
    return found


def pack_kernel(core, *refs, copies, number):
    pieces, send, keep, semaphores = refs[:number], refs[number], refs[number + 1], refs[number + 2]
    for side in (0, 1):

        @pl.when(core[0] == side)
        def _():
            handles = []
            for n, (piece, at, owner, to, rows) in enumerate(copies):
                target = keep if owner % 2 == side else send
                handles.append(
                    pltpu.make_async_copy(
                        pieces[piece].at[pl.ds(at, rows)],
                        target.at[owner // 2, pl.ds(to, rows)],
                        semaphores.at[n],
                    )
                )
            for handle in handles:
                handle.start()
            for handle in handles:
                handle.wait()


def pack(core, pieces, copies, block, name):
    width = pieces[0].shape[1]
    shape = shaped((1 << (BITS - 1), block, width), LOW)
    anywhere = pl.BlockSpec(memory_space=pl.ANY)
    total = sum(piece.size for piece in pieces)
    return call(
        functools.partial(pack_kernel, copies=copies, number=len(pieces)),
        (1,),
        [pl.BlockSpec(memory_space=pltpu.VMEM)] * len(pieces),
        [anywhere, anywhere],
        [shape, shape],
        [pltpu.SemaphoreType.DMA((len(copies),))],
        0,
        4 * total,
        name,
        near=True,
    )(core, *pieces)


def add_low(former, latter):
    return (former.astype(F32) + latter.astype(F32)).astype(LOW)


def swap(values, *bits):
    return lax.ppermute(values, "fsdp", partner(bits))


def reduce_owned(me, send, keep, cut):
    rows, width = send.shape[1:]
    x, y, low, high = (bit_of(me, b) for b in (X, Y, Z_LOW, Z_HIGH))
    (send,) = yield (send,)
    chips = add_low(keep, swap(send, CORE)).reshape(2, 2, 2, 2, rows, width)
    first, second = chips[..., :cut, :], chips[..., cut:, :]
    for_y, for_x = yield (take(first, 2, 1 - y), take(second, 3, 1 - x))
    first = add_low(take(first, 2, y), swap(for_y, Y))
    second = add_low(take(second, 3, x), swap(for_x, X))
    for_x, for_y = yield (take(first, 2, 1 - x), take(second, 2, 1 - y))
    first = add_low(take(first, 2, x), swap(for_x, X))
    second = add_low(take(second, 2, y), swap(for_y, Y))
    column = jnp.concatenate([first, second], axis=2)

    def block(above, beside):
        return take(take(column, 0, above), 0, beside)

    near, far, across = yield (block(high, 1 - low), block(1 - high, low), block(1 - high, 1 - low))
    total = block(high, low).astype(F32)
    for values, bits in ((near, (Z_LOW,)), (far, (Z_HIGH,)), (across, (Z_LOW, Z_HIGH))):
        total = total + swap(values, *bits).astype(F32)
    return total


def ordered(bit, mine, other, axis):
    first = bit == 0
    return jnp.stack([jnp.where(first, mine, other), jnp.where(first, other, mine)], axis=axis)


def gather_owned(me, own):
    x, y, low, high = (bit_of(me, b) for b in (X, Y, Z_LOW, Z_HIGH))
    rows, width = own.shape
    (own,) = yield (own,)
    column = ordered(high, own, swap(own, Z_HIGH), 0)
    (column,) = yield (column,)
    column = ordered(low, column, swap(column, Z_LOW), 1)
    below, above = yield (column[0], column[1])
    below = ordered(x, below, swap(below, X), 1)
    above = ordered(y, above, swap(above, Y), 1)
    below, above = yield (below, above)
    below = ordered(y, below, swap(below, Y), 1).reshape(-1, rows, width)
    above = ordered(x, above, swap(above, X), 2).reshape(-1, rows, width)
    below, above = yield (below, above)
    return [below, swap(below, CORE), above, swap(above, CORE)]


class Rounds:
    def __init__(self, steps):
        self.steps = steps
        self.sent = next(steps)
        self.result = None

    def before(self, *operands):
        sent, operands = lax.optimization_barrier((self.sent, operands))
        self.move(sent)
        return operands[0] if len(operands) == 1 else operands

    def move(self, sent):
        try:
            self.sent = self.steps.send(sent)
        except StopIteration as stop:
            self.sent, self.result = None, stop.value

    def finish(self):
        while self.result is None:
            self.move(self.sent)
        return self.result


def on_device(
    devices,
    src_in,
    tgt_in,
    src_len,
    tgt_len,
    tgt_mask,
    enc_cot,
    dec_cot,
    enc_master,
    enc_first,
    enc_second,
    dec_master,
    dec_first,
    dec_second,
    small_master,
    small_first,
    small_second,
):
    width = src_in.shape[1]
    number = src_in.shape[0]
    me = lax.axis_index("fsdp")
    enc_size, dec_size = enc_master.shape[0], dec_master.shape[0]
    enc_count, dec_count = enc_size * devices, dec_size * devices
    inner = (enc_count - 4 * width) // 2
    ups = inner // width
    enc_map, dec_map = enc_regions(width, inner), dec_regions(width, inner)

    enc_own = arrange_own(enc_master.astype(LOW), me * enc_size, enc_map, to_units)
    dec_own = arrange_own(dec_master.astype(LOW), me * dec_size, dec_map, to_units)
    by_rounds = devices == 1 << BITS
    share = small_master.shape[1]
    held = small_master.size
    own = jnp.zeros((16, width), LOW)
    own = lax.dynamic_update_slice(own, small_master.astype(LOW), (0, me * share))
    core = bit_of(me, CORE)
    src_owner, src_key, src_bounds = owners_of(src_len[0], number)
    tgt_owner, tgt_key, tgt_bounds = owners_of(tgt_len[0], number)
    enc_plan = plan_of(src_bounds, src_bounds, src_len[0], number, core)
    dec_plan = plan_of(tgt_bounds, tgt_bounds, tgt_len[0], number, core)
    cross_plan = plan_of(tgt_bounds, src_bounds, src_len[0], number, core)
    flags = tgt_mask.astype(F32)[None, :]
    if by_rounds:
        ahead = Rounds(gather_owned(me, jnp.concatenate([enc_own, own], axis=0)))
        ahead.move(ahead.sent)
        ahead.move(ahead.sent)
        dec_own = ahead.before(dec_own)
        behind = Rounds(gather_owned(me, dec_own))
        behind.move(behind.sent)
        behind.sent = (ahead.before(*behind.sent),)
        behind.move(behind.sent)
        ahead.sent, behind.sent = lax.optimization_barrier((ahead.sent, behind.sent))
        behind.move(behind.sent)
        ahead.sent, behind.sent = lax.optimization_barrier((ahead.sent, behind.sent))
        enc_far, behind.sent = lax.optimization_barrier((ahead.finish(), behind.sent))
        smalls = sum(jnp.sum(part[:, enc_size:].astype(F32), axis=0) for part in enc_far)
        early = (src_in, src_owner, src_key, tgt_owner, tgt_key, enc_plan, dec_plan, cross_plan, flags)
        src_in, src_owner, src_key, tgt_owner, tgt_key, enc_plan, dec_plan, cross_plan, flags = behind.before(*early)
    else:
        first = core == 0

        def paired(own_rows, size, regions):
            rows = lax.all_gather(own_rows, "fsdp", axis=0, tiled=True)
            rows = arrange_all(rows, size, regions, to_units).reshape(2, OWNERS // 4, 2, -1, width)
            made = []
            for half in range(2):
                even, odd = rows[half, :, 0], rows[half, :, 1]
                made += [jnp.where(first, even, odd), jnp.where(first, odd, even)]
            return made

        enc_far, dec_far = paired(enc_own, enc_size, enc_map), paired(dec_own, dec_size, dec_map)
        smalls = lax.psum(own.astype(F32), "fsdp")

    def enc_part(first, last):
        return row_copies(first, last, enc_count // OWNERS, True)

    def dec_part(first, last):
        return row_copies(first, last, dec_count // OWNERS, True)

    enc_qkv = enc_part(0, 3 * width)
    enc_wo = enc_part(3 * width, 4 * width)
    enc_up = enc_part(4 * width, 4 * width + inner)
    enc_down = enc_part(4 * width + inner, enc_count)
    self_qkv = dec_part(0, 3 * width)
    self_wo = dec_part(3 * width, 4 * width)
    cross_q = dec_part(4 * width, 5 * width)
    cross_kv = dec_part(5 * width, 7 * width)
    cross_wo = dec_part(7 * width, 8 * width)
    dec_up = dec_part(8 * width, 8 * width + inner)
    dec_down = dec_part(8 * width + inner, dec_count)

    start = jnp.where(tgt_mask[:, None] == 1, smalls[10].astype(LOW)[None, :], tgt_in)

    e_q, e_kv, e_ctx, e_lse, e_hat, e_inv, memory, t_hat, t_inv = fwd_block(
        enc_plan, src_in, None, enc_far, (enc_qkv, enc_wo, enc_up, enc_down), True, smalls, 0, src_owner, src_key, True,
        "enc_layer",
    )
    if by_rounds:
        memory = behind.before(memory)
        dec_far = behind.finish()
    s_q, s_kv, s_ctx, s_lse, s_hat, s_inv = fwd_block(
        dec_plan, start, None, dec_far, (self_qkv, self_wo), False, smalls, 4, tgt_owner, tgt_key, False, "dec_block"
    )
    c_q, c_kv, c_lse, decoded, d_two, d_cctx, g_dup, g_ddown, g_cout, sums_d = cross_turn(
        cross_plan, s_hat, memory, dec_cot, dec_far, (cross_kv, cross_wo, cross_q, dec_up, dec_down), smalls, 6,
        tgt_owner, src_key, inner, "cross_turn",
    )

    d_memory, d_one, d_sctx, g_cq, g_ckv, g_sout, sums_c = cross_backward(
        cross_plan, c_q, c_kv, d_cctx, c_lse, tgt_owner, src_key, s_hat, s_inv, d_two, memory, s_ctx, dec_far,
        (cross_kv, cross_q, self_wo), smalls,
    )
    dsq, dsk, dsv, g_sqkv = attention_backward(
        dec_plan, s_q, s_kv, d_sctx, s_lse, tgt_owner, tgt_key, start, "rows", "dec_back"
    )
    dec_pieces = [
        g_sqkv,
        g_sout,
        g_cq,
        g_ckv.reshape(-1, width),
        g_cout,
        g_dup.reshape(-1, width),
        g_ddown,
    ]
    if by_rounds:
        core = core[None].astype(jnp.int32)
        copies = overlaps([p.shape[0] for p in dec_pieces], dec_size)
        send, keep = pack(core, dec_pieces, copies, dec_size, "dec_pack")
        rounds = Rounds(reduce_owned(me, send, keep, dec_size // 2))
        dsq, dsk, dsv = rounds.before(dsq, dsk, dsv)
    tgt_grad, mask_sum = qkv_inputs(
        dec_plan, dsq, dsk, dsv, d_one, dec_far, (self_qkv,), flags, "dec_qkv_inputs"
    )
    if by_rounds:
        d_memory, mask_sum = rounds.before(d_memory, mask_sum)
    d_mid, d_ectx, g_up, g_down, g_out, sums_e = ffn_backward(
        enc_plan, [enc_cot, d_memory], (t_hat, t_inv), (e_hat, e_inv), e_ctx, enc_far,
        (enc_up, enc_down, enc_wo), smalls, 0, inner, "enc_ffn_back",
    )
    if by_rounds:
        d_ectx, g_up = rounds.before(d_ectx, g_up)
    deq, dek, dev, g_qkv = attention_backward(
        enc_plan, e_q, e_kv, d_ectx, e_lse, src_owner, src_key, src_in, "units", "enc_back"
    )

    enc_pieces = [g_qkv.reshape(-1, width), g_out, g_up.reshape(-1, width), g_down]
    small_grad = jnp.concatenate([sums_e[:4], sums_c[:2], sums_d[:4], mask_sum[:1]], axis=0)
    small_wire = small_grad.reshape(-1, devices, share).transpose(1, 0, 2).reshape(devices, -1).astype(LOW)
    small_wire = jnp.pad(small_wire, ((0, 0), (0, 16 * width - held))).reshape(devices * 16, width)
    if by_rounds:
        dec_summed = rounds.finish()
        copies = overlaps([p.shape[0] for p in enc_pieces], enc_size)
        copies += [(len(enc_pieces), 16 * i, i, enc_size, 16) for i in range(devices)]
        send, keep = pack(core, enc_pieces + [small_wire], copies, enc_size + 16, "enc_pack")
        rounds = Rounds(reduce_owned(me, send, keep, enc_size // 2 + 16))
        deq, dek, dev = rounds.before(deq, dek, dev)
    src_grad = qkv_inputs(enc_plan, deq, dek, dev, d_mid, enc_far, (enc_qkv,), None, "enc_qkv_inputs")[0]
    if by_rounds:
        rounds.move(rounds.sent)
        rounds.move(rounds.sent)
        dec_summed = rounds.before(dec_summed)
        enc_summed = rounds.finish()
    else:
        dec_grad = arrange_all(jnp.concatenate(dec_pieces, axis=0), dec_size, dec_map, from_units)
        enc_grad = arrange_all(jnp.concatenate(enc_pieces, axis=0), enc_size, enc_map, from_units)
        enc_wire = jnp.concatenate(
            [enc_grad.reshape(devices, enc_size, width), small_wire.reshape(devices, 16, width)], axis=1
        )
        dec_summed = lax.psum_scatter(dec_grad, "fsdp", scatter_dimension=0, tiled=True).astype(F32)
        enc_summed = lax.psum_scatter(
            enc_wire.reshape(-1, width), "fsdp", scatter_dimension=0, tiled=True
        ).astype(F32)
    small_summed = enc_summed[enc_size:].reshape(-1)[:held].reshape(-1, share)
    enc_summed = arrange_own(enc_summed[:enc_size], me * enc_size, enc_map, from_units)
    dec_summed = arrange_own(dec_summed, me * dec_size, dec_map, from_units)

    part = 1.0 / devices
    enc_summed = enc_summed * part
    dec_summed = dec_summed * part
    small_summed = small_summed * part
    enc_new, enc_first_new, encoder_second_moment_updated = adamw(
        enc_master, enc_summed, enc_first, enc_second
    )
    dec_new, dec_first_new, dec_second_new = adamw(dec_master, dec_summed, dec_first, dec_second)
    small_first_new, small_second_new = moments(small_summed, small_first, small_second)
    return (
        memory,
        decoded,
        src_grad,
        tgt_grad,
        enc_new,
        enc_first_new,
        encoder_second_moment_updated,
        enc_new.astype(LOW),
        dec_new,
        dec_first_new,
        dec_second_new,
        dec_new.astype(LOW),
        small_summed,
        small_first_new,
        small_second_new,
    )


def solution(mesh):
    rows = P("fsdp", None)
    columns = P(None, "fsdp")
    return jax.shard_map(
        functools.partial(on_device, mesh.shape["fsdp"]),
        mesh=mesh,
        in_specs=(rows,) * 4 + (P("fsdp"),) + (rows,) * 8 + (columns,) * 3,
        out_specs=(rows,) * 12 + (columns,) * 3,
        check_vma=False,
    )
```
